32 devices in a mesh: rows: 8 (over z, x), seq: 4 (over y, core).
Axes of the slice: x: 2, y: 2, z: 4, core: 2. Of those that a mesh axis runs over, the one named last changes fastest.
Arguments:
- tokens: bfloat16 [80, 512, 512], P('rows', 'seq'), may hold values from -6 to 6
- seg_ids: int32 [80, 512], P('rows', 'seq'), may hold values from 0 to 3, as said below
- w_query: bfloat16 [512, 384], replicated, may hold values from -0.25 to 0.25
- w_key: bfloat16 [512, 384], replicated, may hold values from -0.0625 to 0.0625
- w_value: bfloat16 [512, 384], replicated, may hold values from -0.25 to 0.25
- w_out: bfloat16 [384, 512], replicated, may hold values from -2.5 to 2.5
- w_gate: bfloat16 [512, 1024], replicated, may hold values from -0.25 to 0.25
- w_up: bfloat16 [512, 1024], replicated, may hold values from -0.25 to 0.25
- w_down: bfloat16 [1024, 512], replicated, may hold values from -0.1875 to 0.1875
- w_head: bfloat16 [512, 768], replicated, may hold values from -0.25 to 0.25
- norm_attn: float32 [512], replicated, may hold values from 0.5 to 1.5
- norm_ffn: float32 [512], replicated, may hold values from 0.5 to 1.5
- bucket_bias_table: float32 [32, 6], replicated, may hold values from -4 to 4
- grad_y: bfloat16 [80, 512, 512], P('rows', 'seq'), may hold values from -6 to 6
- embedding_gradient: float32 [80, 768], P('rows'), may hold values from -6 to 6
Outputs:
- block_out: bfloat16 [80, 512, 512], P('rows', 'seq')
- embedding: float32 [80, 768], P('rows')
- grad_x: bfloat16 [80, 512, 512], P('rows', 'seq')
- grad_query: float32 [512, 384], replicated
- key_weight_gradient: float32 [512, 384], replicated
- grad_value: float32 [512, 384], replicated
- grad_out: float32 [384, 512], replicated
- grad_gate: float32 [512, 1024], replicated
- grad_up: float32 [512, 1024], replicated
- grad_down: float32 [1024, 512], replicated
- grad_head: float32 [512, 768], replicated
- grad_norm_attn: float32 [512], replicated
- grad_norm_ffn: float32 [512], replicated
- grad_table: float32 [32, 6], replicated
The draws below stay inside these ranges and needn't reach their ends.
Inputs may be any that keep to these rules, and one draw needn't show every extreme that they name: `seg_ids`: each row holds exactly three passages, numbered 1, 2, 3 in order of position, followed by padding (0) at the row's end, possibly none.
All inputs are finite; a program needn't handle non-finite values.
Results may differ from the reference program's by a relative error of at most 0.019.
Values may be sent and summed in bfloat16 or wider, within the bound.
No kernel may reach another device: no remote copies, remote signals or barrier semaphores. Data moves between devices by JAX's collectives and lax.ppermute only.
A program may use at most 192 MiB of HBM per device.

```python
import math
import jax
import jax.numpy as jnp
from jax import lax

D = 512
HEADS = 6
DH = 64
FF = 1024
BUCKETS = 32
OUT = 768
L = 512
ROWS = 80


def draw_seg_ids(key, part):
    key = jax.random.fold_in(key, 7)
    first_key, long_key, pad_key = jax.random.split(key, 3)
    spots = jnp.arange(L, dtype=jnp.int32)[None, :]
    first_len = jax.random.randint(first_key, (ROWS, 1), 1, L // 16 + 1)
    long_len = 3 * L // 4 + jax.random.randint(long_key, (ROWS, 1), 1, L // 8 + 1)
    long_end = first_len + long_len
    rest_len = L - long_end
    pad_len = jax.random.randint(pad_key, (ROWS, 1), 0, rest_len // 2 + 1)
    passage = jnp.where(spots < first_len, 1, jnp.where(spots < long_end, 2, 3))
    return jnp.where(spots >= L - pad_len, 0, passage).astype(jnp.int32)


def block_scale(rng, dims, cuts, low, top_value):
    def one(dim, parts):
        heights = jax.random.uniform(jax.random.fold_in(jax.random.fold_in(rng, 6), dim), (parts,), jnp.float32, low / len(cuts), top_value / len(cuts))
        return jnp.repeat(jnp.exp(heights), dims[dim] // parts).reshape((-1,) + (1,) * (len(dims) - dim - 1))

    gain = one(*cuts[0])
    for cut in cuts[1:]:
        gain = gain * one(*cut)
    return gain


def normal_values(stream_key, extent, width, reach, shards=(), kind=jnp.bfloat16):
    drawn = jax.random.normal(stream_key, extent, jnp.float32) * width
    if len(shards) > 0:
        drawn = block_scale(stream_key, extent, shards, -0.22, 0.18) * drawn
    return jnp.clip(drawn, min=-reach, max=reach).astype(kind)


def setup_inputs(seed: int = 0) -> dict:
    arg_keys = jax.random.split(jax.random.key(seed), 16)
    tokens = normal_values(arg_keys[0], (ROWS, L, D), 1.0, 6.0, ((0, 8), (1, 4)))
    seg_ids = draw_seg_ids(jax.random.fold_in(arg_keys[15], 71), 0)
    w_query = normal_values(arg_keys[2], (D, HEADS * DH), D ** -0.5, 0.25)
    w_key = normal_values(arg_keys[3], (D, HEADS * DH), (16 * D) ** -0.5, 0.0625)
    w_value = normal_values(arg_keys[4], (D, HEADS * DH), D ** -0.5, 0.25)
    w_out = normal_values(arg_keys[5], (HEADS * DH, D), (max(1, HEADS * DH // 64)) ** -0.5, 2.5)
    w_gate = normal_values(arg_keys[6], (D, FF), D ** -0.5, 0.25)
    w_up = normal_values(arg_keys[7], (D, FF), D ** -0.5, 0.25)
    w_down = normal_values(arg_keys[8], (FF, D), FF ** -0.5, 0.1875)
    w_head = normal_values(arg_keys[9], (D, OUT), D ** -0.5, 0.25)
    norm_attn = jnp.clip(1.0 + 0.1 * jax.random.normal(arg_keys[10], (D,), jnp.float32), 0.5, 1.5)
    norm_ffn = jnp.clip(1.0 + 0.1 * jax.random.normal(arg_keys[11], (D,), jnp.float32), 0.5, 1.5)
    bucket_bias_table = normal_values(arg_keys[12], (BUCKETS, HEADS), 1.0, 4.0, (), jnp.float32)
    grad_y = normal_values(arg_keys[13], (ROWS, L, D), 1.0, 6.0, ((0, 8), (1, 4)))
    embedding_gradient = normal_values(arg_keys[14], (ROWS, OUT), 1.0, 6.0, ((0, 8),), jnp.float32)
    return {"tokens": tokens, "seg_ids": seg_ids, "w_query": w_query, "w_key": w_key, "w_value": w_value, "w_out": w_out, "w_gate": w_gate, "w_up": w_up, "w_down": w_down, "w_head": w_head, "norm_attn": norm_attn, "norm_ffn": norm_ffn, "bucket_bias_table": bucket_bias_table, "grad_y": grad_y, "embedding_gradient": embedding_gradient}


EPS = 1e-06
LIMITS = (12, 16, 23, 32, 46, 64, 91)
TOP_PRECISION = lax.Precision.HIGHEST

@jax.custom_vjp
def low(v):
    return lax.optimization_barrier(v.astype(jnp.bfloat16)).astype(jnp.float32)

@jax.custom_vjp
def low_back(v):
    return v

def low_keep(v):
    return (low(v), None)

def low_pass(kept, grad):
    return (grad,)

def back_keep(v):
    return (v, None)

def back_low(kept, grad):
    return (low(grad),)
low.defvjp(low_keep, low_pass)
low_back.defvjp(back_keep, back_low)

def bucket_index(offset):
    distance = jnp.abs(offset)
    far_bucket = 8 + sum(((distance >= threshold).astype(jnp.int32) for threshold in LIMITS))
    near_bucket = jnp.where(distance < 8, distance, far_bucket)
    return near_bucket + 16 * (offset > 0).astype(jnp.int32)

def rms_scale(values, weights):
    inverse = lax.rsqrt(lax.optimization_barrier(jnp.mean(values * values, axis=-1, keepdims=True)) + EPS)
    return values * inverse * weights

def row_block(weights_all, buckets, block_x, block_seg):
    w_query, w_key, w_value, w_out, w_gate, w_up, w_down, w_head, norm_attn, norm_ffn, bucket_bias_table = weights_all
    block_rows = block_x.shape[0]
    num_heads = bucket_bias_table.shape[1]
    normed_one = low(rms_scale(block_x, norm_attn))
    q_rows = low_back(low(jnp.dot(normed_one, w_query, precision=TOP_PRECISION)))
    k_rows = low_back(low(jnp.dot(normed_one, w_key, precision=TOP_PRECISION)))
    v_rows = low_back(low(jnp.dot(normed_one, w_value, precision=TOP_PRECISION)))
    q_heads = q_rows.reshape(block_rows, L, num_heads, -1)
    k_heads = k_rows.reshape(block_rows, L, num_heads, -1)
    v_heads = v_rows.reshape(block_rows, L, num_heads, -1)
    bias_full = jnp.transpose(bucket_bias_table[buckets], (2, 0, 1))
    raw_scores = jnp.einsum('gqhd,gkhd->ghqk', q_heads, k_heads, precision=TOP_PRECISION) + bias_full[None]
    raw_scores = low_back(raw_scores)
    same_seg = block_seg[:, :, None] == block_seg[:, None, :]
    scores = jnp.where(same_seg[:, None], raw_scores, -1000000000.0)
    row_max = lax.optimization_barrier(jnp.max(scores, axis=-1, keepdims=True))
    exp_scores = jnp.exp(scores - row_max)
    prob_low = low(exp_scores / lax.optimization_barrier(jnp.sum(exp_scores, axis=-1, keepdims=True)))
    attended = jnp.einsum('ghqk,gkhd->gqhd', prob_low, v_heads, precision=TOP_PRECISION)
    attended = low_back(low(attended.reshape(block_rows, L, -1)))
    mid_stream = block_x + low_back(jnp.dot(attended, w_out, precision=TOP_PRECISION))
    normed_two = low(rms_scale(mid_stream, norm_ffn))
    gate_pre = low_back(jnp.dot(normed_two, w_gate, precision=TOP_PRECISION))
    up_part = low_back(jnp.dot(normed_two, w_up, precision=TOP_PRECISION))
    hidden = low(jax.nn.gelu(gate_pre, approximate=True) * up_part)
    return mid_stream + low_back(jnp.dot(hidden, w_down, precision=TOP_PRECISION))

def reference(tokens, seg_ids, w_query, w_key, w_value, w_out, w_gate, w_up, w_down, w_head, norm_attn, norm_ffn, bucket_bias_table, grad_y, embedding_gradient):
    params = (w_query.astype(jnp.float32), w_key.astype(jnp.float32), w_value.astype(jnp.float32), w_out.astype(jnp.float32), w_gate.astype(jnp.float32), w_up.astype(jnp.float32), w_down.astype(jnp.float32), w_head.astype(jnp.float32), norm_attn, norm_ffn, bucket_bias_table)
    group_rows = math.gcd(ROWS, 8)
    positions = jnp.arange(L, dtype=jnp.int32)
    buckets = bucket_index(positions[None, :] - positions[:, None])
    valid_mask = (seg_ids != 0).astype(jnp.float32)
    counts = lax.optimization_barrier(jnp.sum(valid_mask, axis=1))

    def forward(weights_all, x_float):

        def one_group(pair):
            return row_block(weights_all, buckets, pair[0], pair[1])
        grouped = (x_float.reshape(-1, group_rows, L, D), seg_ids.reshape(-1, group_rows, L))
        out_float = lax.map(jax.checkpoint(one_group), grouped).reshape(ROWS, L, D)
        pooled = lax.optimization_barrier(jnp.sum(out_float * valid_mask[:, :, None], axis=1)) / counts[:, None]
        projected = jnp.dot(pooled, weights_all[7], precision=TOP_PRECISION)
        embedding = projected * lax.rsqrt(lax.optimization_barrier(jnp.sum(projected * projected, axis=-1, keepdims=True)) + EPS)
        return (out_float, embedding)
    (out_float, embedding), pull = jax.vjp(forward, params, tokens.astype(jnp.float32))
    grads, grad_x = pull((grad_y.astype(jnp.float32), embedding_gradient))
    return (out_float.astype(jnp.bfloat16), embedding, grad_x.astype(jnp.bfloat16), grads[0], grads[1], grads[2], grads[3], grads[4], grads[5], grads[6], grads[7], grads[8], grads[9], grads[10])
```

```python
import functools

import jax
import jax.numpy as jnp
from jax import lax
from jax.experimental import pallas as pl
from jax.experimental.pallas import tpu as pltpu
from jax.sharding import PartitionSpec as P

EPS = 1e-06
LIMITS = (12, 16, 23, 32, 46, 64, 91)
TOP_PRECISION = lax.Precision.HIGHEST
F32 = jnp.float32
BF16 = jnp.bfloat16
MASK_STEP = 2.0**30
VMEM = pl.BlockSpec(memory_space=pltpu.VMEM)
SMEM = pl.BlockSpec(memory_space=pltpu.SMEM)
PARAMS = pltpu.CompilerParams(vmem_limit_bytes=56 * 2**20)
LANES = 128


def mm(a, b):
    return lax.dot_general(a, b, (((1,), (0,)), ((), ())), preferred_element_type=F32)


def mm_nt(a, b):
    return lax.dot_general(a, b, (((1,), (1,)), ((), ())), preferred_element_type=F32)


def bucket_index(offset):
    distance = jnp.abs(offset)
    far_bucket = 8 + sum(((distance >= threshold).astype(jnp.int32) for threshold in LIMITS))
    near_bucket = jnp.where(distance < 8, distance, far_bucket)
    return near_bucket + 16 * (offset > 0).astype(jnp.int32)


def parts3(v):
    hi = v.astype(BF16).astype(F32)
    mid = (v - hi).astype(BF16).astype(F32)
    low = (v - hi - mid).astype(BF16).astype(F32)
    row = lax.broadcasted_iota(jnp.int32, v.shape, 0)
    return jnp.where(row == 0, hi, jnp.where(row == 1, mid, jnp.where(row == 2, low, 0.0))).astype(BF16)


def wide_dot(row, mat, dot):
    out = dot(parts3(jnp.broadcast_to(row, (16, row.shape[1]))), mat)
    return jnp.sum(out, axis=0, keepdims=True)


def diagonal_sums(table):
    height, width = table.shape
    acc = table[0:8, :]
    for u in range(8, height, 8):
        acc += pltpu.roll(table[u : u + 8, :], width - u, 1)
    row = lax.broadcasted_iota(jnp.int32, acc.shape, 0)
    for bit in (1, 2, 4):
        acc = jnp.where((row & bit) != 0, pltpu.roll(acc, width - bit, 1), acc)
    return jnp.sum(acc, axis=0, keepdims=True)


def bias_kernel(g_ref, t_ref):
    heads, _, width = t_ref.shape
    for h in range(heads):
        line = jnp.broadcast_to(g_ref[h : h + 1, :], (LANES, width))
        t_ref[h] = pltpu.roll(line, 0, 1, stride=1, stride_axis=0)


def forward_kernel(
    slot, n,
    meta, x0, x1, x2, x3, bias, wqkv_t, wout_t, wg_t, wu_t, wd_t, nattn, nffn,
    q_o, v_o, kt_o, p_o, att_o, x_o, mid_o, a_o, ge_o, hid_o, pooled_o, b0, b1, b2, b3,
    seg, n1, kk, tok,
):
    width = wqkv_t.shape[1]
    inner = wout_t.shape[1]
    heads = bias.shape[0]
    head = inner // heads
    span = x0.shape[0] - 16
    length = n * span

    @pl.when(meta[1 + slot] == 1)
    def _():
        me = meta[0]
        for k, piece in enumerate((x0, x1, x2, x3)):
            at = pl.multiple_of((me ^ k) * span, span)
            tok[pl.ds(at, span), :] = piece[:span, :].astype(F32)
            seg[:, pl.ds(at, span)] = jnp.broadcast_to(piece[span : span + 1, :span].astype(F32), (LANES, span))
        for c in range(n):
            blk = tok[c * span : (c + 1) * span, :].T
            x_o[:, c * span : (c + 1) * span] = blk.astype(BF16)
            inv = lax.rsqrt(jnp.mean(blk * blk, axis=0, keepdims=True) + EPS)
            n1[:, c * span : (c + 1) * span] = (blk * inv * nattn[...]).astype(BF16)
        ids = lax.broadcasted_iota(jnp.int32, (LANES, length), 0).astype(F32)
        one = (seg[...] == ids).astype(F32)
        q_aug = one.astype(BF16)
        k_aug = ((one - 1.0) * MASK_STEP).T.astype(BF16)
        qt = mm(wqkv_t[:inner, :], n1[...]).astype(BF16)
        kt = mm(wqkv_t[inner : 2 * inner, :], n1[...])
        vt = mm(wqkv_t[2 * inner :, :], n1[...])
        kt_o[...] = kt.astype(BF16)
        q_o[...] = qt.astype(F32).T.astype(BF16)
        v_o[...] = vt.T.astype(BF16)
        k_nat = kt.T.astype(BF16)
        vt = vt.astype(BF16)
        for pair in range(heads // 2):
            kk[pair, :, :LANES] = k_nat[:, pair * LANES : (pair + 1) * LANES]
            kk[pair, :, LANES:] = k_aug
        half = length // 2
        zeros = jnp.zeros((head, half), BF16)
        for h in range(heads):
            for qc in range(2):
                qs = slice(qc * half, (qc + 1) * half)
                q_h = qt[h * head : (h + 1) * head, qs]
                rhs = jnp.concatenate([q_h, zeros, q_aug[:, qs]] if h % 2 == 0 else [zeros, q_h, q_aug[:, qs]], axis=0)
                s = []
                top = None
                for a in range(n):
                    start = (n - 1 - a) * LANES + qc * half
                    s_a = mm(kk[h // 2, a * LANES : (a + 1) * LANES, :], rhs) + bias[h, :, start : start + half]
                    s.append(s_a)
                    m_a = jnp.max(s_a, axis=0, keepdims=True)
                    top = m_a if top is None else jnp.maximum(top, m_a)
                e = [jnp.exp(s_a - top) for s_a in s]
                total = sum(jnp.sum(e_a, axis=0, keepdims=True) for e_a in e)
                scale = 1.0 / total
                for a in range(n):
                    p_o[h, a * LANES : (a + 1) * LANES, qs] = (e[a] * scale).astype(BF16)
                att_o[h * head : (h + 1) * head, qs] = mm(
                    vt[h * head : (h + 1) * head, :], p_o[h, :, qs]
                ).astype(BF16)
        mid_o[...] = x_o[...].astype(F32) + mm(wout_t[...], att_o[...])
        for c in range(n):
            blk = mid_o[:, c * span : (c + 1) * span]
            inv = lax.rsqrt(jnp.mean(blk * blk, axis=0, keepdims=True) + EPS)
            n1[:, c * span : (c + 1) * span] = (blk * inv * nffn[...]).astype(BF16)
        ff = wg_t.shape[0]
        step = 256
        for c in range(ff // step):
            cs = slice(c * step, (c + 1) * step)
            gate = mm(wg_t[cs, :], n1[...])
            up = mm(wu_t[cs, :], n1[...])
            sq = gate * gate
            th = jnp.tanh(0.7978845608028654 * gate * (1.0 + 0.044715 * sq))
            half_th = 0.5 * (1.0 + th)
            gelu = gate * half_th
            slope = half_th + (0.5 * 0.7978845608028654) * gate * (1.0 - th * th) * (1.0 + (3 * 0.044715) * sq)
            hid_o[cs, :] = (gelu * up).astype(BF16)
            a_o[cs, :] = (up * slope).astype(BF16)
            ge_o[cs, :] = gelu.astype(BF16)
        tok[...] = mid_o[...] + mm(wd_t[...], hid_o[...])
        valid = (seg[0:1, :] != 0.0).astype(F32)
        count = jnp.sum(valid, axis=1, keepdims=True)
        part = None
        for c in range(n):
            blk = tok[:, c * span : (c + 1) * span] * valid[:, c * span : (c + 1) * span]
            part = blk if part is None else part + blk
        pooled = jnp.sum(part.T, axis=0, keepdims=True) / count
        pooled_o[...] = jnp.broadcast_to(pooled, pooled_o.shape)
        for k, out in enumerate((b0, b1, b2, b3)):
            at = pl.multiple_of((me ^ k) * span, span)
            out[...] = tok[:, pl.ds(at, span)].T.astype(BF16)


def middle_kernel(
    slot, n,
    meta, g0, g1, g2, g3, x0, x1, x2, x3, eg, pooled, mid, a_in, ge_in, w_head, w_down, w_gate, w_up, w_out, nffn,
    n2_o, gb_o, gg_o, gu_o, ga_o, gatt_o, gnf_o, emb_o, pg_o,
    tok, seg,
):
    span = g0.shape[0]
    width = g0.shape[1]

    @pl.when(meta[1 + slot] == 1)
    def _():
        me = meta[0]
        for k, (piece, xp) in enumerate(zip((g0, g1, g2, g3), (x0, x1, x2, x3))):
            at = pl.multiple_of((me ^ k) * span, span)
            tok[pl.ds(at, span), :] = piece[...].astype(F32)
            seg[:, pl.ds(at, span)] = jnp.broadcast_to(xp[span : span + 1, :span].astype(F32), (8, span))
        valid = (seg[0:1, :] != 0.0).astype(F32)
        count = jnp.sum(valid, axis=1, keepdims=True)
        pool = pooled[0:1, :]
        proj = wide_dot(pool, w_head[...], mm)
        inv = lax.rsqrt(jnp.sum(proj * proj, axis=1, keepdims=True) + EPS)
        emb = proj * inv
        cot = eg[pl.ds(meta[4] + slot, 1), :]
        g_proj = inv * (cot - emb * jnp.sum(emb * cot, axis=1, keepdims=True))
        emb_o[...] = jnp.broadcast_to(emb, emb_o.shape)
        pg_o[:, :width] = jnp.broadcast_to(pool, (8, width))
        pg_o[:, width:] = jnp.broadcast_to(g_proj, (8, g_proj.shape[1]))
        g_pool = wide_dot(g_proj, w_head[...], mm_nt) / count
        g_col = jnp.broadcast_to(g_pool, (span, width)).T
        gout = []
        for c in range(n):
            cs = slice(c * span, (c + 1) * span)
            blk = tok[cs, :].T + valid[:, cs] * g_col
            gout.append(blk)
            gb_o[:, cs] = blk.astype(BF16)
        ff = w_down.shape[0]
        step = 256
        for c in range(ff // step):
            cs = slice(c * step, (c + 1) * step)
            g_hid = mm(w_down[cs, :], gb_o[...])
            gg_o[cs, :] = (g_hid * a_in[cs, :].astype(F32)).astype(BF16)
            gu_o[cs, :] = (g_hid * ge_in[cs, :].astype(F32)).astype(BF16)
        tok[...] = mm(w_gate[...], gg_o[...]) + mm(w_up[...], gu_o[...])
        part = None
        for c in range(n):
            cs = slice(c * span, (c + 1) * span)
            m = mid[:, cs]
            inv2 = lax.rsqrt(jnp.mean(m * m, axis=0, keepdims=True) + EPS)
            hat = m * inv2
            n2_o[:, cs] = (hat * nffn[...]).astype(BF16)
            gn = tok[:, cs]
            c2 = gn * nffn[...]
            part = gn * hat if part is None else part + gn * hat
            mean = jnp.mean(c2 * hat, axis=0, keepdims=True)
            ga_o[:, cs] = (gout[c] + inv2 * (c2 - hat * mean)).astype(BF16)
        gnf_o[...] = jnp.broadcast_to(jnp.sum(part.T, axis=0, keepdims=True), gnf_o.shape)
        gatt_o[...] = mm(w_out[...], ga_o[...]).astype(BF16)


def early_grads_kernel(last, meta, *refs):
    slots = [refs[i * 7 : (i + 1) * 7] for i in range(3)]
    out, acc = refs[21], refs[22]
    ff = slots[0][0].shape[0]
    width = slots[0][1].shape[0]
    inner = slots[0][5].shape[0]
    pieces = []
    for c in range(2):
        pieces.append((c * 512, 512, lambda s, c=c: (s[2][...], s[3][c * 512 : (c + 1) * 512, :])))
    for c in range(2):
        pieces.append((ff + c * 512, 512, lambda s, c=c: (s[2][...], s[4][c * 512 : (c + 1) * 512, :])))
    for c in range(2):
        pieces.append((2 * ff + c * width, width, lambda s, c=c: (s[0][c * width : (c + 1) * width, :], s[1][...])))
    pieces.append((2 * ff + 2 * width, inner, lambda s: (s[6][...], s[5][...])))
    for at, size, get in pieces:
        acc[:, at : at + size] = mm_nt(*get(slots[0])) + mm_nt(*get(slots[1]))

    @pl.when(meta[1 + last] == 1)
    def _():
        for at, size, get in pieces:
            acc[:, at : at + size] += mm_nt(*get(slots[2]))

    out[...] = acc[...].astype(BF16)


def backward_kernel(
    slot, n,
    meta, q_nat, v_nat, kt, p_in, att, xt, gatt, ga, w_qkv, nattn,
    n1_o, gqkv_o, line_o, gna_o, o0, o1, o2, o3,
    gs, table, tok,
):
    heads = p_in.shape[0]
    inner = kt.shape[0]
    head = inner // heads
    length = kt.shape[1]
    span = length // n
    lane = lax.broadcasted_iota(jnp.int32, (length, LANES), 1)

    @pl.when(meta[1 + slot] == 1)
    def _():
        me = meta[0]
        gatt_nat = gatt[...].astype(F32).T.astype(BF16)
        zeros = jnp.zeros((head, length), BF16)
        for pair in range(heads // 2):
            ps = slice(pair * LANES, (pair + 1) * LANES)
            gk = []
            gv = []
            for side in range(2):
                h = pair * 2 + side
                hs = slice(h * head, (h + 1) * head)
                g_h = gatt[hs, :]
                delta = jnp.sum(g_h.astype(F32) * att[hs, :].astype(F32), axis=0, keepdims=True)
                rhs = jnp.concatenate([g_h, zeros] if side == 0 else [zeros, g_h], axis=0)
                table[...] = jnp.zeros_like(table)
                for a in range(n):
                    ks = slice(a * LANES, (a + 1) * LANES)
                    g_p = mm(v_nat[ks, ps], rhs)
                    g_s = (p_in[h, ks, :].astype(F32) * (g_p - delta)).astype(BF16)
                    gs[ks, :] = g_s
                    start = (n - 1 - a) * LANES
                    table[:, start : start + length] += g_s.astype(F32)
                line_o[h : h + 1, :] = diagonal_sums(table)
                gqkv_o[hs, :] = mm(kt[hs, :], gs[...]).astype(BF16)
                gk.append(mm(gs[...], q_nat[:, ps]))
                gv.append(mm(p_in[h], gatt_nat[:, ps]))
            gk = jnp.where(lane < head, gk[0], gk[1])
            gv = jnp.where(lane < head, gv[0], gv[1])
            gqkv_o[inner + pair * LANES : inner + (pair + 1) * LANES, :] = gk.T.astype(BF16)
            gqkv_o[2 * inner + pair * LANES : 2 * inner + (pair + 1) * LANES, :] = gv.T.astype(BF16)
        tok[...] = mm(w_qkv[...], gqkv_o[...])
        part = None
        for c in range(n):
            cs = slice(c * span, (c + 1) * span)
            x = xt[:, cs].astype(F32)
            inv = lax.rsqrt(jnp.mean(x * x, axis=0, keepdims=True) + EPS)
            hat = x * inv
            n1_o[:, cs] = (hat * nattn[...]).astype(BF16)
            gn = tok[:, cs]
            c1 = gn * nattn[...]
            part = gn * hat if part is None else part + gn * hat
            mean = jnp.mean(c1 * hat, axis=0, keepdims=True)
            tok[:, cs] = ga[:, cs].astype(F32) + inv * (c1 - hat * mean)
        gna_o[...] = jnp.broadcast_to(jnp.sum(part.T, axis=0, keepdims=True), gna_o.shape)
        for k, out in enumerate((o0, o1, o2, o3)):
            at = pl.multiple_of((me ^ k) * span, span)
            out[...] = tok[:, pl.ds(at, span)].T.astype(BF16)


def late_grads_kernel(last, meta, n1_0, g_0, n1_1, g_1, n1_2, g_2, out, acc):
    acc[...] = mm_nt(n1_0[...], g_0[...]) + mm_nt(n1_1[...], g_1[...])

    @pl.when(meta[1 + last] == 1)
    def _():
        acc[...] += mm_nt(n1_2[...], g_2[...])

    out[...] = acc[...].astype(BF16)


def call(kernel, outs, args, scratch=(), flops=0, name=None):
    specs = [SMEM if i == 0 else VMEM for i in range(len(args))]
    return pl.pallas_call(
        kernel,
        out_shape=outs,
        in_specs=specs,
        out_specs=jax.tree.map(lambda _: VMEM, outs),
        scratch_shapes=list(scratch),
        compiler_params=PARAMS,
        cost_estimate=pl.CostEstimate(flops=flops, bytes_accessed=10_000_000, transcendentals=0),
        name=name,
    )(*args)


def sds(shape, dtype=BF16):
    return jax.ShapeDtypeStruct(shape, dtype)


def swap(x, axis, k, keep=None):
    n = lax.axis_size(axis)
    return lax.ppermute(x, axis, [(i, i ^ k) for i in range(n) if keep is None or keep(i ^ k)])


def radices(n):
    out = []
    stride = 1
    while stride < n:
        r = 2 if stride == 1 or n // stride < 4 else 4
        out.append((stride, r))
        stride *= r
    return out


def steps_of(order):
    seq = [("seq", s, 2) for s in (1, 2)]
    rows = [("rows", s, r) for s, r in radices(lax.axis_size("rows"))]
    first, rest = rows[0], rows[1:]
    if order == "xy":
        return [seq[0], first, seq[1]] + rest
    return [seq[0], seq[1], first] + rest


def digit(axis, stride, radix):
    return (lax.axis_index(axis) // stride) % radix


def scatter_step(v, axis, stride, radix):
    d = digit(axis, stride, radix)
    total = lax.dynamic_index_in_dim(v, d, 0, keepdims=False).astype(F32)
    for k in range(1, radix):
        part = lax.dynamic_index_in_dim(v, d ^ k, 0, keepdims=False)
        total += swap(part, axis, k * stride).astype(F32)
    return total.astype(BF16)


def gather_step(v, axis, stride, radix):
    d = digit(axis, stride, radix)
    at = lax.broadcasted_iota(jnp.int32, (radix,) + (1,) * v.ndim, 0)
    out = jnp.broadcast_to(v[None], (radix,) + v.shape)
    for k in range(1, radix):
        got = swap(v, axis, k * stride)
        out = jnp.where(at == (d ^ k), got[None], out)
    return out


def sum_all(g, order):
    steps = steps_of(order)
    rows, width = g.shape
    blocks = 1
    for _, _, r in steps:
        blocks *= r
    v = g.reshape(tuple(r for _, _, r in steps) + (rows // blocks, width))
    for s in steps:
        v = scatter_step(v, *s)
    for s in steps[::-1]:
        v = gather_step(v, *s)
    return v.reshape(rows, width)


def shards(
    tokens, seg_ids, w_query, w_key, w_value, w_out, w_gate, w_up, w_down, w_head, norm_attn, norm_ffn,
    bucket_bias_table, grad_y, embedding_gradient,
):
    rows, span, width = tokens.shape
    heads = bucket_bias_table.shape[1]
    buckets = bucket_bias_table.shape[0]
    n = lax.axis_size("seq")
    inner = w_query.shape[1]
    ff = w_gate.shape[1]
    wide = w_head.shape[1]
    length = n * span
    starts = [-(-s * rows // n) for s in range(n + 1)]
    counts = [starts[s + 1] - starts[s] for s in range(n)]
    slots = max(counts)
    assert slots == 3 and min(counts) == 2
    me = lax.axis_index("seq")
    starts_arr = jnp.array(starts[:n], jnp.int32)
    counts_arr = jnp.array(counts, jnp.int32)
    reals = [(counts_arr[me] > j).astype(jnp.int32) for j in range(slots)]
    meta = jnp.stack([me, *reals, starts_arr[me], 0, 0, 0]).astype(jnp.int32)

    seg_low = jnp.pad(seg_ids.astype(BF16)[:, None, :], ((0, 0), (0, 15), (0, width - span)))
    ext = jnp.concatenate([tokens, seg_low], axis=1)

    def spread(array, j):
        out = []
        for k in range(n):
            row = jnp.minimum(starts_arr[me ^ k] + j, rows - 1)
            piece = lax.dynamic_index_in_dim(array, row, 0, keepdims=False)
            out.append(piece if k == 0 else swap(piece, "seq", k, lambda d: counts[d] > j))
        return out

    def collect(pieces):
        got = [
            [p if k == 0 else lax.ppermute(p, "seq", [(i, i ^ k) for i in range(n) if counts[i] > j]) for k, p in enumerate(ps)]
            for j, ps in enumerate(pieces)
        ]
        out = []
        for s in range(n):
            for j in range(counts[s]):
                val = got[j][0]
                for k in range(1, n):
                    val = jnp.where(me == (s ^ k), got[j][k], val)
                out.append(val)
        return jnp.stack(out)

    xs = [spread(ext, j) for j in range(slots)]
    gys = [spread(grad_y, j) for j in range(slots)]

    w_qkv = jnp.concatenate([w_query, w_key, w_value], axis=1)
    wqkv_t, wout_t, wg_t, wu_t, wd_t = w_qkv.T, w_out.T, w_gate.T, w_up.T, w_down.T
    nattn = jnp.broadcast_to(norm_attn[:, None], (width, LANES))
    nffn = jnp.broadcast_to(norm_ffn[:, None], (width, LANES))
    line = 2 * length
    col = jnp.arange(line, dtype=jnp.int32)
    offset = length - span - jnp.where(col < line - span, col, col - line)
    indicator = (bucket_index(offset)[None, :] == jnp.arange(buckets, dtype=jnp.int32)[:, None]).astype(F32)
    lines = jnp.einsum("th,tc->hc", bucket_bias_table, indicator, precision=TOP_PRECISION)
    lines = jnp.pad(lines, ((0, 8 - heads), (0, 0)))
    bias = pl.pallas_call(
        bias_kernel, out_shape=sds((heads, LANES, line), F32), in_specs=[VMEM], out_specs=VMEM, compiler_params=PARAMS,
        name="bias",
    )(lines)

    fwd = []
    for j in range(slots):
        outs = (
            sds((length, inner)), sds((length, inner)), sds((inner, length)), sds((heads, length, length)),
            sds((inner, length)), sds((width, length)), sds((width, length), F32), sds((ff, length)), sds((ff, length)),
            sds((ff, length)), sds((8, width), F32), *[sds((span, width))] * 4,
        )
        scratch = (
            pltpu.VMEM((LANES, length), F32), pltpu.VMEM((width, length), BF16),
            pltpu.VMEM((heads // 2, length, 2 * LANES), BF16), pltpu.VMEM((length, width), F32),
        )
        fwd.append(
            call(
                functools.partial(forward_kernel, j, n), outs,
                (meta, *xs[j], bias, wqkv_t, wout_t, wg_t, wu_t, wd_t, nattn, nffn), scratch, 4_000_000_000, "forward",
            )
        )
    block_out = collect([f[11:15] for f in fwd])

    mids = []
    for j in range(slots):
        outs = (
            sds((width, length)), sds((width, length)), sds((ff, length)), sds((ff, length)), sds((width, length)),
            sds((inner, length)), sds((8, width), F32), sds((8, wide), F32), sds((8, width + wide), F32),
        )
        scratch = (pltpu.VMEM((length, width), F32), pltpu.VMEM((8, length), F32))
        f = fwd[j]
        mids.append(
            call(
                functools.partial(middle_kernel, j, n), outs,
                (meta, *gys[j], *xs[j], embedding_gradient, f[10], f[6], f[7], f[8], w_head, w_down, w_gate, w_up, w_out, nffn),
                scratch, 3_000_000_000, "middle",
            )
        )

    packed_w = 2 * ff + 2 * width + inner
    args = [meta]
    for f, m in zip(fwd, mids):
        args += [f[9], m[1], m[0], m[2], m[3], f[4], m[4]]
    early = call(
        functools.partial(early_grads_kernel, slots - 1), sds((width, packed_w)), args,
        [pltpu.VMEM((width, packed_w), F32)], 6_000_000_000, "early_grads",
    )
    half = (packed_w // 2 // LANES) * LANES
    sums_a = sum_all(early[:, :half], "xy")
    sums_b = sum_all(early[:, half:], "yx")

    back = []
    for j in range(slots):
        outs = (
            sds((width, length)), sds((3 * inner, length)), sds((8, line), F32), sds((8, width), F32),
            *[sds((span, width))] * 4,
        )
        scratch = (pltpu.VMEM((length, length), BF16), pltpu.VMEM((LANES, line), F32), pltpu.VMEM((width, length), F32))
        f, m = fwd[j], mids[j]
        back.append(
            call(
                functools.partial(backward_kernel, j, n), outs,
                (meta, f[0], f[1], f[2], f[3], f[4], f[5], m[5], m[4], w_qkv, nattn), scratch, 4_000_000_000, "backward",
            )
        )
    grad_x = collect([b[4:8] for b in back])
    args = [meta]
    for b in back:
        args += [b[0], b[1]]
    late = call(
        functools.partial(late_grads_kernel, slots - 1), sds((width, 3 * inner)), args,
        [pltpu.VMEM((width, 3 * inner), F32)], 2_000_000_000, "late_grads",
    )

    def total(parts):
        return sum(jnp.where(reals[j] == 1, p, 0.0) for j, p in enumerate(parts))

    gnf = total([m[6][0] for m in mids])
    gna = total([b[3][0] for b in back])
    table_lines = total([b[2][:heads] for b in back])
    table = jnp.einsum("tc,hc->th", indicator, table_lines, precision=TOP_PRECISION)
    small = jnp.concatenate([gnf, gna, table.reshape(-1)])
    small = lax.psum(small, ("rows", "seq"))
    grad_norm_ffn, grad_norm_attn = small[:width], small[width : 2 * width]
    grad_table = small[2 * width :].reshape(buckets, heads)
    sums_c = sum_all(late, "xy")

    emb = jnp.stack([m[7][0] for m in mids])
    emb_all = lax.all_gather(emb, "seq", axis=0)
    embedding = jnp.stack([emb_all[s, j] for s in range(n) for j in range(counts[s])])
    pg = jnp.stack([jnp.where(reals[j] == 1, m[8][0], 0.0) for j, m in enumerate(mids)]).astype(BF16)
    pg_all = lax.all_gather(pg, ("rows", "seq"), axis=0, tiled=True)
    grad_head = lax.dot_general(
        pg_all[:, :width], pg_all[:, width:], (((0,), (0,)), ((), ())), preferred_element_type=F32
    )

    sums = jnp.concatenate([sums_a, sums_b], axis=1).astype(F32)
    grad_gate = sums[:, :ff]
    grad_up = sums[:, ff : 2 * ff]
    grad_down = jnp.concatenate([sums[:, 2 * ff : 2 * ff + width], sums[:, 2 * ff + width : 2 * ff + 2 * width]], axis=0)
    grad_out = sums[:, 2 * ff + 2 * width :].T
    qkv = sums_c.astype(F32)
    return (
        block_out, embedding, grad_x, qkv[:, :inner], qkv[:, inner : 2 * inner], qkv[:, 2 * inner :], grad_out,
        grad_gate, grad_up, grad_down, grad_head, grad_norm_attn, grad_norm_ffn, grad_table,
    )


def solution(mesh):
    by_pos = P("rows", "seq", None)
    by_row = P("rows", None)
    return jax.shard_map(
        shards,
        mesh=mesh,
        in_specs=(by_pos, P("rows", "seq"), *[P()] * 11, by_pos, by_row),
        out_specs=(by_pos, by_row, by_pos, *[P()] * 11),
        check_vma=False,
    )
```

```python
import functools

import jax
import jax.numpy as jnp
from jax import lax
from jax.experimental import pallas as pl
from jax.experimental.pallas import tpu as pltpu
from jax.sharding import PartitionSpec as P

EPS = 1e-06
LIMITS = (12, 16, 23, 32, 46, 64, 91)
TOP_PRECISION = lax.Precision.HIGHEST
F32 = jnp.float32
BF16 = jnp.bfloat16
MASK_STEP = 2.0**30
LOG2E = 1.4426950408889634
VMEM = pl.BlockSpec(memory_space=pltpu.VMEM)
ANY = pl.BlockSpec(memory_space=pl.ANY)
LANES = 128
EXT = 16


def mm(a, b):
    return lax.dot_general(a, b, (((1,), (0,)), ((), ())), preferred_element_type=F32)


def mm_nt(a, b):
    return lax.dot_general(a, b, (((1,), (1,)), ((), ())), preferred_element_type=F32)


def bucket_index(offset):
    distance = jnp.abs(offset)
    far_bucket = 8 + sum(((distance >= threshold).astype(jnp.int32) for threshold in LIMITS))
    near_bucket = jnp.where(distance < 8, distance, far_bucket)
    return near_bucket + 16 * (offset > 0).astype(jnp.int32)


def parts3(v):
    hi = v.astype(BF16).astype(F32)
    mid = (v - hi).astype(BF16).astype(F32)
    low = (v - hi - mid).astype(BF16).astype(F32)
    row = lax.broadcasted_iota(jnp.int32, v.shape, 0)
    return jnp.where(row == 0, hi, jnp.where(row == 1, mid, jnp.where(row == 2, low, 0.0))).astype(BF16)


def wide_dot(row, mat, dot):
    out = dot(parts3(jnp.broadcast_to(row, (16, row.shape[1]))), mat)
    return jnp.sum(out, axis=0, keepdims=True)


def fold(x, op):
    while x.shape[0] > 8:
        half = x.shape[0] // 2
        x = op(x[:half], x[half:])
    return x


def col_sum(x):
    return jnp.sum(fold(x, jnp.add), axis=0, keepdims=True)


def diagonal_sums(table):
    height, width = table.shape
    acc = table[0:8, :]
    for u in range(8, height, 8):
        acc += pltpu.roll(table[u : u + 8, :], width - u, 1)
    row = lax.broadcasted_iota(jnp.int32, acc.shape, 0)
    for bit in (1, 2, 4):
        acc = jnp.where((row & bit) != 0, pltpu.roll(acc, width - bit, 1), acc)
    return jnp.sum(acc, axis=0, keepdims=True)


def position():
    me = lax.axis_index("seq")
    return me, me // 2, me % 2


class Copies:
    def __init__(self, sems):
        self.sems = sems
        self.used = 0

    def start(self, src, dst):
        copy = pltpu.make_async_copy(src, dst, self.sems.at[self.used])
        self.used += 1
        copy.start()
        return copy


def pack_kernel(per, slots, ext, *refs):
    if ext:
        tok, seg, *outs = refs
    else:
        tok, *outs = refs
    span = tok.shape[1]
    _, p, c = position()

    def put(out, row):
        out[:span, :] = tok[row]
        if ext:
            ids = jnp.broadcast_to(seg[pl.ds(row, 1), :].astype(F32), (ext, span))
            out[span:, :span] = ids.astype(BF16)

    for i, j in enumerate(slots):
        y, cc = outs[2 * i : 2 * i + 2]
        if j == 2:
            put(y, per * (1 - p) + per - 1)
            put(cc, per * p + per - 1)
        else:
            put(y.at[0], per * (1 - p) + 2 * c + j)
            put(y.at[1], per * (1 - p) + 2 * (1 - c) + j)
            put(cc, per * p + 2 * (1 - c) + j)


def prepare_kernel(
    n, table, norm_a, norm_f, wq, wk, wv, wo, wg, wu, wd,
    bias_o, ind_o, na_o, nf_o, wqkv_o, wqkv_t, wo_t, wg_t, wu_t, wd_t,
):
    heads, _, line = bias_o.shape
    inner = wq.shape[1]
    length = line // 2
    col = lax.broadcasted_iota(jnp.int32, (LANES, line), 1)
    offset = length - LANES - jnp.where(col < line - LANES, col, col - line)
    ind = (bucket_index(offset) == lax.broadcasted_iota(jnp.int32, (LANES, line), 0)).astype(F32).astype(BF16)
    ind_o[...] = ind
    rest = table[...]
    lines = None
    for _ in range(3):
        part = rest.astype(BF16)
        rest = rest - part.astype(F32)
        term = mm(part, ind)
        lines = term if lines is None else lines + term
    lines = lines * LOG2E
    for h in range(heads):
        bias_o[h] = pltpu.roll(jnp.broadcast_to(lines[h : h + 1, :], (LANES, line)), 0, 1, stride=1, stride_axis=0)
    for src, dst in ((norm_a, na_o), (norm_f, nf_o)):
        dst[...] = jnp.broadcast_to(src[...], (LANES, src.shape[1])).T
    for i, w in enumerate((wq, wk, wv)):
        wqkv_o[:, i * inner : (i + 1) * inner] = w[...]
        wqkv_t[i * inner : (i + 1) * inner, :] = w[...].astype(F32).T.astype(BF16)
    for src, dst in ((wo, wo_t), (wg, wg_t), (wu, wu_t), (wd, wd_t)):
        dst[...] = src[...].astype(F32).T.astype(BF16)


def norm_into(out, at, blk, gain):
    inv = lax.rsqrt(col_sum(blk * blk) / blk.shape[0] + EPS)
    out[:, at : at + blk.shape[1]] = (blk * inv * gain).astype(BF16)


def forward_slot(half, n, rows, bufs, w, wait, outs, copies):
    own, c1, y, c2, own_seg = rows
    tok, seg, n1, kk, va, x_b, bias_ready = bufs
    bias, wqkv_t, wout_t, wg_t, wu_t, wd_t, nattn, nffn = w
    o = outs
    width = wqkv_t.shape[1]
    inner = wout_t.shape[1]
    heads = bias.shape[0]
    head = inner // heads
    span = own.shape[0]
    length = n * span
    me, p, c = position()
    for k, (piece, ids) in enumerate(((own, own_seg), (c1, None), (y, None), (c2, None))):
        at = pl.multiple_of((me ^ k) * span, span)
        tok[pl.ds(at, span), :] = piece[:span, :].astype(F32)
        ids = piece[span : span + 1, :span].astype(F32) if ids is None else ids
        seg[:, pl.ds(at, span)] = jnp.broadcast_to(ids, (LANES, span))
    for b in range(n):
        blk = tok[b * span : (b + 1) * span, :].T
        x_b[:, b * span : (b + 1) * span] = blk.astype(BF16)
        norm_into(n1, b * span, blk, nattn[...])
    nq = length // 2 if half else length
    if half:
        mine = pl.ds(pl.multiple_of(c * nq, nq), nq)
        o["x"][...] = x_b[:, mine]
    else:
        mine = slice(0, nq)
        o["x"][...] = x_b[...]
    ids = lax.broadcasted_iota(jnp.int32, (LANES, length), 0).astype(F32)
    one = (seg[...] == ids).astype(F32)
    o["seg"][...] = seg[0:8, :]
    k_aug = ((one - 1.0) * MASK_STEP).T.astype(BF16)
    ids = lax.broadcasted_iota(jnp.int32, (LANES, nq), 0).astype(F32)
    q_aug = (seg[:, mine] == ids).astype(BF16)
    wait("qkv")
    qt = mm(wqkv_t[:inner, :], n1[:, mine]).astype(BF16).astype(F32)
    kt = mm(wqkv_t[inner : 2 * inner, :], n1[...])
    vt = mm(wqkv_t[2 * inner :, :], n1[...])
    o["kt"][...] = kt.astype(BF16)
    o["q"][...] = qt.T.astype(BF16)
    o["v"][...] = vt.T.astype(BF16)
    copies(o["kt"], o["q"], o["v"], o["x"], o["seg"])
    k_nat = kt.T
    lane = lax.broadcasted_iota(jnp.int32, (length, LANES), 1)
    for pair in range(heads // 2):
        both = k_nat[:, pair * LANES : (pair + 1) * LANES]
        turned = pltpu.roll(both, head, 1)
        kk[2 * pair, :, :LANES] = jnp.where(lane < head, both, turned).astype(BF16)
        kk[2 * pair + 1, :, :LANES] = jnp.where(lane < head, turned, both).astype(BF16)
        kk[2 * pair, :, LANES:] = k_aug
        kk[2 * pair + 1, :, LANES:] = k_aug
    vt = vt.astype(BF16)
    for h in range(heads):
        va[h, :head, :] = vt[h * head : (h + 1) * head, :]
        va[h, head:, :] = jnp.ones((EXT, length), BF16)
    q2 = qt * LOG2E
    q_hi = q2.astype(BF16)
    q_lo = (q2 - q_hi.astype(F32)).astype(BF16)
    chunk = length // 2
    wait("bias")
    for h in range(heads):
        hs = slice(h * head, (h + 1) * head)
        for qc in range(nq // chunk):
            qs = slice(qc * chunk, (qc + 1) * chunk)
            rhs = jnp.concatenate([q_hi[hs, qs], q_lo[hs, qs], q_aug[:, qs]], axis=0)
            s = []
            top = None
            for a in range(n):
                if half:
                    at = pl.ds(pl.multiple_of((n - 1 - a) * LANES + c * nq, LANES), chunk)
                else:
                    at = pl.ds((n - 1 - a) * LANES + qc * chunk, chunk)
                s_a = mm(kk[h, a * LANES : (a + 1) * LANES, :], rhs) + bias[h, :, at]
                s.append(s_a)
                m_a = fold(s_a, jnp.maximum)
                top = m_a if top is None else jnp.maximum(top, m_a)
            top = jnp.max(top, axis=0, keepdims=True)
            for a in range(n):
                o["e"][h, a * LANES : (a + 1) * LANES, qs] = jnp.exp2(s[a] - top).astype(BF16)
            raw = mm(va[h], o["e"][h, :, qs])
            inv = 1.0 / raw[head : head + 1, :]
            o["r"][h : h + 1, qs] = inv
            o["att"][hs, qs] = (raw[:head, :] * inv).astype(BF16)
        copies((o["e"], h))
    copies(o["r"], o["att"])
    wait("out")
    if half:
        x_q = x_b[:, mine].astype(F32)
    else:
        x_q = x_b[...].astype(F32)
    o["mid"][...] = x_q + mm(wout_t[...], o["att"][...])
    copies(o["mid"])
    for b in range(nq // span):
        norm_into(n1, b * span, o["mid"][:, b * span : (b + 1) * span], nffn[...])
    ff = wg_t.shape[0]
    step = 256
    wait("ffn")
    for b in range(ff // step):
        cs = slice(b * step, (b + 1) * step)
        gate = mm(wg_t[cs, :], n1[:, :nq])
        up = mm(wu_t[cs, :], n1[:, :nq])
        sq = gate * gate
        th = jnp.tanh(gate * (0.7978845608028654 + (0.7978845608028654 * 0.044715) * sq))
        half_th = 0.5 + 0.5 * th
        gelu = gate * half_th
        slope = half_th + (gelu - gelu * th) * (0.7978845608028654 + (3 * 0.7978845608028654 * 0.044715) * sq)
        o["hid"][cs, :] = (gelu * up).astype(BF16)
        o["a"][cs, :] = (up * slope).astype(BF16)
        o["ge"][cs, :] = gelu.astype(BF16)
    copies(o["hid"], o["a"], o["ge"])
    wait("down")
    res = tok.at[:, :nq]
    res[...] = o["mid"][...] + mm(wd_t[...], o["hid"][...])
    valid = (seg[0:1, mine] != 0.0).astype(F32)
    part = None
    for b in range(nq // span):
        blk = res[:, b * span : (b + 1) * span] * valid[:, b * span : (b + 1) * span]
        part = blk if part is None else part + blk
    o["pool"][...] = jnp.broadcast_to(col_sum(part.T), o["pool"].shape)
    outs_b = (o["b_own"], o["b_c"], o["b_y"].at[0], o["b_y"].at[1])
    send_blocks(half, res, outs_b, span)
    copies(o["pool"], o["b_own"], o["b_c"], o["b_y"])


def send_blocks(half, res, outs, span):
    me, _, c = position()
    for k, out in enumerate(outs):
        block = (c + k) % 2 if half else me ^ k
        at = pl.multiple_of(block * span, span)
        out[:span, :] = res[:, pl.ds(at, span)].T.astype(BF16)


FORWARD_OUTS = ("kt", "q", "v", "x", "seg", "e", "r", "att", "mid", "hid", "a", "ge", "pool", "b_own", "b_c", "b_y")


def forward_outs(half, n, span, width, inner, heads, ff):
    length = n * span
    nq = length // 2 if half else length
    shapes = (
        ((inner, length), BF16), ((nq, inner), BF16), ((length, inner), BF16), ((width, nq), BF16), ((8, length), F32),
        ((heads, length, nq), BF16), ((8, nq), F32), ((inner, nq), BF16), ((width, nq), F32), ((ff, nq), BF16),
        ((ff, nq), BF16), ((ff, nq), BF16), ((8, width), F32), ((span, width), BF16), ((span, width), BF16),
        ((2, span, width), BF16),
    )
    return shapes


def forward_kernel(kinds, n, per, heads, *refs):
    count = len(FORWARD_OUTS)
    tokens, seg_ids, bias, wqkv_t, wout_t, wg_t, wu_t, wd_t, nattn, nffn = refs[:10]
    pieces = refs[10 : 10 + 3 * len(kinds)]
    at = 10 + 3 * len(kinds)
    outs = [refs[at + i * count : at + (i + 1) * count] for i in range(len(kinds))]
    at += count * len(kinds)
    bufs = [refs[at + i * count : at + (i + 1) * count] for i in range(len(kinds))]
    at += count * len(kinds)
    own, tok, seg, n1, kk, va, x_b, bias_b, wqkv_b, wout_b, wg_b, wu_b, wd_b, in_sems, out_sems = refs[at:]
    me, p, c = position()
    ins = Copies(in_sems)
    owns = []
    for i, (slot, half) in enumerate(kinds):
        row = per * p + (per - 1 if half else 2 * c + slot)
        owns.append((ins.start(tokens.at[row], own.at[i]), row))
    waits = {
        "qkv": [ins.start(wqkv_t, wqkv_b)],
        "bias": [ins.start(bias, bias_b)],
        "out": [ins.start(wout_t, wout_b)],
        "ffn": [ins.start(wg_t, wg_b), ins.start(wu_t, wu_b)],
        "down": [ins.start(wd_t, wd_b)],
    }

    def wait(what):
        for copy in waits.pop(what, ()):
            copy.wait()

    writes = Copies(out_sems)
    pending = []
    for i, (slot, half) in enumerate(kinds):
        copy, row = owns[i]
        copy.wait()
        o = dict(zip(FORWARD_OUTS, bufs[i]))
        dst = dict(zip(FORWARD_OUTS, outs[i]))
        names = {id(v): k for k, v in o.items()}

        def copies(*what, o=o, dst=dst, names=names):
            for item in what:
                if isinstance(item, tuple):
                    ref, h = item
                    pending.append(writes.start(ref.at[h], dst[names[id(ref)]].at[h]))
                else:
                    pending.append(writes.start(item, dst[names[id(item)]]))

        c1, y, c2 = pieces[3 * i : 3 * i + 3]
        y_mine = y if half else y.at[0]
        c2_mine = c2 if half else c2.at[1]
        own_seg = seg_ids[pl.ds(row, 1), :].astype(F32)
        forward_slot(
            half, n, (own.at[i], c1, y_mine, c2_mine, own_seg), (tok, seg, n1, kk, va, x_b, None),
            (bias_b, wqkv_b, wout_b, wg_b, wu_b, wd_b, nattn, nffn), wait, o, copies,
        )
    for copy in pending:
        copy.wait()


def middle_kernel(n, per, *refs):
    grad_y, eg, w_head, w_down, w_gate, w_up, w_out, nffn, pool_other = refs[:9]
    at = 9
    gy = [refs[at + 3 * i : at + 3 * i + 3] for i in range(3)]
    at += 9
    names = ("mid", "a", "ge", "hid", "att", "seg", "r", "pool")
    srcs = [dict(zip(names, refs[at + 8 * i : at + 8 * i + 8])) for i in range(3)]
    at += 24
    ga_o, gt_o = refs[at : at + 3], refs[at + 3 : at + 6]
    own_o, send_o, gnf_o, emb_o, pg_o = refs[at + 6 : at + 11]
    at += 11
    big = ("mid", "a", "ge", "hid", "att")
    bufs = [dict(zip(big, refs[at + 5 * i : at + 5 * i + 5])) for i in range(3)]
    at += 15
    own, tok, gout, gb, n2, gg, gu, acc, wh, wd, wg, wu, wo, sems = refs[at:]
    span, width = own.shape[1:]
    length = n * span
    ff = w_gate.shape[1]
    inner = w_out.shape[0]
    head = inner // 6
    wide = w_head.shape[1]
    me, p, c = position()
    ins = Copies(sems)
    owns = []
    for i in range(3):
        row = per * p + (per - 1 if i == 2 else 2 * c + i)
        owns.append(ins.start(grad_y.at[row], own.at[i]))
    weights = {k: ins.start(a, b) for k, a, b in (("h", w_head, wh), ("d", w_down, wd))}
    loads = [{k: ins.start(srcs[0][k], bufs[0][k]) for k in ("a", "ge", "mid", "hid")}]
    for k, a, b in (("g", w_gate, wg), ("u", w_up, wu), ("o", w_out, wo)):
        weights[k] = ins.start(a, b)
    loads[0]["att"] = ins.start(srcs[0]["att"], bufs[0]["att"])
    for i in (1, 2):
        loads.append({k: ins.start(srcs[i][k], bufs[i][k]) for k in big})

    def need(*names):
        for k in names:
            if k in weights:
                weights.pop(k).wait()

    part_total = None
    for i in range(3):
        half = i == 2
        nq = length // 2 if half else length
        src, buf = srcs[i], bufs[i]
        owns[i].wait()
        c1, y, c2 = gy[i]
        for k, piece in enumerate((own.at[i], c1, y if half else y.at[0], c2 if half else c2.at[1])):
            place = pl.multiple_of((me ^ k) * span, span)
            tok[pl.ds(place, span), :] = piece[...].astype(F32)
        seg = src["seg"]
        count = jnp.sum((seg[0:1, :] != 0.0).astype(F32), axis=1, keepdims=True)
        pool = src["pool"][0:1, :]
        if half:
            pool = pool + pool_other[0:1, :]
        pool = pool / count
        need("h")
        proj = wide_dot(pool, wh[...], mm)
        inv = lax.rsqrt(jnp.sum(proj * proj, axis=1, keepdims=True) + EPS)
        emb = proj * inv
        row = per * p + (per - 1 if half else 2 * c + i)
        cot = eg[pl.ds(row, 1), :]
        g_proj = inv * (cot - emb * jnp.sum(emb * cot, axis=1, keepdims=True))
        emb_o[i] = jnp.broadcast_to(emb, emb_o.shape[1:])
        once = jnp.where(c == 0, 1.0, 0.0) if half else 1.0
        for q in range((width + wide) // 256):
            part = pool[:, q * 256 : (q + 1) * 256] if q < width // 256 else g_proj[:, q * 256 - width : (q + 1) * 256 - width]
            pg_o[5 * i + q : 5 * i + q + 1, :] = part * once
        g_pool = wide_dot(g_proj, wh[...], mm_nt) / count
        g_col = jnp.broadcast_to(g_pool, (span, width)).T
        first = c * (nq // span) if half else 0
        for b in range(nq // span):
            bs = slice(b * span, (b + 1) * span)
            if half:
                place = pl.ds(pl.multiple_of((first + b) * span, span), span)
            else:
                place = pl.ds(b * span, span)
            valid = (seg[0:1, place] != 0.0).astype(F32)
            blk = tok[place, :].T + valid * g_col
            gout[:, bs] = blk
            gb[:, bs] = blk.astype(BF16)
        need("d")
        loads[i].pop("a").wait()
        loads[i].pop("ge").wait()
        step = 256
        for b in range(ff // step):
            cs = slice(b * step, (b + 1) * step)
            g_hid = mm(wd[cs, :], gb[:, :nq])
            gg[cs, :nq] = (g_hid * buf["a"][cs, :].astype(F32)).astype(BF16)
            gu[cs, :nq] = (g_hid * buf["ge"][cs, :].astype(F32)).astype(BF16)
        loads[i].pop("mid").wait()
        loads[i].pop("hid").wait()
        need("g", "u")
        res = tok.at[:, :nq]
        res[...] = mm(wg[...], gg[:, :nq]) + mm(wu[...], gu[:, :nq])

        def add(place, value, i=i):
            if i == 0:
                acc[:, place] = value
            else:
                acc[:, place] += value

        for b in range(2):
            add(slice(2 * ff + b * width, 2 * ff + (b + 1) * width), mm_nt(buf["hid"][b * width : (b + 1) * width, :], gb[:, :nq]))
        part = None
        for b in range(nq // span):
            bs = slice(b * span, (b + 1) * span)
            m = buf["mid"][:, bs]
            inv2 = lax.rsqrt(col_sum(m * m) / width + EPS)
            hat = m * inv2
            n2[:, bs] = (hat * nffn[...]).astype(BF16)
            gn = res[:, bs]
            c2_ = gn * nffn[...]
            part = gn * hat if part is None else part + gn * hat
            mean = col_sum(c2_ * hat) / width
            ga_o[i][:, bs] = (gout[:, bs] + inv2 * (c2_ - hat * mean)).astype(BF16)
        part_total = part if part_total is None else part_total + part
        for b in range(2):
            cs = slice(b * 512, (b + 1) * 512)
            add(cs, mm_nt(n2[:, :nq], gg[cs, :nq]))
            add(slice(ff + b * 512, ff + (b + 1) * 512), mm_nt(n2[:, :nq], gu[cs, :nq]))
        need("o")
        gatt = mm(wo[...], ga_o[i][...]).astype(BF16).astype(F32)
        for h in range(6):
            hs = slice(h * head, (h + 1) * head)
            gt_o[i][hs, :] = (gatt[hs, :] * src["r"][h : h + 1, :]).astype(BF16)
        loads[i].pop("att").wait()
        add(slice(2 * ff + 2 * width, 2 * ff + 2 * width + inner), mm_nt(ga_o[i][...], buf["att"][...]))
    gnf_o[...] = jnp.broadcast_to(col_sum(part_total.T), gnf_o.shape)
    pg_o[15:16, :] = jnp.zeros((1, 256), F32)
    rows = own_o.shape[0]
    own_o[...] = acc[pl.ds(pl.multiple_of(c * rows, rows), rows), :].astype(BF16)
    send_o[...] = acc[pl.ds(pl.multiple_of((1 - c) * rows, rows), rows), :].astype(BF16)


def attention_back(half, n, q_nat, v_nat, kt, e_wait, e_b, att, gt, gs, table, line, gq_o, put_kv):
    heads = e_b.shape[0]
    inner = kt.shape[0]
    head = inner // heads
    length = kt.shape[1]
    nq = length // 2 if half else length
    _, _, c = position()
    lane = lax.broadcasted_iota(jnp.int32, (length, LANES), 1)
    gt_nat = gt[...].astype(F32).T.astype(BF16)
    zeros = jnp.zeros((head, nq), BF16)
    for pair in range(heads // 2):
        ps = slice(pair * LANES, (pair + 1) * LANES)
        gk = []
        gv = []
        for side in range(2):
            h = pair * 2 + side
            hs = slice(h * head, (h + 1) * head)
            g_h = gt[hs, :]
            delta = col_sum(g_h.astype(F32) * att[hs, :].astype(F32))
            rhs = jnp.concatenate([g_h, zeros] if side == 0 else [zeros, g_h], axis=0)
            table[...] = jnp.zeros_like(table)
            e_wait(h)
            for a in range(n):
                ks = slice(a * LANES, (a + 1) * LANES)
                g_p = mm(v_nat[ks, ps], rhs)
                g_s = (e_b[h, ks, :].astype(F32) * (g_p - delta)).astype(BF16)
                gs[ks, :nq] = g_s
                if half:
                    at = pl.ds(pl.multiple_of((n - 1 - a) * LANES + c * nq, LANES), nq)
                else:
                    at = pl.ds((n - 1 - a) * LANES, nq)
                table[:, at] += g_s.astype(F32)
            line(h, diagonal_sums(table))
            gq_o[hs, :] = mm(kt[hs, :], gs[:, :nq]).astype(BF16)
            gk.append(mm(gs[:, :nq], q_nat[:, ps]))
            gv.append(mm(e_b[h], gt_nat[:, ps]))
        put_kv(pair, 0, jnp.where(lane < head, gk[0], gk[1]).T)
        put_kv(pair, 1, jnp.where(lane < head, gv[0], gv[1]).T)


def half_back_kernel(n, q_nat, v_nat, kt, e_in, att, gt, gq_o, keep_o, send_o, line_o, e_b, gs, table, kv, sems):
    ins = Copies(sems)
    loads = [ins.start(e_in.at[h], e_b.at[h]) for h in range(e_in.shape[0])]
    inner = kt.shape[0]

    def put(pair, which, value):
        kv[which * inner + pair * LANES : which * inner + (pair + 1) * LANES, :] = value.astype(BF16)

    def line(h, value):
        line_o[h : h + 1, :] = value

    line_o[...] = jnp.zeros_like(line_o)
    attention_back(True, n, q_nat, v_nat, kt, lambda h: loads[h].wait(), e_b, att, gt, gs, table, line, gq_o, put)
    _, _, c = position()
    nq = kt.shape[1] // 2
    keep_o[...] = kv[:, pl.ds(pl.multiple_of(c * nq, nq), nq)]
    send_o[...] = kv[:, pl.ds(pl.multiple_of((1 - c) * nq, nq), nq)]


def input_grads(half, gq, xt, ga, w_qkv, nattn, n1, res, outs, gna, emb, span):
    nq = gq.shape[1]
    width = xt.shape[0]
    res[:, :nq] = mm(w_qkv[...], gq[...])
    part = None
    for b in range(nq // span):
        bs = slice(b * span, (b + 1) * span)
        x = xt[:, bs].astype(F32)
        inv = lax.rsqrt(col_sum(x * x) / width + EPS)
        hat = x * inv
        n1[:, bs] = (hat * nattn[...]).astype(BF16)
        gn = res[:, bs]
        c1 = gn * nattn[...]
        part = gn * hat if part is None else part + gn * hat
        mean = col_sum(c1 * hat) / width
        res[:, bs] = ga[:, bs].astype(F32) + inv * (c1 - hat * mean)
    gna(col_sum(part.T))
    send_blocks(half, res, outs, span)
    high = emb.astype(BF16)
    low = (emb - high.astype(F32)).astype(BF16)
    rest = emb.shape[1] - width
    for out in outs:
        for at, v in ((0, high), (2, low)):
            out[span + at : span + at + 1, :] = v[:, :width]
            out[span + at + 1 : span + at + 2, :rest] = v[:, width:]


def backward_kernel(
    slot, n,
    q_nat, v_nat, kt, e_in, att, gt, xt, ga, w_qkv, nattn, emb, acc_in, gna_in, line_in,
    acc_o, gna_o, line_o, b_own, b_c, b_y,
    e_b, gs, table, res, gq, n1, acc, sems,
):
    ins = Copies(sems)
    loads = [ins.start(e_in.at[h], e_b.at[h]) for h in range(e_in.shape[0])]
    old = ins.start(acc_in, acc) if slot else None
    inner = kt.shape[0]

    def put(pair, which, value):
        at = (1 + which) * inner + pair * LANES
        gq[at : at + LANES, :] = value.astype(BF16)

    def line(h, value):
        line_o[h : h + 1, :] = line_in[h : h + 1, :] + value

    line_o[...] = line_in[...]
    attention_back(False, n, q_nat, v_nat, kt, lambda h: loads[h].wait(), e_b, att, gt, gs, table, line, gq.at[:inner, :], put)

    def gna(value):
        gna_o[...] = gna_in[...] + value

    span = b_own.shape[0] - EXT
    outs = (b_own, b_c, b_y.at[0], b_y.at[1])
    input_grads(False, gq, xt, ga, w_qkv, nattn, n1, res, outs, gna, emb[slot, 0:1, :], span)
    grads = mm_nt(n1[...], gq[...])
    if slot:
        old.wait()
        acc[...] += grads
    else:
        acc[...] = grads
    out = ins.start(acc, acc_o)
    out.wait()


def last_kernel(
    n,
    gq_half, keep, got, xt, ga, w_qkv, nattn, emb, acc_in, gna_in, line_in, gnf, indicator,
    own_o, send_o, b_own, b_c, b_y,
    res, gq, n1, acc,
):
    inner = gq_half.shape[0]
    gq[:inner, :] = gq_half[...]
    gq[inner:, :] = (keep[...].astype(F32) + got[...].astype(F32)).astype(BF16)
    rows, wide = acc.shape
    full = wide - LANES
    small = acc.at[:, full:]
    small[...] = jnp.zeros_like(small)
    width = gnf.shape[1]

    def gna(value):
        value = gna_in[0:1, :] + value
        for i in range(width // LANES):
            small[i : i + 1, :] = gnf[0:1, i * LANES : (i + 1) * LANES]
            small[4 + i : 5 + i, :] = value[:, i * LANES : (i + 1) * LANES]

    span = b_own.shape[0] - EXT
    outs = (b_own, b_c, b_y.at[0], b_y.at[1])
    input_grads(True, gq, xt, ga, w_qkv, nattn, n1, res, outs, gna, emb[2, 0:1, :], span)
    lines = line_in[...]
    hi = lines.astype(BF16)
    lo = (lines - hi.astype(F32)).astype(BF16)
    small[8:16, :] = mm_nt(hi, indicator[...]) + mm_nt(lo, indicator[...])
    acc[:, :full] = acc_in[...] + mm_nt(n1[...], gq[...])
    _, _, c = position()
    rows = own_o.shape[0]
    own_o[...] = acc[pl.ds(pl.multiple_of(c * rows, rows), rows), :].astype(BF16)
    send_o[...] = acc[pl.ds(pl.multiple_of((1 - c) * rows, rows), rows), :].astype(BF16)


def unpack_kernel(per, with_emb, *refs):
    own0, own1, own2, c0, c1, c2, y0, y1, y2, d0, d1, d2, out = refs[:13]
    sems = refs[-1]
    me, p, _ = position()
    rows, span, width = out.shape
    ways = ((own0, c0, y0.at[0], d0.at[1]), (own1, c1, y1.at[0], d1.at[1]), (own2, c2, y2.at[0], d2.at[1]))
    for r in range(rows):
        pair, j = divmod(r, per)
        slot = 2 if j == per - 1 else j % 2
        core = p if slot == 2 else j // 2
        k = me ^ (pair * 2 + core)
        for which in range(4):
            ref = ways[slot][which]

            @pl.when(k == which)
            def _(ref=ref, r=r):
                pltpu.make_async_copy(ref.at[pl.ds(0, span)], out.at[r], sems.at[r]).start()
                if with_emb:
                    pltpu.make_async_copy(ref.at[pl.ds(span, EXT)], refs[14].at[r], sems.at[rows + r]).start()

    if with_emb:
        emb, got = refs[13:15]
        for r in range(rows):
            pltpu.make_async_copy(own0.at[pl.ds(span, EXT)], got.at[r], sems.at[rows + r]).wait()
            value = got[r].astype(F32)
            emb[r : r + 1, :width] = value[0:1, :] + value[2:3, :]
            emb[r : r + 1, width:] = (value[1:2, :] + value[3:4, :])[:, : emb.shape[1] - width]
    for r in range(rows):
        pltpu.make_async_copy(own0.at[pl.ds(0, span)], out.at[r], sems.at[r]).wait()


def finish_early_kernel(a_own, a_got, b_own, b_got, pg_own, pg_got, gate_o, up_o, down_o, out_o, head_o):
    _, _, c = position()
    rows, cut = a_own.shape
    ff = gate_o.shape[1]
    width = gate_o.shape[0]
    inner = out_o.shape[0]
    rest = ff - (cut - ff)
    for a, b, side in ((a_own, b_own, c), (a_got, b_got, 1 - c)):
        at = pl.ds(pl.multiple_of(side * rows, rows), rows)
        gate_o[at, :] = a[:, :ff].astype(F32)
        up_o[at, : cut - ff] = a[:, ff:].astype(F32)
        up_o[at, cut - ff :] = b[:, :rest].astype(F32)
        down_o[at, :] = b[:, rest : rest + width].astype(F32)
        at2 = pl.ds(pl.multiple_of(width + side * rows, rows), rows)
        down_o[at2, :] = b[:, rest + width : rest + 2 * width].astype(F32)
        out_o[:, at] = b[:, rest + 2 * width : rest + 2 * width + inner].astype(F32).T
    count = pg_own.shape[0]
    row = lax.broadcasted_iota(jnp.int32, pg_own.shape, 0) % 16
    for ref in (pg_own, pg_got):
        g = ref[...].astype(F32)
        turned = {t: pltpu.roll(g, count - t, 0).astype(BF16) for t in range(1, 5)}
        for i in range(2):
            kept = jnp.where((row < 15) & (row % 5 == i), g, 0.0).T.astype(BF16)
            for j in range(3):
                term = mm(kept, turned[2 + j - i])
                place = (slice(i * 256, (i + 1) * 256), slice(j * 256, (j + 1) * 256))
                if ref is pg_own:
                    head_o[place] = term
                else:
                    head_o[place] += term


def finish_late_kernel(own, got, q_o, k_o, v_o, nf_o, na_o, table_o):
    _, _, c = position()
    rows = own.shape[0]
    inner = q_o.shape[1]
    for ref, side in ((own, c), (got, 1 - c)):
        at = pl.ds(pl.multiple_of(side * rows, rows), rows)
        for i, out in enumerate((q_o, k_o, v_o)):
            out[at, :] = ref[:, i * inner : (i + 1) * inner].astype(F32)
    small = jnp.where(c == 0, own[:16, 3 * inner :].astype(F32), got[:16, 3 * inner :].astype(F32))
    for i in range(nf_o.shape[1] // LANES):
        nf_o[:, i * LANES : (i + 1) * LANES] = small[i : i + 1, :]
        na_o[:, i * LANES : (i + 1) * LANES] = small[4 + i : 5 + i, :]
    table_o[...] = small[8:16, :].T[: table_o.shape[0], : table_o.shape[1]]


def sds(shape, dtype=BF16):
    return jax.ShapeDtypeStruct(shape, dtype)


def call(kernel, outs, args, scratch=(), specs=None, out_specs=None, flops=0, name=None, vmem=56, deps=()):
    count = len(args)

    def body(*refs):
        kernel(*refs[:count], *refs[count + len(deps) :])

    return pl.pallas_call(
        body,
        out_shape=outs,
        in_specs=list(specs or [VMEM] * count) + [ANY] * len(deps),
        out_specs=out_specs or jax.tree.map(lambda _: VMEM, outs),
        scratch_shapes=list(scratch),
        compiler_params=pltpu.CompilerParams(vmem_limit_bytes=vmem * 2**20),
        cost_estimate=pl.CostEstimate(flops=flops, bytes_accessed=10_000_000, transcendentals=0),
        name=name,
    )(*args, *deps)


def swap(x, axis, k):
    n = lax.axis_size(axis)
    return lax.ppermute(x, axis, [(i, i ^ k) for i in range(n)])


def row_digits():
    n = lax.axis_size("rows")
    out = []
    stride = 1
    while stride < n:
        r = 2 if stride == 1 or n // stride < 4 else 4
        out.append(("rows", stride, r))
        stride *= r
    return out


def digit(step):
    axis, stride, radix = step
    return (lax.axis_index(axis) // stride) % radix


def split(v, step):
    d = digit(step)
    return [lax.dynamic_index_in_dim(v, d ^ k, 0, keepdims=False) for k in range(step[2])]


def exchange(parts, step):
    return [parts[0]] + [swap(p, step[0], k * step[1]) for k, p in enumerate(parts) if k]


def add_up(parts):
    return sum(p.astype(F32) for p in parts).astype(BF16)


def join(parts, step, dtype=BF16):
    d = digit(step)
    at = lax.broadcasted_iota(jnp.int32, (step[2],) + (1,) * parts[0].ndim, 0)
    out = parts[0][None]
    for k in range(1, step[2]):
        out = jnp.where(at == (d ^ k), parts[k][None], out)
    return out.astype(dtype)


def shards(
    tokens, seg_ids, w_query, w_key, w_value, w_out, w_gate, w_up, w_down, w_head, norm_attn, norm_ffn,
    bucket_bias_table, grad_y, embedding_gradient,
):
    rows, span, width = tokens.shape
    buckets, heads = bucket_bias_table.shape
    n = lax.axis_size("seq")
    inner = w_query.shape[1]
    ff = w_gate.shape[1]
    wide = w_head.shape[1]
    length = n * span
    per = rows // 2
    assert n == 4 and per == 5

    def send_rows(array, ids, slots, ext, deps=()):
        size = span + ext
        outs = []
        for j in slots:
            outs += [sds((size, width) if j == 2 else (2, size, width)), sds((size, width))]
        packed = call(
            functools.partial(pack_kernel, per, slots, ext), tuple(outs), (array, ids) if ext else (array,), vmem=16,
            name="pack", deps=deps,
        )
        got = []
        for i in range(len(slots)):
            near = swap(packed[2 * i + 1], "seq", 1)
            far = swap(packed[2 * i], "seq", 2)
            got.append((near, far, swap(far, "seq", 1)))
        return got, packed

    line = 2 * length
    xs, _ = send_rows(tokens, seg_ids, (0,), EXT)
    table_t = jnp.pad(bucket_bias_table.T, ((0, 8 - heads), (0, LANES - buckets)))
    bias, ind, nattn, nffn, w_qkv, wqkv_t, wout_t, wg_t, wu_t, wd_t = call(
        functools.partial(prepare_kernel, n),
        (
            sds((heads, LANES, line), F32), sds((LANES, line)), sds((width, LANES), F32), sds((width, LANES), F32),
            sds((width, 3 * inner)), sds((3 * inner, width)), sds((width, inner)), sds((ff, width)), sds((ff, width)),
            sds((width, ff)),
        ),
        (
            table_t, norm_attn[None], norm_ffn[None], w_query, w_key, w_value, w_out, w_gate, w_up, w_down,
        ),
        name="prepare", flops=4_000_000_000,
    )
    more, packed_x = send_rows(tokens, seg_ids, (1, 2), EXT, deps=(xs[0][1],))
    xs += more

    def run_forward(kinds, deps=()):
        shapes = [s for _, half in kinds for s in forward_outs(half, n, span, width, inner, heads, ff)]
        outs = tuple(sds(*s) for s in shapes)
        args = [tokens, seg_ids, bias, wqkv_t, wout_t, wg_t, wu_t, wd_t, nattn, nffn]
        specs = [ANY, VMEM] + [ANY] * 6 + [VMEM] * 2
        for slot, half in kinds:
            args += list(xs[slot])
            specs += [VMEM] * 3
        scratch = [pltpu.VMEM(*s) for s in shapes]
        scratch += [
            pltpu.VMEM((len(kinds), span, width), BF16), pltpu.VMEM((length, width), F32), pltpu.VMEM((LANES, length), F32),
            pltpu.VMEM((width, length), BF16), pltpu.VMEM((heads, length, 2 * LANES), BF16),
            pltpu.VMEM((heads, inner // heads + EXT, length), BF16), pltpu.VMEM((width, length), BF16),
            pltpu.VMEM(bias.shape, F32), *[pltpu.VMEM(w.shape, BF16) for w in (wqkv_t, wout_t, wg_t, wu_t, wd_t)],
            pltpu.SemaphoreType.DMA((8 + len(kinds),)), pltpu.SemaphoreType.DMA((24 * len(kinds),)),
        ]
        res = call(
            functools.partial(forward_kernel, kinds, n, per, heads), outs, args, scratch, specs, tuple(ANY for _ in outs),
            4_000_000_000 * len(kinds), "forward", deps=deps,
        )
        count = len(FORWARD_OUTS)
        return [dict(zip(FORWARD_OUTS, res[i * count : (i + 1) * count])) for i in range(len(kinds))]

    fwd = run_forward([(0, False)], deps=packed_x)
    gys, packed_g = send_rows(grad_y, None, (0, 1, 2), 0, deps=(fwd[0]["r"],))
    fwd += run_forward([(1, False), (2, True)], deps=packed_g)
    pool_other = swap(fwd[2]["pool"], "seq", 1)

    def collect(owns, cs, ys):
        near = [swap(c, "seq", 1) for c in cs]
        far = [swap(y, "seq", 2) for y in ys]
        again = [swap(f, "seq", 1) for f in far]
        return owns, near, far, again

    def unpack(parts, with_emb):
        args = [a for group in parts for a in group]
        outs = (sds((rows, span, width)),) + ((sds((rows, wide), F32),) if with_emb else ())
        scratch = [pltpu.VMEM((rows, EXT, width), BF16)] if with_emb else []
        return call(
            functools.partial(unpack_kernel, per, with_emb), outs, args, scratch + [pltpu.SemaphoreType.DMA((2 * rows,))],
            [ANY] * 12, (ANY, VMEM)[: len(outs)], vmem=16, name="unpack",
        )

    block_parts = collect([f["b_own"] for f in fwd], [f["b_c"] for f in fwd], [f["b_y"] for f in fwd])

    packed_w = 2 * ff + 2 * width + inner
    nqs = [length, length, length // 2]
    args = [grad_y, embedding_gradient, w_head, w_down, w_gate, w_up, w_out, nffn, pool_other]
    specs = [ANY, VMEM] + [ANY] * 5 + [VMEM] * 2
    for g in gys:
        args += list(g)
        specs += [VMEM] * 3
    for f in fwd:
        args += [f[k] for k in ("mid", "a", "ge", "hid", "att", "seg", "r", "pool")]
        specs += [ANY] * 5 + [VMEM] * 3
    outs = tuple(
        [sds((width, q)) for q in nqs] + [sds((inner, q)) for q in nqs]
        + [sds((width // 2, packed_w))] * 2 + [sds((8, width), F32), sds((3, 8, wide), F32), sds((16, 256), F32)]
    )
    scratch = []
    for q in nqs:
        scratch += [
            pltpu.VMEM((width, q), F32), pltpu.VMEM((ff, q), BF16), pltpu.VMEM((ff, q), BF16), pltpu.VMEM((ff, q), BF16),
            pltpu.VMEM((inner, q), BF16),
        ]
    scratch += [
        pltpu.VMEM((3, span, width), BF16), pltpu.VMEM((length, width), F32), pltpu.VMEM((width, length), F32),
        pltpu.VMEM((width, length), BF16), pltpu.VMEM((width, length), BF16), pltpu.VMEM((ff, length), BF16),
        pltpu.VMEM((ff, length), BF16), pltpu.VMEM((width, packed_w), F32), pltpu.VMEM(w_head.shape, BF16),
        pltpu.VMEM(w_down.shape, BF16), pltpu.VMEM(w_gate.shape, BF16), pltpu.VMEM(w_up.shape, BF16),
        pltpu.VMEM(w_out.shape, BF16), pltpu.SemaphoreType.DMA((23,)),
    ]
    m = call(functools.partial(middle_kernel, n, per), outs, args, scratch, specs, flops=15_000_000_000, name="middle")
    ga, gt = m[:3], m[3:6]
    own, send, gnf, emb, pg = m[6:]

    core = ("seq", 1, 2)
    far = ("seq", 2, 2)
    digits = row_digits()
    radix = [far[2]] + [d[2] for d in digits]
    block = width // 2
    for r in radix:
        block //= r

    def shares(v, s):
        return split(v.reshape((s[2], v.shape[0] // s[2], v.shape[1])), s)

    def reduce_rest(v, steps):
        for s in steps:
            v = add_up(exchange(shares(v, s), s))
        return v

    def gather_rest(v, steps):
        for s in steps[::-1]:
            v = join(exchange([v] * s[2], s), s).reshape(s[2] * v.shape[0], v.shape[1])
        return v

    first = add_up([own, swap(send, "seq", 1)])
    cut = packed_w // 2 // LANES * LANES
    a_steps, b_steps = [digits[0], far], [far, digits[0]]
    stage1 = (shares(first[:, :cut], a_steps[0]), shares(first[:, cut:], b_steps[0]))
    a = add_up(exchange(stage1[0], a_steps[0]))
    b = add_up(exchange(stage1[1], b_steps[0]))
    stage2 = (shares(a, a_steps[1]), shares(b, b_steps[1]))
    a = add_up(exchange(stage2[0], a_steps[1]))
    b = add_up(exchange(stage2[1], b_steps[1]))
    ab = jnp.concatenate([a, b], axis=1)
    stage3 = shares(ab, digits[1])
    ab = add_up(exchange(stage3, digits[1]))
    ab = reduce_rest(ab, digits[2:])
    extra = pg.astype(BF16).reshape(block, -1)
    ab = gather_rest(jnp.concatenate([ab, extra], axis=1), digits[1:])
    a = gather_rest(ab[:, :cut], a_steps)
    b = gather_rest(ab[:, cut:], b_steps)
    waits = ((stage1[0][1], stage1[1][1]), (stage2[0][1], stage2[1][1]), tuple(stage3[1:]))

    half_args = (fwd[2]["q"], fwd[2]["v"], fwd[2]["kt"], fwd[2]["e"], fwd[2]["att"], gt[2])
    nh = length // 2
    gq_half, keep, send_kv, lines_sum = call(
        functools.partial(half_back_kernel, n),
        (sds((inner, nh)), sds((2 * inner, nh)), sds((2 * inner, nh)), sds((8, line), F32)),
        half_args,
        [
            pltpu.VMEM((heads, length, nh), BF16), pltpu.VMEM((length, length), BF16), pltpu.VMEM((LANES, line), F32),
            pltpu.VMEM((2 * inner, length), BF16), pltpu.SemaphoreType.DMA((heads,)),
        ],
        [VMEM] * 3 + [ANY] + [VMEM] * 2, flops=2_000_000_000, name="half_back",
    )
    got_kv = swap(send_kv, "seq", 1)
    acc = jnp.zeros((8, 128), F32)
    gna = jnp.zeros((8, width), F32)
    piece = (sds((span + EXT, width)), sds((span + EXT, width)), sds((2, span + EXT, width)))
    back = []
    for j in range(2):
        f = fwd[j]
        outs = (sds((width, 3 * inner), F32), sds((8, width), F32), sds((8, line), F32), *piece)
        args = (
            f["q"], f["v"], f["kt"], f["e"], f["att"], gt[j], f["x"], ga[j], w_qkv, nattn, emb, acc, gna, lines_sum,
        )
        scratch = [
            pltpu.VMEM((heads, length, length), BF16), pltpu.VMEM((length, length), BF16), pltpu.VMEM((LANES, line), F32),
            pltpu.VMEM((width, length), F32), pltpu.VMEM((3 * inner, length), BF16), pltpu.VMEM((width, length), BF16),
            pltpu.VMEM((width, 3 * inner), F32), pltpu.SemaphoreType.DMA((heads + 2,)),
        ]
        acc, gna, lines_sum, *blocks = call(
            functools.partial(backward_kernel, j, n), outs, args, scratch,
            [VMEM] * 3 + [ANY] + [VMEM] * 7 + [ANY] + [VMEM] * 2, (ANY, VMEM, VMEM, VMEM, VMEM, VMEM),
            flops=4_000_000_000, name="backward", deps=waits[j] + ((gq_half,) if j == 0 else ()),
        )
        back.append(blocks)
    late_w = 3 * inner + LANES
    own, send, *blocks = call(
        functools.partial(last_kernel, n), (sds((width // 2, late_w)), sds((width // 2, late_w)), *piece),
        (gq_half, keep, got_kv, fwd[2]["x"], ga[2], w_qkv, nattn, emb, acc, gna, lines_sum, gnf, ind),
        [
            pltpu.VMEM((width, nh), F32), pltpu.VMEM((3 * inner, nh), BF16), pltpu.VMEM((width, nh), BF16),
            pltpu.VMEM((width, late_w), F32),
        ],
        flops=2_000_000_000, name="last", deps=waits[2],
    )
    back.append(blocks)

    late = add_up([own, swap(send, "seq", 1)])
    late = reduce_rest(late, a_steps + digits[1:])
    late = gather_rest(late, a_steps + digits[1:])

    x_parts = collect(*zip(*back))
    (block_out,) = unpack(block_parts, False)
    grad_x, embedding = unpack(x_parts, True)

    a_got, b_got = swap(a, "seq", 1), swap(b, "seq", 1)
    tail = packed_w - cut
    grad_gate, grad_up, grad_down, grad_out, grad_head = call(
        finish_early_kernel,
        (sds((width, ff), F32), sds((width, ff), F32), sds((ff, width), F32), sds((inner, width), F32), sds((width, wide), F32)),
        (a, a_got, b[:, :tail], b_got[:, :tail], b[:, tail:].reshape(-1, 256), b_got[:, tail:].reshape(-1, 256)),
        name="finish_early",
    )
    grad_query, grad_key, grad_value, grad_norm_ffn, grad_norm_attn, grad_table = call(
        finish_late_kernel,
        (*[sds((width, inner), F32)] * 3, sds((1, width), F32), sds((1, width), F32), sds((buckets, heads), F32)),
        (late, swap(late, "seq", 1)), name="finish_late",
    )
    return (
        block_out, embedding, grad_x, grad_query, grad_key, grad_value, grad_out, grad_gate, grad_up, grad_down, grad_head,
        grad_norm_attn[0], grad_norm_ffn[0], grad_table,
    )


def solution(mesh):
    by_pos = P("rows", "seq", None)
    by_row = P("rows", None)
    return jax.shard_map(
        shards,
        mesh=mesh,
        in_specs=(by_pos, P("rows", "seq"), *[P()] * 11, by_pos, by_row),
        out_specs=(by_pos, by_row, by_pos, *[P()] * 11),
        check_vma=False,
    )
```

```python
import functools

import jax
import jax.numpy as jnp
from jax import lax
from jax.experimental import pallas as pl
from jax.experimental.pallas import tpu as pltpu
from jax.sharding import PartitionSpec as P

EPS = 1e-06
LIMITS = (12, 16, 23, 32, 46, 64, 91)
TOP_PRECISION = lax.Precision.HIGHEST
F32 = jnp.float32
BF16 = jnp.bfloat16
MASK_STEP = 2.0**30
LOG2E = 1.4426950408889634
VMEM = pl.BlockSpec(memory_space=pltpu.VMEM)
ANY = pl.BlockSpec(memory_space=pl.ANY)
LANES = 128
EXT = 16


def mm(a, b):
    return lax.dot_general(a, b, (((1,), (0,)), ((), ())), preferred_element_type=F32)


def mm_nt(a, b):
    return lax.dot_general(a, b, (((1,), (1,)), ((), ())), preferred_element_type=F32)


def bucket_index(offset):
    distance = jnp.abs(offset)
    far_bucket = 8 + sum(((distance >= threshold).astype(jnp.int32) for threshold in LIMITS))
    near_bucket = jnp.where(distance < 8, distance, far_bucket)
    return near_bucket + 16 * (offset > 0).astype(jnp.int32)


def parts3(v):
    hi = v.astype(BF16).astype(F32)
    mid = (v - hi).astype(BF16).astype(F32)
    low = (v - hi - mid).astype(BF16).astype(F32)
    row = lax.broadcasted_iota(jnp.int32, v.shape, 0)
    return jnp.where(row == 0, hi, jnp.where(row == 1, mid, jnp.where(row == 2, low, 0.0))).astype(BF16)


def wide_dot(row, mat, dot):
    out = dot(parts3(jnp.broadcast_to(row, (16, row.shape[1]))), mat)
    return jnp.sum(out, axis=0, keepdims=True)


def fold(x, op):
    while x.shape[0] > 8:
        half = x.shape[0] // 2
        x = op(x[:half], x[half:])
    return x


def col_sum(x):
    return jnp.sum(fold(x, jnp.add), axis=0, keepdims=True)


def diagonal_sums(table):
    height, width = table.shape
    acc = table[0:8, :]
    for u in range(8, height, 8):
        acc += pltpu.roll(table[u : u + 8, :], width - u, 1)
    row = lax.broadcasted_iota(jnp.int32, acc.shape, 0)
    for bit in (1, 2, 4):
        acc = jnp.where((row & bit) != 0, pltpu.roll(acc, width - bit, 1), acc)
    return jnp.sum(acc, axis=0, keepdims=True)


def position():
    me = lax.axis_index("seq")
    return me, me // 2, me % 2


class Copies:
    def __init__(self, sems):
        self.sems = sems
        self.used = 0

    def start(self, src, dst):
        copy = pltpu.make_async_copy(src, dst, self.sems.at[self.used])
        self.used += 1
        copy.start()
        return copy


def pack_kernel(per, slots, ext, *refs):
    if ext:
        tok, seg, *outs = refs
    else:
        tok, *outs = refs
    span = tok.shape[1]
    _, p, c = position()

    def put(out, row):
        out[:span, :] = tok[row]
        if ext:
            ids = jnp.broadcast_to(seg[pl.ds(row, 1), :].astype(F32), (ext, span))
            out[span:, :span] = ids.astype(BF16)

    y, cc = outs
    for i, j in enumerate(slots):
        if j == 2:
            put(y.at[2 * i], per * (1 - p) + per - 1)
            put(cc.at[i], per * p + per - 1)
        else:
            put(y.at[2 * i], per * (1 - p) + 2 * c + j)
            put(y.at[2 * i + 1], per * (1 - p) + 2 * (1 - c) + j)
            put(cc.at[i], per * p + 2 * (1 - c) + j)


def prepare_kernel(
    n, table, norm_a, norm_f, wq, wk, wv, wo, wg, wu, wd,
    bias_o, ind_o, na_o, nf_o, wqkv_o, wqkv_t, wo_t, wg_t, wu_t, wd_t,
    square,
):
    heads, _, line = bias_o.shape
    inner = wq.shape[1]
    length = line // 2
    col = lax.broadcasted_iota(jnp.int32, (LANES, line), 1)
    offset = length - LANES - jnp.where(col < line - LANES, col, col - line)
    ind = (bucket_index(offset) == lax.broadcasted_iota(jnp.int32, (LANES, line), 0)).astype(F32).astype(BF16)
    ind_o[...] = ind
    square[...] = jnp.zeros_like(square)
    square[: table.shape[0], : table.shape[1]] = table[...]
    rest = square[...].T[:8, :]
    lines = None
    for _ in range(3):
        part = rest.astype(BF16)
        rest = rest - part.astype(F32)
        term = mm(part, ind)
        lines = term if lines is None else lines + term
    lines = lines * LOG2E
    for h in range(heads):
        bias_o[h] = pltpu.roll(jnp.broadcast_to(lines[h : h + 1, :], (LANES, line)), 0, 1, stride=1, stride_axis=0)
    for src, dst in ((norm_a, na_o), (norm_f, nf_o)):
        dst[...] = jnp.broadcast_to(src[...], (LANES, src.shape[1])).T
    for i, w in enumerate((wq, wk, wv)):
        wqkv_o[:, i * inner : (i + 1) * inner] = w[...]
        wqkv_t[i * inner : (i + 1) * inner, :] = w[...].astype(F32).T.astype(BF16)
    for src, dst in ((wo, wo_t), (wg, wg_t), (wu, wu_t), (wd, wd_t)):
        dst[...] = src[...].astype(F32).T.astype(BF16)


def norm_into(out, at, blk, gain):
    inv = lax.rsqrt(col_sum(blk * blk) / blk.shape[0] + EPS)
    out[:, at : at + blk.shape[1]] = (blk * inv * gain).astype(BF16)


def forward_slot(half, n, rows, bufs, w, wait, outs, copies):
    own, c1, y, c2, own_seg = rows
    tok, seg, n1, kk, va, x_b, bias_ready = bufs
    bias, wqkv_t, wout_t, wg_t, wu_t, wd_t, nattn, nffn = w
    o = outs
    width = wqkv_t.shape[1]
    inner = wout_t.shape[1]
    heads = bias.shape[0]
    head = inner // heads
    span = own.shape[0]
    length = n * span
    me, p, c = position()
    for k, (piece, ids) in enumerate(((own, own_seg), (c1, None), (y, None), (c2, None))):
        at = pl.multiple_of((me ^ k) * span, span)
        tok[pl.ds(at, span), :] = piece[:span, :].astype(F32)
        ids = piece[span : span + 1, :span].astype(F32) if ids is None else ids
        seg[:, pl.ds(at, span)] = jnp.broadcast_to(ids, (LANES, span))
    for b in range(n):
        blk = tok[b * span : (b + 1) * span, :].T
        x_b[:, b * span : (b + 1) * span] = blk.astype(BF16)
        norm_into(n1, b * span, blk, nattn[...])
    nq = length // 2 if half else length
    if half:
        mine = pl.ds(pl.multiple_of(c * nq, nq), nq)
        o["x"][...] = x_b[:, mine]
    else:
        mine = slice(0, nq)
        o["x"][...] = x_b[...]
    ids = lax.broadcasted_iota(jnp.int32, (LANES, length), 0).astype(F32)
    one = (seg[...] == ids).astype(F32)
    o["seg"][...] = seg[0:8, :]
    k_aug = ((one - 1.0) * MASK_STEP).T.astype(BF16)
    ids = lax.broadcasted_iota(jnp.int32, (LANES, nq), 0).astype(F32)
    q_aug = (seg[:, mine] == ids).astype(BF16)
    wait("qkv")
    qt = mm(wqkv_t[:inner, :], n1[:, mine]).astype(BF16).astype(F32)
    kt = mm(wqkv_t[inner : 2 * inner, :], n1[...])
    vt = mm(wqkv_t[2 * inner :, :], n1[...])
    o["kt"][...] = kt.astype(BF16)
    o["q"][...] = qt.T.astype(BF16)
    o["v"][...] = vt.T.astype(BF16)
    o["n1"][...] = n1[:, mine]
    copies(o["kt"], o["q"], o["v"], o["x"], o["seg"], o["n1"])
    k_nat = kt.T
    lane = lax.broadcasted_iota(jnp.int32, (length, LANES), 1)
    for pair in range(heads // 2):
        both = k_nat[:, pair * LANES : (pair + 1) * LANES]
        turned = pltpu.roll(both, head, 1)
        kk[2 * pair, :, :LANES] = jnp.where(lane < head, both, turned).astype(BF16)
        kk[2 * pair + 1, :, :LANES] = jnp.where(lane < head, turned, both).astype(BF16)
        kk[2 * pair, :, LANES:] = k_aug
        kk[2 * pair + 1, :, LANES:] = k_aug
    vt = vt.astype(BF16)
    for h in range(heads):
        va[h, :head, :] = vt[h * head : (h + 1) * head, :]
        va[h, head:, :] = jnp.ones((EXT, length), BF16)
    q2 = qt * LOG2E
    q_hi = q2.astype(BF16)
    q_lo = (q2 - q_hi.astype(F32)).astype(BF16)
    chunk = length // 2
    wait("bias")
    for h in range(heads):
        hs = slice(h * head, (h + 1) * head)
        for qc in range(nq // chunk):
            qs = slice(qc * chunk, (qc + 1) * chunk)
            rhs = jnp.concatenate([q_hi[hs, qs], q_lo[hs, qs], q_aug[:, qs]], axis=0)
            s = []
            top = None
            for a in range(n):
                if half:
                    at = pl.ds(pl.multiple_of((n - 1 - a) * LANES + c * nq, LANES), chunk)
                else:
                    at = pl.ds((n - 1 - a) * LANES + qc * chunk, chunk)
                s_a = mm(kk[h, a * LANES : (a + 1) * LANES, :], rhs) + bias[h, :, at]
                s.append(s_a)
                m_a = fold(s_a, jnp.maximum)
                top = m_a if top is None else jnp.maximum(top, m_a)
            top = jnp.max(top, axis=0, keepdims=True)
            for a in range(n):
                o["e"][h, a * LANES : (a + 1) * LANES, qs] = jnp.exp2(s[a] - top).astype(BF16)
            raw = mm(va[h], o["e"][h, :, qs])
            inv = 1.0 / raw[head : head + 1, :]
            o["r"][h : h + 1, qs] = inv
            o["att"][hs, qs] = (raw[:head, :] * inv).astype(BF16)
        copies((o["e"], h))
    copies(o["r"], o["att"])
    wait("out")
    if half:
        x_q = x_b[:, mine].astype(F32)
    else:
        x_q = x_b[...].astype(F32)
    o["mid"][...] = x_q + mm(wout_t[...], o["att"][...])
    copies(o["mid"])
    for b in range(nq // span):
        norm_into(n1, b * span, o["mid"][:, b * span : (b + 1) * span], nffn[...])
    ff = wg_t.shape[0]
    step = 256
    wait("ffn")
    for b in range(ff // step):
        cs = slice(b * step, (b + 1) * step)
        gate = mm(wg_t[cs, :], n1[:, :nq])
        up = mm(wu_t[cs, :], n1[:, :nq])
        sq = gate * gate
        th = jnp.tanh(gate * (0.7978845608028654 + (0.7978845608028654 * 0.044715) * sq))
        half_th = 0.5 + 0.5 * th
        gelu = gate * half_th
        slope = half_th + (gelu - gelu * th) * (0.7978845608028654 + (3 * 0.7978845608028654 * 0.044715) * sq)
        o["hid"][cs, :] = (gelu * up).astype(BF16)
        o["a"][cs, :] = (up * slope).astype(BF16)
        o["ge"][cs, :] = gelu.astype(BF16)
    copies(o["hid"], o["a"], o["ge"])
    wait("down")
    res = tok.at[:, :nq]
    res[...] = o["mid"][...] + mm(wd_t[...], o["hid"][...])
    valid = (seg[0:1, mine] != 0.0).astype(F32)
    part = None
    for b in range(nq // span):
        blk = res[:, b * span : (b + 1) * span] * valid[:, b * span : (b + 1) * span]
        part = blk if part is None else part + blk
    o["pool"][...] = jnp.broadcast_to(col_sum(part.T), o["pool"].shape)
    copies(o["pool"])
    send_blocks(half, res, o["blocks"], span)


def send_blocks(half, res, outs, span):
    me, _, c = position()
    for k, out in enumerate(outs):
        block = (c + k) % 2 if half else me ^ k
        at = pl.multiple_of(block * span, span)
        out[:span, :] = res[:, pl.ds(at, span)].T.astype(BF16)


FORWARD_OUTS = ("kt", "q", "v", "x", "seg", "e", "r", "att", "mid", "hid", "a", "ge", "pool", "n1")


def forward_outs(half, n, span, width, inner, heads, ff):
    length = n * span
    nq = length // 2 if half else length
    shapes = (
        ((inner, length), BF16), ((nq, inner), BF16), ((length, inner), BF16), ((width, nq), BF16), ((8, length), F32),
        ((heads, length, nq), BF16), ((8, nq), F32), ((inner, nq), BF16), ((width, nq), F32), ((ff, nq), BF16),
        ((ff, nq), BF16), ((ff, nq), BF16), ((8, width), F32), ((width, nq), BF16),
    )
    return shapes


def forward_kernel(kinds, n, per, heads, *refs):
    count = len(FORWARD_OUTS)
    tokens, seg_ids, bias, wqkv_t, wout_t, wg_t, wu_t, wd_t, nattn, nffn = refs[:10]
    near, far, again = refs[10:13]
    at = 13
    outs = [refs[at + i * count : at + (i + 1) * count] for i in range(len(kinds))]
    at += count * len(kinds)
    block_outs = refs[at : at + 3]
    at += 3
    bufs = [refs[at + i * count : at + (i + 1) * count] for i in range(len(kinds))]
    at += count * len(kinds)
    blocks = refs[at : at + 3]
    at += 3
    own, tok, seg, n1, kk, va, x_b, bias_b, wqkv_b, wout_b, wg_b, wu_b, wd_b, in_sems, out_sems = refs[at:]
    me, p, c = position()
    ins = Copies(in_sems)
    owns = []
    for i, (slot, half) in enumerate(kinds):
        row = per * p + (per - 1 if half else 2 * c + slot)
        owns.append((ins.start(tokens.at[row], own.at[i]), row))
    waits = {
        "qkv": [ins.start(wqkv_t, wqkv_b)],
        "bias": [ins.start(bias, bias_b)],
        "out": [ins.start(wout_t, wout_b)],
        "ffn": [ins.start(wg_t, wg_b), ins.start(wu_t, wu_b)],
        "down": [ins.start(wd_t, wd_b)],
    }

    def wait(what):
        for copy in waits.pop(what, ()):
            copy.wait()

    writes = Copies(out_sems)
    pending = []
    for i, (slot, half) in enumerate(kinds):
        copy, row = owns[i]
        copy.wait()
        o = dict(zip(FORWARD_OUTS, bufs[i]))
        dst = dict(zip(FORWARD_OUTS, outs[i]))
        o["blocks"] = (blocks[0].at[i], blocks[1].at[i], blocks[2].at[2 * i], blocks[2].at[2 * i + 1])
        names = {id(v): k for k, v in o.items()}

        def copies(*what, o=o, dst=dst, names=names):
            for item in what:
                if isinstance(item, tuple):
                    ref, h = item
                    pending.append(writes.start(ref.at[h], dst[names[id(ref)]].at[h]))
                else:
                    pending.append(writes.start(item, dst[names[id(item)]]))

        c1, y_mine, c2_mine = near.at[i], far.at[2 * i], again.at[2 * i + (not half)]
        own_seg = seg_ids[pl.ds(row, 1), :].astype(F32)
        forward_slot(
            half, n, (own.at[i], c1, y_mine, c2_mine, own_seg), (tok, seg, n1, kk, va, x_b, None),
            (bias_b, wqkv_b, wout_b, wg_b, wu_b, wd_b, nattn, nffn), wait, o, copies,
        )
        pending.append(writes.start(blocks[0].at[i], block_outs[0].at[i]))
        pending.append(writes.start(blocks[1].at[i], block_outs[1].at[i]))
        pending.append(writes.start(blocks[2].at[pl.ds(2 * i, 2)], block_outs[2].at[pl.ds(2 * i, 2)]))
    for copy in pending:
        copy.wait()


def middle_kernel(n, per, *refs):
    grad_y, eg, w_head, w_down, w_gate, w_up, w_out, nffn, pool_other = refs[:9]
    at = 9
    near, far, again = refs[at : at + 3]
    at += 3
    names = ("mid", "a", "ge", "hid", "att", "seg", "r", "pool")
    srcs = [dict(zip(names, refs[at + 8 * i : at + 8 * i + 8])) for i in range(3)]
    at += 24
    ga_o, gt_o = refs[at : at + 3], refs[at + 3 : at + 6]
    own_o, send_o, gnf_o, emb_o, pg_o = refs[at + 6 : at + 11]
    at += 11
    big = ("mid", "a", "ge", "hid", "att")
    bufs = [dict(zip(big, refs[at + 5 * i : at + 5 * i + 5])) for i in range(3)]
    at += 15
    own, tok, gout, gb, n2, gg, gu, acc, wh, wd, wg, wu, wo, sems = refs[at:]
    span, width = own.shape[1:]
    length = n * span
    ff = w_gate.shape[1]
    inner = w_out.shape[0]
    head = inner // 6
    wide = w_head.shape[1]
    me, p, c = position()
    ins = Copies(sems)
    owns = []
    for i in range(3):
        row = per * p + (per - 1 if i == 2 else 2 * c + i)
        owns.append(ins.start(grad_y.at[row], own.at[i]))
    weights = {k: ins.start(a, b) for k, a, b in (("h", w_head, wh), ("d", w_down, wd))}
    loads = [{k: ins.start(srcs[0][k], bufs[0][k]) for k in ("a", "ge", "mid", "hid")}]
    for k, a, b in (("g", w_gate, wg), ("u", w_up, wu), ("o", w_out, wo)):
        weights[k] = ins.start(a, b)
    loads[0]["att"] = ins.start(srcs[0]["att"], bufs[0]["att"])
    for i in (1, 2):
        loads.append({k: ins.start(srcs[i][k], bufs[i][k]) for k in big})

    def need(*names):
        for k in names:
            if k in weights:
                weights.pop(k).wait()

    part_total = None
    for i in range(3):
        half = i == 2
        nq = length // 2 if half else length
        src, buf = srcs[i], bufs[i]
        owns[i].wait()
        for k, piece in enumerate((own.at[i], near.at[i], far.at[2 * i], again.at[2 * i + (not half)])):
            place = pl.multiple_of((me ^ k) * span, span)
            tok[pl.ds(place, span), :] = piece[...].astype(F32)
        seg = src["seg"]
        count = jnp.sum((seg[0:1, :] != 0.0).astype(F32), axis=1, keepdims=True)
        pool = src["pool"][0:1, :]
        if half:
            pool = pool + pool_other[0:1, :]
        pool = pool / count
        need("h")
        proj = wide_dot(pool, wh[...], mm)
        inv = lax.rsqrt(jnp.sum(proj * proj, axis=1, keepdims=True) + EPS)
        emb = proj * inv
        row = per * p + (per - 1 if half else 2 * c + i)
        cot = eg[pl.ds(row, 1), :]
        g_proj = inv * (cot - emb * jnp.sum(emb * cot, axis=1, keepdims=True))
        emb_o[i] = jnp.broadcast_to(emb, emb_o.shape[1:])
        once = jnp.where(c == 0, 1.0, 0.0) if half else 1.0
        for q in range((width + wide) // 256):
            part = pool[:, q * 256 : (q + 1) * 256] if q < width // 256 else g_proj[:, q * 256 - width : (q + 1) * 256 - width]
            pg_o[5 * i + q : 5 * i + q + 1, :] = part * once
        g_pool = wide_dot(g_proj, wh[...], mm_nt) / count
        g_col = jnp.broadcast_to(g_pool, (span, width)).T
        first = c * (nq // span) if half else 0
        for b in range(nq // span):
            bs = slice(b * span, (b + 1) * span)
            if half:
                place = pl.ds(pl.multiple_of((first + b) * span, span), span)
            else:
                place = pl.ds(b * span, span)
            valid = (seg[0:1, place] != 0.0).astype(F32)
            blk = tok[place, :].T + valid * g_col
            gout[:, bs] = blk
            gb[:, bs] = blk.astype(BF16)
        need("d")
        loads[i].pop("a").wait()
        loads[i].pop("ge").wait()
        step = 256
        for b in range(ff // step):
            cs = slice(b * step, (b + 1) * step)
            g_hid = mm(wd[cs, :], gb[:, :nq])
            gg[cs, :nq] = (g_hid * buf["a"][cs, :].astype(F32)).astype(BF16)
            gu[cs, :nq] = (g_hid * buf["ge"][cs, :].astype(F32)).astype(BF16)
        loads[i].pop("mid").wait()
        loads[i].pop("hid").wait()
        need("g", "u")
        res = tok.at[:, :nq]
        res[...] = mm(wg[...], gg[:, :nq]) + mm(wu[...], gu[:, :nq])

        def add(place, value, i=i):
            if i == 0:
                acc[:, place] = value
            else:
                acc[:, place] += value

        for b in range(2):
            add(slice(2 * ff + b * width, 2 * ff + (b + 1) * width), mm_nt(buf["hid"][b * width : (b + 1) * width, :], gb[:, :nq]))
        part = None
        for b in range(nq // span):
            bs = slice(b * span, (b + 1) * span)
            m = buf["mid"][:, bs]
            inv2 = lax.rsqrt(col_sum(m * m) / width + EPS)
            hat = m * inv2
            n2[:, bs] = (hat * nffn[...]).astype(BF16)
            gn = res[:, bs]
            c2_ = gn * nffn[...]
            part = gn * hat if part is None else part + gn * hat
            mean = col_sum(c2_ * hat) / width
            ga_o[i][:, bs] = (gout[:, bs] + inv2 * (c2_ - hat * mean)).astype(BF16)
        part_total = part if part_total is None else part_total + part
        for b in range(2):
            cs = slice(b * 512, (b + 1) * 512)
            add(cs, mm_nt(n2[:, :nq], gg[cs, :nq]))
            add(slice(ff + b * 512, ff + (b + 1) * 512), mm_nt(n2[:, :nq], gu[cs, :nq]))
        need("o")
        gatt = mm(wo[...], ga_o[i][...]).astype(BF16).astype(F32)
        for h in range(6):
            hs = slice(h * head, (h + 1) * head)
            gt_o[i][hs, :] = (gatt[hs, :] * src["r"][h : h + 1, :]).astype(BF16)
        loads[i].pop("att").wait()
        add(slice(2 * ff + 2 * width, 2 * ff + 2 * width + inner), mm_nt(ga_o[i][...], buf["att"][...]))
    gnf_o[...] = jnp.broadcast_to(col_sum(part_total.T), gnf_o.shape)
    pg_o[15:16, :] = jnp.zeros((1, 256), F32)
    rows = own_o.shape[0]
    own_o[...] = acc[pl.ds(pl.multiple_of(c * rows, rows), rows), :].astype(BF16)
    send_o[...] = acc[pl.ds(pl.multiple_of((1 - c) * rows, rows), rows), :].astype(BF16)


def attention_back(half, n, q_nat, v_nat, kt, e_wait, e_b, att, gt, gs, table, line, gq_o, put_kv):
    heads = e_b.shape[0]
    inner = kt.shape[0]
    head = inner // heads
    length = kt.shape[1]
    nq = length // 2 if half else length
    _, _, c = position()
    lane = lax.broadcasted_iota(jnp.int32, (length, LANES), 1)
    gt_nat = gt[...].astype(F32).T.astype(BF16)
    zeros = jnp.zeros((head, nq), BF16)
    for pair in range(heads // 2):
        ps = slice(pair * LANES, (pair + 1) * LANES)
        gk = []
        gv = []
        for side in range(2):
            h = pair * 2 + side
            hs = slice(h * head, (h + 1) * head)
            g_h = gt[hs, :]
            delta = col_sum(g_h.astype(F32) * att[hs, :].astype(F32))
            rhs = jnp.concatenate([g_h, zeros] if side == 0 else [zeros, g_h], axis=0)
            table[...] = jnp.zeros_like(table)
            e_wait(h)
            for a in range(n):
                ks = slice(a * LANES, (a + 1) * LANES)
                g_p = mm(v_nat[ks, ps], rhs)
                g_s = (e_b[h, ks, :].astype(F32) * (g_p - delta)).astype(BF16)
                gs[ks, :nq] = g_s
                if half:
                    at = pl.ds(pl.multiple_of((n - 1 - a) * LANES + c * nq, LANES), nq)
                else:
                    at = pl.ds((n - 1 - a) * LANES, nq)
                table[:, at] += g_s.astype(F32)
            line(h, diagonal_sums(table))
            gq_o[hs, :] = mm(kt[hs, :], gs[:, :nq]).astype(BF16)
            gk.append(mm(gs[:, :nq], q_nat[:, ps]))
            gv.append(mm(e_b[h], gt_nat[:, ps]))
        put_kv(pair, 0, jnp.where(lane < head, gk[0], gk[1]).T)
        put_kv(pair, 1, jnp.where(lane < head, gv[0], gv[1]).T)


def half_back_kernel(n, q_nat, v_nat, kt, e_in, att, gt, gq_o, keep_o, send_o, line_o, e_b, gs, table, kv, sems):
    ins = Copies(sems)
    loads = [ins.start(e_in.at[h], e_b.at[h]) for h in range(e_in.shape[0])]
    inner = kt.shape[0]

    def put(pair, which, value):
        kv[which * inner + pair * LANES : which * inner + (pair + 1) * LANES, :] = value.astype(BF16)

    def line(h, value):
        line_o[h : h + 1, :] = value

    line_o[...] = jnp.zeros_like(line_o)
    attention_back(True, n, q_nat, v_nat, kt, lambda h: loads[h].wait(), e_b, att, gt, gs, table, line, gq_o, put)
    _, _, c = position()
    nq = kt.shape[1] // 2
    keep_o[...] = kv[:, pl.ds(pl.multiple_of(c * nq, nq), nq)]
    send_o[...] = kv[:, pl.ds(pl.multiple_of((1 - c) * nq, nq), nq)]


def backward_kernel(
    slot, n,
    q_nat, v_nat, kt, e_in, att, gt, n1, acc_in, line_in,
    acc_o, line_o, gq,
    e_b, gs, table, acc, sems,
):
    ins = Copies(sems)
    loads = [ins.start(e_in.at[h], e_b.at[h]) for h in range(e_in.shape[0])]
    old = ins.start(acc_in, acc) if slot else None
    inner = kt.shape[0]

    def put(pair, which, value):
        at = (1 + which) * inner + pair * LANES
        gq[at : at + LANES, :] = value.astype(BF16)

    def line(h, value):
        line_o[h : h + 1, :] = line_in[h : h + 1, :] + value

    line_o[...] = line_in[...]
    attention_back(False, n, q_nat, v_nat, kt, lambda h: loads[h].wait(), e_b, att, gt, gs, table, line, gq.at[:inner, :], put)
    grads = mm_nt(n1[...], gq[...])
    if slot:
        old.wait()
        acc[...] += grads
    else:
        acc[...] = grads
    out = ins.start(acc, acc_o)
    out.wait()


def last_kernel(gq_half, keep, got, n1, acc_in, own_o, send_o, gq, acc):
    inner = gq_half.shape[0]
    gq[:inner, :] = gq_half[...]
    gq[inner:, :] = (keep[...].astype(F32) + got[...].astype(F32)).astype(BF16)
    acc[...] = acc_in[...] + mm_nt(n1[...], gq[...])
    _, _, c = position()
    rows = own_o.shape[0]
    own_o[...] = acc[pl.ds(pl.multiple_of(c * rows, rows), rows), :].astype(BF16)
    send_o[...] = acc[pl.ds(pl.multiple_of((1 - c) * rows, rows), rows), :].astype(BF16)


def inputs_kernel(
    gq0, gq1, gq2, xt0, xt1, xt2, ga0, ga1, ga2, w_qkv, nattn, emb, line_in, gnf, indicator,
    b_own, b_c, b_y, small,
    res,
):
    width = res.shape[0]
    span = b_own.shape[1] - EXT
    small[...] = jnp.zeros_like(small)
    total = None
    for i, (gq, xt, ga) in enumerate(((gq0, xt0, ga0), (gq1, xt1, ga1), (gq2, xt2, ga2))):
        nq = gq.shape[1]
        res[:, :nq] = mm(w_qkv[...], gq[...])
        for b in range(nq // span):
            bs = slice(b * span, (b + 1) * span)
            x = xt[:, bs].astype(F32)
            inv = lax.rsqrt(col_sum(x * x) / width + EPS)
            hat = x * inv
            gn = res[:, bs]
            c1 = gn * nattn[...]
            total = gn * hat if total is None else total + gn * hat
            mean = col_sum(c1 * hat) / width
            res[:, bs] = ga[:, bs].astype(F32) + inv * (c1 - hat * mean)
        outs = (b_own.at[i], b_c.at[i], b_y.at[2 * i], b_y.at[2 * i + 1])
        send_blocks(i == 2, res, outs, span)
        row = emb[i, 0:1, :]
        high = row.astype(BF16)
        low = (row - high.astype(F32)).astype(BF16)
        rest = row.shape[1] - width
        for out in outs:
            for at, v in ((0, high), (2, low)):
                out[span + at : span + at + 1, :] = v[:, :width]
                out[span + at + 1 : span + at + 2, :rest] = v[:, width:]
    gna = col_sum(total.T)
    for i in range(width // LANES):
        small[i : i + 1, :] = gnf[0:1, i * LANES : (i + 1) * LANES]
        small[4 + i : 5 + i, :] = gna[:, i * LANES : (i + 1) * LANES]
    lines = line_in[...]
    hi = lines.astype(BF16)
    lo = (lines - hi.astype(F32)).astype(BF16)
    small[8:16, :] = mm_nt(hi, indicator[...]) + mm_nt(lo, indicator[...])


def unpack_kernel(per, with_emb, *refs):
    groups = (len(refs) - 1 - (3 if with_emb else 1)) // 4
    out = refs[4 * groups]
    sems = refs[-1]
    ways = []
    for g in range(groups):
        own, c1, y, d = refs[4 * g : 4 * g + 4]
        ways += [(own.at[i], c1.at[i], y.at[2 * i], d.at[2 * i + 1]) for i in range(own.shape[0])]
    own0 = ways[0][0]
    me, p, _ = position()
    rows, span, width = out.shape
    for r in range(rows):
        pair, j = divmod(r, per)
        slot = 2 if j == per - 1 else j % 2
        core = p if slot == 2 else j // 2
        k = me ^ (pair * 2 + core)
        for which in range(4):
            ref = ways[slot][which]

            @pl.when(k == which)
            def _(ref=ref, r=r):
                pltpu.make_async_copy(ref.at[pl.ds(0, span)], out.at[r], sems.at[r]).start()
                if with_emb:
                    pltpu.make_async_copy(ref.at[pl.ds(span, EXT)], refs[4 * groups + 2].at[r], sems.at[rows + r]).start()

    if with_emb:
        emb, got = refs[4 * groups + 1 : 4 * groups + 3]
        for r in range(rows):
            pltpu.make_async_copy(own0.at[pl.ds(span, EXT)], got.at[r], sems.at[rows + r]).wait()
            value = got[r].astype(F32)
            emb[r : r + 1, :width] = value[0:1, :] + value[2:3, :]
            emb[r : r + 1, width:] = (value[1:2, :] + value[3:4, :])[:, : emb.shape[1] - width]
    for r in range(rows):
        pltpu.make_async_copy(own0.at[pl.ds(0, span)], out.at[r], sems.at[r]).wait()


def place(step):
    if step is None:
        return 0, 1
    if step == "square":
        return (lax.axis_index("rows") % 2) + 2 * (lax.axis_index("seq") // 2), 4
    axis, stride, radix = step
    return (lax.axis_index(axis) // stride) % radix, radix


def combine_kernel(plan, *refs):
    at = sum(len(arrays) for pieces, _ in plan for arrays, _, _ in pieces)
    outs = at + sum(place(step)[1] for _, step in plan)
    ins, at, scratch = 0, at, outs
    for pieces, step in plan:
        off = 0
        total = refs[scratch] if step else refs[at]
        for arrays, lo, hi in pieces:
            value = sum(refs[ins + i][..., lo:hi].astype(F32) for i in range(len(arrays)))
            ins += len(arrays)
            total[..., off : off + hi - lo] = value.astype(BF16)
            off += hi - lo
        if step:
            d, radix = place(step)
            for k in range(radix):
                refs[at + k][...] = total[d ^ k]
            at += radix
            scratch += 1
        else:
            at += 1


def join_kernel(plan, *refs):
    ins, at = 0, sum(place(step)[1] for step, _ in plan)
    for step, cuts in plan:
        d, radix = place(step)
        for lo, hi in cuts:
            for k in range(radix):
                refs[at][d ^ k] = refs[ins + k][:, lo:hi]
            at += 1
        ins += radix


def finish_early_kernel(second, *refs):
    if second:
        b_own, a, b, *rest = refs
        gate_o, up_o, down_o, out_o, head_o, gate, up, down, out, head, sems = rest[4:]
    else:
        a, b, gate_o, up_o, down_o, out_o, gate, up, down, out, sems = refs
    _, _, c = position()
    rows, cut = a.shape
    ff = gate.shape[1]
    width = gate_o.shape[0]
    inner = out.shape[0]
    rest = ff - (cut - ff)
    start = pl.multiple_of(((1 - c) if second else c) * rows, rows)
    at = pl.ds(start, rows)
    copies = Copies(sems)
    gate[...] = a[:, :ff].astype(F32)
    pending = [copies.start(gate, gate_o.at[at])]
    down[0] = b[:, rest : rest + width].astype(F32)
    pending.append(copies.start(down.at[0], down_o.at[at]))
    down[1] = b[:, rest + width : rest + 2 * width].astype(F32)
    pending.append(copies.start(down.at[1], down_o.at[pl.ds(pl.multiple_of(width + start, rows), rows)]))
    up[:, : cut - ff] = a[:, ff:].astype(F32)
    up[:, cut - ff :] = b[:, :rest].astype(F32)
    pending.append(copies.start(up, up_o.at[at]))
    out[...] = b[:, rest + 2 * width : rest + 2 * width + inner].astype(F32).T
    pending.append(copies.start(out, out_o.at[:, at]))
    if second:
        row = lax.broadcasted_iota(jnp.int32, (rows, 256), 0) % 16
        for ref in (b_own, b):
            g = ref[:, ref.shape[1] - 256 :].astype(F32)
            turned = {t: pltpu.roll(g, rows - t, 0).astype(BF16) for t in range(1, 5)}
            for i in range(2):
                kept = jnp.where((row < 15) & (row % 5 == i), g, 0.0).T.astype(BF16)
                for j in range(3):
                    term = mm(kept, turned[2 + j - i])
                    place = (slice(i * 256, (i + 1) * 256), slice(j * 256, (j + 1) * 256))
                    if ref is b_own:
                        head[place] = term
                    else:
                        head[place] += term
        pending.append(copies.start(head, head_o))
    for copy in pending:
        copy.wait()


def finish_late_kernel(block, own, got, q_o, k_o, v_o, nf_o, na_o, table_o):
    _, _, c = position()
    rows = own.shape[0]
    inner = q_o.shape[1]
    small = None
    for ref, side in ((own, c), (got, 1 - c)):
        at = pl.ds(pl.multiple_of(side * rows, rows), rows)
        for i, out in enumerate((q_o, k_o, v_o)):
            out[at, :] = ref[:, i * inner : (i + 1) * inner].astype(F32)
        for b in range(0, rows, block):
            value = ref[b : b + 16, 3 * inner :].astype(F32)
            small = value if small is None else small + value
    for i in range(nf_o.shape[1] // LANES):
        nf_o[:, i * LANES : (i + 1) * LANES] = small[i : i + 1, :]
        na_o[:, i * LANES : (i + 1) * LANES] = small[4 + i : 5 + i, :]
    table_o[...] = small[8:16, :].T[: table_o.shape[0], : table_o.shape[1]]


def sds(shape, dtype=BF16):
    return jax.ShapeDtypeStruct(shape, dtype)


def call(kernel, outs, args, scratch=(), specs=None, out_specs=None, flops=0, name=None, vmem=56, deps=(), aliases=None):
    count = len(args)

    def body(*refs):
        kernel(*refs[:count], *refs[count + len(deps) :])

    return pl.pallas_call(
        body,
        out_shape=outs,
        in_specs=list(specs or [VMEM] * count) + [ANY] * len(deps),
        out_specs=out_specs or jax.tree.map(lambda _: VMEM, outs),
        scratch_shapes=list(scratch),
        compiler_params=pltpu.CompilerParams(vmem_limit_bytes=vmem * 2**20),
        cost_estimate=pl.CostEstimate(flops=flops, bytes_accessed=10_000_000, transcendentals=0),
        input_output_aliases=aliases or {},
        name=name,
    )(*args, *deps)


def swap(x, axis, k):
    n = lax.axis_size(axis)
    return lax.ppermute(x, axis, [(i, i ^ k) for i in range(n)])


def after(x, *deps):
    return lax.optimization_barrier((x, *deps))[0]


def together(*trees):
    leaves, shape = jax.tree.flatten(trees)
    return jax.tree.unflatten(shape, lax.optimization_barrier(leaves))


def row_digits():
    n = lax.axis_size("rows")
    out = []
    stride = 1
    while stride < n:
        r = 2 if stride == 1 or n // stride < 4 else 4
        out.append(("rows", stride, r))
        stride *= r
    return out


def shards(
    tokens, seg_ids, w_query, w_key, w_value, w_out, w_gate, w_up, w_down, w_head, norm_attn, norm_ffn,
    bucket_bias_table, grad_y, embedding_gradient,
):
    rows, span, width = tokens.shape
    buckets, heads = bucket_bias_table.shape
    n = lax.axis_size("seq")
    inner = w_query.shape[1]
    ff = w_gate.shape[1]
    wide = w_head.shape[1]
    length = n * span
    per = rows // 2
    assert n == 4 and per == 5

    def send_rows(array, ids, slots, ext, deps=()):
        size = span + ext
        outs = [sds((2 * len(slots) - (2 in slots), size, width)), sds((len(slots), size, width))]
        packed = call(
            functools.partial(pack_kernel, per, slots, ext), tuple(outs), (array, ids) if ext else (array,), vmem=16,
            name="pack", deps=deps,
        )
        return (swap(packed[1], "seq", 1), swap(packed[0], "seq", 2)), packed

    def pass_on(got, *deps):
        near, far = got
        return near, far, swap(after(far, *deps) if deps else far, "seq", 1)

    line = 2 * length
    x_a, _ = send_rows(tokens, seg_ids, (0,), EXT)
    bias, ind, nattn, nffn, w_qkv, wqkv_t, wout_t, wg_t, wu_t, wd_t = call(
        functools.partial(prepare_kernel, n),
        (
            sds((heads, LANES, line), F32), sds((LANES, line)), sds((width, LANES), F32), sds((width, LANES), F32),
            sds((width, 3 * inner)), sds((3 * inner, width)), sds((width, inner)), sds((ff, width)), sds((ff, width)),
            sds((width, ff)),
        ),
        (
            bucket_bias_table, norm_attn[None], norm_ffn[None], w_query, w_key, w_value, w_out, w_gate, w_up, w_down,
        ),
        [pltpu.VMEM((LANES, LANES), F32)], name="prepare", flops=4_000_000_000,
    )
    x_b, packed_x = send_rows(tokens, seg_ids, (1, 2), EXT, deps=(nattn,))
    x_a = pass_on(x_a, packed_x[1])

    def collect(own, c, y):
        return own, swap(c, "seq", 1), swap(y, "seq", 2)

    def collect_rest(part, *deps):
        return *part, swap(after(part[2], *deps), "seq", 1)

    def run_forward(kinds, pieces, deps=()):
        shapes = [s for _, half in kinds for s in forward_outs(half, n, span, width, inner, heads, ff)]
        shapes += [((k * len(kinds), span, width), BF16) for k in (1, 1, 2)]
        outs = tuple(sds(*s) for s in shapes)
        args = [tokens, seg_ids, bias, wqkv_t, wout_t, wg_t, wu_t, wd_t, nattn, nffn]
        specs = [ANY, VMEM] + [ANY] * 6 + [VMEM] * 2
        args += list(pieces)
        specs += [VMEM] * 3
        scratch = [pltpu.VMEM(*s) for s in shapes]
        scratch += [
            pltpu.VMEM((len(kinds), span, width), BF16), pltpu.VMEM((length, width), F32), pltpu.VMEM((LANES, length), F32),
            pltpu.VMEM((width, length), BF16), pltpu.VMEM((heads, length, 2 * LANES), BF16),
            pltpu.VMEM((heads, inner // heads + EXT, length), BF16), pltpu.VMEM((width, length), BF16),
            pltpu.VMEM(bias.shape, F32), *[pltpu.VMEM(w.shape, BF16) for w in (wqkv_t, wout_t, wg_t, wu_t, wd_t)],
            pltpu.SemaphoreType.DMA((8 + len(kinds),)), pltpu.SemaphoreType.DMA((24 * len(kinds),)),
        ]
        res = call(
            functools.partial(forward_kernel, kinds, n, per, heads), outs, args, scratch, specs, tuple(ANY for _ in outs),
            4_000_000_000 * len(kinds), "forward", deps=deps,
        )
        count = len(FORWARD_OUTS)
        return [dict(zip(FORWARD_OUTS, res[i * count : (i + 1) * count])) for i in range(len(kinds))], collect(*res[-3:])

    fwd, blocks_a = run_forward([(0, False)], x_a, deps=packed_x)
    x_b = pass_on(x_b, fwd[0]["r"])
    gys, packed_g = send_rows(grad_y, None, (0, 1, 2), 0, deps=(fwd[0]["r"],))
    fwd_b, blocks_b = run_forward([(1, False), (2, True)], x_b, deps=packed_g)
    fwd += fwd_b
    gys = pass_on(gys, fwd[1]["r"])
    pool_other = swap(fwd[2]["pool"], "seq", 1)

    def unpack(parts, with_emb, deps=()):
        args = [a for group in parts for a in group]
        outs = (sds((rows, span, width)),) + ((sds((rows, wide), F32),) if with_emb else ())
        scratch = [pltpu.VMEM((rows, EXT, width), BF16)] if with_emb else []
        return call(
            functools.partial(unpack_kernel, per, with_emb), outs, args, scratch + [pltpu.SemaphoreType.DMA((2 * rows,))],
            [ANY] * len(args), (ANY, VMEM)[: len(outs)], vmem=16, name="unpack", deps=deps,
        )


    packed_w = 2 * ff + 2 * width + inner
    nqs = [length, length, length // 2]
    args = [grad_y, embedding_gradient, w_head, w_down, w_gate, w_up, w_out, nffn, pool_other]
    specs = [ANY, VMEM] + [ANY] * 5 + [VMEM] * 2
    args += list(gys)
    specs += [VMEM] * 3
    for f in fwd:
        args += [f[k] for k in ("mid", "a", "ge", "hid", "att", "seg", "r", "pool")]
        specs += [ANY] * 5 + [VMEM] * 3
    outs = tuple(
        [sds((width, q)) for q in nqs] + [sds((inner, q)) for q in nqs]
        + [sds((width // 2, packed_w))] * 2 + [sds((8, width), F32), sds((3, 8, wide), F32), sds((16, 256), F32)]
    )
    scratch = []
    for q in nqs:
        scratch += [
            pltpu.VMEM((width, q), F32), pltpu.VMEM((ff, q), BF16), pltpu.VMEM((ff, q), BF16), pltpu.VMEM((ff, q), BF16),
            pltpu.VMEM((inner, q), BF16),
        ]
    scratch += [
        pltpu.VMEM((3, span, width), BF16), pltpu.VMEM((length, width), F32), pltpu.VMEM((width, length), F32),
        pltpu.VMEM((width, length), BF16), pltpu.VMEM((width, length), BF16), pltpu.VMEM((ff, length), BF16),
        pltpu.VMEM((ff, length), BF16), pltpu.VMEM((width, packed_w), F32), pltpu.VMEM(w_head.shape, BF16),
        pltpu.VMEM(w_down.shape, BF16), pltpu.VMEM(w_gate.shape, BF16), pltpu.VMEM(w_up.shape, BF16),
        pltpu.VMEM(w_out.shape, BF16), pltpu.SemaphoreType.DMA((23,)),
    ]
    m = call(functools.partial(middle_kernel, n, per), outs, args, scratch, specs, flops=15_000_000_000, name="middle")
    m, blocks_a, blocks_b = together(m, blocks_a, blocks_b)
    ga, gt = m[:3], m[3:6]
    own, send, gnf, emb, pg = m[6:]

    core = ("seq", 1, 2)
    far = ("seq", 2, 2)
    digits = row_digits()
    block = width // 2 // far[2]
    for d in digits:
        block //= d[2]

    def send_shares(parts, s):
        return [swap(p, s[0], k * s[1]) for k, p in enumerate(parts) if k]

    def send_all(v, s):
        return [swap(v, s[0], k * s[1]) for k in range(1, s[2])]

    strides = [1 << i for i in range(1, lax.axis_size("rows").bit_length() - 1)]

    def swap_square(x, k):
        if k == 1:
            return swap(x, "rows", 1)
        if k == 2:
            return swap(x, "seq", 2)
        nr = lax.axis_size("rows")
        return lax.ppermute(x, ("rows", "seq"), [(r * n + q, (r ^ 1) * n + (q ^ 2)) for r in range(nr) for q in range(n)])

    def send_square(parts):
        return [swap_square(parts[k], k) for k in (1, 2, 3)]

    def send_all_square(v):
        return [swap_square(v, k) for k in (1, 2, 3)]

    def combine(groups, deps=()):
        args, outs, scratch, plan = [], [], [], []
        for pieces, step in groups:
            rows_, wide_ = pieces[0][0][0].shape[0], sum(hi - lo for _, lo, hi in pieces)
            radix = 4 if step == "square" else step[2] if step else 1
            shape = (radix, rows_ // radix) if step else (rows_,)
            for arrays, _, _ in pieces:
                args += [a.reshape(shape + a.shape[-1:]) for a in arrays]
            outs += [sds((rows_ // radix, wide_))] * radix
            scratch += [pltpu.VMEM(shape + (wide_,), BF16)] if step else []
            plan.append((pieces, step))
        plan = [([(range(len(a)), lo, hi) for a, lo, hi in pieces], step) for pieces, step in plan]
        res = call(functools.partial(combine_kernel, plan), tuple(outs), args, scratch, vmem=24, name="combine", deps=deps)
        out = []
        for _, step in plan:
            radix = 4 if step == "square" else step[2] if step else 1
            out.append(list(res[:radix]))
            res = res[radix:]
        return out

    def joined(groups, deps=()):
        args, outs, plan = [], [], []
        for v, got, step, cuts in groups:
            cuts = cuts or [(0, v.shape[1])]
            args += [v] + got
            outs += [sds((4 if step == "square" else step[2], v.shape[0], hi - lo)) for lo, hi in cuts]
            plan.append((step, cuts))
        res = call(functools.partial(join_kernel, plan), tuple(outs), args, vmem=24, name="join", deps=deps)
        return [r.reshape(-1, r.shape[-1]) for r in res]

    def all_of(*arrays):
        return [(list(arrays), 0, arrays[0].shape[1])]

    nh = length // 2
    half = call(
        functools.partial(half_back_kernel, n),
        (sds((inner, nh)), sds((2 * inner, nh)), sds((2 * inner, nh)), sds((8, line), F32)),
        (fwd[2]["q"], fwd[2]["v"], fwd[2]["kt"], fwd[2]["e"], fwd[2]["att"], gt[2]),
        [
            pltpu.VMEM((heads, length, nh), BF16), pltpu.VMEM((length, length), BF16), pltpu.VMEM((LANES, line), F32),
            pltpu.VMEM((2 * inner, length), BF16), pltpu.SemaphoreType.DMA((heads,)),
        ],
        [VMEM] * 3 + [ANY] + [VMEM] * 2, flops=2_000_000_000, name="half_back", deps=(send,),
    )
    got = swap(send, "seq", 1)
    block_parts = [collect_rest(p) for p in (blocks_a, blocks_b)]
    half, got, block_parts = together(half, got, block_parts)
    gq_half, keep, send_kv, lines_sum = half
    got_kv = swap(send_kv, "seq", 1)
    cut = packed_w // 2 // LANES * LANES
    sa, sb = [digits[0], far], [far, digits[0]]
    pa, pb = combine([([([own, got], 0, cut)], sa[0]), ([([own, got], cut, packed_w)], sb[0])])

    piece = tuple(sds((i, span + EXT, width)) for i in (1, 1, 2))
    def run_back(j, acc, lines_sum, deps):
        f = fwd[j]
        outs = (sds((width, 3 * inner), F32), sds((8, line), F32), sds((3 * inner, length)))
        args = (f["q"], f["v"], f["kt"], f["e"], f["att"], gt[j], f["n1"], acc, lines_sum)
        scratch = [
            pltpu.VMEM((heads, length, length), BF16), pltpu.VMEM((length, length), BF16), pltpu.VMEM((LANES, line), F32),
            pltpu.VMEM((width, 3 * inner), F32), pltpu.SemaphoreType.DMA((heads + 2,)),
        ]
        return call(
            functools.partial(backward_kernel, j, n), outs, args, scratch,
            [VMEM] * 3 + [ANY] + [VMEM] * 3 + [ANY, VMEM], (ANY, VMEM, VMEM),
            flops=4_000_000_000, name="backward", deps=deps,
        )

    back = run_back(0, gnf, lines_sum, (pa[1], pb[1]))
    ra, rb = send_shares(pa, sa[0]), send_shares(pb, sb[0])
    back, ra, rb, got_kv = together(back, ra, rb, got_kv)
    pa, pb = combine([(all_of(pa[0], *ra), sa[1]), (all_of(pb[0], *rb), sb[1])])
    back2 = run_back(1, back[0], back[1], (pa[1], pb[1]))
    ra, rb = send_shares(pa, sa[1]), send_shares(pb, sb[1])
    back2, ra, rb = together(back2, ra, rb)
    (parts,) = combine([(all_of(pa[0], *ra) + all_of(pb[0], *rb), digits[1])])
    last = call(
        last_kernel, (sds((width // 2, 3 * inner)), sds((width // 2, 3 * inner)), sds((3 * inner, nh))),
        (gq_half, keep, got_kv, fwd[2]["n1"], back2[0]),
        [pltpu.VMEM((width, 3 * inner), F32)], out_specs=None, flops=2_000_000_000, name="last", deps=tuple(parts[1:]),
    )
    got = send_shares(parts, digits[1])
    last, got = together(last, got)
    for step in digits[2:]:
        (parts,) = combine([(all_of(parts[0], *got), step)])
        got = send_shares(parts, step)
    late_got = swap(last[1], "seq", 1)
    pg_b = pg.astype(BF16).reshape(block, -1)
    ((ab,),) = combine([(all_of(parts[0], *got) + all_of(pg_b), None)])
    for step in digits[:1:-1]:
        (ab,) = joined([(ab, send_all(ab, step), step, None)])
    got_ab = send_all(ab, digits[1])
    (parts,) = combine([(all_of(last[0], late_got), "square")])
    got = send_square(parts)
    *x_blocks, small = call(
        inputs_kernel, (*[sds((3 * i, span + EXT, width)) for i in (1, 1, 2)], sds((width // 8, LANES), F32)),
        (
            back[2], back2[2], last[2], *[f["x"] for f in fwd], *ga, w_qkv, nattn, emb, back2[1], gnf, ind,
        ),
        [pltpu.VMEM((width, length), F32)], flops=3_000_000_000, name="inputs", deps=(ab, *parts[1:]),
    )
    got, got_ab, small, x_blocks = together(got, got_ab, small, x_blocks)
    x_parts = collect(*x_blocks)
    ((late,),) = combine([(all_of(parts[0], *got) + all_of(small), None)])
    a, b = joined([(ab, got_ab, digits[1], [(0, cut), (cut, ab.shape[1])])])
    ga_, gb_ = send_all(a, sa[1]), send_all(b, sb[1])
    (block_out,) = unpack(block_parts, False, deps=(late,))
    for i, stride in enumerate(strides):
        got = swap(late, "rows", stride)
        if i == 0:
            got, block_out = together(got, block_out)
        else:
            got, ga_, gb_, x_parts = together(got, ga_, gb_, x_parts)
        ((late,),) = combine([(all_of(late, got), None)])
    got = send_all_square(late)
    a, b = joined([(a, ga_, sa[1], None), (b, gb_, sb[1], None)])
    ga_, gb_ = send_all(a, sa[0]), send_all(b, sb[0])
    x_parts = collect_rest(x_parts)
    got, x_parts = together(got, x_parts)
    (late,) = joined([(late, got, "square", None)])
    late_got = swap(late, "seq", 1)
    grad_x, embedding = unpack([x_parts], True, deps=(late,))
    ga_, gb_, grad_x = together(ga_, gb_, grad_x)
    a, b = joined([(a, ga_, sa[0], None), (b, gb_, sb[0], None)])
    a_got, b_got = swap(a, "seq", 1), swap(b, "seq", 1)
    outs = (sds((width, ff), F32), sds((width, ff), F32), sds((ff, width), F32), sds((inner, width), F32))
    halves = [
        pltpu.VMEM((width // 2, ff), F32), pltpu.VMEM((width // 2, ff), F32), pltpu.VMEM((2, width // 2, width), F32),
        pltpu.VMEM((inner, width // 2), F32),
    ]
    first = call(
        functools.partial(finish_early_kernel, False), outs, (a, b), halves + [pltpu.SemaphoreType.DMA((5,))],
        out_specs=(ANY,) * 4, name="finish_early",
    )
    first, a_got, b_got = together(first, a_got, b_got)
    grad_gate, grad_up, grad_down, grad_out, grad_head = call(
        functools.partial(finish_early_kernel, True), outs + (sds((width, wide), F32),), (b, a_got, b_got, *first),
        halves + [pltpu.VMEM((width, wide), F32), pltpu.SemaphoreType.DMA((6,))], [VMEM] * 3 + [ANY] * 4, (ANY,) * 5,
        name="finish_early", aliases={3: 0, 4: 1, 5: 2, 6: 3},
    )
    if block != 16:
        tail = packed_w - cut
        pg_all = jnp.concatenate([b[:, tail:], b_got[:, tail:]]).reshape(-1, 16, 256)[:, :15].reshape(-1, width + wide)
        grad_head = lax.dot_general(
            pg_all[:, :width], pg_all[:, width:], (((0,), (0,)), ((), ())), preferred_element_type=F32
        )
    grad_query, grad_key, grad_value, grad_norm_ffn, grad_norm_attn, grad_table = call(
        functools.partial(finish_late_kernel, width // 8),
        (*[sds((width, inner), F32)] * 3, sds((1, width), F32), sds((1, width), F32), sds((buckets, heads), F32)),
        (late, late_got), name="finish_late",
    )
    return (
        block_out, embedding, grad_x, grad_query, grad_key, grad_value, grad_out, grad_gate, grad_up, grad_down, grad_head,
        grad_norm_attn[0], grad_norm_ffn[0], grad_table,
    )


def solution(mesh):
    by_pos = P("rows", "seq", None)
    by_row = P("rows", None)
    return jax.shard_map(
        shards,
        mesh=mesh,
        in_specs=(by_pos, P("rows", "seq"), *[P()] * 11, by_pos, by_row),
        out_specs=(by_pos, by_row, by_pos, *[P()] * 11),
        check_vma=False,
    )
```

```python
import functools

import jax
import jax.numpy as jnp
from jax import lax
from jax.experimental import pallas as pl
from jax.experimental.pallas import tpu as pltpu
from jax.sharding import PartitionSpec as P

EPS = 1e-06
LIMITS = (12, 16, 23, 32, 46, 64, 91)
TOP_PRECISION = lax.Precision.HIGHEST
F32 = jnp.float32
BF16 = jnp.bfloat16
MASK_STEP = 2.0**30
LOG2E = 1.4426950408889634
VMEM = pl.BlockSpec(memory_space=pltpu.VMEM)
ANY = pl.BlockSpec(memory_space=pl.ANY)
LANES = 128
EXT = 16


def mm(a, b):
    return lax.dot_general(a, b, (((1,), (0,)), ((), ())), preferred_element_type=F32)


def mm_nt(a, b):
    return lax.dot_general(a, b, (((1,), (1,)), ((), ())), preferred_element_type=F32)


def bucket_index(offset):
    distance = jnp.abs(offset)
    far_bucket = 8 + sum(((distance >= threshold).astype(jnp.int32) for threshold in LIMITS))
    near_bucket = jnp.where(distance < 8, distance, far_bucket)
    return near_bucket + 16 * (offset > 0).astype(jnp.int32)


def wide_dots(rows, mat, dot):
    at = lax.broadcasted_iota(jnp.int32, (16, rows[0].shape[1]), 0)
    lhs = jnp.zeros(at.shape, F32)
    for i, v in enumerate(rows):
        for j in range(3):
            part = v.astype(BF16).astype(F32)
            lhs = jnp.where(at == 3 * i + j, part, lhs)
            v = v - part
    out = dot(lhs.astype(BF16), mat)
    return [jnp.sum(out[3 * i : 3 * i + 3], axis=0, keepdims=True) for i in range(len(rows))]


def fold(x, op):
    while x.shape[0] > 8:
        half = x.shape[0] // 2
        x = op(x[:half], x[half:])
    return x


def col_sum(x):
    return jnp.sum(fold(x, jnp.add), axis=0, keepdims=True)


def diagonal_sums(table):
    height, width = table.shape
    acc = table[0:8, :]
    for u in range(8, height, 8):
        acc += pltpu.roll(table[u : u + 8, :], width - u, 1)
    row = lax.broadcasted_iota(jnp.int32, acc.shape, 0)
    for bit in (1, 2, 4):
        acc = jnp.where((row & bit) != 0, pltpu.roll(acc, width - bit, 1), acc)
    return jnp.sum(acc, axis=0, keepdims=True)


def position():
    me = lax.axis_index("seq")
    return me, me // 2, me % 2


class Copies:
    def __init__(self, sems):
        self.sems = sems
        self.used = 0

    def start(self, src, dst):
        copy = pltpu.make_async_copy(src, dst, self.sems.at[self.used])
        self.used += 1
        copy.start()
        return copy


def pack_kernel(per, slots, ext, *refs):
    if ext:
        tok, seg, y, cc, ids, sems, id_sems = refs
    else:
        tok, y, cc, sems = refs
    span = tok.shape[1]
    _, p, c = position()
    copies, id_copies = Copies(sems), Copies(id_sems) if ext else None
    todo, pending = [], []
    for i, j in enumerate(slots):
        if j == 2:
            todo += [(y.at[2 * i], per * (1 - p) + per - 1), (cc.at[i], per * p + per - 1)]
        else:
            todo.append((y.at[2 * i], per * (1 - p) + 2 * c + j))
            todo.append((y.at[2 * i + 1], per * (1 - p) + 2 * (1 - c) + j))
            todo.append((cc.at[i], per * p + 2 * (1 - c) + j))
    for out, row in todo:
        pending.append(copies.start(tok.at[row], out.at[pl.ds(0, span)]))
    if ext:
        for k, (out, row) in enumerate(todo):
            value = jnp.broadcast_to(seg[pl.ds(row, 1), :].astype(F32), (ext, span)).astype(BF16)
            ids[k] = jnp.concatenate([value] * (tok.shape[2] // span), axis=1)
        for k, (out, row) in enumerate(todo):
            pending.append(id_copies.start(ids.at[k], out.at[pl.ds(span, ext)]))
    for copy in pending:
        copy.wait()


def prepare_kernel(
    n, table, norm_a, norm_f, wq, wk, wv, wo, wg, wu, wd,
    bias_o, ind_o, na_o, nf_o, wqkv_o, wqkv_t, wo_t, wg_t, wu_t, wd_t,
    square,
):
    heads, _, line = bias_o.shape
    inner = wq.shape[1]
    length = line // 2
    col = lax.broadcasted_iota(jnp.int32, (LANES, line), 1)
    offset = length - LANES - jnp.where(col < line - LANES, col, col - line)
    ind = (bucket_index(offset) == lax.broadcasted_iota(jnp.int32, (LANES, line), 0)).astype(F32).astype(BF16)
    ind_o[...] = ind
    square[...] = jnp.zeros_like(square)
    square[: table.shape[0], : table.shape[1]] = table[...]
    rest = square[:8, :]
    lines = None
    for _ in range(3):
        part = rest.astype(BF16)
        rest = rest - part.astype(F32)
        term = mm(part, ind)
        lines = term if lines is None else lines + term
    lines = lines * LOG2E
    for h in range(heads):
        bias_o[h] = pltpu.roll(jnp.broadcast_to(lines[h : h + 1, :], (LANES, line)), 0, 1, stride=1, stride_axis=0)
    for src, dst in ((norm_a, na_o), (norm_f, nf_o)):
        dst[...] = jnp.broadcast_to(src[...], (LANES, src.shape[1])).T
    for i, w in enumerate((wq, wk, wv)):
        wqkv_o[:, i * inner : (i + 1) * inner] = w[...]
        wqkv_t[i * inner : (i + 1) * inner, :] = w[...].T
    wo_t[...] = wo[...].T
    size = 256
    one = lax.broadcasted_iota(jnp.int32, (size, size), 0) == lax.broadcasted_iota(jnp.int32, (size, size), 1)
    one = one.astype(F32).astype(BF16)
    for src, dst in ((wg, wg_t), (wu, wu_t), (wd, wd_t)):
        for at in range(0, dst.shape[0], size):
            dst[at : at + size, :] = mm_nt(one, src[:, at : at + size]).astype(BF16)


STEP = 64


def chunks(height):
    return [slice(r, r + STEP) for r in range(0, height, STEP)]


def norm_into(out, src, cols, gain):
    total = None
    for r in chunks(src.shape[0]):
        x = src[r, cols].astype(F32)
        x = fold(x * x, jnp.add)
        total = x if total is None else total + x
    inv = lax.rsqrt(jnp.sum(total, axis=0, keepdims=True) / src.shape[0] + EPS)
    for r in chunks(src.shape[0]):
        out[r, cols] = (src[r, cols].astype(F32) * inv * gain[r, :]).astype(BF16)


def forward_slot(half, n, rows, bufs, w, wait, outs, copies):
    own, c1, y, c2, own_seg = rows
    tok, seg, n1, kk, va, x_b, s_buf = bufs
    bias, wqkv_t, wout_t, wg_t, wu_t, wd_t, nattn, nffn = w
    o = outs
    width = wqkv_t.shape[1]
    inner = wout_t.shape[1]
    heads = bias.shape[0]
    head = inner // heads
    span = own.shape[0]
    length = n * span
    me, p, c = position()
    for k, (piece, ids) in enumerate(((own, own_seg), (c1, None), (y, None), (c2, None))):
        at = pl.multiple_of((me ^ k) * span, span)
        x_b[:, pl.ds(at, span)] = piece[:span, :].T
        ids = piece[span : span + 1, :span].astype(F32) if ids is None else ids
        seg[:, pl.ds(at, span)] = jnp.broadcast_to(ids, (LANES, span))
    for b in range(n):
        norm_into(n1, x_b, slice(b * span, (b + 1) * span), nattn)
    nq = length // 2 if half else length
    if half:
        mine = pl.ds(pl.multiple_of(c * nq, nq), nq)
        o["x"][...] = x_b[:, mine]
        o["n1"][...] = n1[:, mine]
    else:
        mine = slice(0, nq)
        o["x"][...] = x_b[...]
        o["n1"][...] = n1[...]
    o["seg"][...] = seg[0:8, :]
    ids = lax.broadcasted_iota(jnp.int32, (LANES, length), 0).astype(F32)
    one = (seg[...] == ids).astype(F32)
    k_aug = ((one - 1.0) * MASK_STEP).T.astype(BF16)
    ids = lax.broadcasted_iota(jnp.int32, (LANES, nq), 0).astype(F32)
    q_aug = (seg[:, mine] == ids).astype(BF16)
    wait("qkv")
    if half:
        qt = mm(wqkv_t[:inner, :], n1[:, mine]).astype(BF16)
        kvt = mm(wqkv_t[inner:, :], n1[...]).astype(BF16)
        kt, vt = kvt[:inner], kvt[inner:]
    else:
        qkvt = mm(wqkv_t[...], n1[...]).astype(BF16)
        qt, kt, vt = qkvt[:inner], qkvt[inner : 2 * inner], qkvt[2 * inner :]
    o["kt"][...] = kt
    q2 = qt.astype(F32) * LOG2E
    q_hi = q2.astype(BF16)
    q_lo = (q2 - q_hi.astype(F32)).astype(BF16)
    lane = lax.broadcasted_iota(jnp.int32, (length, LANES), 1)

    def pair_ready(pair):
        ps = slice(pair * LANES, (pair + 1) * LANES)
        both = kt[ps].T.astype(F32)
        turned = pltpu.roll(both, head, 1)
        kk[2 * pair, :, :LANES] = jnp.where(lane < head, both, turned).astype(BF16)
        kk[2 * pair + 1, :, :LANES] = jnp.where(lane < head, turned, both).astype(BF16)
        for h in (2 * pair, 2 * pair + 1):
            kk[h, :, LANES:] = k_aug
            va[h, :head, :] = vt[h * head : (h + 1) * head]
            va[h, head:, :] = jnp.ones((EXT, length), BF16)

    def naturals(pair):
        ps = slice(pair * LANES, (pair + 1) * LANES)
        o["q"][:, ps] = qt[ps].T
        o["v"][:, ps] = vt[ps].T

    chunk = length // 2
    work = [(h, qc) for h in range(heads) for qc in range(nq // chunk)]
    per_pair = 2 * (nq // chunk)

    def lanes_of(qc):
        return slice(qc * chunk, (qc + 1) * chunk)

    def score(i, a, rhs):
        h, qc = work[i]
        if half:
            at = pl.ds(pl.multiple_of((n - 1 - a) * LANES + c * nq, LANES), chunk)
        else:
            at = pl.ds((n - 1 - a) * LANES + qc * chunk, chunk)
        s_a = mm(kk[h, a * LANES : (a + 1) * LANES, :], rhs) + bias[h, :, at]
        s_buf[i % 2, a * LANES : (a + 1) * LANES, :] = s_a
        return fold(s_a, jnp.maximum)

    def power(i, a, top):
        h, qc = work[i]
        e = jnp.exp2(s_buf[i % 2, a * LANES : (a + 1) * LANES, :] - top)
        o["e"][h, a * LANES : (a + 1) * LANES, lanes_of(qc)] = e.astype(BF16)

    def attend(i):
        h, qc = work[i]
        hs, qs = slice(h * head, (h + 1) * head), lanes_of(qc)
        raw = mm(va[h], o["e"][h, :, qs])
        inv = 1.0 / raw[head : head + 1, :]
        o["r"][h : h + 1, qs] = inv
        o["att"][hs, qs] = (raw[:head, :] * inv).astype(BF16)

    pair_ready(0)
    wait("bias")
    copies(o["x"], o["seg"], o["n1"], o["kt"])
    top = None
    for i in range(len(work) + 1):
        if i == len(work) // 2:
            wait("rest")
            copies(*[(o["e"], h) for h in range(heads // 2 - 1)])
        tops = []
        if i < len(work):
            h, qc = work[i]
            hs, qs = slice(h * head, (h + 1) * head), lanes_of(qc)
            rhs = jnp.concatenate([q_hi[hs, qs], q_lo[hs, qs], q_aug[:, qs]], axis=0)
        for a in range(n):
            if i < len(work):
                tops.append(score(i, a, rhs))
            if i > 0:
                power(i - 1, a, top)
        if i < len(work):
            top = jnp.max(functools.reduce(jnp.maximum, tops), axis=0, keepdims=True)
            if i % per_pair == 0 and i // per_pair < heads // 2 - 1:
                pair_ready(i // per_pair + 1)
            if i % per_pair == 1:
                naturals(i // per_pair)
        if i > 0:
            attend(i - 1)
    if half:
        x_q = x_b[:, mine].astype(F32)
    else:
        x_q = x_b[...].astype(F32)
    o["mid"][...] = x_q + mm(wout_t[...], o["att"][...])
    for b in range(nq // span):
        norm_into(n1, o["mid"], slice(b * span, (b + 1) * span), nffn)
    ff = wg_t.shape[0]
    step = 256
    for b in range(ff // step):
        cs = slice(b * step, (b + 1) * step)
        gate = mm(wg_t[cs, :], n1[:, :nq])
        up = mm(wu_t[cs, :], n1[:, :nq])
        sq = gate * gate
        th = jnp.tanh(gate * (0.7978845608028654 + (0.7978845608028654 * 0.044715) * sq))
        half_th = 0.5 + 0.5 * th
        gelu = gate * half_th
        slope = half_th + (gelu - gelu * th) * (0.7978845608028654 + (3 * 0.7978845608028654 * 0.044715) * sq)
        o["hid"][cs, :] = (gelu * up).astype(BF16)
        o["a"][cs, :] = (up * slope).astype(BF16)
        o["ge"][cs, :] = gelu.astype(BF16)
    copies(*[(o["e"], h) for h in range(heads // 2 - 1, heads)])
    copies(*[o[k] for k in ("r", "att", "q", "v", "mid", "hid", "a", "ge")])
    res = tok.at[:, :nq]
    res[...] = o["mid"][...] + mm(wd_t[...], o["hid"][...])
    valid = (seg[0:1, mine] != 0.0).astype(F32)
    parts = []
    for r in chunks(width):
        part = None
        for b in range(nq // span):
            blk = res[r, b * span : (b + 1) * span] * valid[:, b * span : (b + 1) * span]
            part = blk if part is None else part + blk
        parts.append(part)
    o["pool"][...] = jnp.broadcast_to(col_sum(jnp.concatenate(parts, axis=0).T), o["pool"].shape)
    copies(o["pool"])
    send_blocks(half, res, o["blocks"], span)


def send_blocks(half, res, outs, span):
    me, _, c = position()
    for k, out in enumerate(outs):
        block = (c + k) % 2 if half else me ^ k
        at = pl.multiple_of(block * span, span)
        out[:span, :] = res[:, pl.ds(at, span)].astype(BF16).T


FORWARD_OUTS = ("kt", "q", "v", "x", "seg", "e", "r", "att", "mid", "hid", "a", "ge", "pool", "n1")


def forward_outs(half, n, span, width, inner, heads, ff):
    length = n * span
    nq = length // 2 if half else length
    shapes = (
        ((inner, length), BF16), ((nq, inner), BF16), ((length, inner), BF16), ((width, nq), BF16), ((8, length), F32),
        ((heads, length, nq), BF16), ((8, nq), F32), ((inner, nq), BF16), ((width, nq), F32), ((ff, nq), BF16),
        ((ff, nq), BF16), ((ff, nq), BF16), ((8, width), F32), ((width, nq), BF16),
    )
    return shapes


def forward_kernel(kinds, n, per, heads, *refs):
    count = len(FORWARD_OUTS)
    tokens, seg_ids, bias, wqkv_t, wout_t, wg_t, wu_t, wd_t, nattn, nffn = refs[:10]
    near, far, again = refs[10:13]
    at = 13
    outs = [refs[at + i * count : at + (i + 1) * count] for i in range(len(kinds))]
    at += count * len(kinds)
    block_outs = refs[at : at + 3]
    at += 3
    bufs = [refs[at + i * count : at + (i + 1) * count] for i in range(len(kinds))]
    at += count * len(kinds)
    blocks = refs[at : at + 3]
    at += 3
    own, tok, seg, n1, kk, va, x_b, s_buf, bias_b, wqkv_b, wout_b, wg_b, wu_b, wd_b, in_sems, out_sems = refs[at:]
    me, p, c = position()
    ins = Copies(in_sems)
    owns = []
    for i, (slot, half) in enumerate(kinds):
        row = per * p + (per - 1 if half else 2 * c + slot)
        owns.append((ins.start(tokens.at[row], own.at[i]), row))
    waits = {
        "qkv": [ins.start(wqkv_t, wqkv_b)],
        "bias": [ins.start(bias, bias_b)],
        "rest": [ins.start(a, b) for a, b in ((wout_t, wout_b), (wg_t, wg_b), (wu_t, wu_b), (wd_t, wd_b))],
    }

    def wait(what):
        for copy in waits.pop(what, ()):
            copy.wait()

    writes = Copies(out_sems)
    pending = []
    for i, (slot, half) in enumerate(kinds):
        copy, row = owns[i]
        copy.wait()
        o = dict(zip(FORWARD_OUTS, bufs[i]))
        dst = dict(zip(FORWARD_OUTS, outs[i]))
        o["blocks"] = (blocks[0].at[i], blocks[1].at[i], blocks[2].at[2 * i], blocks[2].at[2 * i + 1])
        names = {id(v): k for k, v in o.items()}

        def copies(*what, o=o, dst=dst, names=names):
            for item in what:
                if isinstance(item, tuple):
                    ref, h = item
                    pending.append(writes.start(ref.at[h], dst[names[id(ref)]].at[h]))
                else:
                    pending.append(writes.start(item, dst[names[id(item)]]))

        c1, y_mine, c2_mine = near.at[i], far.at[2 * i], again.at[2 * i + (not half)]
        own_seg = seg_ids[pl.ds(row, 1), :].astype(F32)
        forward_slot(
            half, n, (own.at[i], c1, y_mine, c2_mine, own_seg), (tok, seg, n1, kk, va, x_b, s_buf),
            (bias_b, wqkv_b, wout_b, wg_b, wu_b, wd_b, nattn, nffn), wait, o, copies,
        )
        pending.append(writes.start(blocks[0].at[i], block_outs[0].at[i]))
        pending.append(writes.start(blocks[1].at[i], block_outs[1].at[i]))
        pending.append(writes.start(blocks[2].at[pl.ds(2 * i, 2)], block_outs[2].at[pl.ds(2 * i, 2)]))
    for copy in pending:
        copy.wait()


def middle_kernel(n, per, *refs):
    grad_y, eg, w_head, w_down, w_gate, w_up, w_out, nffn, pool_other = refs[:9]
    at = 9
    near, far, again = refs[at : at + 3]
    at += 3
    names = ("mid", "a", "ge", "hid", "att", "seg", "r", "pool")
    srcs = [dict(zip(names, refs[at + 8 * i : at + 8 * i + 8])) for i in range(3)]
    at += 24
    ga_o, gt_o = refs[at : at + 3], refs[at + 3 : at + 6]
    own_o, send_o, gnf_o, emb_o, pg_o = refs[at + 6 : at + 11]
    at += 11
    big = ("mid", "a", "ge")
    bufs = [dict(zip(big, refs[at + 3 * i : at + 3 * i + 3])) for i in range(3)]
    at += 9
    own, res, gyt, part, gb, n2, gg, gu, ga, att, hid, packed, wh, wd, wg, wu, wo, sems, out_sems = refs[at:]
    span, width = own.shape[1:]
    length = n * span
    ff = w_gate.shape[1]
    inner = w_out.shape[0]
    head = inner // 6
    wide = w_head.shape[1]
    me, p, c = position()
    ins = Copies(sems)
    owns = []
    for i in range(3):
        row = per * p + (per - 1 if i == 2 else 2 * c + i)
        owns.append(ins.start(grad_y.at[row], own.at[i]))
    weights = {k: ins.start(a, b) for k, a, b in (("h", w_head, wh), ("d", w_down, wd))}
    for k, a, b in (("g", w_gate, wg), ("u", w_up, wu), ("o", w_out, wo)):
        weights[k] = ins.start(a, b)
    lanes = [pl.ds(i * length, length // 2 if i == 2 else length) for i in range(3)]
    loads = []
    for i in range(3):
        loads.append([ins.start(srcs[i][k], bufs[i][k]) for k in big])
    late_loads = []
    for i in range(3):
        late_loads.append(ins.start(srcs[i]["hid"], hid.at[:, lanes[i]]))
        late_loads.append(ins.start(srcs[i]["att"], att.at[:, lanes[i]]))

    def need(*names):
        for k in names:
            if k in weights:
                weights.pop(k).wait()

    for i in range(3):
        owns[i].wait()
    need("h")
    pools, cots, counts = [], [], []
    for i in range(3):
        half = i == 2
        for k, piece in enumerate((own.at[i], near.at[i], far.at[2 * i], again.at[2 * i + (not half)])):
            place = pl.multiple_of((me ^ k) * span, span)
            gyt[i, :, pl.ds(place, span)] = piece[...].T
        count = jnp.sum((srcs[i]["seg"][0:1, :] != 0.0).astype(F32), axis=1, keepdims=True)
        pool = srcs[i]["pool"][0:1, :]
        if half:
            pool = pool + pool_other[0:1, :]
        pools.append(pool / count)
        counts.append(count)
        row = per * p + (per - 1 if half else 2 * c + i)
        cots.append(eg[pl.ds(row, 1), :])
    proj = wide_dots(pools, wh[...], mm)
    g_projs = []
    for i in range(3):
        inv = lax.rsqrt(jnp.sum(proj[i] * proj[i], axis=1, keepdims=True) + EPS)
        emb = proj[i] * inv
        g_proj = inv * (cots[i] - emb * jnp.sum(emb * cots[i], axis=1, keepdims=True))
        emb_o[i] = jnp.broadcast_to(emb, emb_o.shape[1:])
        once = jnp.where(c == 0, 1.0, 0.0) if i == 2 else 1.0
        for q in range((width + wide) // 256):
            piece = pools[i][:, q * 256 : (q + 1) * 256] if q < width // 256 else g_proj[:, q * 256 - width : (q + 1) * 256 - width]
            pg_o[5 * i + q : 5 * i + q + 1, :] = piece * once
        g_projs.append(g_proj)
    g_pools = wide_dots(g_projs, wh[...], mm_nt)
    g_cols = [jnp.broadcast_to(g / k, (span, width)).T for g, k in zip(g_pools, counts)]
    need("d", "g", "u", "o")
    for copy in loads[0]:
        copy.wait()
    sizes = [length, length, length // 2]
    starts = [0, length, 2 * length]

    def outer(i, b, r):
        if i == 2:
            place = pl.ds(pl.multiple_of((c * (sizes[2] // span) + b) * span, span), span)
        else:
            place = pl.ds(b * span, span)
        valid = (srcs[i]["seg"][0:1, place] != 0.0).astype(F32)
        return gyt[i, r, place].astype(F32) + valid * g_cols[i][r, :]

    def branch(i, b):
        for r in chunks(width):
            gb[r, starts[i] + b * span : starts[i] + (b + 1) * span] = outer(i, b, r).astype(BF16)

    step = 256

    def gates(i, b):
        cs, ls = slice(b * step, (b + 1) * step), slice(starts[i], starts[i] + sizes[i])
        g_hid = mm(wd[cs, :], gb[:, ls])
        gg[cs, ls] = (g_hid * bufs[i]["a"][cs, :].astype(F32)).astype(BF16)
        gu[cs, ls] = (g_hid * bufs[i]["ge"][cs, :].astype(F32)).astype(BF16)

    def normed(i):
        ls = slice(starts[i], starts[i] + sizes[i])
        res[i % 2, :, : sizes[i]] = mm(wg[...], gg[:, ls]) + mm(wu[...], gu[:, ls])

    def norm(i, b):
        mid, ds = bufs[i]["mid"], res.at[i % 2]
        bs = slice(b * span, (b + 1) * span)
        ls = slice(starts[i] + b * span, starts[i] + (b + 1) * span)
        sq = cross = None
        for r in chunks(width):
            m = mid[r, bs]
            t = fold(m * m, jnp.add)
            u = fold(ds[r, bs] * nffn[r, :] * m, jnp.add)
            sq, cross = (t, u) if sq is None else (sq + t, cross + u)
        inv2 = lax.rsqrt(jnp.sum(sq, axis=0, keepdims=True) / width + EPS)
        mean = inv2 * jnp.sum(cross, axis=0, keepdims=True) / width
        for r in chunks(width):
            hat = mid[r, bs] * inv2
            n2[r, ls] = (hat * nffn[r, :]).astype(BF16)
            gn = ds[r, bs]
            if i == 0 and b == 0:
                part[r, :] = gn * hat
            else:
                part[r, :] += gn * hat
            ga[r, ls] = (outer(i, b, r) + inv2 * (gn * nffn[r, :] - hat * mean)).astype(BF16)

    def attended(i):
        ls = slice(starts[i], starts[i] + sizes[i])
        ga_o[i][...] = ga[:, ls]
        gatt = mm(wo[...], ga[:, ls]).astype(BF16).astype(F32)
        for h in range(6):
            hs = slice(h * head, (h + 1) * head)
            gt_o[i][hs, :] = (gatt[hs, :] * srcs[i]["r"][h : h + 1, :]).astype(BF16)

    def store(at, value):
        rows = value.shape[0] // 2
        for side in range(2):
            packed[side, :, at : at + value.shape[1]] = value[side * rows : (side + 1) * rows].astype(BF16)

    outs = Copies(out_sems)
    pending = []

    def send(lo, hi):
        pending.append(outs.start(packed.at[c, :, pl.ds(lo, hi - lo)], own_o.at[:, pl.ds(lo, hi - lo)]))
        pending.append(outs.start(packed.at[1 - c, :, pl.ds(lo, hi - lo)], send_o.at[:, pl.ds(lo, hi - lo)]))

    blocks = [k // span for k in sizes]
    for b in range(blocks[0]):
        branch(0, b)
    for b in range(ff // step):
        gates(0, b)
    for i in (1, 2):
        for copy in loads[i]:
            copy.wait()
    normed(0)
    for b in range(blocks[1]):
        branch(1, b)
    for b in range(ff // step):
        gates(1, b)
        norm(0, b)
    normed(1)
    attended(0)
    for b in range(blocks[2]):
        branch(2, b)
    for b in range(ff // step):
        gates(2, b)
        norm(1, b)
    normed(2)
    attended(1)
    for copy in late_loads:
        copy.wait()
    top = 2 * ff
    for b in range(2):
        store(top + b * width, mm_nt(hid[b * width : (b + 1) * width, :], gb[...]))
        norm(2, b)
    attended(2)
    send(top, top + 2 * width)
    for b in range(2):
        cs = slice(b * 512, (b + 1) * 512)
        store(b * 512, mm_nt(n2[...], gg[cs, :]))
    send(0, ff)
    for b in range(2):
        cs = slice(b * 512, (b + 1) * 512)
        store(ff + b * 512, mm_nt(n2[...], gu[cs, :]))
    store(top + 2 * width, mm_nt(ga[...], att[...]))
    gnf_o[...] = jnp.broadcast_to(col_sum(part[...].T), gnf_o.shape)
    pg_o[15:16, :] = jnp.zeros((1, 256), F32)
    send(ff, 2 * ff)
    send(top + 2 * width, top + 2 * width + inner)
    for copy in pending:
        copy.wait()


def attention_back(core, n, q_nat, v_nat, kt, e_wait, e_b, att, gt, gs, table, kv_side, line, gq_o, put_kv):
    heads = e_b.shape[0]
    inner = kt.shape[0]
    head = inner // heads
    length = kt.shape[1]
    half = core is not None
    nq = length // 2 if half else length
    lane = lax.broadcasted_iota(jnp.int32, (length, LANES), 1)
    gt_nat = gt[...].T
    zeros = jnp.zeros((head, nq), BF16)
    width = 4 * LANES
    table[:, :, :LANES] = jnp.zeros((2, LANES, LANES), F32)

    def scores(h, a, rhs, delta, far, seen):
        ps = slice(h // 2 * LANES, (h // 2 + 1) * LANES)
        ks = slice(a * LANES, (a + 1) * LANES)
        g_s = e_b[h, ks, :].astype(F32) * (mm(v_nat[ks, ps], rhs) - delta)
        gs[h % 2, ks, :nq] = g_s.astype(BF16)
        t = table.at[h % 2]
        for b in range(nq // LANES):
            blk = g_s[:, b * LANES : (b + 1) * LANES]
            d = (2 * core if half else 0) + b - a
            if abs(d) <= 1:
                at = (d + 2) * LANES
                if d in seen:
                    t[:, at : at + LANES] += blk
                else:
                    t[:, at : at + LANES] = blk
                    seen.add(d)
            else:
                far[d < 0].append(fold(blk, jnp.add))

    def lines(h, far):
        t = table.at[h % 2]
        line(h, slice(LANES, LANES + width), diagonal_sums(t))
        if far[0]:
            line(h, slice(6 * LANES, 7 * LANES), jnp.sum(sum(far[0]), axis=0, keepdims=True))
        if far[1]:
            line(h, slice(0, LANES), jnp.sum(sum(far[1]), axis=0, keepdims=True))

    def weigh(h, which):
        hs, ps = slice(h * head, (h + 1) * head), slice(h // 2 * LANES, (h // 2 + 1) * LANES)
        g = gs.at[h % 2]
        if which == 0:
            gq_o[hs, :] = mm(kt[hs, :], g[:, :nq]).astype(BF16)
            return
        value = mm(g[:, :nq], q_nat[:, ps]) if which == 1 else mm(e_b[h], gt_nat[:, ps])
        if h % 2 == 0:
            kv_side[which - 1] = value
        else:
            put_kv(h // 2, which - 1, jnp.where(lane < head, kv_side[which - 1], value).astype(BF16).T)

    old = None
    for h in range(heads + 1):
        far = [[], []]
        if h < heads:
            if h % 2 == 0:
                e_wait(h // 2)
            hs = slice(h * head, (h + 1) * head)
            g_h = gt[hs, :]
            delta = col_sum(g_h.astype(F32) * att[hs, :].astype(F32))
            rhs = jnp.concatenate([g_h, zeros] if h % 2 == 0 else [zeros, g_h], axis=0)
            seen = set()
        for a in range(n):
            if h < heads:
                scores(h, a, rhs, delta, far, seen)
            if h > 0:
                if a < 3:
                    weigh(h - 1, a)
                else:
                    lines(h - 1, old)
        old = far


def half_back_kernel(n, q_nat, v_nat, kt, e_in, att, gt, gq_o, keep_o, send_o, line_o, e_b, gs, table, kv_side, kv, sems):
    ins = Copies(sems)
    loads = [ins.start(e_in.at[pl.ds(h, 2)], e_b.at[pl.ds(h, 2)]) for h in range(0, e_in.shape[0], 2)]
    inner = kt.shape[0]

    def put(pair, which, value):
        kv[which * inner + pair * LANES : which * inner + (pair + 1) * LANES, :] = value.astype(BF16)

    def line(h, lanes, value):
        line_o[h : h + 1, lanes] = value

    line_o[...] = jnp.zeros_like(line_o)
    _, _, c = position()
    for core in range(2):

        @pl.when(c == core)
        def _(core=core):
            attention_back(
                core, n, q_nat, v_nat, kt, lambda p: loads[p].wait(), e_b, att, gt, gs, table, kv_side, line, gq_o, put
            )

    nq = kt.shape[1] // 2
    keep_o[...] = kv[:, pl.ds(pl.multiple_of(c * nq, nq), nq)]
    send_o[...] = kv[:, pl.ds(pl.multiple_of((1 - c) * nq, nq), nq)]


def backward_kernel(
    slot, n,
    q_nat, v_nat, kt, e_in, att, gt, line_in, xt, ga, w_qkv, nattn, emb, part_in, *refs,
):
    if slot:
        gq0, gq_half, keep, got, n1_0, n1_1, n1_2, own_o, send_o, gq2, *refs = refs
        *refs, m0, m1, m2, g0, packed = refs
    line_o, gq, b_own, b_c, b_y, part_o, e_b, gs, table, kv_side, res, xb, gb, wb, part, sems = refs
    ins = Copies(sems)
    loads = [ins.start(e_in.at[pl.ds(h, 2)], e_b.at[pl.ds(h, 2)]) for h in range(0, e_in.shape[0], 2)]
    inner = kt.shape[0]

    def put(pair, which, value):
        at = (1 + which) * inner + pair * LANES
        gq[at : at + LANES, :] = value.astype(BF16)

    def line(h, lanes, value):
        line_o[h : h + 1, lanes] = line_in[h : h + 1, lanes] + value

    line_o[...] = line_in[...]
    more = [ins.start(a, b) for a, b in ((w_qkv, wb), (xt, xb), (ga, gb))]
    if slot:
        more += [ins.start(a, b) for a, b in ((gq0, g0), (n1_0, m0), (n1_1, m1), (n1_2, m2))]
        gq2[:inner, :] = gq_half[...]
        gq2[inner:, :] = (keep[...].astype(F32) + got[...].astype(F32)).astype(BF16)
    attention_back(
        None, n, q_nat, v_nat, kt, lambda p: loads[p].wait(), e_b, att, gt, gs, table, kv_side, line, gq.at[:inner, :], put
    )
    for copy in more:
        copy.wait()
    if slot:
        part[...] = part_in[...]
        rows = own_o.shape[0]
        for at in range(0, 3 * inner, inner):
            cs = slice(at, at + inner)
            value = mm_nt(m0[...], g0[cs, :]) + mm_nt(m1[...], gq[cs, :]) + mm_nt(m2[...], gq2[cs, :])
            for side in range(2):
                packed[side, :, cs] = value[side * rows : (side + 1) * rows].astype(BF16)
    span = b_own.shape[1] - EXT
    input_rows(slot, False, gq, xb, gb, wb, nattn, emb, res, part, (b_own.at[0], b_c.at[0], b_y.at[0], b_y.at[1]), span)
    part_o[...] = part[...]
    if slot:
        _, _, c = position()
        own_o[...] = packed[c]
        send_o[...] = packed[1 - c]


def input_rows(slot, half, gq, xt, ga, w_qkv, nattn, emb, res, part, outs, span):
    width, nq = res.shape[0], gq.shape[1]
    res[:, :nq] = mm(w_qkv[...], gq[...])
    for b in range(nq // span):
        bs = slice(b * span, (b + 1) * span)
        sq = cross = None
        for r in chunks(width):
            x = xt[r, bs].astype(F32)
            t = fold(x * x, jnp.add)
            u = fold(res[r, bs] * nattn[r, :] * x, jnp.add)
            sq, cross = (t, u) if sq is None else (sq + t, cross + u)
        inv = lax.rsqrt(jnp.sum(sq, axis=0, keepdims=True) / width + EPS)
        mean = inv * jnp.sum(cross, axis=0, keepdims=True) / width
        for r in chunks(width):
            hat = xt[r, bs].astype(F32) * inv
            gn = res[r, bs]
            if slot == 0 and b == 0:
                part[r, :] = gn * hat
            else:
                part[r, :] += gn * hat
            res[r, bs] = ga[r, bs].astype(F32) + inv * (gn * nattn[r, :] - hat * mean)
    send_blocks(half, res, outs, span)
    row = emb[slot, 0:1, :]
    high = row.astype(BF16)
    low = (row - high.astype(F32)).astype(BF16)
    rest = row.shape[1] - width
    for out in outs:
        for at, v in ((0, high), (2, low)):
            out[span + at : span + at + 1, :] = v[:, :width]
            out[span + at + 1 : span + at + 2, :rest] = v[:, width:]


def inputs_kernel(
    gq, xt, ga, w_qkv, nattn, emb, part_in, line_in, gnf, indicator,
    b_own, b_c, b_y, small,
    res, part,
):
    small[...] = jnp.zeros_like(small)
    part[...] = part_in[...]
    width = res.shape[0]
    span = b_own.shape[1] - EXT
    input_rows(2, True, gq, xt, ga, w_qkv, nattn, emb, res, part, (b_own.at[0], b_c.at[0], b_y.at[0], b_y.at[1]), span)
    gna = col_sum(part[...].T)
    for i in range(width // LANES):
        small[i : i + 1, :] = gnf[0:1, i * LANES : (i + 1) * LANES]
        small[4 + i : 5 + i, :] = gna[:, i * LANES : (i + 1) * LANES]
    lines = line_in[...]
    hi = lines.astype(BF16)
    lo = (lines - hi.astype(F32)).astype(BF16)
    small[8:16, :] = mm_nt(hi, indicator[...]) + mm_nt(lo, indicator[...])


def unpack_kernel(per, with_emb, *refs):
    groups = (len(refs) - 1 - (3 if with_emb else 1)) // 4
    out = refs[4 * groups]
    sems = refs[-1]
    ways = []
    for g in range(groups):
        own, c1, y, d = refs[4 * g : 4 * g + 4]
        ways += [(own.at[i], c1.at[i], y.at[2 * i], d.at[2 * i + 1]) for i in range(own.shape[0])]
    own0 = ways[0][0]
    me, p, _ = position()
    rows, span, width = out.shape
    for r in range(rows):
        pair, j = divmod(r, per)
        slot = 2 if j == per - 1 else j % 2
        core = p if slot == 2 else j // 2
        k = me ^ (pair * 2 + core)
        for which in range(4):
            ref = ways[slot][which]

            @pl.when(k == which)
            def _(ref=ref, r=r):
                pltpu.make_async_copy(ref.at[pl.ds(0, span)], out.at[r], sems.at[r]).start()
                if with_emb:
                    pltpu.make_async_copy(ref.at[pl.ds(span, EXT)], refs[4 * groups + 2].at[r], sems.at[rows + r]).start()

    if with_emb:
        emb, got = refs[4 * groups + 1 : 4 * groups + 3]
        for r in range(rows):
            pltpu.make_async_copy(own0.at[pl.ds(span, EXT)], got.at[r], sems.at[rows + r]).wait()
            value = got[r].astype(F32)
            emb[r : r + 1, :width] = value[0:1, :] + value[2:3, :]
            emb[r : r + 1, width:] = (value[1:2, :] + value[3:4, :])[:, : emb.shape[1] - width]
    for r in range(rows):
        pltpu.make_async_copy(own0.at[pl.ds(0, span)], out.at[r], sems.at[r]).wait()


def place(step):
    if step is None:
        return 0, 1
    axis, stride, radix = step
    return (lax.axis_index(axis) // stride) % radix, radix


def combine_kernel(plan, *refs):
    at = sum(len(arrays) for pieces, _ in plan for arrays, _, _ in pieces)
    outs = at + sum(place(step)[1] for _, step in plan)
    ins, at, scratch = 0, at, outs
    for pieces, step in plan:
        off = 0
        total = refs[scratch] if step else refs[at]
        for arrays, lo, hi in pieces:
            value = sum(refs[ins + i][..., lo:hi].astype(F32) for i in range(len(arrays)))
            ins += len(arrays)
            total[..., off : off + hi - lo] = value.astype(BF16)
            off += hi - lo
        if step:
            d, radix = place(step)
            for k in range(radix):
                refs[at + k][...] = total[d ^ k]
            at += radix
            scratch += 1
        else:
            at += 1


def join_kernel(plan, *refs):
    ins, at = 0, sum(place(step)[1] for step, _ in plan)
    for step, cuts in plan:
        d, radix = place(step)
        for lo, hi in cuts:
            for k in range(radix):
                refs[at][d ^ k] = refs[ins + k][:, lo:hi]
            at += 1
        ins += radix


def merge_kernel(step, cut, late_cut, own, got, late, late_got, a_o, b_o):
    d, _ = place(step)
    total = (late[...].astype(F32) + late_got[...].astype(F32)).astype(BF16)
    rows, wide = own.shape
    for src, at in ((own, d), (got, d ^ 1)):
        a_o[at, :, :cut] = src[:, :cut]
        b_o[at, :, : wide - cut] = src[:, cut:]
    for side in range(2):
        part = total[side * rows : (side + 1) * rows]
        a_o[side, :, cut:] = part[:, :late_cut]
        b_o[side, :, wide - cut :] = part[:, late_cut:]


FINISH_OUTS = 7


def finish_kernel(second, cut, block, *refs):
    if second:
        b_own, a, b, *rest = refs
        outs, rest = rest[FINISH_OUTS : 2 * FINISH_OUTS], rest[2 * FINISH_OUTS :]
        head_o, nf_o, na_o, table_o, gate, up, down, out, qkv, head, sems = rest
    else:
        a, b, *rest = refs
        outs, (gate, up, down, out, qkv, sems) = rest[:FINISH_OUTS], rest[FINISH_OUTS:]
    gate_o, up_o, down_o, out_o, *qkv_o = outs
    _, _, c = position()
    rows = a.shape[0]
    ff = gate.shape[1]
    width = gate_o.shape[0]
    inner = out.shape[0]
    rest = ff - (cut - ff)
    start = pl.multiple_of(((1 - c) if second else c) * rows, rows)
    at = pl.ds(start, rows)
    copies = Copies(sems)
    gate[...] = a[:, :ff].astype(F32)
    pending = [copies.start(gate, gate_o.at[at])]
    down[0] = b[:, rest : rest + width].astype(F32)
    pending.append(copies.start(down.at[0], down_o.at[at]))
    down[1] = b[:, rest + width : rest + 2 * width].astype(F32)
    pending.append(copies.start(down.at[1], down_o.at[pl.ds(pl.multiple_of(width + start, rows), rows)]))
    up[:, : cut - ff] = a[:, ff:cut].astype(F32)
    up[:, cut - ff :] = b[:, :rest].astype(F32)
    pending.append(copies.start(up, up_o.at[at]))
    late_a = a.shape[1] - cut
    late_b = b.shape[1] - LANES - (3 * inner - late_a)
    for i in range(3):
        lo, hi = i * inner, (i + 1) * inner
        mid = min(max(late_a, lo), hi)
        if mid > lo:
            qkv[i, :, : mid - lo] = a[:, cut + lo : cut + mid].astype(F32)
        if mid < hi:
            qkv[i, :, mid - lo :] = b[:, late_b + mid - late_a : late_b + hi - late_a].astype(F32)
        pending.append(copies.start(qkv.at[i], qkv_o[i].at[at]))
    out[...] = b[:, rest + 2 * width : rest + 2 * width + inner].astype(F32).T
    pending.append(copies.start(out, out_o.at[:, at]))
    if second:
        row = lax.broadcasted_iota(jnp.int32, (rows, 256), 0) % 16
        small = None
        for ref in (b_own, b):
            g = ref[:, late_b - 256 : late_b].astype(F32)
            turned = {t: pltpu.roll(g, rows - t, 0).astype(BF16) for t in range(1, 5)}
            for i in range(2):
                kept = jnp.where((row < 15) & (row % 5 == i), g, 0.0).T.astype(BF16)
                for j in range(3):
                    term = mm(kept, turned[2 + j - i])
                    place_ = (slice(i * 256, (i + 1) * 256), slice(j * 256, (j + 1) * 256))
                    if ref is b_own:
                        head[place_] = term
                    else:
                        head[place_] += term
            for r in range(0, rows, block):
                value = ref[r : r + 16, ref.shape[1] - LANES :].astype(F32)
                small = value if small is None else small + value
        pending.append(copies.start(head, head_o))
        for i in range(nf_o.shape[1] // LANES):
            nf_o[:, i * LANES : (i + 1) * LANES] = small[i : i + 1, :]
            na_o[:, i * LANES : (i + 1) * LANES] = small[4 + i : 5 + i, :]
        table_o[...] = small[8 : 8 + table_o.shape[0], : table_o.shape[1]]
    for copy in pending:
        copy.wait()


def sds(shape, dtype=BF16):
    return jax.ShapeDtypeStruct(shape, dtype)


def call(kernel, outs, args, scratch=(), specs=None, out_specs=None, flops=0, name=None, vmem=56, deps=(), aliases=None):
    count = len(args)

    def body(*refs):
        kernel(*refs[:count], *refs[count + len(deps) :])

    return pl.pallas_call(
        body,
        out_shape=outs,
        in_specs=list(specs or [VMEM] * count) + [ANY] * len(deps),
        out_specs=out_specs or jax.tree.map(lambda _: VMEM, outs),
        scratch_shapes=list(scratch),
        compiler_params=pltpu.CompilerParams(vmem_limit_bytes=vmem * 2**20),
        cost_estimate=pl.CostEstimate(flops=flops, bytes_accessed=10_000_000, transcendentals=0),
        input_output_aliases=aliases or {},
        name=name,
    )(*args, *deps)


def swap(x, axis, k):
    n = lax.axis_size(axis)
    return lax.ppermute(x, axis, [(i, i ^ k) for i in range(n)])


def after(x, *deps):
    return lax.optimization_barrier((x, *deps))[0]


def together(*trees):
    leaves, shape = jax.tree.flatten(trees)
    return jax.tree.unflatten(shape, lax.optimization_barrier(leaves))


def row_digits():
    return [("rows", 1 << i, 2) for i in range(lax.axis_size("rows").bit_length() - 1)]


def shards(
    tokens, seg_ids, w_query, w_key, w_value, w_out, w_gate, w_up, w_down, w_head, norm_attn, norm_ffn,
    bucket_bias_table, grad_y, embedding_gradient,
):
    rows, span, width = tokens.shape
    buckets, heads = bucket_bias_table.shape
    n = lax.axis_size("seq")
    inner = w_query.shape[1]
    ff = w_gate.shape[1]
    wide = w_head.shape[1]
    length = n * span
    per = rows // 2
    assert n == 4 and per == 5

    def send_rows(array, ids, slots, ext, deps=()):
        size = span + ext
        outs = [sds((2 * len(slots) - (2 in slots), size, width)), sds((len(slots), size, width))]
        todo = outs[0].shape[0] + len(slots)
        sems = [pltpu.SemaphoreType.DMA((todo,))]
        packed = call(
            functools.partial(pack_kernel, per, slots, ext), tuple(outs), (array, ids) if ext else (array,),
            [pltpu.VMEM((todo, ext, width), BF16), *sems, *sems] if ext else sems, [ANY, VMEM] if ext else [ANY],
            (ANY, ANY), vmem=16, name="pack", deps=deps,
        )
        return (swap(packed[1], "seq", 1), swap(packed[0], "seq", 2)), packed

    def pass_on(got, *deps):
        near, far = got
        return near, far, swap(after(far, *deps) if deps else far, "seq", 1)

    line = 2 * length
    x_a, _ = send_rows(tokens, seg_ids, (0,), EXT)
    bias, ind, nattn, nffn, w_qkv, wqkv_t, wout_t, wg_t, wu_t, wd_t = call(
        functools.partial(prepare_kernel, n),
        (
            sds((heads, LANES, line), F32), sds((LANES, line)), sds((width, LANES), F32), sds((width, LANES), F32),
            sds((width, 3 * inner)), sds((3 * inner, width)), sds((width, inner)), sds((ff, width)), sds((ff, width)),
            sds((width, ff)),
        ),
        (
            bucket_bias_table.T, norm_attn[None], norm_ffn[None], w_query, w_key, w_value, w_out, w_gate, w_up, w_down,
        ),
        [pltpu.VMEM((LANES, LANES), F32)], name="prepare", flops=4_000_000_000,
    )
    x_b, packed_x = send_rows(tokens, seg_ids, (1, 2), EXT, deps=(nattn,))
    x_a = pass_on(x_a, packed_x[1])

    def collect(own, c, y):
        return own, swap(c, "seq", 1), swap(y, "seq", 2)

    def collect_rest(part, *deps):
        return *part, swap(after(part[2], *deps), "seq", 1)

    def run_forward(kinds, pieces, deps=()):
        shapes = [s for _, half in kinds for s in forward_outs(half, n, span, width, inner, heads, ff)]
        shapes += [((k * len(kinds), span, width), BF16) for k in (1, 1, 2)]
        outs = tuple(sds(*s) for s in shapes)
        args = [tokens, seg_ids, bias, wqkv_t, wout_t, wg_t, wu_t, wd_t, nattn, nffn]
        specs = [ANY, VMEM] + [ANY] * 6 + [VMEM] * 2
        args += list(pieces)
        specs += [VMEM] * 3
        scratch = [pltpu.VMEM(*s) for s in shapes]
        scratch += [
            pltpu.VMEM((len(kinds), span, width), BF16), pltpu.VMEM((length, width), F32), pltpu.VMEM((LANES, length), F32),
            pltpu.VMEM((width, length), BF16), pltpu.VMEM((heads, length, 2 * LANES), BF16),
            pltpu.VMEM((heads, inner // heads + EXT, length), BF16), pltpu.VMEM((width, length), BF16),
            pltpu.VMEM((2, length, length // 2), F32), pltpu.VMEM(bias.shape, F32), *[pltpu.VMEM(w.shape, BF16) for w in (wqkv_t, wout_t, wg_t, wu_t, wd_t)],
            pltpu.SemaphoreType.DMA((8 + len(kinds),)), pltpu.SemaphoreType.DMA((24 * len(kinds),)),
        ]
        res = call(
            functools.partial(forward_kernel, kinds, n, per, heads), outs, args, scratch, specs, tuple(ANY for _ in outs),
            4_000_000_000 * len(kinds), "forward", deps=deps,
        )
        count = len(FORWARD_OUTS)
        return [dict(zip(FORWARD_OUTS, res[i * count : (i + 1) * count])) for i in range(len(kinds))], collect(*res[-3:])

    fwd, blocks_a = run_forward([(0, False)], x_a, deps=packed_x)
    x_b = pass_on(x_b, fwd[0]["r"])
    gys, packed_g = send_rows(grad_y, None, (0, 1, 2), 0, deps=(fwd[0]["r"],))
    fwd_b, blocks_b = run_forward([(1, False), (2, True)], x_b, deps=packed_g)
    fwd += fwd_b
    gys = pass_on(gys, fwd[1]["r"])
    pool_other = swap(fwd[2]["pool"], "seq", 1)

    def unpack(parts, with_emb, deps=()):
        args = [a for group in parts for a in group]
        outs = (sds((rows, span, width)),) + ((sds((rows, wide), F32),) if with_emb else ())
        scratch = [pltpu.VMEM((rows, EXT, width), BF16)] if with_emb else []
        return call(
            functools.partial(unpack_kernel, per, with_emb), outs, args, scratch + [pltpu.SemaphoreType.DMA((2 * rows,))],
            [ANY] * len(args), (ANY, VMEM)[: len(outs)], vmem=16, name="unpack", deps=deps,
        )


    packed_w = 2 * ff + 2 * width + inner
    nqs = [length, length, length // 2]
    args = [grad_y, embedding_gradient, w_head, w_down, w_gate, w_up, w_out, nffn, pool_other]
    specs = [ANY, VMEM] + [ANY] * 5 + [VMEM] * 2
    args += list(gys)
    specs += [VMEM] * 3
    for f in fwd:
        args += [f[k] for k in ("mid", "a", "ge", "hid", "att", "seg", "r", "pool")]
        specs += [ANY] * 5 + [VMEM] * 3
    outs = tuple(
        [sds((width, q)) for q in nqs] + [sds((inner, q)) for q in nqs]
        + [sds((width // 2, packed_w))] * 2 + [sds((8, width), F32), sds((3, 8, wide), F32), sds((16, 256), F32)]
    )
    scratch = []
    for q in nqs:
        scratch += [pltpu.VMEM((width, q), F32), pltpu.VMEM((ff, q), BF16), pltpu.VMEM((ff, q), BF16)]
    total = sum(nqs)
    scratch += [
        pltpu.VMEM((3, span, width), BF16), pltpu.VMEM((2, width, length), F32), pltpu.VMEM((3, width, length), BF16),
        pltpu.VMEM((width, LANES), F32), pltpu.VMEM((width, total), BF16), pltpu.VMEM((width, total), BF16),
        pltpu.VMEM((ff, total), BF16), pltpu.VMEM((ff, total), BF16), pltpu.VMEM((width, total), BF16),
        pltpu.VMEM((inner, total), BF16), pltpu.VMEM((ff, total), BF16), pltpu.VMEM((2, width // 2, packed_w), BF16),
        *[pltpu.VMEM(w.shape, BF16) for w in (w_head, w_down, w_gate, w_up, w_out)],
        pltpu.SemaphoreType.DMA((23,)), pltpu.SemaphoreType.DMA((8,)),
    ]
    m = call(functools.partial(middle_kernel, n, per), outs, args, scratch, specs, [VMEM] * 6 + [ANY] * 2 + [VMEM] * 3, flops=15_000_000_000, name="middle")
    m, blocks_a, blocks_b = together(m, blocks_a, blocks_b)
    ga, gt = m[:3], m[3:6]
    own, send, gnf, emb, pg = m[6:]

    core = ("seq", 1, 2)
    far = ("seq", 2, 2)
    digits = row_digits()
    block = width // 2 // far[2]
    for d in digits:
        block //= d[2]

    def send_shares(parts, s):
        return [swap(p, s[0], k * s[1]) for k, p in enumerate(parts) if k]

    def send_all(v, s):
        return [swap(v, s[0], k * s[1]) for k in range(1, s[2])]

    def combine(groups, deps=()):
        args, outs, scratch, plan = [], [], [], []
        for pieces, step in groups:
            rows_, wide_ = pieces[0][0][0].shape[0], sum(hi - lo for _, lo, hi in pieces)
            radix = step[2] if step else 1
            shape = (radix, rows_ // radix) if step else (rows_,)
            for arrays, _, _ in pieces:
                args += [a.reshape(shape + a.shape[-1:]) for a in arrays]
            outs += [sds((rows_ // radix, wide_))] * radix
            scratch += [pltpu.VMEM(shape + (wide_,), BF16)] if step else []
            plan.append((pieces, step))
        plan = [([(range(len(a)), lo, hi) for a, lo, hi in pieces], step) for pieces, step in plan]
        res = call(functools.partial(combine_kernel, plan), tuple(outs), args, scratch, vmem=24, name="combine", deps=deps)
        out = []
        for _, step in plan:
            radix = step[2] if step else 1
            out.append(list(res[:radix]))
            res = res[radix:]
        return out

    def joined(groups, deps=()):
        args, outs, plan = [], [], []
        for v, got, step, cuts in groups:
            cuts = cuts or [(0, v.shape[1])]
            args += [v] + got
            outs += [sds((step[2], v.shape[0], hi - lo)) for lo, hi in cuts]
            plan.append((step, cuts))
        res = call(functools.partial(join_kernel, plan), tuple(outs), args, vmem=24, name="join", deps=deps)
        return [r.reshape(-1, r.shape[-1]) for r in res]

    def all_of(*arrays):
        return [(list(arrays), 0, arrays[0].shape[1])]

    nh = length // 2
    half = call(
        functools.partial(half_back_kernel, n),
        (sds((inner, nh)), sds((2 * inner, nh)), sds((2 * inner, nh)), sds((8, line), F32)),
        (fwd[2]["q"], fwd[2]["v"], fwd[2]["kt"], fwd[2]["e"], fwd[2]["att"], gt[2]),
        [
            pltpu.VMEM((heads, length, nh), BF16), pltpu.VMEM((2, length, nh), BF16), pltpu.VMEM((2, LANES, 4 * LANES), F32),
            pltpu.VMEM((2, length, LANES), F32), pltpu.VMEM((2 * inner, length), BF16), pltpu.SemaphoreType.DMA((heads,)),
        ],
        [VMEM] * 3 + [ANY] + [VMEM] * 2, flops=2_000_000_000, name="half_back", deps=(send,),
    )
    got = swap(send, "seq", 1)
    block_parts = [collect_rest(p) for p in (blocks_a, blocks_b)]
    half, got, block_parts = together(half, got, block_parts)
    gq_half, keep, send_kv, lines_sum = half
    got_kv = swap(send_kv, "seq", 1)
    cut = packed_w // 2 // LANES * LANES
    sa, sb = [digits[0], far], [far, digits[0]]
    pa, pb = combine([([([own, got], 0, cut)], sa[0]), ([([own, got], cut, packed_w)], sb[0])])

    piece = tuple(sds((i, span + EXT, width)) for i in (1, 1, 2))

    def run_back(j, lines_sum, part, deps, extra=()):
        f = fwd[j]
        scratch = [
            pltpu.VMEM((heads, length, length), BF16), pltpu.VMEM((2, length, length), BF16),
            pltpu.VMEM((2, LANES, 4 * LANES), F32), pltpu.VMEM((2, length, LANES), F32), pltpu.VMEM((width, length), F32),
            pltpu.VMEM((width, length), BF16), pltpu.VMEM((width, length), BF16), pltpu.VMEM(w_qkv.shape, BF16),
            pltpu.VMEM((width, LANES), F32), pltpu.SemaphoreType.DMA((heads // 2 + 7,)),
        ]
        late_outs = ()
        if extra:
            late_outs = (sds((width // 2, 3 * inner)), sds((width // 2, 3 * inner)), sds((3 * inner, nh)))
            scratch += [pltpu.VMEM((width, q), BF16) for q in nqs]
            scratch += [pltpu.VMEM((3 * inner, length), BF16), pltpu.VMEM((2, width // 2, 3 * inner), BF16)]
        res = call(
            functools.partial(backward_kernel, j, n),
            (*late_outs, sds((8, line), F32), sds((3 * inner, length)), *piece, sds((width, LANES), F32)),
            (f["q"], f["v"], f["kt"], f["e"], f["att"], gt[j], lines_sum, f["x"], ga[j], w_qkv, nattn, emb, part, *extra),
            scratch, [VMEM] * 3 + [ANY] + [VMEM] * 3 + [ANY] * 3 + [VMEM] * 3 + ([ANY] + [VMEM] * 3 + [ANY] * 3 if extra else []),
            flops=4_000_000_000, name="backward", deps=deps,
        )
        late, (line_o, gq, *blocks, part) = res[: len(late_outs)], res[len(late_outs) :]
        return line_o, gq, blocks, part, late

    back = run_back(0, lines_sum, nattn, (pa[1], pb[1]))
    ra, rb = send_shares(pa, sa[0]), send_shares(pb, sb[0])
    back, ra, rb, got_kv = together(back, ra, rb, got_kv)
    pa, pb = combine([(all_of(pa[0], *ra), sa[1]), (all_of(pb[0], *rb), sb[1])])
    back2 = run_back(
        1, back[0], back[3], (pa[1], pb[1]), (back[1], gq_half, keep, got_kv, *[f["n1"] for f in fwd])
    )
    x_a = collect(*back[2])
    ra, rb = send_shares(pa, sa[1]), send_shares(pb, sb[1])
    back2, ra, rb, x_a = together(back2, ra, rb, x_a)
    late_own, late_send, gq2 = back2[4]

    late_got = swap(late_send, "seq", 1)
    x_b = collect(*back2[2])
    x_a = collect_rest(x_a)
    (parts,) = combine([(all_of(pa[0], *ra) + all_of(pb[0], *rb), digits[1])])
    z_got = send_shares(parts, digits[1])
    late_cut = (3 * inner // 2 + LANES - 1) // LANES * LANES
    la, lb = combine([([([late_own, late_got], 0, late_cut)], sa[0]), ([([late_own, late_got], late_cut, 3 * inner)], sb[0])])
    lga, lgb = send_shares(la, sa[0]), send_shares(lb, sb[0])
    late_sends = (la[1], lb[1])
    for step in digits[2:]:
        (parts,) = combine([(all_of(parts[0], *z_got), step)], deps=late_sends)
        z_got = send_shares(parts, step)
        late_sends = ()
    *x_c, small = call(
        inputs_kernel, (*piece, sds((width // 8, LANES), F32)),
        (gq2, fwd[2]["x"], ga[2], w_qkv, nattn, emb, back2[3], back2[0], gnf, ind),
        [pltpu.VMEM((width, nh), F32), pltpu.VMEM((width, LANES), F32)], flops=3_000_000_000, name="inputs",
        deps=tuple(parts[1:]) + late_sends,
    )
    lga, lgb, x_c, small, x_a = together(lga, lgb, x_c, small, x_a)
    la, lb = combine([(all_of(la[0], *lga), sa[1]), (all_of(lb[0], *lgb), sb[1])])
    lga, lgb = send_shares(la, sa[1]), send_shares(lb, sb[1])
    x_c = collect(*x_c)
    pg_b = pg.astype(BF16).reshape(block, -1)
    z_got, x_b = together(z_got, x_b)
    ((ab,),) = combine([(all_of(parts[0], *z_got) + all_of(pg_b), None)], deps=(la[1], lb[1]))
    ab_got = send_all(ab, digits[-1])
    lga, lgb = together(lga, lgb)
    ((late,),) = combine([(all_of(la[0], *lga) + all_of(lb[0], *lgb) + all_of(small), None)], deps=(ab,))
    strides = digits[1:]
    for step, back_step in zip(strides[:-1], strides[:0:-1]):
        late_got = swap(late, *step[:2])
        x_b = collect_rest(x_b) if len(x_b) == 3 else x_b
        ab_got, late_got = together(ab_got, late_got)
        (ab,) = joined([(ab, ab_got, back_step, None)])
        ab_got = send_all(ab, digits[digits.index(back_step) - 1])
        ((late,),) = combine([(all_of(late, late_got), None)], deps=(ab,))
    late_got = swap(late, *strides[-1][:2])
    (block_out,) = unpack(block_parts, False, deps=(late,))
    late_got, ab_got, block_out, x_b, x_c = together(late_got, ab_got, block_out, x_b, x_c)
    wide_a, wide_b = cut + late_cut, ab.shape[1] - cut + late.shape[1] - late_cut
    a, b = call(
        functools.partial(merge_kernel, digits[1], cut, late_cut),
        (sds((2, ab.shape[0], wide_a)), sds((2, ab.shape[0], wide_b))), (ab, *ab_got, late, late_got), vmem=24, name="merge",
    )
    a, b = a.reshape(-1, wide_a), b.reshape(-1, wide_b)
    ga_, gb_ = send_all(a, sa[1]), send_all(b, sb[1])
    x_c = collect_rest(x_c)
    ga_, gb_, x_c = together(ga_, gb_, x_c)
    a, b = joined([(a, ga_, sa[1], None), (b, gb_, sb[1], None)])
    ga_, gb_ = send_all(a, sa[0]), send_all(b, sb[0])
    grad_x, embedding = unpack([x_a, x_b, x_c], True, deps=(a, b))
    ga_, gb_, grad_x = together(ga_, gb_, grad_x)
    a, b = joined([(a, ga_, sa[0], None), (b, gb_, sb[0], None)])
    a_got, b_got = swap(a, "seq", 1), swap(b, "seq", 1)
    outs = (
        sds((width, ff), F32), sds((width, ff), F32), sds((ff, width), F32), sds((inner, width), F32),
        *[sds((width, inner), F32)] * 3,
    )
    halves = [
        pltpu.VMEM((width // 2, ff), F32), pltpu.VMEM((width // 2, ff), F32), pltpu.VMEM((2, width // 2, width), F32),
        pltpu.VMEM((inner, width // 2), F32), pltpu.VMEM((3, width // 2, inner), F32),
    ]
    first = call(
        functools.partial(finish_kernel, False, cut, width // 8), outs, (a, b), halves + [pltpu.SemaphoreType.DMA((9,))],
        out_specs=(ANY,) * FINISH_OUTS, name="finish",
    )
    first, a_got, b_got = together(first, a_got, b_got)
    *grads, grad_head, grad_norm_ffn, grad_norm_attn, grad_table = call(
        functools.partial(finish_kernel, True, cut, width // 8),
        outs + (sds((width, wide), F32), sds((1, width), F32), sds((1, width), F32), sds((heads, buckets), F32)),
        (b, a_got, b_got, *first), halves + [pltpu.VMEM((width, wide), F32), pltpu.SemaphoreType.DMA((9,))],
        [VMEM] * 3 + [ANY] * FINISH_OUTS, (ANY,) * (FINISH_OUTS + 1) + (VMEM,) * 3, name="finish",
        aliases={3 + i: i for i in range(FINISH_OUTS)},
    )
    if block != 16:
        lo, hi = packed_w - cut, ab.shape[1] - cut
        pg_all = jnp.concatenate([b[:, lo:hi], b_got[:, lo:hi]]).reshape(-1, 16, 256)[:, :15].reshape(-1, width + wide)
        grad_head = lax.dot_general(
            pg_all[:, :width], pg_all[:, width:], (((0,), (0,)), ((), ())), preferred_element_type=F32
        )
    grad_gate, grad_up, grad_down, grad_out, grad_query, grad_key, grad_value = grads
    return (
        block_out, embedding, grad_x, grad_query, grad_key, grad_value, grad_out, grad_gate, grad_up, grad_down, grad_head,
        grad_norm_attn[0], grad_norm_ffn[0], grad_table.T,
    )


def solution(mesh):
    by_pos = P("rows", "seq", None)
    by_row = P("rows", None)
    return jax.shard_map(
        shards,
        mesh=mesh,
        in_specs=(by_pos, P("rows", "seq"), *[P()] * 11, by_pos, by_row),
        out_specs=(by_pos, by_row, by_pos, *[P()] * 11),
        check_vma=False,
    )
```

```python
import functools

import jax
import jax.numpy as jnp
from jax import lax
from jax.experimental import pallas as pl
from jax.experimental.pallas import tpu as pltpu
from jax.sharding import PartitionSpec as P

EPS = 1e-06
LIMITS = (12, 16, 23, 32, 46, 64, 91)
TOP_PRECISION = lax.Precision.HIGHEST
F32 = jnp.float32
BF16 = jnp.bfloat16
MASK_STEP = 2.0**30
LOG2E = 1.4426950408889634
VMEM = pl.BlockSpec(memory_space=pltpu.VMEM)
ANY = pl.BlockSpec(memory_space=pl.ANY)
LANES = 128
EXT = 16


def mm(a, b):
    return lax.dot_general(a, b, (((1,), (0,)), ((), ())), preferred_element_type=F32)


def mm_nt(a, b):
    return lax.dot_general(a, b, (((1,), (1,)), ((), ())), preferred_element_type=F32)


def bucket_index(offset):
    distance = jnp.abs(offset)
    far_bucket = 8 + sum(((distance >= threshold).astype(jnp.int32) for threshold in LIMITS))
    near_bucket = jnp.where(distance < 8, distance, far_bucket)
    return near_bucket + 16 * (offset > 0).astype(jnp.int32)


def wide_dots(rows, mat, dot):
    at = lax.broadcasted_iota(jnp.int32, (16, rows[0].shape[1]), 0)
    lhs = jnp.zeros(at.shape, F32)
    for i, v in enumerate(rows):
        for j in range(3):
            part = v.astype(BF16).astype(F32)
            lhs = jnp.where(at == 3 * i + j, part, lhs)
            v = v - part
    out = dot(lhs.astype(BF16), mat)
    return [jnp.sum(out[3 * i : 3 * i + 3], axis=0, keepdims=True) for i in range(len(rows))]


def fold(x, op):
    while x.shape[0] > 8:
        half = x.shape[0] // 2
        x = op(x[:half], x[half:])
    return x


def col_sum(x):
    return jnp.sum(fold(x, jnp.add), axis=0, keepdims=True)


def diagonal_sums(table):
    height, width = table.shape
    acc = table[0:8, :]
    for u in range(8, height, 8):
        acc += pltpu.roll(table[u : u + 8, :], width - u, 1)
    row = lax.broadcasted_iota(jnp.int32, acc.shape, 0)
    for bit in (1, 2, 4):
        acc = jnp.where((row & bit) != 0, pltpu.roll(acc, width - bit, 1), acc)
    return jnp.sum(acc, axis=0, keepdims=True)


def position():
    me = lax.axis_index("seq")
    return me, me // 2, me % 2


class Copies:
    def __init__(self, sems):
        self.sems = sems
        self.used = 0

    def start(self, src, dst):
        copy = pltpu.make_async_copy(src, dst, self.sems.at[self.used])
        self.used += 1
        copy.start()
        return copy


def rows_to_send(per, slots):
    _, p, c = position()
    todo = []
    for i, j in enumerate(slots):
        if j == 2:
            todo += [(0, 2 * i, per * (1 - p) + per - 1), (1, i, per * p + per - 1)]
        else:
            todo.append((0, 2 * i, per * (1 - p) + 2 * c + j))
            todo.append((0, 2 * i + 1, per * (1 - p) + 2 * (1 - c) + j))
            todo.append((1, i, per * p + 2 * (1 - c) + j))
    return todo


def pack_kernel(per, groups, ext, tok, seg, *refs):
    outs, (buf, sems) = refs[:-2], refs[-2:]
    span = tok.shape[1]
    copies = Copies(sems)
    todo = [(2 * g, *t) for g, slots in enumerate(groups) for t in rows_to_send(per, slots)]
    loads = [copies.start(tok.at[row], buf.at[k, pl.ds(0, span)]) for k, (_, _, _, row) in enumerate(todo)]
    yield
    for k, (_, _, _, row) in enumerate(todo):
        value = jnp.broadcast_to(seg[pl.ds(row, 1), :].astype(F32), (ext, span)).astype(BF16)
        buf[k, span:, :] = jnp.concatenate([value] * (tok.shape[2] // span), axis=1)
    stores = []
    for k, (at, which, i, _) in enumerate(todo):
        loads[k].wait()
        stores.append(copies.start(buf.at[k], outs[at + which].at[i]))
    for copy in stores:
        copy.wait()


def prepare_kernel(
    n, table, norm_a, norm_f, wq, wk, wv, wo, wg, wu, wd,
    bias_o, ind_o, na_o, nf_o, wqkv_t, wo_t, wg_t, wu_t, wd_t,
    square,
):
    yield
    heads, _, line = bias_o.shape
    inner = wq.shape[1]
    length = line // 2
    col = lax.broadcasted_iota(jnp.int32, (LANES, line), 1)
    offset = length - LANES - jnp.where(col < line - LANES, col, col - line)
    ind = (bucket_index(offset) == lax.broadcasted_iota(jnp.int32, (LANES, line), 0)).astype(F32).astype(BF16)
    ind_o[...] = ind
    square[...] = jnp.zeros_like(square)
    square[: table.shape[0], : table.shape[1]] = table[...]
    rest = square[:8, :]
    lines = None
    for _ in range(3):
        part = rest.astype(BF16)
        rest = rest - part.astype(F32)
        term = mm(part, ind)
        lines = term if lines is None else lines + term
    lines = lines * LOG2E
    for h in range(heads):
        bias_o[h] = pltpu.roll(jnp.broadcast_to(lines[h : h + 1, :], (LANES, line)), 0, 1, stride=1, stride_axis=0)
    for src, dst in ((norm_a, na_o), (norm_f, nf_o)):
        dst[...] = jnp.broadcast_to(src[...], (LANES, src.shape[1])).T
    for i, w in enumerate((wq, wk, wv)):
        wqkv_t[i * inner : (i + 1) * inner, :] = w[...].T
    wo_t[...] = wo[...].T
    size = 256
    one = lax.broadcasted_iota(jnp.int32, (size, size), 0) == lax.broadcasted_iota(jnp.int32, (size, size), 1)
    one = one.astype(F32).astype(BF16)
    for src, dst in ((wg, wg_t), (wu, wu_t), (wd, wd_t)):
        for at in range(0, dst.shape[0], size):
            dst[at : at + size, :] = mm_nt(one, src[:, at : at + size]).astype(BF16)


STEP = 64


def chunks(height):
    return [slice(r, r + STEP) for r in range(0, height, STEP)]


def norm_into(out, src, cols, gain):
    total = None
    for r in chunks(src.shape[0]):
        x = src[r, cols].astype(F32)
        x = fold(x * x, jnp.add)
        total = x if total is None else total + x
    inv = lax.rsqrt(jnp.sum(total, axis=0, keepdims=True) / src.shape[0] + EPS)
    for r in chunks(src.shape[0]):
        out[r, cols] = (src[r, cols].astype(F32) * inv * gain[r, :]).astype(BF16)


def forward_slot(half, n, rows, bufs, w, wait, outs, copies):
    own, c1, y, c2, own_seg = rows
    tok, seg, n1, kk, va, x_b, s_buf = bufs
    bias, wqkv_t, wout_t, wg_t, wu_t, wd_t, nattn, nffn = w
    o = outs
    width = wqkv_t.shape[1]
    inner = wout_t.shape[1]
    heads = bias.shape[0]
    head = inner // heads
    span = own.shape[0]
    length = n * span
    me, p, c = position()
    for k, (piece, ids) in enumerate(((own, own_seg), (c1, None), (y, None), (c2, None))):
        at = pl.multiple_of((me ^ k) * span, span)
        x_b[:, pl.ds(at, span)] = piece[:span, :].T
        ids = piece[span : span + 1, :span].astype(F32) if ids is None else ids
        seg[:, pl.ds(at, span)] = jnp.broadcast_to(ids, (LANES, span))
    for b in range(n):
        norm_into(n1, x_b, slice(b * span, (b + 1) * span), nattn)
    nq = length // 2 if half else length
    if half:
        mine = pl.ds(pl.multiple_of(c * nq, nq), nq)
        o["x"][...] = x_b[:, mine]
        o["n1"][...] = n1[:, mine]
    else:
        mine = slice(0, nq)
        o["x"][...] = x_b[...]
        o["n1"][...] = n1[...]
    o["seg"][...] = seg[0:8, :]
    ids = lax.broadcasted_iota(jnp.int32, (LANES, length), 0).astype(F32)
    one = (seg[...] == ids).astype(F32)
    k_aug = ((one - 1.0) * MASK_STEP).T.astype(BF16)
    ids = lax.broadcasted_iota(jnp.int32, (LANES, nq), 0).astype(F32)
    q_aug = (seg[:, mine] == ids).astype(BF16)
    wait("qkv")
    if half:
        qt = mm(wqkv_t[:inner, :], n1[:, mine]).astype(BF16)
        kvt = mm(wqkv_t[inner:, :], n1[...]).astype(BF16)
        kt, vt = kvt[:inner], kvt[inner:]
    else:
        qkvt = mm(wqkv_t[...], n1[...]).astype(BF16)
        qt, kt, vt = qkvt[:inner], qkvt[inner : 2 * inner], qkvt[2 * inner :]
    o["kt"][...] = kt
    q2 = qt.astype(F32) * LOG2E
    q_hi = q2.astype(BF16)
    q_lo = (q2 - q_hi.astype(F32)).astype(BF16)
    lane = lax.broadcasted_iota(jnp.int32, (length, LANES), 1)

    def pair_ready(pair):
        ps = slice(pair * LANES, (pair + 1) * LANES)
        both = kt[ps].T.astype(F32)
        turned = pltpu.roll(both, head, 1)
        kk[2 * pair, :, :LANES] = jnp.where(lane < head, both, turned).astype(BF16)
        kk[2 * pair + 1, :, :LANES] = jnp.where(lane < head, turned, both).astype(BF16)
        for h in (2 * pair, 2 * pair + 1):
            kk[h, :, LANES:] = k_aug
            va[h, :head, :] = vt[h * head : (h + 1) * head]
            va[h, head:, :] = jnp.ones((EXT, length), BF16)

    def naturals(pair):
        ps = slice(pair * LANES, (pair + 1) * LANES)
        o["q"][:, ps] = qt[ps].T
        o["v"][:, ps] = vt[ps].T

    chunk = length // 2
    work = [(h, qc) for h in range(heads) for qc in range(nq // chunk)]
    per_pair = 2 * (nq // chunk)

    def lanes_of(qc):
        return slice(qc * chunk, (qc + 1) * chunk)

    def score(i, a, rhs):
        h, qc = work[i]
        if half:
            at = pl.ds(pl.multiple_of((n - 1 - a) * LANES + c * nq, LANES), chunk)
        else:
            at = pl.ds((n - 1 - a) * LANES + qc * chunk, chunk)
        s_a = mm(kk[h, a * LANES : (a + 1) * LANES, :], rhs) + bias[h, :, at]
        s_buf[i % 2, a * LANES : (a + 1) * LANES, :] = s_a
        return fold(s_a, jnp.maximum)

    def power(i, a, top):
        h, qc = work[i]
        e = jnp.exp2(s_buf[i % 2, a * LANES : (a + 1) * LANES, :] - top)
        o["e"][h, a * LANES : (a + 1) * LANES, lanes_of(qc)] = e.astype(BF16)

    def attend(i):
        h, qc = work[i]
        hs, qs = slice(h * head, (h + 1) * head), lanes_of(qc)
        raw = mm(va[h], o["e"][h, :, qs])
        inv = 1.0 / raw[head : head + 1, :]
        o["r"][h : h + 1, qs] = inv
        o["att"][hs, qs] = (raw[:head, :] * inv).astype(BF16)

    pair_ready(0)
    wait("bias")
    copies(o["x"], o["seg"], o["n1"], o["kt"])
    top = None
    for i in range(len(work) + 1):
        if i == len(work) // 2:
            wait("rest")
            o["through"]()
            copies(*[(o["e"], h) for h in range(heads // 2 - 1)])
        tops = []
        if i < len(work):
            h, qc = work[i]
            hs, qs = slice(h * head, (h + 1) * head), lanes_of(qc)
            rhs = jnp.concatenate([q_hi[hs, qs], q_lo[hs, qs], q_aug[:, qs]], axis=0)
        for a in range(n):
            if i < len(work):
                tops.append(score(i, a, rhs))
            if i > 0:
                power(i - 1, a, top)
        if i < len(work):
            top = jnp.max(functools.reduce(jnp.maximum, tops), axis=0, keepdims=True)
            if i % per_pair == 0 and i // per_pair < heads // 2 - 1:
                pair_ready(i // per_pair + 1)
            if i % per_pair == 1:
                naturals(i // per_pair)
        if i > 0:
            attend(i - 1)
    if half:
        x_q = x_b[:, mine].astype(F32)
    else:
        x_q = x_b[...].astype(F32)
    o["mid"][...] = x_q + mm(wout_t[...], o["att"][...])
    for b in range(nq // span):
        norm_into(n1, o["mid"], slice(b * span, (b + 1) * span), nffn)
    ff = wg_t.shape[0]
    step = 256
    for b in range(ff // step):
        cs = slice(b * step, (b + 1) * step)
        gate = mm(wg_t[cs, :], n1[:, :nq])
        up = mm(wu_t[cs, :], n1[:, :nq])
        sq = gate * gate
        th = jnp.tanh(gate * (0.7978845608028654 + (0.7978845608028654 * 0.044715) * sq))
        half_th = 0.5 + 0.5 * th
        gelu = gate * half_th
        slope = half_th + (gelu - gelu * th) * (0.7978845608028654 + (3 * 0.7978845608028654 * 0.044715) * sq)
        o["hid"][cs, :] = (gelu * up).astype(BF16)
        o["a"][cs, :] = (up * slope).astype(BF16)
        o["ge"][cs, :] = gelu.astype(BF16)
    copies(*[(o["e"], h) for h in range(heads // 2 - 1, heads)])
    copies(*[o[k] for k in ("r", "att", "q", "v", "mid", "hid", "a", "ge")])
    res = tok.at[:, :nq]
    res[...] = o["mid"][...] + mm(wd_t[...], o["hid"][...])
    valid = (seg[0:1, mine] != 0.0).astype(F32)
    parts = []
    for r in chunks(width):
        part = None
        for b in range(nq // span):
            blk = res[r, b * span : (b + 1) * span] * valid[:, b * span : (b + 1) * span]
            part = blk if part is None else part + blk
        parts.append(part)
    o["pool"][...] = jnp.broadcast_to(col_sum(jnp.concatenate(parts, axis=0).T), o["pool"].shape)
    copies(o["pool"])
    send_blocks(half, res, o["blocks"], span)


def send_blocks(half, res, outs, span):
    me, _, c = position()
    for k, out in enumerate(outs):
        block = (c + k) % 2 if half else me ^ k
        at = pl.multiple_of(block * span, span)
        out[:span, :] = res[:, pl.ds(at, span)].astype(BF16).T


FORWARD_OUTS = ("kt", "q", "v", "x", "seg", "e", "r", "att", "mid", "hid", "a", "ge", "pool", "n1")


def forward_outs(half, n, span, width, inner, heads, ff):
    length = n * span
    nq = length // 2 if half else length
    shapes = (
        ((inner, length), BF16), ((nq, inner), BF16), ((length, inner), BF16), ((width, nq), BF16), ((8, length), F32),
        ((heads, length, nq), BF16), ((8, nq), F32), ((inner, nq), BF16), ((width, nq), F32), ((ff, nq), BF16),
        ((ff, nq), BF16), ((ff, nq), BF16), ((8, width), F32), ((width, nq), BF16),
    )
    return shapes


def forward_kernel(kinds, n, per, heads, *refs):
    yield
    count = len(FORWARD_OUTS)
    tokens, seg_ids, bias, wqkv_t, wout_t, wg_t, wu_t, wd_t, nattn, nffn = refs[:10]
    near, far, again = refs[10:13]
    had = 0 if kinds[0][0] == 0 else 1
    before = refs[13 : 16 if had else 14]
    at = 16 if had else 14
    outs = [refs[at + i * count : at + (i + 1) * count] for i in range(len(kinds))]
    at += count * len(kinds)
    extra = 3 if had else 5
    block_outs = refs[at : at + extra]
    at += extra
    bufs = [refs[at + i * count : at + (i + 1) * count] for i in range(len(kinds))]
    at += count * len(kinds)
    blocks = refs[at : at + extra]
    at += extra
    own, tok, seg, n1, kk, va, x_b, s_buf, bias_b, wqkv_b, wout_b, wg_b, wu_b, wd_b, in_sems, out_sems = refs[at:]
    me, p, c = position()
    ins = Copies(in_sems)
    owns = []
    for i, (slot, half) in enumerate(kinds):
        row = per * p + (per - 1 if half else 2 * c + slot)
        owns.append((ins.start(tokens.at[row], own.at[i]), row))
    waits = {
        "qkv": [ins.start(wqkv_t, wqkv_b)],
        "bias": [ins.start(bias, bias_b)],
        "rest": [ins.start(a, b) for a, b in ((wout_t, wout_b), (wg_t, wg_b), (wu_t, wu_b), (wd_t, wd_b))],
    }

    def wait(what):
        for copy in waits.pop(what, ()):
            copy.wait()

    writes = Copies(out_sems)
    pending = []
    if had:
        through = [ins.start(a, b.at[pl.ds(0, a.shape[0])]) for a, b in zip(before, blocks)]
    else:
        todo = rows_to_send(per, (0, 1, 2))
        through = [ins.start(before[0].at[row], blocks[3 + which].at[i]) for which, i, row in todo]

    def pass_through():
        while through:
            through.pop().wait()
            if not through:
                if had:
                    pending.extend(writes.start(b.at[pl.ds(0, a.shape[0])], o.at[pl.ds(0, a.shape[0])]) for a, b, o in zip(before, blocks, block_outs))
                else:
                    pending.extend(writes.start(b, o) for b, o in zip(blocks[3:], block_outs[3:]))

    for i, (slot, half) in enumerate(kinds):
        copy, row = owns[i]
        copy.wait()
        o = dict(zip(FORWARD_OUTS, bufs[i]))
        dst = dict(zip(FORWARD_OUTS, outs[i]))
        b = had + i
        o["blocks"] = (blocks[0].at[b], blocks[1].at[b], blocks[2].at[2 * b], blocks[2].at[2 * b + 1])
        o["through"] = pass_through
        names = {id(v): k for k, v in o.items()}

        def copies(*what, o=o, dst=dst, names=names):
            for item in what:
                if isinstance(item, tuple):
                    ref, h = item
                    pending.append(writes.start(ref.at[h], dst[names[id(ref)]].at[h]))
                else:
                    pending.append(writes.start(item, dst[names[id(item)]]))

        c1, y_mine, c2_mine = near.at[i], far.at[2 * i], again.at[2 * i + (not half)]
        own_seg = seg_ids[pl.ds(row, 1), :].astype(F32)
        forward_slot(
            half, n, (own.at[i], c1, y_mine, c2_mine, own_seg), (tok, seg, n1, kk, va, x_b, s_buf),
            (bias_b, wqkv_b, wout_b, wg_b, wu_b, wd_b, nattn, nffn), wait, o, copies,
        )
        pending.append(writes.start(blocks[0].at[b], block_outs[0].at[b]))
        pending.append(writes.start(blocks[1].at[b], block_outs[1].at[b]))
        pending.append(writes.start(blocks[2].at[pl.ds(2 * b, 2)], block_outs[2].at[pl.ds(2 * b, 2)]))
    for copy in pending:
        copy.wait()


def middle_kernel(n, per, *refs):
    yield
    grad_y, eg, w_head, w_down, w_gate, w_up, w_out, nffn, pool_other = refs[:9]
    at = 9
    near, far, again = refs[at : at + 3]
    at += 3
    names = ("mid", "a", "ge", "hid", "att", "seg", "r", "pool")
    srcs = [dict(zip(names, refs[at + 8 * i : at + 8 * i + 8])) for i in range(3)]
    at += 24
    ga_o, gt_o = refs[at : at + 3], refs[at + 3 : at + 6]
    own_o, send_o, gnf_o, emb_o, pg_o = refs[at + 6 : at + 11]
    at += 11
    big = ("mid", "a", "ge")
    bufs = [dict(zip(big, refs[at + 3 * i : at + 3 * i + 3])) for i in range(3)]
    at += 9
    own, res, gyt, part, gb, n2, gg, gu, ga, att, hid, packed, wh, wd, wg, wu, wo, sems, out_sems = refs[at:]
    span, width = own.shape[1:]
    length = n * span
    ff = w_gate.shape[1]
    inner = w_out.shape[0]
    head = inner // 6
    wide = w_head.shape[1]
    me, p, c = position()
    ins = Copies(sems)
    owns = []
    for i in range(3):
        row = per * p + (per - 1 if i == 2 else 2 * c + i)
        owns.append(ins.start(grad_y.at[row], own.at[i]))
    weights = {k: ins.start(a, b) for k, a, b in (("h", w_head, wh), ("d", w_down, wd))}
    for k, a, b in (("g", w_gate, wg), ("u", w_up, wu), ("o", w_out, wo)):
        weights[k] = ins.start(a, b)
    lanes = [pl.ds(i * length, length // 2 if i == 2 else length) for i in range(3)]
    loads = []
    for i in range(3):
        loads.append([ins.start(srcs[i][k], bufs[i][k]) for k in big])
    late_loads = []
    for i in range(3):
        late_loads.append(ins.start(srcs[i]["hid"], hid.at[:, lanes[i]]))
        late_loads.append(ins.start(srcs[i]["att"], att.at[:, lanes[i]]))

    def need(*names):
        for k in names:
            if k in weights:
                weights.pop(k).wait()

    for i in range(3):
        owns[i].wait()
    need("h")
    pools, cots, counts = [], [], []
    for i in range(3):
        half = i == 2
        for k, piece in enumerate((own.at[i], near.at[i], far.at[2 * i], again.at[2 * i + (not half)])):
            place = pl.multiple_of((me ^ k) * span, span)
            gyt[i, :, pl.ds(place, span)] = piece[...].T
        count = jnp.sum((srcs[i]["seg"][0:1, :] != 0.0).astype(F32), axis=1, keepdims=True)
        pool = srcs[i]["pool"][0:1, :]
        if half:
            pool = pool + pool_other[0:1, :]
        pools.append(pool / count)
        counts.append(count)
        row = per * p + (per - 1 if half else 2 * c + i)
        cots.append(eg[pl.ds(row, 1), :])
    proj = wide_dots(pools, wh[...], mm)
    g_projs = []
    for i in range(3):
        inv = lax.rsqrt(jnp.sum(proj[i] * proj[i], axis=1, keepdims=True) + EPS)
        emb = proj[i] * inv
        g_proj = inv * (cots[i] - emb * jnp.sum(emb * cots[i], axis=1, keepdims=True))
        emb_o[i] = jnp.broadcast_to(emb, emb_o.shape[1:])
        once = jnp.where(c == 0, 1.0, 0.0) if i == 2 else 1.0
        for q in range((width + wide) // 256):
            piece = pools[i][:, q * 256 : (q + 1) * 256] if q < width // 256 else g_proj[:, q * 256 - width : (q + 1) * 256 - width]
            pg_o[5 * i + q : 5 * i + q + 1, :] = piece * once
        g_projs.append(g_proj)
    g_pools = wide_dots(g_projs, wh[...], mm_nt)
    g_cols = [jnp.broadcast_to(g / k, (span, width)).T for g, k in zip(g_pools, counts)]
    need("d", "g", "u", "o")
    for copy in loads[0]:
        copy.wait()
    sizes = [length, length, length // 2]
    starts = [0, length, 2 * length]

    def outer(i, b, r):
        if i == 2:
            place = pl.ds(pl.multiple_of((c * (sizes[2] // span) + b) * span, span), span)
        else:
            place = pl.ds(b * span, span)
        valid = (srcs[i]["seg"][0:1, place] != 0.0).astype(F32)
        return gyt[i, r, place].astype(F32) + valid * g_cols[i][r, :]

    def branch(i, b):
        for r in chunks(width):
            gb[r, starts[i] + b * span : starts[i] + (b + 1) * span] = outer(i, b, r).astype(BF16)

    step = 256

    def gates(i, b):
        cs, ls = slice(b * step, (b + 1) * step), slice(starts[i], starts[i] + sizes[i])
        g_hid = mm(wd[cs, :], gb[:, ls])
        gg[cs, ls] = (g_hid * bufs[i]["a"][cs, :].astype(F32)).astype(BF16)
        gu[cs, ls] = (g_hid * bufs[i]["ge"][cs, :].astype(F32)).astype(BF16)

    def normed(i):
        ls = slice(starts[i], starts[i] + sizes[i])
        res[i % 2, :, : sizes[i]] = mm(wg[...], gg[:, ls]) + mm(wu[...], gu[:, ls])

    def norm(i, b):
        mid, ds = bufs[i]["mid"], res.at[i % 2]
        bs = slice(b * span, (b + 1) * span)
        ls = slice(starts[i] + b * span, starts[i] + (b + 1) * span)
        sq = cross = None
        for r in chunks(width):
            m = mid[r, bs]
            t = fold(m * m, jnp.add)
            u = fold(ds[r, bs] * nffn[r, :] * m, jnp.add)
            sq, cross = (t, u) if sq is None else (sq + t, cross + u)
        inv2 = lax.rsqrt(jnp.sum(sq, axis=0, keepdims=True) / width + EPS)
        mean = inv2 * jnp.sum(cross, axis=0, keepdims=True) / width
        for r in chunks(width):
            hat = mid[r, bs] * inv2
            n2[r, ls] = (hat * nffn[r, :]).astype(BF16)
            gn = ds[r, bs]
            if i == 0 and b == 0:
                part[r, :] = gn * hat
            else:
                part[r, :] += gn * hat
            ga[r, ls] = (outer(i, b, r) + inv2 * (gn * nffn[r, :] - hat * mean)).astype(BF16)

    def attended(i):
        ls = slice(starts[i], starts[i] + sizes[i])
        ga_o[i][...] = ga[:, ls]
        gatt = mm(wo[...], ga[:, ls]).astype(BF16).astype(F32)
        for h in range(6):
            hs = slice(h * head, (h + 1) * head)
            gt_o[i][hs, :] = (gatt[hs, :] * srcs[i]["r"][h : h + 1, :]).astype(BF16)

    def store(at, value):
        rows = value.shape[0] // 2
        for side in range(2):
            packed[side, :, at : at + value.shape[1]] = value[side * rows : (side + 1) * rows].astype(BF16)

    outs = Copies(out_sems)
    pending = []

    def send(lo, hi):
        pending.append(outs.start(packed.at[c, :, pl.ds(lo, hi - lo)], own_o.at[:, pl.ds(lo, hi - lo)]))
        pending.append(outs.start(packed.at[1 - c, :, pl.ds(lo, hi - lo)], send_o.at[:, pl.ds(lo, hi - lo)]))

    blocks = [k // span for k in sizes]
    for b in range(blocks[0]):
        branch(0, b)
    for b in range(ff // step):
        gates(0, b)
    for i in (1, 2):
        for copy in loads[i]:
            copy.wait()
    normed(0)
    for b in range(blocks[1]):
        branch(1, b)
    for b in range(ff // step):
        gates(1, b)
        norm(0, b)
    normed(1)
    attended(0)
    for b in range(blocks[2]):
        branch(2, b)
    for b in range(ff // step):
        gates(2, b)
        norm(1, b)
    normed(2)
    attended(1)
    for copy in late_loads:
        copy.wait()
    top = 2 * ff
    for b in range(2):
        store(top + b * width, mm_nt(hid[b * width : (b + 1) * width, :], gb[...]))
        norm(2, b)
    attended(2)
    send(top, top + 2 * width)
    for b in range(2):
        cs = slice(b * 512, (b + 1) * 512)
        store(b * 512, mm_nt(n2[...], gg[cs, :]))
    send(0, ff)
    for b in range(2):
        cs = slice(b * 512, (b + 1) * 512)
        store(ff + b * 512, mm_nt(n2[...], gu[cs, :]))
    store(top + 2 * width, mm_nt(ga[...], att[...]))
    gnf_o[...] = jnp.broadcast_to(col_sum(part[...].T), gnf_o.shape)
    pg_o[15:16, :] = jnp.zeros((1, 256), F32)
    send(ff, 2 * ff)
    send(top + 2 * width, top + 2 * width + inner)
    for copy in pending:
        copy.wait()


def attention_back(core, n, q_nat, v_nat, kt, e_wait, e_b, att, gt, gs, table, kv_side, line, gq_o, put_kv):
    heads = e_b.shape[0]
    inner = kt.shape[0]
    head = inner // heads
    length = kt.shape[1]
    half = core is not None
    nq = length // 2 if half else length
    lane = lax.broadcasted_iota(jnp.int32, (length, LANES), 1)
    gt_nat = gt[...].T
    zeros = jnp.zeros((head, nq), BF16)
    width = 4 * LANES
    table[:, :, :LANES] = jnp.zeros((2, LANES, LANES), F32)

    def scores(h, a, rhs, delta, far, seen):
        ps = slice(h // 2 * LANES, (h // 2 + 1) * LANES)
        ks = slice(a * LANES, (a + 1) * LANES)
        g_s = e_b[h, ks, :].astype(F32) * (mm(v_nat[ks, ps], rhs) - delta)
        gs[h % 2, ks, :nq] = g_s.astype(BF16)
        t = table.at[h % 2]
        for b in range(nq // LANES):
            blk = g_s[:, b * LANES : (b + 1) * LANES]
            d = (2 * core if half else 0) + b - a
            if abs(d) <= 1:
                at = (d + 2) * LANES
                if d in seen:
                    t[:, at : at + LANES] += blk
                else:
                    t[:, at : at + LANES] = blk
                    seen.add(d)
            else:
                far[d < 0].append(fold(blk, jnp.add))

    def lines(h, far):
        t = table.at[h % 2]
        line(h, slice(LANES, LANES + width), diagonal_sums(t))
        if far[0]:
            line(h, slice(6 * LANES, 7 * LANES), jnp.sum(sum(far[0]), axis=0, keepdims=True))
        if far[1]:
            line(h, slice(0, LANES), jnp.sum(sum(far[1]), axis=0, keepdims=True))

    def weigh(h, which):
        hs, ps = slice(h * head, (h + 1) * head), slice(h // 2 * LANES, (h // 2 + 1) * LANES)
        g = gs.at[h % 2]
        if which == 0:
            gq_o[hs, :] = mm(kt[hs, :], g[:, :nq]).astype(BF16)
            return
        value = mm(g[:, :nq], q_nat[:, ps]) if which == 1 else mm(e_b[h], gt_nat[:, ps])
        if h % 2 == 0:
            kv_side[which - 1] = value
        else:
            put_kv(h // 2, which - 1, jnp.where(lane < head, kv_side[which - 1], value).astype(BF16).T)

    old = None
    for h in range(heads + 1):
        far = [[], []]
        if h < heads:
            if h % 2 == 0:
                e_wait(h // 2)
            hs = slice(h * head, (h + 1) * head)
            g_h = gt[hs, :]
            delta = col_sum(g_h.astype(F32) * att[hs, :].astype(F32))
            rhs = jnp.concatenate([g_h, zeros] if h % 2 == 0 else [zeros, g_h], axis=0)
            seen = set()
        for a in range(n):
            if h < heads:
                scores(h, a, rhs, delta, far, seen)
            if h > 0:
                if a < 3:
                    weigh(h - 1, a)
                else:
                    lines(h - 1, old)
        old = far


def half_back_kernel(n, q_nat, v_nat, kt, e_in, att, gt, gq_o, keep_o, send_o, line_o, e_b, gs, table, kv_side, kv, sems):
    ins = Copies(sems)
    loads = [ins.start(e_in.at[pl.ds(0, 2)], e_b.at[pl.ds(0, 2)])]
    yield
    loads += [ins.start(e_in.at[pl.ds(h, 2)], e_b.at[pl.ds(h, 2)]) for h in range(2, e_in.shape[0], 2)]
    inner = kt.shape[0]

    def put(pair, which, value):
        kv[which * inner + pair * LANES : which * inner + (pair + 1) * LANES, :] = value.astype(BF16)

    def line(h, lanes, value):
        line_o[h : h + 1, lanes] = value

    line_o[...] = jnp.zeros_like(line_o)
    _, _, c = position()
    for core in range(2):

        @pl.when(c == core)
        def _(core=core):
            attention_back(
                core, n, q_nat, v_nat, kt, lambda p: loads[p].wait(), e_b, att, gt, gs, table, kv_side, line, gq_o, put
            )

    nq = kt.shape[1] // 2
    keep_o[...] = kv[:, pl.ds(pl.multiple_of(c * nq, nq), nq)]
    send_o[...] = kv[:, pl.ds(pl.multiple_of((1 - c) * nq, nq), nq)]


def backward_kernel(
    slot, n,
    q_nat, v_nat, kt, e_in, att, gt, line_in, xt, ga, w_query, w_key, w_value, nattn, emb, part_in, *refs,
):
    if slot:
        gq0, gq_half, keep, got, n1_0, n1_1, n1_2, own_o, send_o, gq2, *refs = refs
        *refs, m0, m1, m2, g0, packed = refs
    line_o, gq_o, b_own, b_c, b_y, part_o, gq, e_b, gs, table, kv_side, res, xb, gb, wb, part, sems = refs
    ins = Copies(sems)
    loads = [ins.start(e_in.at[pl.ds(0, 2)], e_b.at[pl.ds(0, 2)])]
    yield
    loads += [ins.start(e_in.at[pl.ds(h, 2)], e_b.at[pl.ds(h, 2)]) for h in range(2, e_in.shape[0], 2)]
    more = [ins.start(a, b) for a, b in ((xt, xb), (ga, gb))]
    more += [ins.start(w, wb.at[:, pl.ds(i * w.shape[1], w.shape[1])]) for i, w in enumerate((w_query, w_key, w_value))]
    if slot:
        more += [ins.start(a, b) for a, b in ((gq0, g0), (n1_0, m0), (n1_1, m1), (n1_2, m2))]
    inner = kt.shape[0]

    def put(pair, which, value):
        at = (1 + which) * inner + pair * LANES
        gq[at : at + LANES, :] = value.astype(BF16)

    def line(h, lanes, value):
        line_o[h : h + 1, lanes] = line_in[h : h + 1, lanes] + value

    line_o[...] = line_in[...]
    if slot:
        gq2[:inner, :] = gq_half[...]
        gq2[inner:, :] = (keep[...].astype(F32) + got[...].astype(F32)).astype(BF16)
    attention_back(
        None, n, q_nat, v_nat, kt, lambda p: loads[p].wait(), e_b, att, gt, gs, table, kv_side, line, gq.at[:inner, :], put
    )
    for copy in more:
        copy.wait()
    if slot:
        part[...] = part_in[...]
        _, _, c = position()
        rows = own_o.shape[0]
        for at in range(0, 3 * inner, inner):
            cs = slice(at, at + inner)
            value = mm_nt(m0[...], g0[cs, :]) + mm_nt(m1[...], gq[cs, :]) + mm_nt(m2[...], gq2[cs, :])
            for side in range(2):
                packed[side, :, cs] = value[side * rows : (side + 1) * rows].astype(BF16)
    span = b_own.shape[1] - EXT
    input_rows(slot, False, gq, xb, gb, wb, nattn, emb, res, part, (b_own.at[0], b_c.at[0], b_y.at[0], b_y.at[1]), span)
    part_o[...] = part[...]
    outs = [ins.start(gq, gq_o)]
    if slot:
        outs += [ins.start(packed.at[c], own_o), ins.start(packed.at[1 - c], send_o)]
    for copy in outs:
        copy.wait()


def input_rows(slot, half, gq, xt, ga, w_qkv, nattn, emb, res, part, outs, span):
    width, nq = res.shape[0], gq.shape[1]
    res[:, :nq] = mm(w_qkv[...], gq[...])
    for b in range(nq // span):
        bs = slice(b * span, (b + 1) * span)
        sq = cross = None
        for r in chunks(width):
            x = xt[r, bs].astype(F32)
            t = fold(x * x, jnp.add)
            u = fold(res[r, bs] * nattn[r, :] * x, jnp.add)
            sq, cross = (t, u) if sq is None else (sq + t, cross + u)
        inv = lax.rsqrt(jnp.sum(sq, axis=0, keepdims=True) / width + EPS)
        mean = inv * jnp.sum(cross, axis=0, keepdims=True) / width
        for r in chunks(width):
            hat = xt[r, bs].astype(F32) * inv
            gn = res[r, bs]
            if slot == 0 and b == 0:
                part[r, :] = gn * hat
            else:
                part[r, :] += gn * hat
            res[r, bs] = ga[r, bs].astype(F32) + inv * (gn * nattn[r, :] - hat * mean)
    send_blocks(half, res, outs, span)
    row = emb[slot, 0:1, :]
    high = row.astype(BF16)
    low = (row - high.astype(F32)).astype(BF16)
    rest = row.shape[1] - width
    for out in outs:
        for at, v in ((0, high), (2, low)):
            out[span + at : span + at + 1, :] = v[:, :width]
            out[span + at + 1 : span + at + 2, :rest] = v[:, width:]


def inputs_kernel(
    gq, xt, ga, w_query, w_key, w_value, nattn, emb, part_in, line_in, gnf, indicator,
    b_own, b_c, b_y, small,
    res, part, w_qkv,
):
    small[...] = jnp.zeros_like(small)
    part[...] = part_in[...]
    for i, w in enumerate((w_query, w_key, w_value)):
        w_qkv[:, i * w.shape[1] : (i + 1) * w.shape[1]] = w[...]
    width = res.shape[0]
    span = b_own.shape[1] - EXT
    input_rows(2, True, gq, xt, ga, w_qkv, nattn, emb, res, part, (b_own.at[0], b_c.at[0], b_y.at[0], b_y.at[1]), span)
    gna = col_sum(part[...].T)
    for i in range(width // LANES):
        small[i : i + 1, :] = gnf[0:1, i * LANES : (i + 1) * LANES]
        small[4 + i : 5 + i, :] = gna[:, i * LANES : (i + 1) * LANES]
    lines = line_in[...]
    hi = lines.astype(BF16)
    lo = (lines - hi.astype(F32)).astype(BF16)
    small[8:16, :] = mm_nt(hi, indicator[...]) + mm_nt(lo, indicator[...])


def unpack_kernel(per, with_emb, *refs):
    groups = (len(refs) - 1 - (3 if with_emb else 1)) // 4
    out = refs[4 * groups]
    sems = refs[-1]
    ways = []
    for g in range(groups):
        own, c1, y, d = refs[4 * g : 4 * g + 4]
        ways += [(own.at[i], c1.at[i], y.at[2 * i], d.at[2 * i + 1]) for i in range(own.shape[0])]
    own0 = ways[0][0]
    me, p, _ = position()
    rows, span, width = out.shape
    for r in range(rows):
        pair, j = divmod(r, per)
        slot = 2 if j == per - 1 else j % 2
        core = p if slot == 2 else j // 2
        k = me ^ (pair * 2 + core)
        for which in range(4):
            ref = ways[slot][which]

            @pl.when(k == which)
            def _(ref=ref, r=r):
                pltpu.make_async_copy(ref.at[pl.ds(0, span)], out.at[r], sems.at[r]).start()
                if with_emb:
                    pltpu.make_async_copy(ref.at[pl.ds(span, EXT)], refs[4 * groups + 2].at[r], sems.at[rows + r]).start()

    if with_emb:
        emb, got = refs[4 * groups + 1 : 4 * groups + 3]
        for r in range(rows):
            pltpu.make_async_copy(own0.at[pl.ds(span, EXT)], got.at[r], sems.at[rows + r]).wait()
            value = got[r].astype(F32)
            emb[r : r + 1, :width] = value[0:1, :] + value[2:3, :]
            emb[r : r + 1, width:] = (value[1:2, :] + value[3:4, :])[:, : emb.shape[1] - width]
    for r in range(rows):
        pltpu.make_async_copy(own0.at[pl.ds(0, span)], out.at[r], sems.at[r]).wait()


def place(step):
    if step is None:
        return 0, 1
    axis, stride, radix = step
    return (lax.axis_index(axis) // stride) % radix, radix


def combine_kernel(plan, *refs):
    at = sum(len(arrays) for pieces, _ in plan for arrays, _, _ in pieces)
    outs = at + sum(place(step)[1] for _, step in plan)
    ins, at, scratch = 0, at, outs
    for pieces, step in plan:
        off = 0
        total = refs[scratch] if step else refs[at]
        for arrays, lo, hi in pieces:
            value = sum(refs[ins + i][..., lo:hi].astype(F32) for i in range(len(arrays)))
            ins += len(arrays)
            total[..., off : off + hi - lo] = value.astype(BF16)
            off += hi - lo
        if step:
            d, radix = place(step)
            for k in range(radix):
                refs[at + k][...] = total[d ^ k]
            at += radix
            scratch += 1
        else:
            at += 1


def join_kernel(plan, *refs):
    ins, at = 0, sum(place(step)[1] for step, _ in plan)
    for step, cuts in plan:
        d, radix = place(step)
        for lo, hi in cuts:
            for k in range(radix):
                refs[at][d ^ k] = refs[ins + k][:, lo:hi]
            at += 1
        ins += radix


def merge_kernel(step, cut, late_cut, own, got, late, late_got, a_o, b_o):
    d, _ = place(step)
    total = (late[...].astype(F32) + late_got[...].astype(F32)).astype(BF16)
    rows, wide = own.shape
    for src, at in ((own, d), (got, d ^ 1)):
        a_o[at, :, :cut] = src[:, :cut]
        b_o[at, :, : wide - cut] = src[:, cut:]
    for side in range(2):
        part = total[side * rows : (side + 1) * rows]
        a_o[side, :, cut:] = part[:, :late_cut]
        b_o[side, :, wide - cut :] = part[:, late_cut:]


FINISH_OUTS = 7


def finish_kernel(second, cut, block, *refs):
    if second:
        b_own, a, b, *rest = refs
        outs, rest = rest[FINISH_OUTS : 2 * FINISH_OUTS], rest[2 * FINISH_OUTS :]
        head_o, nf_o, na_o, table_o, gate, up, down, out, qkv, head, sems = rest
    else:
        a, b, *rest = refs
        outs, (gate, up, down, out, qkv, sems) = rest[:FINISH_OUTS], rest[FINISH_OUTS:]
    gate_o, up_o, down_o, out_o, *qkv_o = outs
    _, _, c = position()
    rows = a.shape[0]
    ff = gate.shape[1]
    width = gate_o.shape[0]
    inner = out.shape[0]
    rest = ff - (cut - ff)
    start = pl.multiple_of(((1 - c) if second else c) * rows, rows)
    at = pl.ds(start, rows)
    copies = Copies(sems)
    gate[...] = a[:, :ff].astype(F32)
    pending = [copies.start(gate, gate_o.at[at])]
    down[0] = b[:, rest : rest + width].astype(F32)
    pending.append(copies.start(down.at[0], down_o.at[at]))
    down[1] = b[:, rest + width : rest + 2 * width].astype(F32)
    pending.append(copies.start(down.at[1], down_o.at[pl.ds(pl.multiple_of(width + start, rows), rows)]))
    up[:, : cut - ff] = a[:, ff:cut].astype(F32)
    up[:, cut - ff :] = b[:, :rest].astype(F32)
    pending.append(copies.start(up, up_o.at[at]))
    late_a = a.shape[1] - cut
    late_b = b.shape[1] - LANES - (3 * inner - late_a)
    for i in range(3):
        lo, hi = i * inner, (i + 1) * inner
        mid = min(max(late_a, lo), hi)
        if mid > lo:
            qkv[i, :, : mid - lo] = a[:, cut + lo : cut + mid].astype(F32)
        if mid < hi:
            qkv[i, :, mid - lo :] = b[:, late_b + mid - late_a : late_b + hi - late_a].astype(F32)
        pending.append(copies.start(qkv.at[i], qkv_o[i].at[at]))
    out[...] = b[:, rest + 2 * width : rest + 2 * width + inner].astype(F32).T
    pending.append(copies.start(out, out_o.at[:, at]))
    if second:
        row = lax.broadcasted_iota(jnp.int32, (rows, 256), 0) % 16
        small = None
        for ref in (b_own, b):
            g = ref[:, late_b - 256 : late_b].astype(F32)
            turned = {t: pltpu.roll(g, rows - t, 0).astype(BF16) for t in range(1, 5)}
            for i in range(2):
                kept = jnp.where((row < 15) & (row % 5 == i), g, 0.0).T.astype(BF16)
                for j in range(3):
                    term = mm(kept, turned[2 + j - i])
                    place_ = (slice(i * 256, (i + 1) * 256), slice(j * 256, (j + 1) * 256))
                    if ref is b_own:
                        head[place_] = term
                    else:
                        head[place_] += term
            for r in range(0, rows, block):
                value = ref[r : r + 16, ref.shape[1] - LANES :].astype(F32)
                small = value if small is None else small + value
        pending.append(copies.start(head, head_o))
        for i in range(nf_o.shape[1] // LANES):
            nf_o[:, i * LANES : (i + 1) * LANES] = small[i : i + 1, :]
            na_o[:, i * LANES : (i + 1) * LANES] = small[4 + i : 5 + i, :]
        table_o[...] = small[8 : 8 + table_o.shape[0], : table_o.shape[1]]
    for copy in pending:
        copy.wait()


def sds(shape, dtype=BF16):
    return jax.ShapeDtypeStruct(shape, dtype)


def call(
    kernel, outs, args, scratch=(), specs=None, out_specs=None, flops=0, name=None, vmem=56, deps=(), aliases=None, overlap=False
):
    count, n_out = len(args), len(outs) if isinstance(outs, tuple) else 1
    specs = list(specs or [VMEM] * count)
    out_specs = list(out_specs or [VMEM] * n_out)
    out_list = list(outs) if isinstance(outs, tuple) else [outs]
    loads = [i for i in range(count) if overlap and specs[i] is VMEM]
    stores = [i for i in range(n_out) if overlap and out_specs[i] is VMEM]
    bufs = [pltpu.VMEM(args[i].shape, args[i].dtype) for i in loads] + [pltpu.VMEM(out_list[i].shape, out_list[i].dtype) for i in stores]
    if overlap:
        bufs.append(pltpu.SemaphoreType.DMA((len(loads) + len(stores),)))

    def body(*refs):
        ins, refs = list(refs[:count]), refs[count + len(deps) :]
        res, refs = list(refs[:n_out]), refs[n_out:]
        if overlap:
            bufs_, refs = refs[: len(bufs)], refs[len(bufs) :]
            copies = Copies(bufs_[-1])
            pending = []
            for i, buf in zip(loads, bufs_):
                pending.append(copies.start(ins[i], buf))
                ins[i] = buf
            out_refs = list(res)
            for i, buf in zip(stores, bufs_[len(loads) :]):
                res[i] = buf
            run = kernel(*ins, *res, *refs)
            if run is not None:
                next(run)
            for copy in pending:
                copy.wait()
            if run is not None:
                next(run, None)
        else:
            kernel(*ins, *res, *refs)
        if overlap:
            pending = [copies.start(res[i], out_refs[i]) for i in stores]
            for copy in pending:
                copy.wait()

    if overlap:
        specs = [ANY if s is VMEM else s for s in specs]
        out_specs = [ANY if s is VMEM else s for s in out_specs]
    return pl.pallas_call(
        body,
        out_shape=outs,
        in_specs=specs + [ANY] * len(deps),
        out_specs=tuple(out_specs) if isinstance(outs, tuple) else out_specs[0],
        scratch_shapes=bufs + list(scratch),
        compiler_params=pltpu.CompilerParams(vmem_limit_bytes=vmem * 2**20),
        cost_estimate=pl.CostEstimate(flops=flops, bytes_accessed=10_000_000, transcendentals=0),
        input_output_aliases=aliases or {},
        name=name,
    )(*args, *deps)


def swap(x, axis, k):
    n = lax.axis_size(axis)
    return lax.ppermute(x, axis, [(i, i ^ k) for i in range(n)])


def after(x, *deps):
    return lax.optimization_barrier((x, *deps))[0]


def together(*trees):
    leaves, shape = jax.tree.flatten(trees)
    return jax.tree.unflatten(shape, lax.optimization_barrier(leaves))


def row_digits():
    return [("rows", 1 << i, 2) for i in range(lax.axis_size("rows").bit_length() - 1)]


def shards(
    tokens, seg_ids, w_query, w_key, w_value, w_out, w_gate, w_up, w_down, w_head, norm_attn, norm_ffn,
    bucket_bias_table, grad_y, embedding_gradient,
):
    rows, span, width = tokens.shape
    buckets, heads = bucket_bias_table.shape
    n = lax.axis_size("seq")
    inner = w_query.shape[1]
    ff = w_gate.shape[1]
    wide = w_head.shape[1]
    length = n * span
    per = rows // 2
    assert n == 4 and per == 5
    slots = 3

    groups = ((0,), (1, 2))
    shapes = [(k, span + EXT, width) for slots in groups for k in (2 * len(slots) - (2 in slots), len(slots))]
    todo = sum(k for k, _, _ in shapes)
    y_a, c_a, y_b, c_b = call(
        functools.partial(pack_kernel, per, groups, EXT), tuple(sds(k) for k in shapes), (tokens, seg_ids),
        [pltpu.VMEM((todo, span + EXT, width), BF16), pltpu.SemaphoreType.DMA((2 * todo,))], [ANY, VMEM], (ANY,) * 4,
        vmem=60, name="pack", overlap=True,
    )

    def pass_on(got, *deps):
        near, far = got
        return near, far, swap(after(far, *deps) if deps else far, "seq", 1)

    line = 2 * length
    x_a = swap(c_a, "seq", 1), swap(y_a, "seq", 2)
    bias, ind, nattn, nffn, wqkv_t, wout_t, wg_t, wu_t, wd_t = call(
        functools.partial(prepare_kernel, n),
        (
            sds((heads, LANES, line), F32), sds((LANES, line)), sds((width, LANES), F32), sds((width, LANES), F32),
            sds((3 * inner, width)), sds((width, inner)), sds((ff, width)), sds((ff, width)),
            sds((width, ff)),
        ),
        (
            bucket_bias_table.T, norm_attn[None], norm_ffn[None], w_query, w_key, w_value, w_out, w_gate, w_up, w_down,
        ),
        [pltpu.VMEM((LANES, LANES), F32)], name="prepare", flops=4_000_000_000, overlap=True,
    )
    x_a, y_b, c_b, nattn = together(x_a, y_b, c_b, nattn)
    x_b = swap(c_b, "seq", 1), swap(y_b, "seq", 2)
    x_a = pass_on(x_a)

    def collect(own, c, y):
        return own, swap(c, "seq", 1), swap(y, "seq", 2)

    def collect_rest(part, *deps):
        return *part, swap(after(part[2], *deps), "seq", 1)

    def run_forward(kinds, pieces, before=(), deps=()):
        shapes = [s for _, half in kinds for s in forward_outs(half, n, span, width, inner, heads, ff)]
        had = len(before) and before[0].shape[0]
        shapes += [((k * (len(kinds) + had), span, width), BF16) for k in (1, 1, 2)]
        if not had:
            shapes += [((2 * slots - 1, span, width), BF16), ((slots, span, width), BF16)]
        outs = tuple(sds(*s) for s in shapes)
        args = [tokens, seg_ids, bias, wqkv_t, wout_t, wg_t, wu_t, wd_t, nattn, nffn]
        specs = [ANY, VMEM] + [ANY] * 6 + [VMEM] * 2
        args += [*pieces, *(before or (grad_y,))]
        specs += [VMEM] * 3 + [ANY] * (3 if had else 1)
        scratch = [pltpu.VMEM(*s) for s in shapes]
        scratch += [
            pltpu.VMEM((len(kinds), span, width), BF16), pltpu.VMEM((length, width), F32), pltpu.VMEM((LANES, length), F32),
            pltpu.VMEM((width, length), BF16), pltpu.VMEM((heads, length, 2 * LANES), BF16),
            pltpu.VMEM((heads, inner // heads + EXT, length), BF16), pltpu.VMEM((width, length), BF16),
            pltpu.VMEM((2, length, length // 2), F32), pltpu.VMEM(bias.shape, F32), *[pltpu.VMEM(w.shape, BF16) for w in (wqkv_t, wout_t, wg_t, wu_t, wd_t)],
            pltpu.SemaphoreType.DMA((12 + len(kinds) + 3 * slots,)), pltpu.SemaphoreType.DMA((24 * len(kinds) + 6,)),
        ]
        res = call(
            functools.partial(forward_kernel, kinds, n, per, heads), outs, args, scratch, specs, tuple(ANY for _ in outs),
            4_000_000_000 * len(kinds), "forward", deps=deps, overlap=True,
        )
        count = len(FORWARD_OUTS)
        at = count * len(kinds)
        rows_ = [dict(zip(FORWARD_OUTS, res[i * count : (i + 1) * count])) for i in range(len(kinds))]
        return rows_, res[at : at + 3], res[at + 3 :]

    fwd, blocks, packed_g = run_forward([(0, False)], x_a, deps=(y_b, c_b))
    x_b = pass_on(x_b, fwd[0]["r"])
    gys = swap(packed_g[1], "seq", 1), swap(packed_g[0], "seq", 2)
    fwd_b, blocks, _ = run_forward([(1, False), (2, True)], x_b, blocks, deps=packed_g)
    blocks = collect(*blocks)
    fwd += fwd_b
    gys = pass_on(gys, fwd[1]["r"])
    pool_other = swap(fwd[2]["pool"], "seq", 1)

    def unpack(parts, with_emb, deps=()):
        args = [a for group in parts for a in group]
        outs = (sds((rows, span, width)),) + ((sds((rows, wide), F32),) if with_emb else ())
        scratch = [pltpu.VMEM((rows, EXT, width), BF16)] if with_emb else []
        return call(
            functools.partial(unpack_kernel, per, with_emb), outs, args, scratch + [pltpu.SemaphoreType.DMA((2 * rows,))],
            [ANY] * len(args), (ANY, VMEM)[: len(outs)], vmem=16, name="unpack", deps=deps,
        )


    packed_w = 2 * ff + 2 * width + inner
    nqs = [length, length, length // 2]
    args = [grad_y, embedding_gradient, w_head, w_down, w_gate, w_up, w_out, nffn, pool_other]
    specs = [ANY, VMEM] + [ANY] * 5 + [VMEM] * 2
    args += list(gys)
    specs += [VMEM] * 3
    for f in fwd:
        args += [f[k] for k in ("mid", "a", "ge", "hid", "att", "seg", "r", "pool")]
        specs += [ANY] * 5 + [VMEM] * 3
    outs = tuple(
        [sds((width, q)) for q in nqs] + [sds((inner, q)) for q in nqs]
        + [sds((width // 2, packed_w))] * 2 + [sds((8, width), F32), sds((3, 8, wide), F32), sds((16, 256), F32)]
    )
    scratch = []
    for q in nqs:
        scratch += [pltpu.VMEM((width, q), F32), pltpu.VMEM((ff, q), BF16), pltpu.VMEM((ff, q), BF16)]
    total = sum(nqs)
    scratch += [
        pltpu.VMEM((3, span, width), BF16), pltpu.VMEM((2, width, length), F32), pltpu.VMEM((3, width, length), BF16),
        pltpu.VMEM((width, LANES), F32), pltpu.VMEM((width, total), BF16), pltpu.VMEM((width, total), BF16),
        pltpu.VMEM((ff, total), BF16), pltpu.VMEM((ff, total), BF16), pltpu.VMEM((width, total), BF16),
        pltpu.VMEM((inner, total), BF16), pltpu.VMEM((ff, total), BF16), pltpu.VMEM((2, width // 2, packed_w), BF16),
        *[pltpu.VMEM(w.shape, BF16) for w in (w_head, w_down, w_gate, w_up, w_out)],
        pltpu.SemaphoreType.DMA((23,)), pltpu.SemaphoreType.DMA((8,)),
    ]
    m = call(functools.partial(middle_kernel, n, per), outs, args, scratch, specs, [VMEM] * 6 + [ANY] * 2 + [VMEM] * 3, flops=15_000_000_000, name="middle", overlap=True)
    m, blocks = together(m, blocks)
    ga, gt = m[:3], m[3:6]
    own, send, gnf, emb, pg = m[6:]

    core = ("seq", 1, 2)
    far = ("seq", 2, 2)
    digits = row_digits()
    block = width // 2 // far[2]
    for d in digits:
        block //= d[2]

    def send_shares(parts, s):
        return [swap(p, s[0], k * s[1]) for k, p in enumerate(parts) if k]

    def send_all(v, s):
        return [swap(v, s[0], k * s[1]) for k in range(1, s[2])]

    def combine(groups, deps=()):
        args, outs, scratch, plan = [], [], [], []
        for pieces, step in groups:
            rows_, wide_ = pieces[0][0][0].shape[0], sum(hi - lo for _, lo, hi in pieces)
            radix = step[2] if step else 1
            shape = (radix, rows_ // radix) if step else (rows_,)
            for arrays, _, _ in pieces:
                args += [a.reshape(shape + a.shape[-1:]) for a in arrays]
            outs += [sds((rows_ // radix, wide_))] * radix
            scratch += [pltpu.VMEM(shape + (wide_,), BF16)] if step else []
            plan.append((pieces, step))
        plan = [([(range(len(a)), lo, hi) for a, lo, hi in pieces], step) for pieces, step in plan]
        res = call(functools.partial(combine_kernel, plan), tuple(outs), args, scratch, vmem=24, name="combine", deps=deps)
        out = []
        for _, step in plan:
            radix = step[2] if step else 1
            out.append(list(res[:radix]))
            res = res[radix:]
        return out

    def joined(groups, deps=()):
        args, outs, plan = [], [], []
        for v, got, step, cuts in groups:
            cuts = cuts or [(0, v.shape[1])]
            args += [v] + got
            outs += [sds((step[2], v.shape[0], hi - lo)) for lo, hi in cuts]
            plan.append((step, cuts))
        res = call(functools.partial(join_kernel, plan), tuple(outs), args, vmem=24, name="join", deps=deps)
        return [r.reshape(-1, r.shape[-1]) for r in res]

    def all_of(*arrays):
        return [(list(arrays), 0, arrays[0].shape[1])]

    nh = length // 2
    half = call(
        functools.partial(half_back_kernel, n),
        (sds((inner, nh)), sds((2 * inner, nh)), sds((2 * inner, nh)), sds((8, line), F32)),
        (fwd[2]["q"], fwd[2]["v"], fwd[2]["kt"], fwd[2]["e"], fwd[2]["att"], gt[2]),
        [
            pltpu.VMEM((heads, length, nh), BF16), pltpu.VMEM((2, length, nh), BF16), pltpu.VMEM((2, LANES, 4 * LANES), F32),
            pltpu.VMEM((2, length, LANES), F32), pltpu.VMEM((2 * inner, length), BF16), pltpu.SemaphoreType.DMA((heads,)),
        ],
        [VMEM] * 3 + [ANY] + [VMEM] * 2, flops=2_000_000_000, name="half_back", deps=(send,), overlap=True,
    )
    got = swap(send, "seq", 1)
    block_parts = [collect_rest(blocks)]
    half, got, block_parts = together(half, got, block_parts)
    gq_half, keep, send_kv, lines_sum = half
    got_kv = swap(send_kv, "seq", 1)
    cut = packed_w // 2 // LANES * LANES
    sa, sb = [digits[0], far], [far, digits[0]]
    pa, pb = combine([([([own, got], 0, cut)], sa[0]), ([([own, got], cut, packed_w)], sb[0])])

    piece = tuple(sds((i, span + EXT, width)) for i in (1, 1, 2))

    def run_back(j, lines_sum, part, deps, extra=()):
        f = fwd[j]
        scratch = [
            pltpu.VMEM((3 * inner, length), BF16), pltpu.VMEM((heads, length, length), BF16),
            pltpu.VMEM((2, length, length), BF16), pltpu.VMEM((2, LANES, 4 * LANES), F32), pltpu.VMEM((2, length, LANES), F32), pltpu.VMEM((width, length), F32),
            pltpu.VMEM((width, length), BF16), pltpu.VMEM((width, length), BF16), pltpu.VMEM((width, 3 * inner), BF16),
            pltpu.VMEM((width, LANES), F32), pltpu.SemaphoreType.DMA((heads // 2 + 14,)),
        ]
        late_outs = ()
        if extra:
            late_outs = (sds((width // 2, 3 * inner)), sds((width // 2, 3 * inner)), sds((3 * inner, nh)))
            scratch += [pltpu.VMEM((width, q), BF16) for q in nqs]
            scratch += [pltpu.VMEM((3 * inner, length), BF16), pltpu.VMEM((2, width // 2, 3 * inner), BF16)]
        res = call(
            functools.partial(backward_kernel, j, n),
            (*late_outs, sds((8, line), F32), sds((3 * inner, length)), *piece, sds((width, LANES), F32)),
            (f["q"], f["v"], f["kt"], f["e"], f["att"], gt[j], lines_sum, f["x"], ga[j], w_query, w_key, w_value, nattn, emb, part, *extra),
            scratch, [VMEM] * 3 + [ANY] + [VMEM] * 3 + [ANY] * 5 + [VMEM] * 3 + ([ANY] + [VMEM] * 3 + [ANY] * 3 if extra else []),
            ([ANY] * 2 + [VMEM] if extra else []) + [VMEM, ANY] + [VMEM] * 4, flops=4_000_000_000, name="backward", deps=deps, overlap=True,
        )
        late, (line_o, gq, *blocks, part) = res[: len(late_outs)], res[len(late_outs) :]
        return line_o, gq, blocks, part, late

    back = run_back(0, lines_sum, nattn, (pa[1], pb[1]))
    ra, rb = send_shares(pa, sa[0]), send_shares(pb, sb[0])
    back, ra, rb, got_kv = together(back, ra, rb, got_kv)
    pa, pb = combine([(all_of(pa[0], *ra), sa[1]), (all_of(pb[0], *rb), sb[1])])
    back2 = run_back(
        1, back[0], back[3], (pa[1], pb[1]), (back[1], gq_half, keep, got_kv, *[f["n1"] for f in fwd])
    )
    x_a = collect(*back[2])
    ra, rb = send_shares(pa, sa[1]), send_shares(pb, sb[1])
    back2, ra, rb, x_a = together(back2, ra, rb, x_a)
    late_own, late_send, gq2 = back2[4]

    late_got = swap(late_send, "seq", 1)
    x_a = collect_rest(x_a)
    (parts,) = combine([(all_of(pa[0], *ra) + all_of(pb[0], *rb), digits[1])])
    z_got = send_shares(parts, digits[1])
    late_got, x_a = together(late_got, x_a)
    x_b = collect(*back2[2])
    late_cut = (3 * inner // 2 + LANES - 1) // LANES * LANES
    la, lb = combine([([([late_own, late_got], 0, late_cut)], sa[0]), ([([late_own, late_got], late_cut, 3 * inner)], sb[0])])
    lga, lgb = send_shares(la, sa[0]), send_shares(lb, sb[0])
    late_sends = (la[1], lb[1])
    for step in digits[2:]:
        (parts,) = combine([(all_of(parts[0], *z_got), step)], deps=late_sends)
        z_got = send_shares(parts, step)
        late_sends = ()
    lga, lgb = together(lga, lgb)
    la, lb = combine([(all_of(la[0], *lga), sa[1]), (all_of(lb[0], *lgb), sb[1])])
    lga, lgb = send_shares(la, sa[1]), send_shares(lb, sb[1])
    *x_c, small = call(
        inputs_kernel, (*piece, sds((width // 8, LANES), F32)),
        (gq2, fwd[2]["x"], ga[2], w_query, w_key, w_value, nattn, emb, back2[3], back2[0], gnf, ind),
        [pltpu.VMEM((width, nh), F32), pltpu.VMEM((width, LANES), F32), pltpu.VMEM((width, 3 * inner), BF16)],
        flops=3_000_000_000, name="inputs", vmem=16,
        deps=tuple(parts[1:]) + (la[1], lb[1]),
    )
    pg_b = pg.astype(BF16).reshape(block, -1)
    ((ab,),) = combine([(all_of(parts[0], *z_got) + all_of(pg_b), None)], deps=(la[1], lb[1]))
    ab_got = send_all(ab, digits[-1])
    lga, lgb, x_c, small, x_b = together(lga, lgb, x_c, small, x_b)
    x_c = collect(*x_c)
    ((late,),) = combine([(all_of(la[0], *lga) + all_of(lb[0], *lgb) + all_of(small), None)], deps=(ab,))
    strides = digits[1:]
    for step, back_step in zip(strides[:-1], strides[:0:-1]):
        late_got = swap(late, *step[:2])
        x_b = collect_rest(x_b) if len(x_b) == 3 else x_b
        ab_got, late_got = together(ab_got, late_got)
        (ab,) = joined([(ab, ab_got, back_step, None)])
        ab_got = send_all(ab, digits[digits.index(back_step) - 1])
        ((late,),) = combine([(all_of(late, late_got), None)], deps=(ab,))
    late_got = swap(late, *strides[-1][:2])
    (block_out,) = unpack(block_parts, False, deps=(late,))
    late_got, ab_got, block_out, x_b, x_c = together(late_got, ab_got, block_out, x_b, x_c)
    wide_a, wide_b = cut + late_cut, ab.shape[1] - cut + late.shape[1] - late_cut
    a, b = call(
        functools.partial(merge_kernel, digits[1], cut, late_cut),
        (sds((2, ab.shape[0], wide_a)), sds((2, ab.shape[0], wide_b))), (ab, *ab_got, late, late_got), vmem=24, name="merge",
    )
    a, b = a.reshape(-1, wide_a), b.reshape(-1, wide_b)
    ga_, gb_ = send_all(a, sa[1]), send_all(b, sb[1])
    x_c = collect_rest(x_c)
    ga_, gb_, x_c = together(ga_, gb_, x_c)
    a, b = joined([(a, ga_, sa[1], None), (b, gb_, sb[1], None)])
    ga_, gb_ = send_all(a, sa[0]), send_all(b, sb[0])
    grad_x, embedding = unpack([x_a, x_b, x_c], True, deps=(a, b))
    ga_, gb_, grad_x = together(ga_, gb_, grad_x)
    a, b = joined([(a, ga_, sa[0], None), (b, gb_, sb[0], None)])
    a_got, b_got = swap(a, "seq", 1), swap(b, "seq", 1)
    outs = (
        sds((width, ff), F32), sds((width, ff), F32), sds((ff, width), F32), sds((inner, width), F32),
        *[sds((width, inner), F32)] * 3,
    )
    halves = [
        pltpu.VMEM((width // 2, ff), F32), pltpu.VMEM((width // 2, ff), F32), pltpu.VMEM((2, width // 2, width), F32),
        pltpu.VMEM((inner, width // 2), F32), pltpu.VMEM((3, width // 2, inner), F32),
    ]
    first = call(
        functools.partial(finish_kernel, False, cut, width // 8), outs, (a, b), halves + [pltpu.SemaphoreType.DMA((9,))],
        out_specs=(ANY,) * FINISH_OUTS, name="finish", vmem=24,
    )
    first, a_got, b_got = together(first, a_got, b_got)
    *grads, grad_head, grad_norm_ffn, grad_norm_attn, grad_table = call(
        functools.partial(finish_kernel, True, cut, width // 8),
        outs + (sds((width, wide), F32), sds((1, width), F32), sds((1, width), F32), sds((heads, buckets), F32)),
        (b, a_got, b_got, *first), halves + [pltpu.VMEM((width, wide), F32), pltpu.SemaphoreType.DMA((9,))],
        [VMEM] * 3 + [ANY] * FINISH_OUTS, (ANY,) * (FINISH_OUTS + 1) + (VMEM,) * 3, name="finish", vmem=24,
        aliases={3 + i: i for i in range(FINISH_OUTS)},
    )
    if block != 16:
        lo, hi = packed_w - cut, ab.shape[1] - cut
        pg_all = jnp.concatenate([b[:, lo:hi], b_got[:, lo:hi]]).reshape(-1, 16, 256)[:, :15].reshape(-1, width + wide)
        grad_head = lax.dot_general(
            pg_all[:, :width], pg_all[:, width:], (((0,), (0,)), ((), ())), preferred_element_type=F32
        )
    grad_gate, grad_up, grad_down, grad_out, grad_query, grad_key, grad_value = grads
    return (
        block_out, embedding, grad_x, grad_query, grad_key, grad_value, grad_out, grad_gate, grad_up, grad_down, grad_head,
        grad_norm_attn[0], grad_norm_ffn[0], grad_table.T,
    )


def solution(mesh):
    by_pos = P("rows", "seq", None)
    by_row = P("rows", None)
    return jax.shard_map(
        shards,
        mesh=mesh,
        in_specs=(by_pos, P("rows", "seq"), *[P()] * 11, by_pos, by_row),
        out_specs=(by_pos, by_row, by_pos, *[P()] * 11),
        check_vma=False,
    )
```

```python
import functools

import jax
import jax.numpy as jnp
from jax import lax
from jax.experimental import pallas as pl
from jax.experimental.pallas import tpu as pltpu
from jax.sharding import PartitionSpec as P

EPS = 1e-06
LIMITS = (12, 16, 23, 32, 46, 64, 91)
TOP_PRECISION = lax.Precision.HIGHEST
F32 = jnp.float32
BF16 = jnp.bfloat16
MASK_STEP = 2.0**30
LOG2E = 1.4426950408889634
VMEM = pl.BlockSpec(memory_space=pltpu.VMEM)
ANY = pl.BlockSpec(memory_space=pl.ANY)
LANES = 128
EXT = 16


def mm(a, b):
    return lax.dot_general(a, b, (((1,), (0,)), ((), ())), preferred_element_type=F32)


def mm_nt(a, b):
    return lax.dot_general(a, b, (((1,), (1,)), ((), ())), preferred_element_type=F32)


def bucket_index(offset):
    distance = jnp.abs(offset)
    far_bucket = 8 + sum(((distance >= threshold).astype(jnp.int32) for threshold in LIMITS))
    near_bucket = jnp.where(distance < 8, distance, far_bucket)
    return near_bucket + 16 * (offset > 0).astype(jnp.int32)


def wide_dots(rows, mat, dot):
    at = lax.broadcasted_iota(jnp.int32, (16, rows[0].shape[1]), 0)
    lhs = jnp.zeros(at.shape, F32)
    for i, v in enumerate(rows):
        for j in range(3):
            part = v.astype(BF16).astype(F32)
            lhs = jnp.where(at == 3 * i + j, part, lhs)
            v = v - part
    out = dot(lhs.astype(BF16), mat)
    return [jnp.sum(out[3 * i : 3 * i + 3], axis=0, keepdims=True) for i in range(len(rows))]


def fold(x, op):
    while x.shape[0] > 8:
        half = x.shape[0] // 2
        x = op(x[:half], x[half:])
    return x


def col_sum(x):
    return jnp.sum(fold(x, jnp.add), axis=0, keepdims=True)


def diagonal_sums(table):
    height, width = table.shape
    acc = table[0:8, :]
    for u in range(8, height, 8):
        acc += pltpu.roll(table[u : u + 8, :], width - u, 1)
    row = lax.broadcasted_iota(jnp.int32, acc.shape, 0)
    for bit in (1, 2, 4):
        acc = jnp.where((row & bit) != 0, pltpu.roll(acc, width - bit, 1), acc)
    return jnp.sum(acc, axis=0, keepdims=True)


def position():
    me = lax.axis_index("seq")
    return me, me // 2, me % 2


class Copies:
    def __init__(self, sems):
        self.sems = sems
        self.used = 0

    def start(self, src, dst):
        copy = pltpu.make_async_copy(src, dst, self.sems.at[self.used])
        self.used += 1
        copy.start()
        return copy


def rows_to_send(per, slots):
    _, p, c = position()
    todo = []
    for i, j in enumerate(slots):
        if j == 2:
            todo += [(0, 2 * i, per * (1 - p) + per - 1), (1, i, per * p + per - 1)]
        else:
            todo.append((0, 2 * i, per * (1 - p) + 2 * c + j))
            todo.append((0, 2 * i + 1, per * (1 - p) + 2 * (1 - c) + j))
            todo.append((1, i, per * p + 2 * (1 - c) + j))
    return todo


def pack_kernel(per, groups, ext, tok, seg, *refs):
    outs, (buf, sems) = refs[:-2], refs[-2:]
    span = tok.shape[1]
    copies = Copies(sems)
    todo = [(2 * g, *t) for g, slots in enumerate(groups) for t in rows_to_send(per, slots)]
    loads = [copies.start(tok.at[row], buf.at[k, pl.ds(0, span)]) for k, (_, _, _, row) in enumerate(todo)]
    yield
    for k, (_, _, _, row) in enumerate(todo):
        value = jnp.broadcast_to(seg[pl.ds(row, 1), :].astype(F32), (ext, span)).astype(BF16)
        buf[k, span:, :] = jnp.concatenate([value] * (tok.shape[2] // span), axis=1)
    stores = []
    for k, (at, which, i, _) in enumerate(todo):
        loads[k].wait()
        stores.append(copies.start(buf.at[k], outs[at + which].at[i]))
    for copy in stores:
        copy.wait()


def prepare_kernel(
    n, table, norm_a, norm_f, wq, wk, wv, wo, wg, wu, wd,
    bias_o, ind_o, na_o, nf_o, wqkv_t, wo_t, wg_t, wu_t, wd_t,
    square,
):
    yield
    heads, _, line = bias_o.shape
    inner = wq.shape[1]
    length = line // 2
    col = lax.broadcasted_iota(jnp.int32, (LANES, line), 1)
    offset = length - LANES - jnp.where(col < line - LANES, col, col - line)
    ind = (bucket_index(offset) == lax.broadcasted_iota(jnp.int32, (LANES, line), 0)).astype(F32).astype(BF16)
    ind_o[...] = ind
    square[...] = jnp.zeros_like(square)
    square[: table.shape[0], : table.shape[1]] = table[...]
    rest = square[:8, :]
    lines = None
    for _ in range(3):
        part = rest.astype(BF16)
        rest = rest - part.astype(F32)
        term = mm(part, ind)
        lines = term if lines is None else lines + term
    lines = lines * LOG2E
    for h in range(heads):
        bias_o[h] = pltpu.roll(jnp.broadcast_to(lines[h : h + 1, :], (LANES, line)), 0, 1, stride=1, stride_axis=0)
    for src, dst in ((norm_a, na_o), (norm_f, nf_o)):
        dst[...] = jnp.broadcast_to(src[...], (LANES, src.shape[1])).T
    for i, w in enumerate((wq, wk, wv)):
        wqkv_t[i * inner : (i + 1) * inner, :] = w[...].T
    wo_t[...] = wo[...].T
    size = 256
    one = lax.broadcasted_iota(jnp.int32, (size, size), 0) == lax.broadcasted_iota(jnp.int32, (size, size), 1)
    one = one.astype(F32).astype(BF16)
    for src, dst in ((wg, wg_t), (wu, wu_t), (wd, wd_t)):
        for at in range(0, dst.shape[0], size):
            dst[at : at + size, :] = mm_nt(one, src[:, at : at + size]).astype(BF16)


STEP = 64


def chunks(height):
    return [slice(r, r + STEP) for r in range(0, height, STEP)]


def norm_into(out, src, cols, gain):
    total = None
    for r in chunks(src.shape[0]):
        x = src[r, cols].astype(F32)
        x = fold(x * x, jnp.add)
        total = x if total is None else total + x
    inv = lax.rsqrt(jnp.sum(total, axis=0, keepdims=True) / src.shape[0] + EPS)
    for r in chunks(src.shape[0]):
        out[r, cols] = (src[r, cols].astype(F32) * inv * gain[r, :]).astype(BF16)


def forward_slot(half, n, rows, bufs, w, wait, outs, copies):
    own, c1, y, c2, own_seg = rows
    tok, seg, n1, kk, va, x_b, s_buf = bufs
    bias, wqkv_t, wout_t, wg_t, wu_t, wd_t, nattn, nffn = w
    o = outs
    width = wqkv_t.shape[1]
    inner = wout_t.shape[1]
    heads = bias.shape[0]
    head = inner // heads
    span = own.shape[0]
    length = n * span
    me, p, c = position()
    for k, (piece, ids) in enumerate(((own, own_seg), (c1, None), (y, None), (c2, None))):
        at = pl.multiple_of((me ^ k) * span, span)
        x_b[:, pl.ds(at, span)] = piece[:span, :].T
        ids = piece[span : span + 1, :span].astype(F32) if ids is None else ids
        seg[:, pl.ds(at, span)] = jnp.broadcast_to(ids, (LANES, span))
    for b in range(n):
        norm_into(n1, x_b, slice(b * span, (b + 1) * span), nattn)
    nq = length // 2 if half else length
    if half:
        mine = pl.ds(pl.multiple_of(c * nq, nq), nq)
        o["x"][...] = x_b[:, mine]
        o["n1"][...] = n1[:, mine]
    else:
        mine = slice(0, nq)
        o["x"][...] = x_b[...]
        o["n1"][...] = n1[...]
    o["seg"][...] = seg[0:8, :]
    ids = lax.broadcasted_iota(jnp.int32, (LANES, length), 0).astype(F32)
    one = (seg[...] == ids).astype(F32)
    k_aug = ((one - 1.0) * MASK_STEP).T.astype(BF16)
    ids = lax.broadcasted_iota(jnp.int32, (LANES, nq), 0).astype(F32)
    q_aug = (seg[:, mine] == ids).astype(BF16)
    wait("qkv")
    if half:
        qt = mm(wqkv_t[:inner, :], n1[:, mine]).astype(BF16)
        kvt = mm(wqkv_t[inner:, :], n1[...]).astype(BF16)
        kt, vt = kvt[:inner], kvt[inner:]
    else:
        qkvt = mm(wqkv_t[...], n1[...]).astype(BF16)
        qt, kt, vt = qkvt[:inner], qkvt[inner : 2 * inner], qkvt[2 * inner :]
    o["kt"][...] = kt
    q2 = qt.astype(F32) * LOG2E
    q_hi = q2.astype(BF16)
    q_lo = (q2 - q_hi.astype(F32)).astype(BF16)
    lane = lax.broadcasted_iota(jnp.int32, (length, LANES), 1)

    def pair_ready(pair):
        ps = slice(pair * LANES, (pair + 1) * LANES)
        both = kt[ps].T.astype(F32)
        turned = pltpu.roll(both, head, 1)
        kk[2 * pair, :, :LANES] = jnp.where(lane < head, both, turned).astype(BF16)
        kk[2 * pair + 1, :, :LANES] = jnp.where(lane < head, turned, both).astype(BF16)
        for h in (2 * pair, 2 * pair + 1):
            kk[h, :, LANES:] = k_aug
            va[h, :head, :] = vt[h * head : (h + 1) * head]
            va[h, head:, :] = jnp.ones((EXT, length), BF16)

    def naturals(pair):
        ps = slice(pair * LANES, (pair + 1) * LANES)
        o["q"][:, ps] = qt[ps].T
        o["v"][:, ps] = vt[ps].T

    chunk = nq
    work = [(h, qc) for h in range(heads) for qc in range(nq // chunk)]
    per_pair = 2 * (nq // chunk)

    def lanes_of(qc):
        return slice(qc * chunk, (qc + 1) * chunk)

    def score(i, a, rhs):
        h, qc = work[i]
        if half:
            at = pl.ds(pl.multiple_of((n - 1 - a) * LANES + c * nq, LANES), chunk)
        else:
            at = pl.ds((n - 1 - a) * LANES + qc * chunk, chunk)
        s_a = mm(kk[h, a * LANES : (a + 1) * LANES, :], rhs) + bias[h, :, at]
        s_buf[i % 2, a * LANES : (a + 1) * LANES, :chunk] = s_a
        return fold(s_a, jnp.maximum)

    def power(i, a, top):
        h, qc = work[i]
        e = jnp.exp2(s_buf[i % 2, a * LANES : (a + 1) * LANES, :chunk] - top)
        o["e"][h, a * LANES : (a + 1) * LANES, lanes_of(qc)] = e.astype(BF16)

    def attend(i):
        h, qc = work[i]
        hs, qs = slice(h * head, (h + 1) * head), lanes_of(qc)
        raw = mm(va[h], o["e"][h, :, qs])
        inv = 1.0 / raw[head : head + 1, :]
        o["r"][h : h + 1, qs] = inv
        o["att"][hs, qs] = (raw[:head, :] * inv).astype(BF16)

    pair_ready(0)
    wait("bias")
    copies(o["x"], o["seg"], o["n1"], o["kt"])
    top = None
    for i in range(len(work) + 1):
        if i == len(work) // 2:
            wait("rest")
            o["through"]()
            copies(*[(o["e"], h) for h in range(heads // 2 - 1)])
        tops = []
        if i < len(work):
            h, qc = work[i]
            hs, qs = slice(h * head, (h + 1) * head), lanes_of(qc)
            rhs = jnp.concatenate([q_hi[hs, qs], q_lo[hs, qs], q_aug[:, qs]], axis=0)
        for a in range(n):
            if i < len(work):
                tops.append(score(i, a, rhs))
            if i > 0:
                power(i - 1, a, top)
        if i < len(work):
            top = jnp.max(functools.reduce(jnp.maximum, tops), axis=0, keepdims=True)
            if i % per_pair == 0 and i // per_pair < heads // 2 - 1:
                pair_ready(i // per_pair + 1)
            if i % per_pair == 1:
                naturals(i // per_pair)
        if i > 0:
            attend(i - 1)
    if half:
        x_q = x_b[:, mine].astype(F32)
    else:
        x_q = x_b[...].astype(F32)
    o["mid"][...] = x_q + mm(wout_t[...], o["att"][...])
    for b in range(nq // span):
        norm_into(n1, o["mid"], slice(b * span, (b + 1) * span), nffn)
    ff = wg_t.shape[0]
    step = 256
    for b in range(ff // step):
        cs = slice(b * step, (b + 1) * step)
        gate = mm(wg_t[cs, :], n1[:, :nq])
        up = mm(wu_t[cs, :], n1[:, :nq])
        sq = gate * gate
        th = jnp.tanh(gate * (0.7978845608028654 + (0.7978845608028654 * 0.044715) * sq))
        half_th = 0.5 + 0.5 * th
        gelu = gate * half_th
        slope = half_th + (gelu - gelu * th) * (0.7978845608028654 + (3 * 0.7978845608028654 * 0.044715) * sq)
        o["hid"][cs, :] = (gelu * up).astype(BF16)
        o["a"][cs, :] = (up * slope).astype(BF16)
        o["ge"][cs, :] = gelu.astype(BF16)
    copies(*[(o["e"], h) for h in range(heads // 2 - 1, heads)])
    copies(*[o[k] for k in ("r", "att", "q", "v", "mid", "hid", "a", "ge")])
    res = tok.at[:, :nq]
    res[...] = o["mid"][...] + mm(wd_t[...], o["hid"][...])
    valid = (seg[0:1, mine] != 0.0).astype(F32)
    parts = []
    for r in chunks(width):
        part = None
        for b in range(nq // span):
            blk = res[r, b * span : (b + 1) * span] * valid[:, b * span : (b + 1) * span]
            part = blk if part is None else part + blk
        parts.append(part)
    o["pool"][...] = jnp.broadcast_to(col_sum(jnp.concatenate(parts, axis=0).T), o["pool"].shape)
    copies(o["pool"])
    send_blocks(half, res, o["blocks"], span)


def send_blocks(half, res, outs, span):
    me, _, c = position()
    for k, out in enumerate(outs):
        block = (c + k) % 2 if half else me ^ k
        at = pl.multiple_of(block * span, span)
        out[:span, :] = res[:, pl.ds(at, span)].astype(BF16).T


FORWARD_OUTS = ("kt", "q", "v", "x", "seg", "e", "r", "att", "mid", "hid", "a", "ge", "pool", "n1")


def forward_outs(half, n, span, width, inner, heads, ff):
    length = n * span
    nq = length // 2 if half else length
    shapes = (
        ((inner, length), BF16), ((nq, inner), BF16), ((length, inner), BF16), ((width, nq), BF16), ((8, length), F32),
        ((heads, length, nq), BF16), ((8, nq), F32), ((inner, nq), BF16), ((width, nq), F32), ((ff, nq), BF16),
        ((ff, nq), BF16), ((ff, nq), BF16), ((8, width), F32), ((width, nq), BF16),
    )
    return shapes


def forward_kernel(kinds, n, per, heads, *refs):
    yield
    count = len(FORWARD_OUTS)
    tokens, seg_ids, bias, wqkv_t, wout_t, wg_t, wu_t, wd_t, nattn, nffn = refs[:10]
    near, far, again = refs[10:13]
    had = 0 if kinds[0][0] == 0 else 1
    before = refs[13 : 16 if had else 14]
    at = 16 if had else 14
    outs = [refs[at + i * count : at + (i + 1) * count] for i in range(len(kinds))]
    at += count * len(kinds)
    extra = 3 if had else 5
    block_outs = refs[at : at + extra]
    at += extra
    bufs = [refs[at + i * count : at + (i + 1) * count] for i in range(len(kinds))]
    at += count * len(kinds)
    blocks = refs[at : at + extra]
    at += extra
    own, tok, seg, n1, kk, va, x_b, s_buf, bias_b, wqkv_b, wout_b, wg_b, wu_b, wd_b, in_sems, out_sems = refs[at:]
    me, p, c = position()
    ins = Copies(in_sems)
    owns = []
    for i, (slot, half) in enumerate(kinds):
        row = per * p + (per - 1 if half else 2 * c + slot)
        owns.append((ins.start(tokens.at[row], own.at[i]), row))
    waits = {
        "qkv": [ins.start(wqkv_t, wqkv_b)],
        "bias": [ins.start(bias, bias_b)],
        "rest": [ins.start(a, b) for a, b in ((wout_t, wout_b), (wg_t, wg_b), (wu_t, wu_b), (wd_t, wd_b))],
    }

    def wait(what):
        for copy in waits.pop(what, ()):
            copy.wait()

    writes = Copies(out_sems)
    pending = []
    if had:
        through = [ins.start(a, b.at[pl.ds(0, a.shape[0])]) for a, b in zip(before, blocks)]
    else:
        todo = rows_to_send(per, (0, 1, 2))
        through = [ins.start(before[0].at[row], blocks[3 + which].at[i]) for which, i, row in todo]

    def pass_through():
        while through:
            through.pop().wait()
            if not through:
                if had:
                    pending.extend(writes.start(b.at[pl.ds(0, a.shape[0])], o.at[pl.ds(0, a.shape[0])]) for a, b, o in zip(before, blocks, block_outs))
                else:
                    pending.extend(writes.start(b, o) for b, o in zip(blocks[3:], block_outs[3:]))

    for i, (slot, half) in enumerate(kinds):
        copy, row = owns[i]
        copy.wait()
        o = dict(zip(FORWARD_OUTS, bufs[i]))
        dst = dict(zip(FORWARD_OUTS, outs[i]))
        b = had + i
        o["blocks"] = (blocks[0].at[b], blocks[1].at[b], blocks[2].at[2 * b], blocks[2].at[2 * b + 1])
        o["through"] = pass_through
        names = {id(v): k for k, v in o.items()}

        def copies(*what, o=o, dst=dst, names=names):
            for item in what:
                if isinstance(item, tuple):
                    ref, h = item
                    pending.append(writes.start(ref.at[h], dst[names[id(ref)]].at[h]))
                else:
                    pending.append(writes.start(item, dst[names[id(item)]]))

        c1, y_mine, c2_mine = near.at[i], far.at[2 * i], again.at[2 * i + (not half)]
        own_seg = seg_ids[pl.ds(row, 1), :].astype(F32)
        forward_slot(
            half, n, (own.at[i], c1, y_mine, c2_mine, own_seg), (tok, seg, n1, kk, va, x_b, s_buf),
            (bias_b, wqkv_b, wout_b, wg_b, wu_b, wd_b, nattn, nffn), wait, o, copies,
        )
        pending.append(writes.start(blocks[0].at[b], block_outs[0].at[b]))
        pending.append(writes.start(blocks[1].at[b], block_outs[1].at[b]))
        pending.append(writes.start(blocks[2].at[pl.ds(2 * b, 2)], block_outs[2].at[pl.ds(2 * b, 2)]))
    for copy in pending:
        copy.wait()


def middle_kernel(n, per, *refs):
    yield
    grad_y, eg, w_head, w_down, w_gate, w_up, w_out, nffn, pool_other = refs[:9]
    at = 9
    near, far, again = refs[at : at + 3]
    at += 3
    names = ("mid", "a", "ge", "hid", "att", "seg", "r", "pool")
    srcs = [dict(zip(names, refs[at + 8 * i : at + 8 * i + 8])) for i in range(3)]
    at += 24
    ga_o, gt_o = refs[at : at + 3], refs[at + 3 : at + 6]
    own_o, send_o, gnf_o, emb_o, pg_o = refs[at + 6 : at + 11]
    at += 11
    big = ("mid", "a", "ge")
    bufs = [dict(zip(big, refs[at + 3 * i : at + 3 * i + 3])) for i in range(3)]
    at += 9
    own, res, gyt, part, gb, n2, gg, gu, ga, att, hid, packed, gt, wh, wd, wg, wu, wo, sems, out_sems = refs[at:]
    span, width = own.shape[1:]
    length = n * span
    ff = w_gate.shape[1]
    inner = w_out.shape[0]
    head = inner // 6
    wide = w_head.shape[1]
    me, p, c = position()
    ins = Copies(sems)
    owns = []
    for i in range(3):
        row = per * p + (per - 1 if i == 2 else 2 * c + i)
        owns.append(ins.start(grad_y.at[row], own.at[i]))
    weights = {k: ins.start(a, b) for k, a, b in (("h", w_head, wh), ("d", w_down, wd))}
    for k, a, b in (("g", w_gate, wg), ("u", w_up, wu), ("o", w_out, wo)):
        weights[k] = ins.start(a, b)
    lanes = [pl.ds(i * length, length // 2 if i == 2 else length) for i in range(3)]
    loads = []
    for i in range(3):
        loads.append([ins.start(srcs[i][k], bufs[i][k]) for k in big])
    late_loads = []
    for i in range(3):
        late_loads.append(ins.start(srcs[i]["hid"], hid.at[:, lanes[i]]))
        late_loads.append(ins.start(srcs[i]["att"], att.at[:, lanes[i]]))

    def need(*names):
        for k in names:
            if k in weights:
                weights.pop(k).wait()

    for i in range(3):
        owns[i].wait()
    need("h")
    pools, cots, counts = [], [], []
    for i in range(3):
        half = i == 2
        for k, piece in enumerate((own.at[i], near.at[i], far.at[2 * i], again.at[2 * i + (not half)])):
            place = pl.multiple_of((me ^ k) * span, span)
            gyt[i, :, pl.ds(place, span)] = piece[...].T
        count = jnp.sum((srcs[i]["seg"][0:1, :] != 0.0).astype(F32), axis=1, keepdims=True)
        pool = srcs[i]["pool"][0:1, :]
        if half:
            pool = pool + pool_other[0:1, :]
        pools.append(pool / count)
        counts.append(count)
        row = per * p + (per - 1 if half else 2 * c + i)
        cots.append(eg[pl.ds(row, 1), :])
    proj = wide_dots(pools, wh[...], mm)
    g_projs = []
    for i in range(3):
        inv = lax.rsqrt(jnp.sum(proj[i] * proj[i], axis=1, keepdims=True) + EPS)
        emb = proj[i] * inv
        g_proj = inv * (cots[i] - emb * jnp.sum(emb * cots[i], axis=1, keepdims=True))
        emb_o[i] = jnp.broadcast_to(emb, emb_o.shape[1:])
        once = jnp.where(c == 0, 1.0, 0.0) if i == 2 else 1.0
        for q in range((width + wide) // 256):
            piece = pools[i][:, q * 256 : (q + 1) * 256] if q < width // 256 else g_proj[:, q * 256 - width : (q + 1) * 256 - width]
            pg_o[5 * i + q : 5 * i + q + 1, :] = piece * once
        g_projs.append(g_proj)
    g_pools = wide_dots(g_projs, wh[...], mm_nt)
    g_cols = [jnp.broadcast_to(g / k, (span, width)).T for g, k in zip(g_pools, counts)]
    need("d", "g", "u", "o")
    for copy in loads[0]:
        copy.wait()
    sizes = [length, length, length // 2]
    starts = [0, length, 2 * length]

    def outer(i, b, r):
        if i == 2:
            place = pl.ds(pl.multiple_of((c * (sizes[2] // span) + b) * span, span), span)
        else:
            place = pl.ds(b * span, span)
        valid = (srcs[i]["seg"][0:1, place] != 0.0).astype(F32)
        return gyt[i, r, place].astype(F32) + valid * g_cols[i][r, :]

    def branch(i, b):
        for r in chunks(width):
            gb[r, starts[i] + b * span : starts[i] + (b + 1) * span] = outer(i, b, r).astype(BF16)

    step = 256

    def gates(i, b):
        cs, ls = slice(b * step, (b + 1) * step), slice(starts[i], starts[i] + sizes[i])
        g_hid = mm(wd[cs, :], gb[:, ls])
        gg[cs, ls] = (g_hid * bufs[i]["a"][cs, :].astype(F32)).astype(BF16)
        gu[cs, ls] = (g_hid * bufs[i]["ge"][cs, :].astype(F32)).astype(BF16)

    def normed(i):
        ls = slice(starts[i], starts[i] + sizes[i])
        res[i % 2, :, : sizes[i]] = mm(wg[...], gg[:, ls]) + mm(wu[...], gu[:, ls])

    def norm(i, b):
        mid, ds = bufs[i]["mid"], res.at[i % 2]
        bs = slice(b * span, (b + 1) * span)
        ls = slice(starts[i] + b * span, starts[i] + (b + 1) * span)
        sq = cross = None
        for r in chunks(width):
            m = mid[r, bs]
            t = fold(m * m, jnp.add)
            u = fold(ds[r, bs] * nffn[r, :] * m, jnp.add)
            sq, cross = (t, u) if sq is None else (sq + t, cross + u)
        inv2 = lax.rsqrt(jnp.sum(sq, axis=0, keepdims=True) / width + EPS)
        mean = inv2 * jnp.sum(cross, axis=0, keepdims=True) / width
        for r in chunks(width):
            hat = mid[r, bs] * inv2
            n2[r, ls] = (hat * nffn[r, :]).astype(BF16)
            gn = ds[r, bs]
            if i == 0 and b == 0:
                part[r, :] = gn * hat
            else:
                part[r, :] += gn * hat
            ga[r, ls] = (outer(i, b, r) + inv2 * (gn * nffn[r, :] - hat * mean)).astype(BF16)

    def attended(i):
        ls = slice(starts[i], starts[i] + sizes[i])
        gatt = mm(wo[...], ga[:, ls]).astype(BF16).astype(F32)
        for h in range(6):
            hs = slice(h * head, (h + 1) * head)
            gt[hs, ls] = (gatt[hs, :] * srcs[i]["r"][h : h + 1, :]).astype(BF16)

    def store(at, value):
        rows = value.shape[0] // 2
        for side in range(2):
            packed[side, :, at : at + value.shape[1]] = value[side * rows : (side + 1) * rows].astype(BF16)

    outs = Copies(out_sems)
    pending = []

    def send(lo, hi):
        pending.append(outs.start(packed.at[c, :, pl.ds(lo, hi - lo)], own_o.at[:, pl.ds(lo, hi - lo)]))
        pending.append(outs.start(packed.at[1 - c, :, pl.ds(lo, hi - lo)], send_o.at[:, pl.ds(lo, hi - lo)]))

    blocks = [k // span for k in sizes]
    for b in range(blocks[0]):
        branch(0, b)
    for b in range(ff // step):
        gates(0, b)
    for i in (1, 2):
        for copy in loads[i]:
            copy.wait()
    normed(0)
    for b in range(blocks[1]):
        branch(1, b)
    for b in range(ff // step):
        gates(1, b)
        norm(0, b)
    normed(1)
    attended(0)
    for b in range(blocks[2]):
        branch(2, b)
    for b in range(ff // step):
        gates(2, b)
        norm(1, b)
    normed(2)
    attended(1)
    for copy in late_loads:
        copy.wait()
    top = 2 * ff
    for b in range(2):
        store(top + b * width, mm_nt(hid[b * width : (b + 1) * width, :], gb[...]))
        norm(2, b)
    attended(2)
    for i in range(3):
        ls = pl.ds(starts[i], sizes[i])
        pending.append(outs.start(ga.at[:, ls], ga_o[i]))
        pending.append(outs.start(gt.at[:, ls], gt_o[i]))
    send(top, top + 2 * width)
    for b in range(2):
        cs = slice(b * 512, (b + 1) * 512)
        store(b * 512, mm_nt(n2[...], gg[cs, :]))
    send(0, ff)
    for b in range(2):
        cs = slice(b * 512, (b + 1) * 512)
        store(ff + b * 512, mm_nt(n2[...], gu[cs, :]))
    store(top + 2 * width, mm_nt(ga[...], att[...]))
    gnf_o[...] = jnp.broadcast_to(col_sum(part[...].T), gnf_o.shape)
    pg_o[15:16, :] = jnp.zeros((1, 256), F32)
    send(ff, 2 * ff)
    send(top + 2 * width, top + 2 * width + inner)
    for copy in pending:
        copy.wait()


def attention_back(core, n, q_nat, v_nat, kt, e_wait, e_b, att, gt, gs, table, kv_side, line, gq_o, put_kv):
    heads = e_b.shape[0]
    inner = kt.shape[0]
    head = inner // heads
    length = kt.shape[1]
    half = core is not None
    nq = length // 2 if half else length
    lane = lax.broadcasted_iota(jnp.int32, (length, LANES), 1)
    gt_nat = gt[...].T
    zeros = jnp.zeros((head, nq), BF16)
    width = 4 * LANES
    table[:, :, :LANES] = jnp.zeros((2, LANES, LANES), F32)

    def scores(h, a, rhs, delta, far, seen):
        ps = slice(h // 2 * LANES, (h // 2 + 1) * LANES)
        ks = slice(a * LANES, (a + 1) * LANES)
        g_s = e_b[h, ks, :].astype(F32) * (mm(v_nat[ks, ps], rhs) - delta)
        gs[h % 2, ks, :nq] = g_s.astype(BF16)
        t = table.at[h % 2]
        for b in range(nq // LANES):
            blk = g_s[:, b * LANES : (b + 1) * LANES]
            d = (2 * core if half else 0) + b - a
            if abs(d) <= 1:
                at = (d + 2) * LANES
                if d in seen:
                    t[:, at : at + LANES] += blk
                else:
                    t[:, at : at + LANES] = blk
                    seen.add(d)
            else:
                far[d < 0].append(fold(blk, jnp.add))

    def lines(h, far):
        t = table.at[h % 2]
        line(h, slice(LANES, LANES + width), diagonal_sums(t))
        if far[0]:
            line(h, slice(6 * LANES, 7 * LANES), jnp.sum(sum(far[0]), axis=0, keepdims=True))
        if far[1]:
            line(h, slice(0, LANES), jnp.sum(sum(far[1]), axis=0, keepdims=True))

    def weigh(h, which):
        hs, ps = slice(h * head, (h + 1) * head), slice(h // 2 * LANES, (h // 2 + 1) * LANES)
        g = gs.at[h % 2]
        if which == 0:
            gq_o[hs, :] = mm(kt[hs, :], g[:, :nq]).astype(BF16)
            return
        value = mm(g[:, :nq], q_nat[:, ps]) if which == 1 else mm(e_b[h], gt_nat[:, ps])
        if h % 2 == 0:
            kv_side[which - 1] = value
        else:
            put_kv(h // 2, which - 1, jnp.where(lane < head, kv_side[which - 1], value).astype(BF16).T)

    old = None
    for h in range(heads + 1):
        far = [[], []]
        if h < heads:
            if h % 2 == 0:
                e_wait(h // 2)
            hs = slice(h * head, (h + 1) * head)
            g_h = gt[hs, :]
            delta = col_sum(g_h.astype(F32) * att[hs, :].astype(F32))
            rhs = jnp.concatenate([g_h, zeros] if h % 2 == 0 else [zeros, g_h], axis=0)
            seen = set()
        for a in range(n):
            if h < heads:
                scores(h, a, rhs, delta, far, seen)
            if h > 0:
                if a < 3:
                    weigh(h - 1, a)
                else:
                    lines(h - 1, old)
        old = far


def half_back_kernel(n, q_nat, v_nat, kt, e_in, att, gt, gq_o, keep_o, send_o, line_o, e_b, gs, table, kv_side, kv, sems):
    ins = Copies(sems)
    loads = [ins.start(e_in.at[pl.ds(0, 2)], e_b.at[pl.ds(0, 2)])]
    yield
    loads += [ins.start(e_in.at[pl.ds(h, 2)], e_b.at[pl.ds(h, 2)]) for h in range(2, e_in.shape[0], 2)]
    inner = kt.shape[0]

    def put(pair, which, value):
        kv[which * inner + pair * LANES : which * inner + (pair + 1) * LANES, :] = value.astype(BF16)

    def line(h, lanes, value):
        line_o[h : h + 1, lanes] = value

    line_o[...] = jnp.zeros_like(line_o)
    _, _, c = position()
    for core in range(2):

        @pl.when(c == core)
        def _(core=core):
            attention_back(
                core, n, q_nat, v_nat, kt, lambda p: loads[p].wait(), e_b, att, gt, gs, table, kv_side, line, gq_o, put
            )

    nq = kt.shape[1] // 2
    keep_o[...] = kv[:, pl.ds(pl.multiple_of(c * nq, nq), nq)]
    send_o[...] = kv[:, pl.ds(pl.multiple_of((1 - c) * nq, nq), nq)]


def backward_kernel(
    slot, n,
    q_nat, v_nat, kt, e_in, att, gt, line_in, xt, ga, w_query, w_key, w_value, nattn, emb, part_in, *refs,
):
    if slot:
        gq0, gq_half, keep, got, n1_0, n1_1, n1_2, own_o, send_o, gq2, *refs = refs
        *refs, m0, m1, m2, g0, packed = refs
    line_o, gq_o, b_own, b_c, b_y, part_o, gq, e_b, gs, table, kv_side, res, xb, gb, wb, part, sems = refs
    ins = Copies(sems)
    loads = [ins.start(e_in.at[pl.ds(0, 2)], e_b.at[pl.ds(0, 2)])]
    yield
    loads += [ins.start(e_in.at[pl.ds(h, 2)], e_b.at[pl.ds(h, 2)]) for h in range(2, e_in.shape[0], 2)]
    more = [ins.start(a, b) for a, b in ((xt, xb), (ga, gb))]
    more += [ins.start(w, wb.at[:, pl.ds(i * w.shape[1], w.shape[1])]) for i, w in enumerate((w_query, w_key, w_value))]
    if slot:
        more += [ins.start(a, b) for a, b in ((gq0, g0), (n1_0, m0), (n1_1, m1), (n1_2, m2))]
    inner = kt.shape[0]

    def put(pair, which, value):
        at = (1 + which) * inner + pair * LANES
        gq[at : at + LANES, :] = value.astype(BF16)

    def line(h, lanes, value):
        line_o[h : h + 1, lanes] = line_in[h : h + 1, lanes] + value

    line_o[...] = line_in[...]
    if slot:
        gq2[:inner, :] = gq_half[...]
        gq2[inner:, :] = (keep[...].astype(F32) + got[...].astype(F32)).astype(BF16)
    attention_back(
        None, n, q_nat, v_nat, kt, lambda p: loads[p].wait(), e_b, att, gt, gs, table, kv_side, line, gq.at[:inner, :], put
    )
    for copy in more:
        copy.wait()
    if slot:
        part[...] = part_in[...]
        _, _, c = position()
    span = b_own.shape[1] - EXT

    def late_sums(b):
        lo, hi = b * 256, (b + 1) * 256 if b < 3 else 3 * inner
        cs = slice(lo, hi)
        value = mm_nt(m0[...], g0[cs, :]) + mm_nt(m1[...], gq[cs, :]) + mm_nt(m2[...], gq2[cs, :])
        rows = own_o.shape[0]
        for side in range(2):
            packed[side, :, cs] = value[side * rows : (side + 1) * rows].astype(BF16)

    input_rows(
        slot, False, gq, xb, gb, wb, nattn, emb, res, part, (b_own.at[0], b_c.at[0], b_y.at[0], b_y.at[1]), span,
        late_sums if slot else None,
    )
    part_o[...] = part[...]
    outs = [ins.start(gq, gq_o)]
    if slot:
        outs += [ins.start(packed.at[c], own_o), ins.start(packed.at[1 - c], send_o)]
    for copy in outs:
        copy.wait()


def input_rows(slot, half, gq, xt, ga, w_qkv, nattn, emb, res, part, outs, span, between=None):
    width, nq = res.shape[0], gq.shape[1]
    res[:, :nq] = mm(w_qkv[...], gq[...])
    for b in range(nq // span):
        bs = slice(b * span, (b + 1) * span)
        sq = cross = None
        for r in chunks(width):
            x = xt[r, bs].astype(F32)
            t = fold(x * x, jnp.add)
            u = fold(res[r, bs] * nattn[r, :] * x, jnp.add)
            sq, cross = (t, u) if sq is None else (sq + t, cross + u)
        inv = lax.rsqrt(jnp.sum(sq, axis=0, keepdims=True) / width + EPS)
        mean = inv * jnp.sum(cross, axis=0, keepdims=True) / width
        for r in chunks(width):
            hat = xt[r, bs].astype(F32) * inv
            gn = res[r, bs]
            if slot == 0 and b == 0:
                part[r, :] = gn * hat
            else:
                part[r, :] += gn * hat
            res[r, bs] = ga[r, bs].astype(F32) + inv * (gn * nattn[r, :] - hat * mean)
        if between is not None:
            between(b)
    send_blocks(half, res, outs, span)
    row = emb[slot, 0:1, :]
    high = row.astype(BF16)
    low = (row - high.astype(F32)).astype(BF16)
    rest = row.shape[1] - width
    for out in outs:
        for at, v in ((0, high), (2, low)):
            out[span + at : span + at + 1, :] = v[:, :width]
            out[span + at + 1 : span + at + 2, :rest] = v[:, width:]


def inputs_kernel(
    gq, xt, ga, w_query, w_key, w_value, nattn, emb, part_in, line_in, gnf, indicator,
    b_own, b_c, b_y, small,
    res, part, w_qkv,
):
    small[...] = jnp.zeros_like(small)
    part[...] = part_in[...]
    for i, w in enumerate((w_query, w_key, w_value)):
        w_qkv[:, i * w.shape[1] : (i + 1) * w.shape[1]] = w[...]
    width = res.shape[0]
    span = b_own.shape[1] - EXT
    input_rows(2, True, gq, xt, ga, w_qkv, nattn, emb, res, part, (b_own.at[0], b_c.at[0], b_y.at[0], b_y.at[1]), span)
    gna = col_sum(part[...].T)
    for i in range(width // LANES):
        small[i : i + 1, :] = gnf[0:1, i * LANES : (i + 1) * LANES]
        small[4 + i : 5 + i, :] = gna[:, i * LANES : (i + 1) * LANES]
    lines = line_in[...]
    hi = lines.astype(BF16)
    lo = (lines - hi.astype(F32)).astype(BF16)
    small[8:16, :] = mm_nt(hi, indicator[...]) + mm_nt(lo, indicator[...])


def unpack_kernel(per, with_emb, *refs):
    groups = (len(refs) - 1 - (3 if with_emb else 1)) // 4
    out = refs[4 * groups]
    sems = refs[-1]
    ways = []
    for g in range(groups):
        own, c1, y, d = refs[4 * g : 4 * g + 4]
        ways += [(own.at[i], c1.at[i], y.at[2 * i], d.at[2 * i + 1]) for i in range(own.shape[0])]
    own0 = ways[0][0]
    me, p, _ = position()
    rows, span, width = out.shape
    for r in range(rows):
        pair, j = divmod(r, per)
        slot = 2 if j == per - 1 else j % 2
        core = p if slot == 2 else j // 2
        k = me ^ (pair * 2 + core)
        for which in range(4):
            ref = ways[slot][which]

            @pl.when(k == which)
            def _(ref=ref, r=r):
                pltpu.make_async_copy(ref.at[pl.ds(0, span)], out.at[r], sems.at[r]).start()
                if with_emb:
                    pltpu.make_async_copy(ref.at[pl.ds(span, EXT)], refs[4 * groups + 2].at[r], sems.at[rows + r]).start()

    if with_emb:
        emb, got = refs[4 * groups + 1 : 4 * groups + 3]
        for r in range(rows):
            pltpu.make_async_copy(own0.at[pl.ds(span, EXT)], got.at[r], sems.at[rows + r]).wait()
            value = got[r].astype(F32)
            emb[r : r + 1, :width] = value[0:1, :] + value[2:3, :]
            emb[r : r + 1, width:] = (value[1:2, :] + value[3:4, :])[:, : emb.shape[1] - width]
    for r in range(rows):
        pltpu.make_async_copy(own0.at[pl.ds(0, span)], out.at[r], sems.at[r]).wait()


def place(step):
    if step is None:
        return 0, 1
    axis, stride, radix = step
    return (lax.axis_index(axis) // stride) % radix, radix


def combine_kernel(plan, *refs):
    at = sum(len(arrays) for pieces, _ in plan for arrays, _, _ in pieces)
    outs = at + sum(place(step)[1] for _, step in plan)
    ins, at, scratch = 0, at, outs
    for pieces, step in plan:
        off = 0
        total = refs[scratch] if step else refs[at]
        for arrays, lo, hi in pieces:
            value = sum(refs[ins + i][..., lo:hi].astype(F32) for i in range(len(arrays)))
            ins += len(arrays)
            total[..., off : off + hi - lo] = value.astype(BF16)
            off += hi - lo
        if step:
            d, radix = place(step)
            for k in range(radix):
                refs[at + k][...] = total[d ^ k]
            at += radix
            scratch += 1
        else:
            at += 1


def join_kernel(plan, *refs):
    ins, at = 0, sum(place(step)[1] for step, _ in plan)
    for step, cuts in plan:
        d, radix = place(step)
        for lo, hi in cuts:
            for k in range(radix):
                refs[at][d ^ k] = refs[ins + k][:, lo:hi]
            at += 1
        ins += radix


def merge_kernel(step, cut, late_cut, own, got, late, late_got, a_o, b_o):
    d, _ = place(step)
    total = (late[...].astype(F32) + late_got[...].astype(F32)).astype(BF16)
    rows, wide = own.shape
    for src, at in ((own, d), (got, d ^ 1)):
        a_o[at, :, :cut] = src[:, :cut]
        b_o[at, :, : wide - cut] = src[:, cut:]
    for side in range(2):
        part = total[side * rows : (side + 1) * rows]
        a_o[side, :, cut:] = part[:, :late_cut]
        b_o[side, :, wide - cut :] = part[:, late_cut:]


FINISH_OUTS = 7


def finish_kernel(second, cut, block, *refs):
    if second:
        b_own, a, b, *rest = refs
        outs, rest = rest[FINISH_OUTS : 2 * FINISH_OUTS], rest[2 * FINISH_OUTS :]
        head_o, nf_o, na_o, table_o, gate, up, down, out, qkv, head, sems = rest
    else:
        a, b, *rest = refs
        outs, (gate, up, down, out, qkv, sems) = rest[:FINISH_OUTS], rest[FINISH_OUTS:]
    gate_o, up_o, down_o, out_o, *qkv_o = outs
    _, _, c = position()
    rows = a.shape[0]
    ff = gate.shape[1]
    width = gate_o.shape[0]
    inner = out.shape[0]
    rest = ff - (cut - ff)
    start = pl.multiple_of(((1 - c) if second else c) * rows, rows)
    at = pl.ds(start, rows)
    copies = Copies(sems)
    gate[...] = a[:, :ff].astype(F32)
    pending = [copies.start(gate, gate_o.at[at])]
    down[0] = b[:, rest : rest + width].astype(F32)
    pending.append(copies.start(down.at[0], down_o.at[at]))
    down[1] = b[:, rest + width : rest + 2 * width].astype(F32)
    pending.append(copies.start(down.at[1], down_o.at[pl.ds(pl.multiple_of(width + start, rows), rows)]))
    up[:, : cut - ff] = a[:, ff:cut].astype(F32)
    up[:, cut - ff :] = b[:, :rest].astype(F32)
    pending.append(copies.start(up, up_o.at[at]))
    late_a = a.shape[1] - cut
    late_b = b.shape[1] - LANES - (3 * inner - late_a)
    for i in range(3):
        lo, hi = i * inner, (i + 1) * inner
        mid = min(max(late_a, lo), hi)
        if mid > lo:
            qkv[i, :, : mid - lo] = a[:, cut + lo : cut + mid].astype(F32)
        if mid < hi:
            qkv[i, :, mid - lo :] = b[:, late_b + mid - late_a : late_b + hi - late_a].astype(F32)
        pending.append(copies.start(qkv.at[i], qkv_o[i].at[at]))
    out[...] = b[:, rest + 2 * width : rest + 2 * width + inner].astype(F32).T
    pending.append(copies.start(out, out_o.at[:, at]))
    if second:
        row = lax.broadcasted_iota(jnp.int32, (rows, 256), 0) % 16
        small = None
        for ref in (b_own, b):
            g = ref[:, late_b - 256 : late_b].astype(F32)
            turned = {t: pltpu.roll(g, rows - t, 0).astype(BF16) for t in range(1, 5)}
            for i in range(2):
                kept = jnp.where((row < 15) & (row % 5 == i), g, 0.0).T.astype(BF16)
                for j in range(3):
                    term = mm(kept, turned[2 + j - i])
                    place_ = (slice(i * 256, (i + 1) * 256), slice(j * 256, (j + 1) * 256))
                    if ref is b_own:
                        head[place_] = term
                    else:
                        head[place_] += term
            for r in range(0, rows, block):
                value = ref[r : r + 16, ref.shape[1] - LANES :].astype(F32)
                small = value if small is None else small + value
        pending.append(copies.start(head, head_o))
        for i in range(nf_o.shape[1] // LANES):
            nf_o[:, i * LANES : (i + 1) * LANES] = small[i : i + 1, :]
            na_o[:, i * LANES : (i + 1) * LANES] = small[4 + i : 5 + i, :]
        table_o[...] = small[8 : 8 + table_o.shape[0], : table_o.shape[1]]
    for copy in pending:
        copy.wait()


def sds(shape, dtype=BF16):
    return jax.ShapeDtypeStruct(shape, dtype)


def call(
    kernel, outs, args, scratch=(), specs=None, out_specs=None, flops=0, name=None, vmem=56, deps=(), aliases=None, overlap=False
):
    count, n_out = len(args), len(outs) if isinstance(outs, tuple) else 1
    specs = list(specs or [VMEM] * count)
    out_specs = list(out_specs or [VMEM] * n_out)
    out_list = list(outs) if isinstance(outs, tuple) else [outs]
    loads = [i for i in range(count) if overlap and specs[i] is VMEM]
    stores = [i for i in range(n_out) if overlap and out_specs[i] is VMEM]
    bufs = [pltpu.VMEM(args[i].shape, args[i].dtype) for i in loads] + [pltpu.VMEM(out_list[i].shape, out_list[i].dtype) for i in stores]
    if overlap:
        bufs.append(pltpu.SemaphoreType.DMA((len(loads) + len(stores),)))

    def body(*refs):
        ins, refs = list(refs[:count]), refs[count + len(deps) :]
        res, refs = list(refs[:n_out]), refs[n_out:]
        if overlap:
            bufs_, refs = refs[: len(bufs)], refs[len(bufs) :]
            copies = Copies(bufs_[-1])
            pending = []
            for i, buf in zip(loads, bufs_):
                pending.append(copies.start(ins[i], buf))
                ins[i] = buf
            out_refs = list(res)
            for i, buf in zip(stores, bufs_[len(loads) :]):
                res[i] = buf
            run = kernel(*ins, *res, *refs)
            if run is not None:
                next(run)
            for copy in pending:
                copy.wait()
            if run is not None:
                next(run, None)
        else:
            kernel(*ins, *res, *refs)
        if overlap:
            pending = [copies.start(res[i], out_refs[i]) for i in stores]
            for copy in pending:
                copy.wait()

    if overlap:
        specs = [ANY if s is VMEM else s for s in specs]
        out_specs = [ANY if s is VMEM else s for s in out_specs]
    return pl.pallas_call(
        body,
        out_shape=outs,
        in_specs=specs + [ANY] * len(deps),
        out_specs=tuple(out_specs) if isinstance(outs, tuple) else out_specs[0],
        scratch_shapes=bufs + list(scratch),
        compiler_params=pltpu.CompilerParams(vmem_limit_bytes=vmem * 2**20),
        cost_estimate=pl.CostEstimate(flops=flops, bytes_accessed=10_000_000, transcendentals=0),
        input_output_aliases=aliases or {},
        name=name,
    )(*args, *deps)


def swap(x, axis, k):
    n = lax.axis_size(axis)
    return lax.ppermute(x, axis, [(i, i ^ k) for i in range(n)])


def after(x, *deps):
    return lax.optimization_barrier((x, *deps))[0]


def together(*trees):
    leaves, shape = jax.tree.flatten(trees)
    return jax.tree.unflatten(shape, lax.optimization_barrier(leaves))


def row_digits():
    return [("rows", 1 << i, 2) for i in range(lax.axis_size("rows").bit_length() - 1)]


def shards(
    tokens, seg_ids, w_query, w_key, w_value, w_out, w_gate, w_up, w_down, w_head, norm_attn, norm_ffn,
    bucket_bias_table, grad_y, embedding_gradient,
):
    rows, span, width = tokens.shape
    buckets, heads = bucket_bias_table.shape
    n = lax.axis_size("seq")
    inner = w_query.shape[1]
    ff = w_gate.shape[1]
    wide = w_head.shape[1]
    length = n * span
    per = rows // 2
    assert n == 4 and per == 5
    slots = 3

    groups = ((0,), (1, 2))
    shapes = [(k, span + EXT, width) for slots in groups for k in (2 * len(slots) - (2 in slots), len(slots))]
    todo = sum(k for k, _, _ in shapes)
    y_a, c_a, y_b, c_b = call(
        functools.partial(pack_kernel, per, groups, EXT), tuple(sds(k) for k in shapes), (tokens, seg_ids),
        [pltpu.VMEM((todo, span + EXT, width), BF16), pltpu.SemaphoreType.DMA((2 * todo,))], [ANY, VMEM], (ANY,) * 4,
        vmem=60, name="pack", overlap=True,
    )

    def pass_on(got, *deps):
        near, far = got
        return near, far, swap(after(far, *deps) if deps else far, "seq", 1)

    line = 2 * length
    x_a = swap(c_a, "seq", 1), swap(y_a, "seq", 2)
    bias, ind, nattn, nffn, wqkv_t, wout_t, wg_t, wu_t, wd_t = call(
        functools.partial(prepare_kernel, n),
        (
            sds((heads, LANES, line), F32), sds((LANES, line)), sds((width, LANES), F32), sds((width, LANES), F32),
            sds((3 * inner, width)), sds((width, inner)), sds((ff, width)), sds((ff, width)),
            sds((width, ff)),
        ),
        (
            bucket_bias_table.T, norm_attn[None], norm_ffn[None], w_query, w_key, w_value, w_out, w_gate, w_up, w_down,
        ),
        [pltpu.VMEM((LANES, LANES), F32)], name="prepare", flops=4_000_000_000, overlap=True,
    )
    x_a, y_b, c_b, nattn = together(x_a, y_b, c_b, nattn)
    x_b = swap(c_b, "seq", 1), swap(y_b, "seq", 2)
    x_a = pass_on(x_a)

    def collect(own, c, y):
        return own, swap(c, "seq", 1), swap(y, "seq", 2)

    def collect_rest(part, *deps):
        return *part, swap(after(part[2], *deps), "seq", 1)

    def run_forward(kinds, pieces, before=(), deps=()):
        shapes = [s for _, half in kinds for s in forward_outs(half, n, span, width, inner, heads, ff)]
        had = len(before) and before[0].shape[0]
        shapes += [((k * (len(kinds) + had), span, width), BF16) for k in (1, 1, 2)]
        if not had:
            shapes += [((2 * slots - 1, span, width), BF16), ((slots, span, width), BF16)]
        outs = tuple(sds(*s) for s in shapes)
        args = [tokens, seg_ids, bias, wqkv_t, wout_t, wg_t, wu_t, wd_t, nattn, nffn]
        specs = [ANY, VMEM] + [ANY] * 6 + [VMEM] * 2
        args += [*pieces, *(before or (grad_y,))]
        specs += [VMEM] * 3 + [ANY] * (3 if had else 1)
        scratch = [pltpu.VMEM(*s) for s in shapes]
        scratch += [
            pltpu.VMEM((len(kinds), span, width), BF16), pltpu.VMEM((length, width), F32), pltpu.VMEM((LANES, length), F32),
            pltpu.VMEM((width, length), BF16), pltpu.VMEM((heads, length, 2 * LANES), BF16),
            pltpu.VMEM((heads, inner // heads + EXT, length), BF16), pltpu.VMEM((width, length), BF16),
            pltpu.VMEM((2, length, length), F32), pltpu.VMEM(bias.shape, F32), *[pltpu.VMEM(w.shape, BF16) for w in (wqkv_t, wout_t, wg_t, wu_t, wd_t)],
            pltpu.SemaphoreType.DMA((12 + len(kinds) + 3 * slots,)), pltpu.SemaphoreType.DMA((24 * len(kinds) + 6,)),
        ]
        res = call(
            functools.partial(forward_kernel, kinds, n, per, heads), outs, args, scratch, specs, tuple(ANY for _ in outs),
            4_000_000_000 * len(kinds), "forward", deps=deps, overlap=True,
        )
        count = len(FORWARD_OUTS)
        at = count * len(kinds)
        rows_ = [dict(zip(FORWARD_OUTS, res[i * count : (i + 1) * count])) for i in range(len(kinds))]
        return rows_, res[at : at + 3], res[at + 3 :]

    fwd, blocks, packed_g = run_forward([(0, False)], x_a, deps=(y_b, c_b))
    x_b = pass_on(x_b, fwd[0]["r"])
    gys = swap(packed_g[1], "seq", 1), swap(packed_g[0], "seq", 2)
    fwd_b, blocks, _ = run_forward([(1, False), (2, True)], x_b, blocks, deps=packed_g)
    blocks = collect(*blocks)
    fwd += fwd_b
    gys = pass_on(gys, fwd[1]["r"])
    pool_other = swap(fwd[2]["pool"], "seq", 1)

    def unpack(parts, with_emb, deps=()):
        args = [a for group in parts for a in group]
        outs = (sds((rows, span, width)),) + ((sds((rows, wide), F32),) if with_emb else ())
        scratch = [pltpu.VMEM((rows, EXT, width), BF16)] if with_emb else []
        return call(
            functools.partial(unpack_kernel, per, with_emb), outs, args, scratch + [pltpu.SemaphoreType.DMA((2 * rows,))],
            [ANY] * len(args), (ANY, VMEM)[: len(outs)], vmem=16, name="unpack", deps=deps,
        )


    packed_w = 2 * ff + 2 * width + inner
    nqs = [length, length, length // 2]
    args = [grad_y, embedding_gradient, w_head, w_down, w_gate, w_up, w_out, nffn, pool_other]
    specs = [ANY, VMEM] + [ANY] * 5 + [VMEM] * 2
    args += list(gys)
    specs += [VMEM] * 3
    for f in fwd:
        args += [f[k] for k in ("mid", "a", "ge", "hid", "att", "seg", "r", "pool")]
        specs += [ANY] * 5 + [VMEM] * 3
    outs = tuple(
        [sds((width, q)) for q in nqs] + [sds((inner, q)) for q in nqs]
        + [sds((width // 2, packed_w))] * 2 + [sds((8, width), F32), sds((3, 8, wide), F32), sds((16, 256), F32)]
    )
    scratch = []
    for q in nqs:
        scratch += [pltpu.VMEM((width, q), F32), pltpu.VMEM((ff, q), BF16), pltpu.VMEM((ff, q), BF16)]
    total = sum(nqs)
    scratch += [
        pltpu.VMEM((3, span, width), BF16), pltpu.VMEM((2, width, length), F32), pltpu.VMEM((3, width, length), BF16),
        pltpu.VMEM((width, LANES), F32), pltpu.VMEM((width, total), BF16), pltpu.VMEM((width, total), BF16),
        pltpu.VMEM((ff, total), BF16), pltpu.VMEM((ff, total), BF16), pltpu.VMEM((width, total), BF16),
        pltpu.VMEM((inner, total), BF16), pltpu.VMEM((ff, total), BF16), pltpu.VMEM((2, width // 2, packed_w), BF16), pltpu.VMEM((inner, total), BF16),
        *[pltpu.VMEM(w.shape, BF16) for w in (w_head, w_down, w_gate, w_up, w_out)],
        pltpu.SemaphoreType.DMA((23,)), pltpu.SemaphoreType.DMA((14,)),
    ]
    m = call(functools.partial(middle_kernel, n, per), outs, args, scratch, specs, [ANY] * 8 + [VMEM] * 3, flops=15_000_000_000, name="middle", overlap=True)
    m, blocks = together(m, blocks)
    ga, gt = m[:3], m[3:6]
    own, send, gnf, emb, pg = m[6:]

    core = ("seq", 1, 2)
    far = ("seq", 2, 2)
    digits = row_digits()
    block = width // 2 // far[2]
    for d in digits:
        block //= d[2]

    def send_shares(parts, s):
        return [swap(p, s[0], k * s[1]) for k, p in enumerate(parts) if k]

    def send_all(v, s):
        return [swap(v, s[0], k * s[1]) for k in range(1, s[2])]

    def combine(groups, deps=()):
        args, outs, scratch, plan = [], [], [], []
        for pieces, step in groups:
            rows_, wide_ = pieces[0][0][0].shape[0], sum(hi - lo for _, lo, hi in pieces)
            radix = step[2] if step else 1
            shape = (radix, rows_ // radix) if step else (rows_,)
            for arrays, _, _ in pieces:
                args += [a.reshape(shape + a.shape[-1:]) for a in arrays]
            outs += [sds((rows_ // radix, wide_))] * radix
            scratch += [pltpu.VMEM(shape + (wide_,), BF16)] if step else []
            plan.append((pieces, step))
        plan = [([(range(len(a)), lo, hi) for a, lo, hi in pieces], step) for pieces, step in plan]
        res = call(functools.partial(combine_kernel, plan), tuple(outs), args, scratch, vmem=24, name="combine", deps=deps)
        out = []
        for _, step in plan:
            radix = step[2] if step else 1
            out.append(list(res[:radix]))
            res = res[radix:]
        return out

    def joined(groups, deps=()):
        args, outs, plan = [], [], []
        for v, got, step, cuts in groups:
            cuts = cuts or [(0, v.shape[1])]
            args += [v] + got
            outs += [sds((step[2], v.shape[0], hi - lo)) for lo, hi in cuts]
            plan.append((step, cuts))
        res = call(functools.partial(join_kernel, plan), tuple(outs), args, vmem=24, name="join", deps=deps)
        return [r.reshape(-1, r.shape[-1]) for r in res]

    def all_of(*arrays):
        return [(list(arrays), 0, arrays[0].shape[1])]

    nh = length // 2
    half = call(
        functools.partial(half_back_kernel, n),
        (sds((inner, nh)), sds((2 * inner, nh)), sds((2 * inner, nh)), sds((8, line), F32)),
        (fwd[2]["q"], fwd[2]["v"], fwd[2]["kt"], fwd[2]["e"], fwd[2]["att"], gt[2]),
        [
            pltpu.VMEM((heads, length, nh), BF16), pltpu.VMEM((2, length, nh), BF16), pltpu.VMEM((2, LANES, 4 * LANES), F32),
            pltpu.VMEM((2, length, LANES), F32), pltpu.VMEM((2 * inner, length), BF16), pltpu.SemaphoreType.DMA((heads,)),
        ],
        [VMEM] * 3 + [ANY] + [VMEM] * 2, flops=2_000_000_000, name="half_back", deps=(send,), overlap=True,
    )
    got = swap(send, "seq", 1)
    block_parts = [collect_rest(blocks)]
    half, got, block_parts = together(half, got, block_parts)
    gq_half, keep, send_kv, lines_sum = half
    got_kv = swap(send_kv, "seq", 1)
    cut = packed_w // 2 // LANES * LANES
    sa, sb = [digits[0], far], [far, digits[0]]
    pa, pb = combine([([([own, got], 0, cut)], sa[0]), ([([own, got], cut, packed_w)], sb[0])])

    piece = tuple(sds((i, span + EXT, width)) for i in (1, 1, 2))

    def run_back(j, lines_sum, part, deps, extra=()):
        f = fwd[j]
        scratch = [
            pltpu.VMEM((3 * inner, length), BF16), pltpu.VMEM((heads, length, length), BF16),
            pltpu.VMEM((2, length, length), BF16), pltpu.VMEM((2, LANES, 4 * LANES), F32), pltpu.VMEM((2, length, LANES), F32), pltpu.VMEM((width, length), F32),
            pltpu.VMEM((width, length), BF16), pltpu.VMEM((width, length), BF16), pltpu.VMEM((width, 3 * inner), BF16),
            pltpu.VMEM((width, LANES), F32), pltpu.SemaphoreType.DMA((heads // 2 + 14,)),
        ]
        late_outs = ()
        if extra:
            late_outs = (sds((width // 2, 3 * inner)), sds((width // 2, 3 * inner)), sds((3 * inner, nh)))
            scratch += [pltpu.VMEM((width, q), BF16) for q in nqs]
            scratch += [pltpu.VMEM((3 * inner, length), BF16), pltpu.VMEM((2, width // 2, 3 * inner), BF16)]
        res = call(
            functools.partial(backward_kernel, j, n),
            (*late_outs, sds((8, line), F32), sds((3 * inner, length)), *piece, sds((width, LANES), F32)),
            (f["q"], f["v"], f["kt"], f["e"], f["att"], gt[j], lines_sum, f["x"], ga[j], w_query, w_key, w_value, nattn, emb, part, *extra),
            scratch, [VMEM] * 3 + [ANY] + [VMEM] * 3 + [ANY] * 5 + [VMEM] * 3 + ([ANY] + [VMEM] * 3 + [ANY] * 3 if extra else []),
            ([ANY] * 2 + [VMEM] if extra else []) + [VMEM, ANY] + [VMEM] * 4, flops=4_000_000_000, name="backward", deps=deps, overlap=True,
        )
        late, (line_o, gq, *blocks, part) = res[: len(late_outs)], res[len(late_outs) :]
        return line_o, gq, blocks, part, late

    back = run_back(0, lines_sum, nattn, (pa[1], pb[1]))
    ra, rb = send_shares(pa, sa[0]), send_shares(pb, sb[0])
    back, ra, rb, got_kv = together(back, ra, rb, got_kv)
    pa, pb = combine([(all_of(pa[0], *ra), sa[1]), (all_of(pb[0], *rb), sb[1])])
    back2 = run_back(
        1, back[0], back[3], (pa[1], pb[1]), (back[1], gq_half, keep, got_kv, *[f["n1"] for f in fwd])
    )
    x_a = collect(*back[2])
    ra, rb = send_shares(pa, sa[1]), send_shares(pb, sb[1])
    back2, ra, rb, x_a = together(back2, ra, rb, x_a)
    late_own, late_send, gq2 = back2[4]

    late_got = swap(late_send, "seq", 1)
    x_a = collect_rest(x_a)
    (parts,) = combine([(all_of(pa[0], *ra) + all_of(pb[0], *rb), digits[1])])
    z_got = send_shares(parts, digits[1])
    late_got, x_a = together(late_got, x_a)
    x_b = collect(*back2[2])
    late_cut = 2 * inner
    la, lb = combine([([([late_own, late_got], 0, late_cut)], sa[0]), ([([late_own, late_got], late_cut, 3 * inner)], sb[0])])
    lga, lgb = send_shares(la, sa[0]), send_shares(lb, sb[0])
    late_sends = (la[1], lb[1])
    for step in digits[2:]:
        (parts,) = combine([(all_of(parts[0], *z_got), step)], deps=late_sends)
        z_got = send_shares(parts, step)
        late_sends = ()
    lga, lgb = together(lga, lgb)
    la, lb = combine([(all_of(la[0], *lga), sa[1]), (all_of(lb[0], *lgb), sb[1])])
    lga, lgb = send_shares(la, sa[1]), send_shares(lb, sb[1])
    *x_c, small = call(
        inputs_kernel, (*piece, sds((width // 8, LANES), F32)),
        (gq2, fwd[2]["x"], ga[2], w_query, w_key, w_value, nattn, emb, back2[3], back2[0], gnf, ind),
        [pltpu.VMEM((width, nh), F32), pltpu.VMEM((width, LANES), F32), pltpu.VMEM((width, 3 * inner), BF16)],
        flops=3_000_000_000, name="inputs", vmem=16,
        deps=tuple(parts[1:]) + (la[1], lb[1]),
    )
    pg_b = pg.astype(BF16).reshape(block, -1)
    ((ab,),) = combine([(all_of(parts[0], *z_got) + all_of(pg_b), None)], deps=(la[1], lb[1]))
    ab_got = send_all(ab, digits[-1])
    lga, lgb, x_c, small, x_b = together(lga, lgb, x_c, small, x_b)
    x_c = collect(*x_c)
    ((late,),) = combine([(all_of(la[0], *lga) + all_of(lb[0], *lgb) + all_of(small), None)], deps=(ab,))
    strides = digits[1:]
    for step, back_step in zip(strides[:-1], strides[:0:-1]):
        late_got = swap(late, *step[:2])
        x_b = collect_rest(x_b) if len(x_b) == 3 else x_b
        ((late,),) = combine([(all_of(late, late_got), None)])
        (ab,) = joined([(ab, ab_got, back_step, None)], deps=(late,))
        ab_got = send_all(ab, digits[digits.index(back_step) - 1])
    late_got = swap(late, *strides[-1][:2])
    (block_out,) = unpack(block_parts, False, deps=(late,))
    late_got, ab_got, block_out, x_b, x_c = together(late_got, ab_got, block_out, x_b, x_c)
    wide_a, wide_b = cut + late_cut, ab.shape[1] - cut + late.shape[1] - late_cut
    a, b = call(
        functools.partial(merge_kernel, digits[1], cut, late_cut),
        (sds((2, ab.shape[0], wide_a)), sds((2, ab.shape[0], wide_b))), (ab, *ab_got, late, late_got), vmem=24, name="merge",
    )
    a, b = a.reshape(-1, wide_a), b.reshape(-1, wide_b)
    ga_, gb_ = send_all(a, sa[1]), send_all(b, sb[1])
    x_c = collect_rest(x_c)
    ga_, gb_, x_c = together(ga_, gb_, x_c)
    a, b = joined([(a, ga_, sa[1], None), (b, gb_, sb[1], None)])
    ga_, gb_ = send_all(a, sa[0]), send_all(b, sb[0])
    grad_x, embedding = unpack([x_a, x_b, x_c], True, deps=(a, b))
    ga_, gb_, grad_x = together(ga_, gb_, grad_x)
    a, b = joined([(a, ga_, sa[0], None), (b, gb_, sb[0], None)])
    a_got, b_got = swap(a, "seq", 1), swap(b, "seq", 1)
    outs = (
        sds((width, ff), F32), sds((width, ff), F32), sds((ff, width), F32), sds((inner, width), F32),
        *[sds((width, inner), F32)] * 3,
    )
    halves = [
        pltpu.VMEM((width // 2, ff), F32), pltpu.VMEM((width // 2, ff), F32), pltpu.VMEM((2, width // 2, width), F32),
        pltpu.VMEM((inner, width // 2), F32), pltpu.VMEM((3, width // 2, inner), F32),
    ]
    first = call(
        functools.partial(finish_kernel, False, cut, width // 8), outs, (a, b), halves + [pltpu.SemaphoreType.DMA((9,))],
        out_specs=(ANY,) * FINISH_OUTS, name="finish", vmem=24,
    )
    first, a_got, b_got = together(first, a_got, b_got)
    *grads, grad_head, grad_norm_ffn, grad_norm_attn, grad_table = call(
        functools.partial(finish_kernel, True, cut, width // 8),
        outs + (sds((width, wide), F32), sds((1, width), F32), sds((1, width), F32), sds((heads, buckets), F32)),
        (b, a_got, b_got, *first), halves + [pltpu.VMEM((width, wide), F32), pltpu.SemaphoreType.DMA((9,))],
        [VMEM] * 3 + [ANY] * FINISH_OUTS, (ANY,) * (FINISH_OUTS + 1) + (VMEM,) * 3, name="finish", vmem=24,
        aliases={3 + i: i for i in range(FINISH_OUTS)},
    )
    if block != 16:
        lo, hi = packed_w - cut, ab.shape[1] - cut
        pg_all = jnp.concatenate([b[:, lo:hi], b_got[:, lo:hi]]).reshape(-1, 16, 256)[:, :15].reshape(-1, width + wide)
        grad_head = lax.dot_general(
            pg_all[:, :width], pg_all[:, width:], (((0,), (0,)), ((), ())), preferred_element_type=F32
        )
    grad_gate, grad_up, grad_down, grad_out, grad_query, grad_key, grad_value = grads
    return (
        block_out, embedding, grad_x, grad_query, grad_key, grad_value, grad_out, grad_gate, grad_up, grad_down, grad_head,
        grad_norm_attn[0], grad_norm_ffn[0], grad_table.T,
    )


def solution(mesh):
    by_pos = P("rows", "seq", None)
    by_row = P("rows", None)
    return jax.shard_map(
        shards,
        mesh=mesh,
        in_specs=(by_pos, P("rows", "seq"), *[P()] * 11, by_pos, by_row),
        out_specs=(by_pos, by_row, by_pos, *[P()] * 11),
        check_vma=False,
    )
```

```python
import functools

import jax
import jax.numpy as jnp
from jax import lax
from jax.experimental import pallas as pl
from jax.experimental.pallas import tpu as pltpu
from jax.sharding import PartitionSpec as P

EPS = 1e-06
LIMITS = (12, 16, 23, 32, 46, 64, 91)
TOP_PRECISION = lax.Precision.HIGHEST
F32 = jnp.float32
BF16 = jnp.bfloat16
MASK_STEP = 2.0**30
LOG2E = 1.4426950408889634
VMEM = pl.BlockSpec(memory_space=pltpu.VMEM)
ANY = pl.BlockSpec(memory_space=pl.ANY)
LANES = 128
EXT = 16


def mm(a, b):
    return lax.dot_general(a, b, (((1,), (0,)), ((), ())), preferred_element_type=F32)


def mm_nt(a, b):
    return lax.dot_general(a, b, (((1,), (1,)), ((), ())), preferred_element_type=F32)


def bucket_index(offset):
    distance = jnp.abs(offset)
    far_bucket = 8 + sum(((distance >= threshold).astype(jnp.int32) for threshold in LIMITS))
    near_bucket = jnp.where(distance < 8, distance, far_bucket)
    return near_bucket + 16 * (offset > 0).astype(jnp.int32)


def wide_dots(rows, mat, dot):
    at = lax.broadcasted_iota(jnp.int32, (16, rows[0].shape[1]), 0)
    lhs = jnp.zeros(at.shape, F32)
    for i, v in enumerate(rows):
        for j in range(3):
            part = v.astype(BF16).astype(F32)
            lhs = jnp.where(at == 3 * i + j, part, lhs)
            v = v - part
    out = dot(lhs.astype(BF16), mat)
    return [jnp.sum(out[3 * i : 3 * i + 3], axis=0, keepdims=True) for i in range(len(rows))]


def fold(x, op):
    while x.shape[0] > 8:
        half = x.shape[0] // 2
        x = op(x[:half], x[half:])
    return x


def col_sum(x):
    return jnp.sum(fold(x, jnp.add), axis=0, keepdims=True)


def diagonal_sums(table):
    height, width = table.shape
    acc = table[0:8, :]
    for u in range(8, height, 8):
        acc += pltpu.roll(table[u : u + 8, :], width - u, 1)
    row = lax.broadcasted_iota(jnp.int32, acc.shape, 0)
    for bit in (1, 2, 4):
        acc = jnp.where((row & bit) != 0, pltpu.roll(acc, width - bit, 1), acc)
    return jnp.sum(acc, axis=0, keepdims=True)


def position():
    me = lax.axis_index("seq")
    return me, me // 2, me % 2


class Copies:
    def __init__(self, sems):
        self.sems = sems
        self.used = 0

    def start(self, src, dst):
        copy = pltpu.make_async_copy(src, dst, self.sems.at[self.used])
        self.used += 1
        copy.start()
        return copy


def rows_to_send(per, slots):
    _, p, c = position()
    todo = []
    for i, j in enumerate(slots):
        if j == 2:
            todo += [(0, 2 * i, per * (1 - p) + per - 1), (1, i, per * p + per - 1)]
        else:
            todo.append((0, 2 * i, per * (1 - p) + 2 * c + j))
            todo.append((0, 2 * i + 1, per * (1 - p) + 2 * (1 - c) + j))
            todo.append((1, i, per * p + 2 * (1 - c) + j))
    return todo


def pack_kernel(per, groups, ext, tok, seg, *refs):
    outs, (buf, sems) = refs[:-2], refs[-2:]
    span = tok.shape[1]
    copies = Copies(sems)
    todo = [(2 * g, *t) for g, slots in enumerate(groups) for t in rows_to_send(per, slots)]
    loads = [copies.start(tok.at[row], buf.at[k, pl.ds(0, span)]) for k, (_, _, _, row) in enumerate(todo)]
    yield
    for k, (_, _, _, row) in enumerate(todo):
        value = jnp.broadcast_to(seg[pl.ds(row, 1), :].astype(F32), (ext, span)).astype(BF16)
        buf[k, span:, :] = jnp.concatenate([value] * (tok.shape[2] // span), axis=1)
    stores = []
    for k, (at, which, i, _) in enumerate(todo):
        loads[k].wait()
        stores.append(copies.start(buf.at[k], outs[at + which].at[i]))
    for copy in stores:
        copy.wait()


def prepare_kernel(
    n, table, norm_a, norm_f, wq, wk, wv, wo, wg, wu, wd,
    bias_o, ind_o, na_o, nf_o, wqkv_t, wo_t, wg_t, wu_t, wd_t,
    square,
):
    yield
    heads, _, line = bias_o.shape
    inner = wq.shape[1]
    length = line // 2
    col = lax.broadcasted_iota(jnp.int32, (LANES, line), 1)
    offset = length - LANES - jnp.where(col < line - LANES, col, col - line)
    ind = (bucket_index(offset) == lax.broadcasted_iota(jnp.int32, (LANES, line), 0)).astype(F32).astype(BF16)
    ind_o[...] = ind
    square[...] = jnp.zeros_like(square)
    square[: table.shape[0], : table.shape[1]] = table[...]
    rest = square[:8, :]
    lines = None
    for _ in range(3):
        part = rest.astype(BF16)
        rest = rest - part.astype(F32)
        term = mm(part, ind)
        lines = term if lines is None else lines + term
    lines = lines * LOG2E
    for h in range(heads):
        bias_o[h] = pltpu.roll(jnp.broadcast_to(lines[h : h + 1, :], (LANES, line)), 0, 1, stride=1, stride_axis=0)
    for src, dst in ((norm_a, na_o), (norm_f, nf_o)):
        dst[...] = jnp.broadcast_to(src[...], (LANES, src.shape[1])).T
    for i, w in enumerate((wq, wk, wv)):
        wqkv_t[i * inner : (i + 1) * inner, :] = w[...].T
    wo_t[...] = wo[...].T
    size = 256
    one = lax.broadcasted_iota(jnp.int32, (size, size), 0) == lax.broadcasted_iota(jnp.int32, (size, size), 1)
    one = one.astype(F32).astype(BF16)
    for src, dst in ((wg, wg_t), (wu, wu_t), (wd, wd_t)):
        for at in range(0, dst.shape[0], size):
            dst[at : at + size, :] = mm_nt(one, src[:, at : at + size]).astype(BF16)


STEP = 32


def chunks(height):
    return [slice(r, r + STEP) for r in range(0, height, STEP)]


def norm_into(out, src, cols, gain):
    total = None
    for r in chunks(src.shape[0]):
        x = src[r, cols].astype(F32)
        x = fold(x * x, jnp.add)
        total = x if total is None else total + x
    inv = lax.rsqrt(jnp.sum(total, axis=0, keepdims=True) / src.shape[0] + EPS)
    for r in chunks(src.shape[0]):
        out[r, cols] = (src[r, cols].astype(F32) * inv * gain[r, :]).astype(BF16)


def forward_slot(half, n, rows, bufs, w, wait, outs, copies):
    own, c1, y, c2, own_seg = rows
    tok, seg, n1, kk, va, x_b, s_buf = bufs
    bias, wqkv_t, wout_t, wg_t, wu_t, wd_t, nattn, nffn = w
    o = outs
    width = wqkv_t.shape[1]
    inner = wout_t.shape[1]
    heads = bias.shape[0]
    head = inner // heads
    span = own.shape[0]
    length = n * span
    me, p, c = position()
    for k, (piece, ids) in enumerate(((own, own_seg), (c1, None), (y, None), (c2, None))):
        at = pl.multiple_of((me ^ k) * span, span)
        x_b[:, pl.ds(at, span)] = piece[:span, :].T
        ids = piece[span : span + EXT, :span].astype(F32)[0:1, :] if ids is None else ids
        seg[:, pl.ds(at, span)] = jnp.broadcast_to(ids, (LANES, span))
    for b in range(n):
        norm_into(n1, x_b, slice(b * span, (b + 1) * span), nattn)
    nq = length // 2 if half else length
    if half:
        mine = pl.ds(pl.multiple_of(c * nq, nq), nq)
        o["x"][...] = x_b[:, mine]
        o["n1"][...] = n1[:, mine]
    else:
        mine = slice(0, nq)
        o["x"][...] = x_b[...]
        o["n1"][...] = n1[...]
    o["seg"][...] = seg[0:8, :]
    ids = lax.broadcasted_iota(jnp.int32, (LANES, length), 0).astype(F32)
    one = (seg[...] == ids).astype(F32)
    k_aug = ((one - 1.0) * MASK_STEP).T.astype(BF16)
    ids = lax.broadcasted_iota(jnp.int32, (LANES, nq), 0).astype(F32)
    q_aug = (seg[:, mine] == ids).astype(BF16)
    wait("qkv")
    if half:
        qt = mm(wqkv_t[:inner, :], n1[:, mine]).astype(BF16)
        kvt = mm(wqkv_t[inner:, :], n1[...]).astype(BF16)
        kt, vt = kvt[:inner], kvt[inner:]
    else:
        qkvt = mm(wqkv_t[...], n1[...]).astype(BF16)
        qt, kt, vt = qkvt[:inner], qkvt[inner : 2 * inner], qkvt[2 * inner :]
    o["kt"][...] = kt
    q2 = qt.astype(F32) * LOG2E
    q_hi = q2.astype(BF16)
    q_lo = (q2 - q_hi.astype(F32)).astype(BF16)
    lane = lax.broadcasted_iota(jnp.int32, (length, LANES), 1)

    def pair_ready(pair):
        ps = slice(pair * LANES, (pair + 1) * LANES)
        both = kt[ps].T.astype(F32)
        turned = pltpu.roll(both, head, 1)
        kk[2 * pair, :, :LANES] = jnp.where(lane < head, both, turned).astype(BF16)
        kk[2 * pair + 1, :, :LANES] = jnp.where(lane < head, turned, both).astype(BF16)
        for h in (2 * pair, 2 * pair + 1):
            kk[h, :, LANES:] = k_aug
            va[h, :head, :] = vt[h * head : (h + 1) * head]
            va[h, head:, :] = jnp.ones((EXT, length), BF16)

    def naturals(pair):
        ps = slice(pair * LANES, (pair + 1) * LANES)
        o["q"][:, ps] = qt[ps].T
        o["v"][:, ps] = vt[ps].T

    chunk = nq
    work = [(h, qc) for h in range(heads) for qc in range(nq // chunk)]
    per_pair = 2 * (nq // chunk)

    def lanes_of(qc):
        return slice(qc * chunk, (qc + 1) * chunk)

    def score(i, a, rhs):
        h, qc = work[i]
        if half:
            at = pl.ds(pl.multiple_of((n - 1 - a) * LANES + c * nq, LANES), chunk)
        else:
            at = pl.ds((n - 1 - a) * LANES + qc * chunk, chunk)
        s_a = mm(kk[h, a * LANES : (a + 1) * LANES, :], rhs) + bias[h, :, at]
        s_buf[i % 2, a * LANES : (a + 1) * LANES, :chunk] = s_a
        return fold(s_a, jnp.maximum)

    def power(i, a, top):
        h, qc = work[i]
        e = jnp.exp2(s_buf[i % 2, a * LANES : (a + 1) * LANES, :chunk] - top)
        o["e"][h, a * LANES : (a + 1) * LANES, lanes_of(qc)] = e.astype(BF16)

    def attend(i):
        h, qc = work[i]
        hs, qs = slice(h * head, (h + 1) * head), lanes_of(qc)
        raw = mm(va[h], o["e"][h, :, qs])
        inv = 1.0 / raw[head : head + 1, :]
        o["r"][h : h + 1, qs] = inv
        o["att"][hs, qs] = (raw[:head, :] * inv).astype(BF16)

    pair_ready(0)
    wait("bias")
    copies(o["x"], o["seg"], o["n1"], o["kt"])
    top = None
    for i in range(len(work) + 1):
        if i == len(work) // 2:
            wait("rest")
            o["through"]()
            copies(*[(o["e"], h) for h in range(heads // 2 - 1)])
        tops = []
        if i < len(work):
            h, qc = work[i]
            hs, qs = slice(h * head, (h + 1) * head), lanes_of(qc)
            rhs = jnp.concatenate([q_hi[hs, qs], q_lo[hs, qs], q_aug[:, qs]], axis=0)
        for a in range(n):
            if i < len(work):
                tops.append(score(i, a, rhs))
            if i > 0:
                power(i - 1, a, top)
        if i < len(work):
            top = jnp.max(functools.reduce(jnp.maximum, tops), axis=0, keepdims=True)
            if i % per_pair == 0 and i // per_pair < heads // 2 - 1:
                pair_ready(i // per_pair + 1)
            if i % per_pair == 1:
                naturals(i // per_pair)
        if i > 0:
            attend(i - 1)
    if half:
        x_q = x_b[:, mine].astype(F32)
    else:
        x_q = x_b[...].astype(F32)
    o["mid"][...] = x_q + mm(wout_t[...], o["att"][...])
    for b in range(nq // span):
        norm_into(n1, o["mid"], slice(b * span, (b + 1) * span), nffn)
    ff = wg_t.shape[0]
    step = 256
    for b in range(ff // step):
        cs = slice(b * step, (b + 1) * step)
        gate = mm(wg_t[cs, :], n1[:, :nq])
        up = mm(wu_t[cs, :], n1[:, :nq])
        sq = gate * gate
        th = jnp.tanh(gate * (0.7978845608028654 + (0.7978845608028654 * 0.044715) * sq))
        half_th = 0.5 + 0.5 * th
        gelu = gate * half_th
        slope = half_th + (gelu - gelu * th) * (0.7978845608028654 + (3 * 0.7978845608028654 * 0.044715) * sq)
        o["hid"][cs, :] = (gelu * up).astype(BF16)
        o["a"][cs, :] = (up * slope).astype(BF16)
        o["ge"][cs, :] = gelu.astype(BF16)
    copies(*[(o["e"], h) for h in range(heads // 2 - 1, heads)])
    copies(*[o[k] for k in ("r", "att", "q", "v", "mid", "hid", "a", "ge")])
    res = tok.at[:, :nq]
    res[...] = o["mid"][...] + mm(wd_t[...], o["hid"][...])
    valid = (seg[0:1, mine] != 0.0).astype(F32)
    parts = []
    for r in chunks(width):
        part = None
        for b in range(nq // span):
            blk = res[r, b * span : (b + 1) * span] * valid[:, b * span : (b + 1) * span]
            part = blk if part is None else part + blk
        parts.append(part)
    o["pool"][...] = jnp.broadcast_to(col_sum(jnp.concatenate(parts, axis=0).T), o["pool"].shape)
    send_blocks(half, res, o["blocks"], span)


def send_blocks(half, res, outs, span):
    me, _, c = position()
    for k, out in enumerate(outs):
        block = (c + k) % 2 if half else me ^ k
        at = pl.multiple_of(block * span, span)
        out[:span, :] = res[:, pl.ds(at, span)].astype(BF16).T


FORWARD_OUTS = ("kt", "q", "v", "x", "seg", "e", "r", "att", "mid", "hid", "a", "ge", "pool", "n1")


def forward_outs(half, n, span, width, inner, heads, ff):
    length = n * span
    nq = length // 2 if half else length
    shapes = (
        ((inner, length), BF16), ((nq, inner), BF16), ((length, inner), BF16), ((width, nq), BF16), ((8, length), F32),
        ((heads, length, nq), BF16), ((8, nq), F32), ((inner, nq), BF16), ((width, nq), F32), ((ff, nq), BF16),
        ((ff, nq), BF16), ((ff, nq), BF16), ((8, width), F32), ((width, nq), BF16),
    )
    return shapes


def forward_kernel(kinds, n, per, heads, *refs):
    yield
    count = len(FORWARD_OUTS)
    tokens, seg_ids, bias, wqkv_t, wout_t, wg_t, wu_t, wd_t, nattn, nffn = refs[:10]
    near, far, again = refs[10:13]
    had = 0 if kinds[0][0] == 0 else 1
    before = refs[13 : 16 if had else 14]
    at = 16 if had else 14
    outs = [refs[at + i * count : at + (i + 1) * count] for i in range(len(kinds))]
    at += count * len(kinds)
    extra = 3 if had else 5
    block_outs = refs[at : at + extra]
    at += extra
    bufs = [refs[at + i * count : at + (i + 1) * count] for i in range(len(kinds))]
    at += count * len(kinds)
    blocks = refs[at : at + extra]
    at += extra
    own, tok, seg, n1, kk, va, x_b, s_buf, bias_b, wqkv_b, wout_b, wg_b, wu_b, wd_b, in_sems, out_sems = refs[at:]
    me, p, c = position()
    ins = Copies(in_sems)
    owns = []
    for i, (slot, half) in enumerate(kinds):
        row = per * p + (per - 1 if half else 2 * c + slot)
        owns.append((ins.start(tokens.at[row], own.at[i]), row))
    waits = {
        "qkv": [ins.start(wqkv_t, wqkv_b)],
        "bias": [ins.start(bias, bias_b)],
        "rest": [ins.start(a, b) for a, b in ((wout_t, wout_b), (wg_t, wg_b), (wu_t, wu_b), (wd_t, wd_b))],
    }

    def wait(what):
        for copy in waits.pop(what, ()):
            copy.wait()

    writes = Copies(out_sems)
    pending = []
    if had:
        through = [ins.start(a, b.at[pl.ds(0, a.shape[0])]) for a, b in zip(before, blocks)]
    else:
        todo = rows_to_send(per, (0, 1, 2))
        through = [ins.start(before[0].at[row], blocks[3 + which].at[i]) for which, i, row in todo]

    def pass_through():
        while through:
            through.pop().wait()
            if not through:
                if had:
                    pending.extend(writes.start(b.at[pl.ds(0, a.shape[0])], o.at[pl.ds(0, a.shape[0])]) for a, b, o in zip(before, blocks, block_outs))
                else:
                    pending.extend(writes.start(b, o) for b, o in zip(blocks[3:], block_outs[3:]))

    for copy, _ in owns:
        copy.wait()
    deferred = []

    def flush():
        while deferred:
            deferred.pop(0)()

    for i, (slot, half) in enumerate(kinds):
        row = owns[i][1]
        o = dict(zip(FORWARD_OUTS, bufs[i]))
        dst = dict(zip(FORWARD_OUTS, outs[i]))
        b = had + i
        o["blocks"] = (blocks[0].at[b], blocks[1].at[b], blocks[2].at[2 * b], blocks[2].at[2 * b + 1])
        o["through"] = pass_through
        names = {id(v): k for k, v in o.items()}

        def copies(*what, o=o, dst=dst, names=names):
            flush()
            for item in what:
                if isinstance(item, tuple):
                    ref, h = item
                    pending.append(writes.start(ref.at[h], dst[names[id(ref)]].at[h]))
                else:
                    pending.append(writes.start(item, dst[names[id(item)]]))

        c1, y_mine, c2_mine = near.at[i], far.at[2 * i], again.at[2 * i + (not half)]
        own_seg = seg_ids[pl.ds(row, 1), :].astype(F32)
        forward_slot(
            half, n, (own.at[i], c1, y_mine, c2_mine, own_seg), (tok, seg.at[i], n1.at[i], kk, va, x_b.at[i], s_buf),
            (bias_b, wqkv_b, wout_b, wg_b, wu_b, wd_b, nattn, nffn), wait, o, copies,
        )
        def ends(o=o, dst=dst, b=b):
            pending.append(writes.start(o["pool"], dst["pool"]))
            pending.append(writes.start(blocks[0].at[b], block_outs[0].at[b]))
            pending.append(writes.start(blocks[1].at[b], block_outs[1].at[b]))
            pending.append(writes.start(blocks[2].at[pl.ds(2 * b, 2)], block_outs[2].at[pl.ds(2 * b, 2)]))

        deferred.append(ends)
    flush()
    for copy in pending:
        copy.wait()


def middle_kernel(n, per, *refs):
    yield
    grad_y, eg, w_head, w_down, w_gate, w_up, w_out, nffn, pool_other = refs[:9]
    at = 9
    near, far, again = refs[at : at + 3]
    at += 3
    names = ("mid", "a", "ge", "hid", "att", "seg", "r", "pool")
    srcs = [dict(zip(names, refs[at + 8 * i : at + 8 * i + 8])) for i in range(3)]
    at += 24
    ga_o, gt_o = refs[at : at + 3], refs[at + 3 : at + 6]
    own_o, send_o, gnf_o, emb_o, pg_o = refs[at + 6 : at + 11]
    at += 11
    big = ("mid", "a", "ge")
    bufs = [dict(zip(big, refs[at + 3 * i : at + 3 * i + 3])) for i in range(3)]
    at += 9
    own, res, gyt, part, gb, n2, gg, gu, ga, att, hid, packed, gt, wh, wd, wg, wu, wo, sems, out_sems = refs[at:]
    span, width = own.shape[1:]
    length = n * span
    ff = w_gate.shape[1]
    inner = w_out.shape[0]
    head = inner // 6
    wide = w_head.shape[1]
    me, p, c = position()
    ins = Copies(sems)
    owns = []
    for i in range(3):
        row = per * p + (per - 1 if i == 2 else 2 * c + i)
        owns.append(ins.start(grad_y.at[row], own.at[i]))
    weights = {k: ins.start(a, b) for k, a, b in (("h", w_head, wh), ("d", w_down, wd))}
    for k, a, b in (("g", w_gate, wg), ("u", w_up, wu), ("o", w_out, wo)):
        weights[k] = ins.start(a, b)
    lanes = [pl.ds(i * length, length // 2 if i == 2 else length) for i in range(3)]
    loads = []
    for i in range(3):
        loads.append([ins.start(srcs[i][k], bufs[i][k]) for k in big])
    late_loads = []
    for i in range(3):
        late_loads.append(ins.start(srcs[i]["hid"], hid.at[:, lanes[i]]))
        late_loads.append(ins.start(srcs[i]["att"], att.at[:, lanes[i]]))

    def need(*names):
        for k in names:
            if k in weights:
                weights.pop(k).wait()

    for i in range(3):
        owns[i].wait()
    need("h")
    pools, cots, counts = [], [], []
    for i in range(3):
        half = i == 2
        for k, piece in enumerate((own.at[i], near.at[i], far.at[2 * i], again.at[2 * i + (not half)])):
            place = pl.multiple_of((me ^ k) * span, span)
            gyt[i, :, pl.ds(place, span)] = piece[...].T
        count = jnp.sum((srcs[i]["seg"][0:1, :] != 0.0).astype(F32), axis=1, keepdims=True)
        pool = srcs[i]["pool"][0:1, :]
        if half:
            pool = pool + pool_other[0:1, :]
        pools.append(pool / count)
        counts.append(count)
        row = per * p + (per - 1 if half else 2 * c + i)
        cots.append(eg[pl.ds(row, 1), :])
    proj = wide_dots(pools, wh[...], mm)
    g_projs = []
    for i in range(3):
        inv = lax.rsqrt(jnp.sum(proj[i] * proj[i], axis=1, keepdims=True) + EPS)
        emb = proj[i] * inv
        g_proj = inv * (cots[i] - emb * jnp.sum(emb * cots[i], axis=1, keepdims=True))
        emb_o[i] = jnp.broadcast_to(emb, emb_o.shape[1:])
        once = jnp.where(c == 0, 1.0, 0.0) if i == 2 else 1.0
        for q in range((width + wide) // 256):
            piece = pools[i][:, q * 256 : (q + 1) * 256] if q < width // 256 else g_proj[:, q * 256 - width : (q + 1) * 256 - width]
            pg_o[5 * i + q : 5 * i + q + 1, :] = piece * once
        g_projs.append(g_proj)
    g_pools = wide_dots(g_projs, wh[...], mm_nt)
    g_cols = [jnp.broadcast_to(g / k, (span, width)).T for g, k in zip(g_pools, counts)]
    need("d", "g", "u", "o")
    for copy in loads[0]:
        copy.wait()
    sizes = [length, length, length // 2]
    starts = [0, length, 2 * length]

    def outer(i, b, r):
        if i == 2:
            place = pl.ds(pl.multiple_of((c * (sizes[2] // span) + b) * span, span), span)
        else:
            place = pl.ds(b * span, span)
        valid = (srcs[i]["seg"][0:1, place] != 0.0).astype(F32)
        return gyt[i, r, place].astype(F32) + valid * g_cols[i][r, :]

    def branch(i, b):
        for r in chunks(width):
            gb[r, starts[i] + b * span : starts[i] + (b + 1) * span] = outer(i, b, r).astype(BF16)

    step = 256

    def gates(i, b):
        cs, ls = slice(b * step, (b + 1) * step), slice(starts[i], starts[i] + sizes[i])
        g_hid = mm(wd[cs, :], gb[:, ls])
        gg[cs, ls] = (g_hid * bufs[i]["a"][cs, :].astype(F32)).astype(BF16)
        gu[cs, ls] = (g_hid * bufs[i]["ge"][cs, :].astype(F32)).astype(BF16)

    def normed(i):
        ls = slice(starts[i], starts[i] + sizes[i])
        res[i % 2, :, : sizes[i]] = mm(wg[...], gg[:, ls]) + mm(wu[...], gu[:, ls])

    def norm(i, b):
        mid, ds = bufs[i]["mid"], res.at[i % 2]
        bs = slice(b * span, (b + 1) * span)
        ls = slice(starts[i] + b * span, starts[i] + (b + 1) * span)
        sq = cross = None
        for r in chunks(width):
            m = mid[r, bs]
            t = fold(m * m, jnp.add)
            u = fold(ds[r, bs] * nffn[r, :] * m, jnp.add)
            sq, cross = (t, u) if sq is None else (sq + t, cross + u)
        inv2 = lax.rsqrt(jnp.sum(sq, axis=0, keepdims=True) / width + EPS)
        mean = inv2 * jnp.sum(cross, axis=0, keepdims=True) / width
        for r in chunks(width):
            hat = mid[r, bs] * inv2
            n2[r, ls] = (hat * nffn[r, :]).astype(BF16)
            gn = ds[r, bs]
            if i == 0 and b == 0:
                part[r, :] = gn * hat
            else:
                part[r, :] += gn * hat
            ga[r, ls] = (outer(i, b, r) + inv2 * (gn * nffn[r, :] - hat * mean)).astype(BF16)

    def attended(i):
        ls = slice(starts[i], starts[i] + sizes[i])
        gatt = mm(wo[...], ga[:, ls]).astype(BF16).astype(F32)
        for h in range(6):
            hs = slice(h * head, (h + 1) * head)
            gt[hs, ls] = (gatt[hs, :] * srcs[i]["r"][h : h + 1, :]).astype(BF16)

    def store(at, value):
        rows = value.shape[0] // 2
        for side in range(2):
            packed[side, :, at : at + value.shape[1]] = value[side * rows : (side + 1) * rows].astype(BF16)

    outs = Copies(out_sems)
    pending = []

    def send(lo, hi):
        pending.append(outs.start(packed.at[c, :, pl.ds(lo, hi - lo)], own_o.at[:, pl.ds(lo, hi - lo)]))
        pending.append(outs.start(packed.at[1 - c, :, pl.ds(lo, hi - lo)], send_o.at[:, pl.ds(lo, hi - lo)]))

    blocks = [k // span for k in sizes]
    for b in range(blocks[0]):
        branch(0, b)
    for b in range(ff // step):
        gates(0, b)
    for i in (1, 2):
        for copy in loads[i]:
            copy.wait()
    normed(0)
    for b in range(blocks[1]):
        branch(1, b)
    for b in range(ff // step):
        gates(1, b)
        norm(0, b)
    normed(1)
    attended(0)
    for b in range(blocks[2]):
        branch(2, b)
    for b in range(ff // step):
        gates(2, b)
        norm(1, b)
    normed(2)
    attended(1)
    for copy in late_loads:
        copy.wait()
    top = 2 * ff
    for b in range(2):
        store(top + b * width, mm_nt(hid[b * width : (b + 1) * width, :], gb[...]))
        norm(2, b)
    attended(2)
    for i in range(3):
        ls = pl.ds(starts[i], sizes[i])
        pending.append(outs.start(ga.at[:, ls], ga_o[i]))
        pending.append(outs.start(gt.at[:, ls], gt_o[i]))
    send(top, top + 2 * width)
    for b in range(2):
        cs = slice(b * 512, (b + 1) * 512)
        store(b * 512, mm_nt(n2[...], gg[cs, :]))
    send(0, ff)
    for b in range(2):
        cs = slice(b * 512, (b + 1) * 512)
        store(ff + b * 512, mm_nt(n2[...], gu[cs, :]))
    store(top + 2 * width, mm_nt(ga[...], att[...]))
    gnf_o[...] = jnp.broadcast_to(col_sum(part[...].T), gnf_o.shape)
    pg_o[15:16, :] = jnp.zeros((1, 256), F32)
    send(ff, 2 * ff)
    send(top + 2 * width, top + 2 * width + inner)
    for copy in pending:
        copy.wait()


def attention_back(core, n, q_nat, v_nat, kt, e_wait, e_b, att, gt, gs, table, kv_side, line, gq_o, put_kv):
    heads = e_b.shape[0]
    inner = kt.shape[0]
    head = inner // heads
    length = kt.shape[1]
    half = core is not None
    nq = length // 2 if half else length
    lane = lax.broadcasted_iota(jnp.int32, (length, LANES), 1)
    gt_nat = gt[...].T
    zeros = jnp.zeros((head, nq), BF16)
    width = 4 * LANES
    table[:, :, :LANES] = jnp.zeros((2, LANES, LANES), F32)

    def scores(h, a, rhs, delta, far, seen):
        ps = slice(h // 2 * LANES, (h // 2 + 1) * LANES)
        ks = slice(a * LANES, (a + 1) * LANES)
        g_s = e_b[h, ks, :].astype(F32) * (mm(v_nat[ks, ps], rhs) - delta)
        gs[h % 2, ks, :nq] = g_s.astype(BF16)
        t = table.at[h % 2]
        for b in range(nq // LANES):
            blk = g_s[:, b * LANES : (b + 1) * LANES]
            d = (2 * core if half else 0) + b - a
            if abs(d) <= 1:
                at = (d + 2) * LANES
                if d in seen:
                    t[:, at : at + LANES] += blk
                else:
                    t[:, at : at + LANES] = blk
                    seen.add(d)
            else:
                far[d < 0].append(fold(blk, jnp.add))

    def lines(h, far):
        t = table.at[h % 2]
        line(h, slice(LANES, LANES + width), diagonal_sums(t))
        if far[0]:
            line(h, slice(6 * LANES, 7 * LANES), jnp.sum(sum(far[0]), axis=0, keepdims=True))
        if far[1]:
            line(h, slice(0, LANES), jnp.sum(sum(far[1]), axis=0, keepdims=True))

    def weigh(h, which):
        hs, ps = slice(h * head, (h + 1) * head), slice(h // 2 * LANES, (h // 2 + 1) * LANES)
        g = gs.at[h % 2]
        if which == 0:
            gq_o[hs, :] = mm(kt[hs, :], g[:, :nq]).astype(BF16)
            return
        value = mm(g[:, :nq], q_nat[:, ps]) if which == 1 else mm(e_b[h], gt_nat[:, ps])
        if h % 2 == 0:
            kv_side[which - 1] = value
        else:
            put_kv(h // 2, which - 1, jnp.where(lane < head, kv_side[which - 1], value).astype(BF16).T)

    old = None
    for h in range(heads + 1):
        far = [[], []]
        if h < heads:
            if h % 2 == 0:
                e_wait(h // 2)
            hs = slice(h * head, (h + 1) * head)
            g_h = gt[hs, :]
            delta = col_sum(g_h.astype(F32) * att[hs, :].astype(F32))
            rhs = jnp.concatenate([g_h, zeros] if h % 2 == 0 else [zeros, g_h], axis=0)
            seen = set()
        for a in range(n):
            if h < heads:
                scores(h, a, rhs, delta, far, seen)
            if h > 0:
                if a < 3:
                    weigh(h - 1, a)
                else:
                    lines(h - 1, old)
        old = far


def half_back_kernel(n, q_nat, v_nat, kt, e_in, att, gt, gq_o, keep_o, send_o, line_o, e_b, gs, table, kv_side, kv, sems):
    ins = Copies(sems)
    loads = [ins.start(e_in.at[pl.ds(0, 2)], e_b.at[pl.ds(0, 2)])]
    yield
    loads += [ins.start(e_in.at[pl.ds(h, 2)], e_b.at[pl.ds(h, 2)]) for h in range(2, e_in.shape[0], 2)]
    inner = kt.shape[0]

    def put(pair, which, value):
        kv[which * inner + pair * LANES : which * inner + (pair + 1) * LANES, :] = value.astype(BF16)

    def line(h, lanes, value):
        line_o[h : h + 1, lanes] = value

    line_o[...] = jnp.zeros_like(line_o)
    _, _, c = position()
    for core in range(2):

        @pl.when(c == core)
        def _(core=core):
            attention_back(
                core, n, q_nat, v_nat, kt, lambda p: loads[p].wait(), e_b, att, gt, gs, table, kv_side, line, gq_o, put
            )

    nq = kt.shape[1] // 2
    keep_o[...] = kv[:, pl.ds(pl.multiple_of(c * nq, nq), nq)]
    send_o[...] = kv[:, pl.ds(pl.multiple_of((1 - c) * nq, nq), nq)]


def backward_kernel(
    slot, n,
    q_nat, v_nat, kt, e_in, att, gt, line_in, xt, ga, w_query, w_key, w_value, nattn, emb, part_in, *refs,
):
    if slot:
        gq0, gq_half, keep, got, n1_0, n1_1, n1_2, own_o, send_o, gq2, *refs = refs
        *refs, m0, m1, m2, g0, packed = refs
    line_o, gq_o, b_own, b_c, b_y, part_o, gq, e_b, gs, table, kv_side, res, xb, gb, wb, part, sems = refs
    ins = Copies(sems)
    loads = [ins.start(e_in.at[pl.ds(0, 2)], e_b.at[pl.ds(0, 2)])]
    yield
    loads += [ins.start(e_in.at[pl.ds(h, 2)], e_b.at[pl.ds(h, 2)]) for h in range(2, e_in.shape[0], 2)]
    more = [ins.start(a, b) for a, b in ((xt, xb), (ga, gb))]
    more += [ins.start(w, wb.at[:, pl.ds(i * w.shape[1], w.shape[1])]) for i, w in enumerate((w_query, w_key, w_value))]
    if slot:
        more += [ins.start(a, b) for a, b in ((gq0, g0), (n1_0, m0), (n1_1, m1), (n1_2, m2))]
    inner = kt.shape[0]

    def put(pair, which, value):
        at = (1 + which) * inner + pair * LANES
        gq[at : at + LANES, :] = value.astype(BF16)

    def line(h, lanes, value):
        line_o[h : h + 1, lanes] = line_in[h : h + 1, lanes] + value

    line_o[...] = line_in[...]
    if slot:
        gq2[:inner, :] = gq_half[...]
        gq2[inner:, :] = (keep[...].astype(F32) + got[...].astype(F32)).astype(BF16)
    attention_back(
        None, n, q_nat, v_nat, kt, lambda p: loads[p].wait(), e_b, att, gt, gs, table, kv_side, line, gq.at[:inner, :], put
    )
    for copy in more:
        copy.wait()
    if slot:
        part[...] = part_in[...]
        _, _, c = position()
    span = b_own.shape[1] - EXT

    def late_sums(b):
        lo, hi = b * 256, (b + 1) * 256 if b < 3 else 3 * inner
        cs = slice(lo, hi)
        value = mm_nt(m0[...], g0[cs, :]) + mm_nt(m1[...], gq[cs, :]) + mm_nt(m2[...], gq2[cs, :])
        rows = own_o.shape[0]
        for side in range(2):
            packed[side, :, cs] = value[side * rows : (side + 1) * rows].astype(BF16)

    input_rows(
        slot, False, gq, xb, gb, wb, nattn, emb, res, part, (b_own.at[0], b_c.at[0], b_y.at[0], b_y.at[1]), span,
        late_sums if slot else None,
    )
    part_o[...] = part[...]
    outs = [ins.start(gq, gq_o)]
    if slot:
        outs += [ins.start(packed.at[c], own_o), ins.start(packed.at[1 - c], send_o)]
    for copy in outs:
        copy.wait()


def input_rows(slot, half, gq, xt, ga, w_qkv, nattn, emb, res, part, outs, span, between=None):
    width, nq = res.shape[0], gq.shape[1]
    res[:, :nq] = mm(w_qkv[...], gq[...])
    for b in range(nq // span):
        bs = slice(b * span, (b + 1) * span)
        sq = cross = None
        for r in chunks(width):
            x = xt[r, bs].astype(F32)
            t = fold(x * x, jnp.add)
            u = fold(res[r, bs] * nattn[r, :] * x, jnp.add)
            sq, cross = (t, u) if sq is None else (sq + t, cross + u)
        inv = lax.rsqrt(jnp.sum(sq, axis=0, keepdims=True) / width + EPS)
        mean = inv * jnp.sum(cross, axis=0, keepdims=True) / width
        for r in chunks(width):
            hat = xt[r, bs].astype(F32) * inv
            gn = res[r, bs]
            if slot == 0 and b == 0:
                part[r, :] = gn * hat
            else:
                part[r, :] += gn * hat
            res[r, bs] = ga[r, bs].astype(F32) + inv * (gn * nattn[r, :] - hat * mean)
        if between is not None:
            between(b)
    send_blocks(half, res, outs, span)
    row = emb[slot, 0:1, :]
    high = row.astype(BF16).astype(F32)
    rest = jnp.zeros((1, 2 * width - row.shape[1]), F32)
    at = lax.broadcasted_iota(jnp.int32, (EXT, width), 0)
    lines = jnp.zeros((EXT, width), F32)
    for i, v in enumerate((high, row - high)):
        lines = jnp.where(at == 2 * i, v[:, :width], lines)
        lines = jnp.where(at == 2 * i + 1, jnp.concatenate([v[:, width:], rest], axis=1), lines)
    for out in outs:
        out[span:, :] = lines.astype(BF16)


def inputs_kernel(
    gq, xt, ga, w_query, w_key, w_value, nattn, emb, part_in, line_in, gnf, indicator,
    b_own, b_c, b_y, small,
    res, part, w_qkv,
):
    small[...] = jnp.zeros_like(small)
    part[...] = part_in[...]
    for i, w in enumerate((w_query, w_key, w_value)):
        w_qkv[:, i * w.shape[1] : (i + 1) * w.shape[1]] = w[...]
    width = res.shape[0]
    span = b_own.shape[1] - EXT
    input_rows(2, True, gq, xt, ga, w_qkv, nattn, emb, res, part, (b_own.at[0], b_c.at[0], b_y.at[0], b_y.at[1]), span)
    gna = col_sum(part[...].T)
    for i in range(width // LANES):
        small[i : i + 1, :] = gnf[0:1, i * LANES : (i + 1) * LANES]
        small[4 + i : 5 + i, :] = gna[:, i * LANES : (i + 1) * LANES]
    lines = line_in[...]
    hi = lines.astype(BF16)
    lo = (lines - hi.astype(F32)).astype(BF16)
    small[8:16, :] = mm_nt(hi, indicator[...]) + mm_nt(lo, indicator[...])


def unpack_kernel(per, with_emb, *refs):
    groups = (len(refs) - 1 - (3 if with_emb else 1)) // 4
    out = refs[4 * groups]
    sems = refs[-1]
    ways = []
    for g in range(groups):
        own, c1, y, d = refs[4 * g : 4 * g + 4]
        ways += [(own.at[i], c1.at[i], y.at[2 * i], d.at[2 * i + 1]) for i in range(own.shape[0])]
    own0 = ways[0][0]
    me, p, _ = position()
    rows, span, width = out.shape
    for r in range(rows):
        pair, j = divmod(r, per)
        slot = 2 if j == per - 1 else j % 2
        core = p if slot == 2 else j // 2
        k = me ^ (pair * 2 + core)
        for which in range(4):
            ref = ways[slot][which]

            @pl.when(k == which)
            def _(ref=ref, r=r):
                pltpu.make_async_copy(ref.at[pl.ds(0, span)], out.at[r], sems.at[r]).start()
                if with_emb:
                    pltpu.make_async_copy(ref.at[pl.ds(span, EXT)], refs[4 * groups + 2].at[r], sems.at[rows + r]).start()

    if with_emb:
        emb, got = refs[4 * groups + 1 : 4 * groups + 3]
        for r in range(rows):
            pltpu.make_async_copy(own0.at[pl.ds(span, EXT)], got.at[r], sems.at[rows + r]).wait()
            value = got[r].astype(F32)
            emb[r : r + 1, :width] = value[0:1, :] + value[2:3, :]
            emb[r : r + 1, width:] = (value[1:2, :] + value[3:4, :])[:, : emb.shape[1] - width]
    for r in range(rows):
        pltpu.make_async_copy(own0.at[pl.ds(0, span)], out.at[r], sems.at[r]).wait()


def place(step):
    if step is None:
        return 0, 1
    axis, stride, radix = step
    return (lax.axis_index(axis) // stride) % radix, radix


def combine_kernel(plan, *refs):
    at = sum(len(arrays) for pieces, _ in plan for arrays, _, _ in pieces)
    outs = at + sum(place(step)[1] for _, step in plan)
    ins, at, scratch = 0, at, outs
    for pieces, step in plan:
        off = 0
        total = refs[scratch] if step else refs[at]
        for arrays, lo, hi in pieces:
            value = sum(refs[ins + i][..., lo:hi].astype(F32) for i in range(len(arrays)))
            ins += len(arrays)
            total[..., off : off + hi - lo] = value.astype(BF16)
            off += hi - lo
        if step:
            d, radix = place(step)
            for k in range(radix):
                refs[at + k][...] = total[d ^ k]
            at += radix
            scratch += 1
        else:
            at += 1


def join_kernel(plan, *refs):
    ins, at = 0, sum(place(step)[1] for step, _ in plan)
    for step, cuts in plan:
        d, radix = place(step)
        for lo, hi in cuts:
            for k in range(radix):
                refs[at][d ^ k] = refs[ins + k][:, lo:hi]
            at += 1
        ins += radix


def merge_kernel(step, cut, late_cut, own, got, late, late_got, a_o, b_o):
    d, _ = place(step)
    total = (late[...].astype(F32) + late_got[...].astype(F32)).astype(BF16)
    rows, wide = own.shape
    for src, at in ((own, d), (got, d ^ 1)):
        a_o[at, :, :cut] = src[:, :cut]
        b_o[at, :, : wide - cut] = src[:, cut:]
    for side in range(2):
        part = total[side * rows : (side + 1) * rows]
        a_o[side, :, cut:] = part[:, :late_cut]
        b_o[side, :, wide - cut :] = part[:, late_cut:]


FINISH_OUTS = 7


def finish_kernel(second, cut, block, *refs):
    if second:
        b_own, a, b, *rest = refs
        outs, rest = rest[FINISH_OUTS : 2 * FINISH_OUTS], rest[2 * FINISH_OUTS :]
        head_o, nf_o, na_o, table_o, gate, up, down, out, qkv, head, sems = rest
    else:
        a, b, *rest = refs
        outs, (gate, up, down, out, qkv, sems) = rest[:FINISH_OUTS], rest[FINISH_OUTS:]
    gate_o, up_o, down_o, out_o, *qkv_o = outs
    _, _, c = position()
    rows = a.shape[0]
    ff = gate.shape[1]
    width = gate_o.shape[0]
    inner = out.shape[0]
    rest = ff - (cut - ff)
    start = pl.multiple_of(((1 - c) if second else c) * rows, rows)
    at = pl.ds(start, rows)
    copies = Copies(sems)
    gate[...] = a[:, :ff].astype(F32)
    pending = [copies.start(gate, gate_o.at[at])]
    down[0] = b[:, rest : rest + width].astype(F32)
    pending.append(copies.start(down.at[0], down_o.at[at]))
    down[1] = b[:, rest + width : rest + 2 * width].astype(F32)
    pending.append(copies.start(down.at[1], down_o.at[pl.ds(pl.multiple_of(width + start, rows), rows)]))
    up[:, : cut - ff] = a[:, ff:cut].astype(F32)
    up[:, cut - ff :] = b[:, :rest].astype(F32)
    pending.append(copies.start(up, up_o.at[at]))
    late_a = a.shape[1] - cut
    late_b = b.shape[1] - LANES - (3 * inner - late_a)
    for i in range(3):
        lo, hi = i * inner, (i + 1) * inner
        mid = min(max(late_a, lo), hi)
        if mid > lo:
            qkv[i, :, : mid - lo] = a[:, cut + lo : cut + mid].astype(F32)
        if mid < hi:
            qkv[i, :, mid - lo :] = b[:, late_b + mid - late_a : late_b + hi - late_a].astype(F32)
        pending.append(copies.start(qkv.at[i], qkv_o[i].at[at]))
    out[...] = b[:, rest + 2 * width : rest + 2 * width + inner].astype(F32).T
    pending.append(copies.start(out, out_o.at[:, at]))
    if second:
        row = lax.broadcasted_iota(jnp.int32, (rows, 256), 0) % 16
        small = None
        for ref in (b_own, b):
            g = ref[:, late_b - 256 : late_b].astype(F32)
            turned = {t: pltpu.roll(g, rows - t, 0).astype(BF16) for t in range(1, 5)}
            for i in range(2):
                kept = jnp.where((row < 15) & (row % 5 == i), g, 0.0).T.astype(BF16)
                for j in range(3):
                    term = mm(kept, turned[2 + j - i])
                    place_ = (slice(i * 256, (i + 1) * 256), slice(j * 256, (j + 1) * 256))
                    if ref is b_own:
                        head[place_] = term
                    else:
                        head[place_] += term
            for r in range(0, rows, block):
                value = ref[r : r + 16, ref.shape[1] - LANES :].astype(F32)
                small = value if small is None else small + value
        pending.append(copies.start(head, head_o))
        for i in range(nf_o.shape[1] // LANES):
            nf_o[:, i * LANES : (i + 1) * LANES] = small[i : i + 1, :]
            na_o[:, i * LANES : (i + 1) * LANES] = small[4 + i : 5 + i, :]
        table_o[...] = small[8 : 8 + table_o.shape[0], : table_o.shape[1]]
    for copy in pending:
        copy.wait()


def sds(shape, dtype=BF16):
    return jax.ShapeDtypeStruct(shape, dtype)


def call(
    kernel, outs, args, scratch=(), specs=None, out_specs=None, flops=0, name=None, vmem=56, deps=(), aliases=None, overlap=False
):
    count, n_out = len(args), len(outs) if isinstance(outs, tuple) else 1
    specs = list(specs or [VMEM] * count)
    out_specs = list(out_specs or [VMEM] * n_out)
    out_list = list(outs) if isinstance(outs, tuple) else [outs]
    loads = [i for i in range(count) if overlap and specs[i] is VMEM]
    stores = [i for i in range(n_out) if overlap and out_specs[i] is VMEM]
    bufs = [pltpu.VMEM(args[i].shape, args[i].dtype) for i in loads] + [pltpu.VMEM(out_list[i].shape, out_list[i].dtype) for i in stores]
    if overlap:
        bufs.append(pltpu.SemaphoreType.DMA((len(loads) + len(stores),)))

    def body(*refs):
        ins, refs = list(refs[:count]), refs[count + len(deps) :]
        res, refs = list(refs[:n_out]), refs[n_out:]
        if overlap:
            bufs_, refs = refs[: len(bufs)], refs[len(bufs) :]
            copies = Copies(bufs_[-1])
            pending = []
            for i, buf in zip(loads, bufs_):
                pending.append(copies.start(ins[i], buf))
                ins[i] = buf
            out_refs = list(res)
            for i, buf in zip(stores, bufs_[len(loads) :]):
                res[i] = buf
            run = kernel(*ins, *res, *refs)
            if run is not None:
                next(run)
            for copy in pending:
                copy.wait()
            if run is not None:
                next(run, None)
        else:
            kernel(*ins, *res, *refs)
        if overlap:
            pending = [copies.start(res[i], out_refs[i]) for i in stores]
            for copy in pending:
                copy.wait()

    if overlap:
        specs = [ANY if s is VMEM else s for s in specs]
        out_specs = [ANY if s is VMEM else s for s in out_specs]
    return pl.pallas_call(
        body,
        out_shape=outs,
        in_specs=specs + [ANY] * len(deps),
        out_specs=tuple(out_specs) if isinstance(outs, tuple) else out_specs[0],
        scratch_shapes=bufs + list(scratch),
        compiler_params=pltpu.CompilerParams(vmem_limit_bytes=vmem * 2**20),
        cost_estimate=pl.CostEstimate(flops=flops, bytes_accessed=10_000_000, transcendentals=0),
        input_output_aliases=aliases or {},
        name=name,
    )(*args, *deps)


def swap(x, axis, k):
    n = lax.axis_size(axis)
    return lax.ppermute(x, axis, [(i, i ^ k) for i in range(n)])


def after(x, *deps):
    return lax.optimization_barrier((x, *deps))[0]


def together(*trees):
    leaves, shape = jax.tree.flatten(trees)
    return jax.tree.unflatten(shape, lax.optimization_barrier(leaves))


def row_digits():
    return [("rows", 1 << i, 2) for i in range(lax.axis_size("rows").bit_length() - 1)]


def shards(
    tokens, seg_ids, w_query, w_key, w_value, w_out, w_gate, w_up, w_down, w_head, norm_attn, norm_ffn,
    bucket_bias_table, grad_y, embedding_gradient,
):
    rows, span, width = tokens.shape
    buckets, heads = bucket_bias_table.shape
    n = lax.axis_size("seq")
    inner = w_query.shape[1]
    ff = w_gate.shape[1]
    wide = w_head.shape[1]
    length = n * span
    per = rows // 2
    assert n == 4 and per == 5
    slots = 3

    groups = ((0,), (1, 2))
    shapes = [(k, span + EXT, width) for slots in groups for k in (2 * len(slots) - (2 in slots), len(slots))]
    todo = sum(k for k, _, _ in shapes)
    y_a, c_a, y_b, c_b = call(
        functools.partial(pack_kernel, per, groups, EXT), tuple(sds(k) for k in shapes), (tokens, seg_ids),
        [pltpu.VMEM((todo, span + EXT, width), BF16), pltpu.SemaphoreType.DMA((2 * todo,))], [ANY, VMEM], (ANY,) * 4,
        vmem=60, name="pack", overlap=True,
    )

    def pass_on(got, *deps):
        near, far = got
        return near, far, swap(after(far, *deps) if deps else far, "seq", 1)

    line = 2 * length
    x_a = swap(c_a, "seq", 1), swap(y_a, "seq", 2)
    bias, ind, nattn, nffn, wqkv_t, wout_t, wg_t, wu_t, wd_t = call(
        functools.partial(prepare_kernel, n),
        (
            sds((heads, LANES, line), F32), sds((LANES, line)), sds((width, LANES), F32), sds((width, LANES), F32),
            sds((3 * inner, width)), sds((width, inner)), sds((ff, width)), sds((ff, width)),
            sds((width, ff)),
        ),
        (
            bucket_bias_table.T, norm_attn[None], norm_ffn[None], w_query, w_key, w_value, w_out, w_gate, w_up, w_down,
        ),
        [pltpu.VMEM((LANES, LANES), F32)], name="prepare", flops=4_000_000_000, overlap=True,
    )
    x_a, y_b, c_b, nattn = together(x_a, y_b, c_b, nattn)
    x_b = swap(c_b, "seq", 1), swap(y_b, "seq", 2)
    x_a = pass_on(x_a)

    def collect(own, c, y):
        return own, swap(c, "seq", 1), swap(y, "seq", 2)

    def collect_rest(part, *deps):
        return *part, swap(after(part[2], *deps), "seq", 1)

    def run_forward(kinds, pieces, before=(), deps=()):
        shapes = [s for _, half in kinds for s in forward_outs(half, n, span, width, inner, heads, ff)]
        had = len(before) and before[0].shape[0]
        shapes += [((k * (len(kinds) + had), span, width), BF16) for k in (1, 1, 2)]
        if not had:
            shapes += [((2 * slots - 1, span, width), BF16), ((slots, span, width), BF16)]
        outs = tuple(sds(*s) for s in shapes)
        args = [tokens, seg_ids, bias, wqkv_t, wout_t, wg_t, wu_t, wd_t, nattn, nffn]
        specs = [ANY, VMEM] + [ANY] * 6 + [VMEM] * 2
        args += [*pieces, *(before or (grad_y,))]
        specs += [VMEM] * 3 + [ANY] * (3 if had else 1)
        scratch = [pltpu.VMEM(*s) for s in shapes]
        scratch += [
            pltpu.VMEM((len(kinds), span, width), BF16), pltpu.VMEM((length, width), F32),
            pltpu.VMEM((len(kinds), LANES, length), F32), pltpu.VMEM((len(kinds), width, length), BF16),
            pltpu.VMEM((heads, length, 2 * LANES), BF16), pltpu.VMEM((heads, inner // heads + EXT, length), BF16),
            pltpu.VMEM((len(kinds), width, length), BF16),
            pltpu.VMEM((2, length, length), F32), pltpu.VMEM(bias.shape, F32), *[pltpu.VMEM(w.shape, BF16) for w in (wqkv_t, wout_t, wg_t, wu_t, wd_t)],
            pltpu.SemaphoreType.DMA((12 + len(kinds) + 3 * slots,)), pltpu.SemaphoreType.DMA((24 * len(kinds) + 6,)),
        ]
        res = call(
            functools.partial(forward_kernel, kinds, n, per, heads), outs, args, scratch, specs, tuple(ANY for _ in outs),
            4_000_000_000 * len(kinds), "forward", deps=deps, overlap=True,
        )
        count = len(FORWARD_OUTS)
        at = count * len(kinds)
        rows_ = [dict(zip(FORWARD_OUTS, res[i * count : (i + 1) * count])) for i in range(len(kinds))]
        return rows_, res[at : at + 3], res[at + 3 :]

    fwd, blocks, packed_g = run_forward([(0, False)], x_a, deps=(y_b, c_b))
    x_b = pass_on(x_b, fwd[0]["r"])
    gys = swap(packed_g[1], "seq", 1), swap(packed_g[0], "seq", 2)
    fwd_b, blocks, _ = run_forward([(1, False), (2, True)], x_b, blocks, deps=packed_g)
    blocks = collect(*blocks)
    fwd += fwd_b
    gys = pass_on(gys, fwd[1]["r"])
    pool_other = swap(fwd[2]["pool"], "seq", 1)

    def unpack(parts, with_emb, deps=()):
        args = [a for group in parts for a in group]
        outs = (sds((rows, span, width)),) + ((sds((rows, wide), F32),) if with_emb else ())
        scratch = [pltpu.VMEM((rows, EXT, width), BF16)] if with_emb else []
        return call(
            functools.partial(unpack_kernel, per, with_emb), outs, args, scratch + [pltpu.SemaphoreType.DMA((2 * rows,))],
            [ANY] * len(args), (ANY, VMEM)[: len(outs)], vmem=16, name="unpack", deps=deps,
        )


    packed_w = 2 * ff + 2 * width + inner
    nqs = [length, length, length // 2]
    args = [grad_y, embedding_gradient, w_head, w_down, w_gate, w_up, w_out, nffn, pool_other]
    specs = [ANY, VMEM] + [ANY] * 5 + [VMEM] * 2
    args += list(gys)
    specs += [VMEM] * 3
    for f in fwd:
        args += [f[k] for k in ("mid", "a", "ge", "hid", "att", "seg", "r", "pool")]
        specs += [ANY] * 5 + [VMEM] * 3
    outs = tuple(
        [sds((width, q)) for q in nqs] + [sds((inner, q)) for q in nqs]
        + [sds((width // 2, packed_w))] * 2 + [sds((8, width), F32), sds((3, 8, wide), F32), sds((16, 256), F32)]
    )
    scratch = []
    for q in nqs:
        scratch += [pltpu.VMEM((width, q), F32), pltpu.VMEM((ff, q), BF16), pltpu.VMEM((ff, q), BF16)]
    total = sum(nqs)
    scratch += [
        pltpu.VMEM((3, span, width), BF16), pltpu.VMEM((2, width, length), F32), pltpu.VMEM((3, width, length), BF16),
        pltpu.VMEM((width, LANES), F32), pltpu.VMEM((width, total), BF16), pltpu.VMEM((width, total), BF16),
        pltpu.VMEM((ff, total), BF16), pltpu.VMEM((ff, total), BF16), pltpu.VMEM((width, total), BF16),
        pltpu.VMEM((inner, total), BF16), pltpu.VMEM((ff, total), BF16), pltpu.VMEM((2, width // 2, packed_w), BF16), pltpu.VMEM((inner, total), BF16),
        *[pltpu.VMEM(w.shape, BF16) for w in (w_head, w_down, w_gate, w_up, w_out)],
        pltpu.SemaphoreType.DMA((23,)), pltpu.SemaphoreType.DMA((14,)),
    ]
    m = call(functools.partial(middle_kernel, n, per), outs, args, scratch, specs, [ANY] * 8 + [VMEM] * 3, flops=15_000_000_000, name="middle", overlap=True)
    m, blocks = together(m, blocks)
    ga, gt = m[:3], m[3:6]
    own, send, gnf, emb, pg = m[6:]

    core = ("seq", 1, 2)
    far = ("seq", 2, 2)
    digits = row_digits()
    block = width // 2 // far[2]
    for d in digits:
        block //= d[2]

    def send_shares(parts, s):
        return [swap(p, s[0], k * s[1]) for k, p in enumerate(parts) if k]

    def send_all(v, s):
        return [swap(v, s[0], k * s[1]) for k in range(1, s[2])]

    def combine(groups, deps=()):
        args, outs, scratch, plan = [], [], [], []
        for pieces, step in groups:
            rows_, wide_ = pieces[0][0][0].shape[0], sum(hi - lo for _, lo, hi in pieces)
            radix = step[2] if step else 1
            shape = (radix, rows_ // radix) if step else (rows_,)
            for arrays, _, _ in pieces:
                args += [a.reshape(shape + a.shape[-1:]) for a in arrays]
            outs += [sds((rows_ // radix, wide_))] * radix
            scratch += [pltpu.VMEM(shape + (wide_,), BF16)] if step else []
            plan.append((pieces, step))
        plan = [([(range(len(a)), lo, hi) for a, lo, hi in pieces], step) for pieces, step in plan]
        res = call(functools.partial(combine_kernel, plan), tuple(outs), args, scratch, vmem=24, name="combine", deps=deps)
        out = []
        for _, step in plan:
            radix = step[2] if step else 1
            out.append(list(res[:radix]))
            res = res[radix:]
        return out

    def joined(groups, deps=()):
        args, outs, plan = [], [], []
        for v, got, step, cuts in groups:
            cuts = cuts or [(0, v.shape[1])]
            args += [v] + got
            outs += [sds((step[2], v.shape[0], hi - lo)) for lo, hi in cuts]
            plan.append((step, cuts))
        res = call(functools.partial(join_kernel, plan), tuple(outs), args, vmem=24, name="join", deps=deps)
        return [r.reshape(-1, r.shape[-1]) for r in res]

    def all_of(*arrays):
        return [(list(arrays), 0, arrays[0].shape[1])]

    nh = length // 2
    half = call(
        functools.partial(half_back_kernel, n),
        (sds((inner, nh)), sds((2 * inner, nh)), sds((2 * inner, nh)), sds((8, line), F32)),
        (fwd[2]["q"], fwd[2]["v"], fwd[2]["kt"], fwd[2]["e"], fwd[2]["att"], gt[2]),
        [
            pltpu.VMEM((heads, length, nh), BF16), pltpu.VMEM((2, length, nh), BF16), pltpu.VMEM((2, LANES, 4 * LANES), F32),
            pltpu.VMEM((2, length, LANES), F32), pltpu.VMEM((2 * inner, length), BF16), pltpu.SemaphoreType.DMA((heads,)),
        ],
        [VMEM] * 3 + [ANY] + [VMEM] * 2, flops=2_000_000_000, name="half_back", deps=(send,), overlap=True,
    )
    got = swap(send, "seq", 1)
    block_parts = [collect_rest(blocks)]
    half, got, block_parts = together(half, got, block_parts)
    gq_half, keep, send_kv, lines_sum = half
    got_kv = swap(send_kv, "seq", 1)
    cut = packed_w // 2 // LANES * LANES
    sa, sb = [digits[0], far], [far, digits[0]]
    pa, pb = combine([([([own, got], 0, cut)], sa[0]), ([([own, got], cut, packed_w)], sb[0])])

    piece = tuple(sds((i, span + EXT, width)) for i in (1, 1, 2))

    def run_back(j, lines_sum, part, deps, extra=()):
        f = fwd[j]
        scratch = [
            pltpu.VMEM((3 * inner, length), BF16), pltpu.VMEM((heads, length, length), BF16),
            pltpu.VMEM((2, length, length), BF16), pltpu.VMEM((2, LANES, 4 * LANES), F32), pltpu.VMEM((2, length, LANES), F32), pltpu.VMEM((width, length), F32),
            pltpu.VMEM((width, length), BF16), pltpu.VMEM((width, length), BF16), pltpu.VMEM((width, 3 * inner), BF16),
            pltpu.VMEM((width, LANES), F32), pltpu.SemaphoreType.DMA((heads // 2 + 14,)),
        ]
        late_outs = ()
        if extra:
            late_outs = (sds((width // 2, 3 * inner)), sds((width // 2, 3 * inner)), sds((3 * inner, nh)))
            scratch += [pltpu.VMEM((width, q), BF16) for q in nqs]
            scratch += [pltpu.VMEM((3 * inner, length), BF16), pltpu.VMEM((2, width // 2, 3 * inner), BF16)]
        res = call(
            functools.partial(backward_kernel, j, n),
            (*late_outs, sds((8, line), F32), sds((3 * inner, length)), *piece, sds((width, LANES), F32)),
            (f["q"], f["v"], f["kt"], f["e"], f["att"], gt[j], lines_sum, f["x"], ga[j], w_query, w_key, w_value, nattn, emb, part, *extra),
            scratch, [VMEM] * 3 + [ANY] + [VMEM] * 3 + [ANY] * 5 + [VMEM] * 3 + ([ANY] + [VMEM] * 3 + [ANY] * 3 if extra else []),
            ([ANY] * 2 + [VMEM] if extra else []) + [VMEM, ANY] + [VMEM] * 4, flops=4_000_000_000, name="backward", deps=deps, overlap=True,
        )
        late, (line_o, gq, *blocks, part) = res[: len(late_outs)], res[len(late_outs) :]
        return line_o, gq, blocks, part, late

    back = run_back(0, lines_sum, nattn, (pa[1], pb[1]))
    ra, rb = send_shares(pa, sa[0]), send_shares(pb, sb[0])
    back, ra, rb, got_kv = together(back, ra, rb, got_kv)
    pa, pb = combine([(all_of(pa[0], *ra), sa[1]), (all_of(pb[0], *rb), sb[1])])
    back2 = run_back(
        1, back[0], back[3], (pa[1], pb[1]), (back[1], gq_half, keep, got_kv, *[f["n1"] for f in fwd])
    )
    x_a = collect(*back[2])
    ra, rb = send_shares(pa, sa[1]), send_shares(pb, sb[1])
    back2, ra, rb, x_a = together(back2, ra, rb, x_a)
    late_own, late_send, gq2 = back2[4]

    late_got = swap(late_send, "seq", 1)
    x_a = collect_rest(x_a)
    (parts,) = combine([(all_of(pa[0], *ra) + all_of(pb[0], *rb), digits[1])])
    z_got = send_shares(parts, digits[1])
    late_got, x_a = together(late_got, x_a)
    x_b = collect(*back2[2])
    late_cut = 2 * inner
    la, lb = combine([([([late_own, late_got], 0, late_cut)], sa[0]), ([([late_own, late_got], late_cut, 3 * inner)], sb[0])])
    lga, lgb = send_shares(la, sa[0]), send_shares(lb, sb[0])
    late_sends = (la[1], lb[1])
    for step in digits[2:]:
        (parts,) = combine([(all_of(parts[0], *z_got), step)], deps=late_sends)
        z_got = send_shares(parts, step)
        late_sends = ()
    lga, lgb = together(lga, lgb)
    la, lb = combine([(all_of(la[0], *lga), sa[1]), (all_of(lb[0], *lgb), sb[1])])
    lga, lgb = send_shares(la, sa[1]), send_shares(lb, sb[1])
    *x_c, small = call(
        inputs_kernel, (*piece, sds((width // 8, LANES), F32)),
        (gq2, fwd[2]["x"], ga[2], w_query, w_key, w_value, nattn, emb, back2[3], back2[0], gnf, ind),
        [pltpu.VMEM((width, nh), F32), pltpu.VMEM((width, LANES), F32), pltpu.VMEM((width, 3 * inner), BF16)],
        flops=3_000_000_000, name="inputs", vmem=16,
        deps=tuple(parts[1:]) + (la[1], lb[1]),
    )
    pg_b = pg.astype(BF16).reshape(block, -1)
    ((ab,),) = combine([(all_of(parts[0], *z_got) + all_of(pg_b), None)], deps=(la[1], lb[1]))
    ab_got = send_all(ab, digits[-1])
    lga, lgb, x_c, small, x_b = together(lga, lgb, x_c, small, x_b)
    x_c = collect(*x_c)
    ((late,),) = combine([(all_of(la[0], *lga) + all_of(lb[0], *lgb) + all_of(small), None)], deps=(ab,))
    strides = digits[1:]
    for step, back_step in zip(strides[:-1], strides[:0:-1]):
        late_got = swap(late, *step[:2])
        x_b = collect_rest(x_b) if len(x_b) == 3 else x_b
        ((late,),) = combine([(all_of(late, late_got), None)])
        (ab,) = joined([(ab, ab_got, back_step, None)], deps=(late,))
        ab_got = send_all(ab, digits[digits.index(back_step) - 1])
    late_got = swap(late, *strides[-1][:2])
    (block_out,) = unpack(block_parts, False, deps=(late,))
    late_got, ab_got, block_out, x_b, x_c = together(late_got, ab_got, block_out, x_b, x_c)
    wide_a, wide_b = cut + late_cut, ab.shape[1] - cut + late.shape[1] - late_cut
    a, b = call(
        functools.partial(merge_kernel, digits[1], cut, late_cut),
        (sds((2, ab.shape[0], wide_a)), sds((2, ab.shape[0], wide_b))), (ab, *ab_got, late, late_got), vmem=24, name="merge",
    )
    a, b = a.reshape(-1, wide_a), b.reshape(-1, wide_b)
    ga_, gb_ = send_all(a, sa[1]), send_all(b, sb[1])
    x_c = collect_rest(x_c)
    ga_, gb_, x_c = together(ga_, gb_, x_c)
    a, b = joined([(a, ga_, sa[1], None), (b, gb_, sb[1], None)])
    ga_, gb_ = send_all(a, sa[0]), send_all(b, sb[0])
    grad_x, embedding = unpack([x_a, x_b, x_c], True, deps=(a, b))
    ga_, gb_, grad_x = together(ga_, gb_, grad_x)
    a, b = joined([(a, ga_, sa[0], None), (b, gb_, sb[0], None)])
    a_got, b_got = swap(a, "seq", 1), swap(b, "seq", 1)
    outs = (
        sds((width, ff), F32), sds((width, ff), F32), sds((ff, width), F32), sds((inner, width), F32),
        *[sds((width, inner), F32)] * 3,
    )
    halves = [
        pltpu.VMEM((width // 2, ff), F32), pltpu.VMEM((width // 2, ff), F32), pltpu.VMEM((2, width // 2, width), F32),
        pltpu.VMEM((inner, width // 2), F32), pltpu.VMEM((3, width // 2, inner), F32),
    ]
    first = call(
        functools.partial(finish_kernel, False, cut, width // 8), outs, (a, b), halves + [pltpu.SemaphoreType.DMA((9,))],
        out_specs=(ANY,) * FINISH_OUTS, name="finish", vmem=24,
    )
    first, a_got, b_got = together(first, a_got, b_got)
    *grads, grad_head, grad_norm_ffn, grad_norm_attn, grad_table = call(
        functools.partial(finish_kernel, True, cut, width // 8),
        outs + (sds((width, wide), F32), sds((1, width), F32), sds((1, width), F32), sds((heads, buckets), F32)),
        (b, a_got, b_got, *first), halves + [pltpu.VMEM((width, wide), F32), pltpu.SemaphoreType.DMA((9,))],
        [VMEM] * 3 + [ANY] * FINISH_OUTS, (ANY,) * (FINISH_OUTS + 1) + (VMEM,) * 3, name="finish", vmem=24,
        aliases={3 + i: i for i in range(FINISH_OUTS)},
    )
    if block != 16:
        lo, hi = packed_w - cut, ab.shape[1] - cut
        pg_all = jnp.concatenate([b[:, lo:hi], b_got[:, lo:hi]]).reshape(-1, 16, 256)[:, :15].reshape(-1, width + wide)
        grad_head = lax.dot_general(
            pg_all[:, :width], pg_all[:, width:], (((0,), (0,)), ((), ())), preferred_element_type=F32
        )
    grad_gate, grad_up, grad_down, grad_out, grad_query, grad_key, grad_value = grads
    return (
        block_out, embedding, grad_x, grad_query, grad_key, grad_value, grad_out, grad_gate, grad_up, grad_down, grad_head,
        grad_norm_attn[0], grad_norm_ffn[0], grad_table.T,
    )


def solution(mesh):
    by_pos = P("rows", "seq", None)
    by_row = P("rows", None)
    return jax.shard_map(
        shards,
        mesh=mesh,
        in_specs=(by_pos, P("rows", "seq"), *[P()] * 11, by_pos, by_row),
        out_specs=(by_pos, by_row, by_pos, *[P()] * 11),
        check_vma=False,
    )
```

```python
import functools

import jax
import jax.numpy as jnp
from jax import lax
from jax.experimental import pallas as pl
from jax.experimental.pallas import tpu as pltpu
from jax.sharding import PartitionSpec as P

EPS = 1e-06
LIMITS = (12, 16, 23, 32, 46, 64, 91)
TOP_PRECISION = lax.Precision.HIGHEST
F32 = jnp.float32
BF16 = jnp.bfloat16
MASK_STEP = 2.0**30
LOG2E = 1.4426950408889634
VMEM = pl.BlockSpec(memory_space=pltpu.VMEM)
ANY = pl.BlockSpec(memory_space=pl.ANY)
LANES = 128
EXT = 16


def mm(a, b):
    return lax.dot_general(a, b, (((1,), (0,)), ((), ())), preferred_element_type=F32)


def mm_nt(a, b):
    return lax.dot_general(a, b, (((1,), (1,)), ((), ())), preferred_element_type=F32)


def bucket_index(offset):
    distance = jnp.abs(offset)
    far_bucket = 8 + sum(((distance >= threshold).astype(jnp.int32) for threshold in LIMITS))
    near_bucket = jnp.where(distance < 8, distance, far_bucket)
    return near_bucket + 16 * (offset > 0).astype(jnp.int32)


def wide_dots(rows, mat, dot):
    at = lax.broadcasted_iota(jnp.int32, (16, rows[0].shape[1]), 0)
    lhs = jnp.zeros(at.shape, F32)
    for i, v in enumerate(rows):
        for j in range(3):
            part = v.astype(BF16).astype(F32)
            lhs = jnp.where(at == 3 * i + j, part, lhs)
            v = v - part
    out = dot(lhs.astype(BF16), mat)
    return [jnp.sum(out[3 * i : 3 * i + 3], axis=0, keepdims=True) for i in range(len(rows))]


def fold(x, op):
    while x.shape[0] > 8:
        half = x.shape[0] // 2
        x = op(x[:half], x[half:])
    return x


def col_sum(x):
    return jnp.sum(fold(x, jnp.add), axis=0, keepdims=True)


def diagonal_sums(table):
    height, width = table.shape
    acc = table[0:8, :]
    for u in range(8, height, 8):
        acc += pltpu.roll(table[u : u + 8, :], width - u, 1)
    row = lax.broadcasted_iota(jnp.int32, acc.shape, 0)
    for bit in (1, 2, 4):
        acc = jnp.where((row & bit) != 0, pltpu.roll(acc, width - bit, 1), acc)
    return jnp.sum(acc, axis=0, keepdims=True)


def position():
    me = lax.axis_index("seq")
    return me, me // 2, me % 2


class Copies:
    def __init__(self, sems):
        self.sems = sems
        self.used = 0

    def start(self, src, dst):
        copy = pltpu.make_async_copy(src, dst, self.sems.at[self.used])
        self.used += 1
        copy.start()
        return copy


def rows_to_send(per, slots):
    _, p, c = position()
    todo = []
    for i, j in enumerate(slots):
        if j == 2:
            todo += [(0, 2 * i, per * (1 - p) + per - 1), (1, i, per * p + per - 1)]
        else:
            todo.append((0, 2 * i, per * (1 - p) + 2 * c + j))
            todo.append((0, 2 * i + 1, per * (1 - p) + 2 * (1 - c) + j))
            todo.append((1, i, per * p + 2 * (1 - c) + j))
    return todo


def pack_kernel(per, groups, ext, tok, seg, *refs):
    outs, (buf, sems) = refs[:-2], refs[-2:]
    span = tok.shape[1]
    copies = Copies(sems)
    todo = [(2 * g, *t) for g, slots in enumerate(groups) for t in rows_to_send(per, slots)]
    loads = [copies.start(tok.at[row], buf.at[k, pl.ds(0, span)]) for k, (_, _, _, row) in enumerate(todo)]
    yield
    for k, (_, _, _, row) in enumerate(todo):
        value = jnp.broadcast_to(seg[pl.ds(row, 1), :].astype(F32), (ext, span)).astype(BF16)
        buf[k, span:, :] = jnp.concatenate([value] * (tok.shape[2] // span), axis=1)
    stores = []
    for k, (at, which, i, _) in enumerate(todo):
        loads[k].wait()
        stores.append(copies.start(buf.at[k], outs[at + which].at[i]))
    for copy in stores:
        copy.wait()


def prepare_kernel(
    n, table, norm_a, norm_f, wq, wk, wv, wo, wg, wu, wd,
    bias_o, ind_o, na_o, nf_o, wqkv_t, wo_t, wg_t, wu_t, wd_t,
    square,
):
    yield
    heads, _, line = bias_o.shape
    inner = wq.shape[1]
    length = line // 2
    col = lax.broadcasted_iota(jnp.int32, (LANES, line), 1)
    offset = length - LANES - jnp.where(col < line - LANES, col, col - line)
    ind = (bucket_index(offset) == lax.broadcasted_iota(jnp.int32, (LANES, line), 0)).astype(F32).astype(BF16)
    ind_o[...] = ind
    square[...] = jnp.zeros_like(square)
    square[: table.shape[0], : table.shape[1]] = table[...]
    rest = square[:8, :]
    lines = None
    for _ in range(3):
        part = rest.astype(BF16)
        rest = rest - part.astype(F32)
        term = mm(part, ind)
        lines = term if lines is None else lines + term
    lines = lines * LOG2E
    for h in range(heads):
        bias_o[h] = pltpu.roll(jnp.broadcast_to(lines[h : h + 1, :], (LANES, line)), 0, 1, stride=1, stride_axis=0)
    for src, dst in ((norm_a, na_o), (norm_f, nf_o)):
        dst[...] = jnp.broadcast_to(src[...], (LANES, src.shape[1])).T
    for i, w in enumerate((wq, wk, wv)):
        wqkv_t[i * inner : (i + 1) * inner, :] = w[...].T
    wo_t[...] = wo[...].T
    size = 256
    one = lax.broadcasted_iota(jnp.int32, (size, size), 0) == lax.broadcasted_iota(jnp.int32, (size, size), 1)
    one = one.astype(F32).astype(BF16)
    for src, dst in ((wg, wg_t), (wu, wu_t), (wd, wd_t)):
        for at in range(0, dst.shape[0], size):
            dst[at : at + size, :] = mm_nt(one, src[:, at : at + size]).astype(BF16)


STEP = 32


def chunks(height):
    return [slice(r, r + STEP) for r in range(0, height, STEP)]


def norm_into(out, src, cols, gain):
    total = None
    for r in chunks(src.shape[0]):
        x = src[r, cols].astype(F32)
        x = fold(x * x, jnp.add)
        total = x if total is None else total + x
    inv = lax.rsqrt(jnp.sum(total, axis=0, keepdims=True) / src.shape[0] + EPS)
    for r in chunks(src.shape[0]):
        out[r, cols] = (src[r, cols].astype(F32) * inv * gain[r, :]).astype(BF16)


def forward_slot(half, n, rows, bufs, w, wait, outs, copies):
    own, c1, y, c2, own_seg = rows
    tok, seg, n1, kk, va, x_b, s_buf = bufs
    bias, wqkv_t, wout_t, wg_t, wu_t, wd_t, nattn, nffn = w
    o = outs
    width = wqkv_t.shape[1]
    inner = wout_t.shape[1]
    heads = bias.shape[0]
    head = inner // heads
    span = own.shape[0]
    length = n * span
    me, p, c = position()
    for k, (piece, ids) in enumerate(((own, own_seg), (c1, None), (y, None), (c2, None))):
        at = pl.multiple_of((me ^ k) * span, span)
        x_b[:, pl.ds(at, span)] = piece[:span, :].T
        ids = piece[span : span + EXT, :span].astype(F32)[0:1, :] if ids is None else ids
        seg[:, pl.ds(at, span)] = jnp.broadcast_to(ids, (LANES, span))
    for b in range(n):
        norm_into(n1, x_b, slice(b * span, (b + 1) * span), nattn)
    nq = length // 2 if half else length
    if half:
        mine = pl.ds(pl.multiple_of(c * nq, nq), nq)
        o["x"][...] = x_b[:, mine]
        o["n1"][...] = n1[:, mine]
    else:
        mine = slice(0, nq)
        o["x"][...] = x_b[...]
        o["n1"][...] = n1[...]
    o["seg"][...] = seg[0:8, :]
    ids = lax.broadcasted_iota(jnp.int32, (LANES, length), 0).astype(F32)
    one = (seg[...] == ids).astype(F32)
    k_aug = ((one - 1.0) * MASK_STEP).T.astype(BF16)
    ids = lax.broadcasted_iota(jnp.int32, (LANES, nq), 0).astype(F32)
    q_aug = (seg[:, mine] == ids).astype(BF16)
    wait("qkv")
    if half:
        qt = mm(wqkv_t[:inner, :], n1[:, mine]).astype(BF16)
        kvt = mm(wqkv_t[inner:, :], n1[...]).astype(BF16)
        kt, vt = kvt[:inner], kvt[inner:]
    else:
        qkvt = mm(wqkv_t[...], n1[...]).astype(BF16)
        qt, kt, vt = qkvt[:inner], qkvt[inner : 2 * inner], qkvt[2 * inner :]
    o["kt"][...] = kt
    q2 = qt.astype(F32) * LOG2E
    q_hi = q2.astype(BF16)
    q_lo = (q2 - q_hi.astype(F32)).astype(BF16)
    lane = lax.broadcasted_iota(jnp.int32, (length, LANES), 1)

    def pair_ready(pair):
        ps = slice(pair * LANES, (pair + 1) * LANES)
        both = kt[ps].T.astype(F32)
        turned = pltpu.roll(both, head, 1)
        kk[2 * pair, :, :LANES] = jnp.where(lane < head, both, turned).astype(BF16)
        kk[2 * pair + 1, :, :LANES] = jnp.where(lane < head, turned, both).astype(BF16)
        for h in (2 * pair, 2 * pair + 1):
            kk[h, :, LANES:] = k_aug
            va[h, :head, :] = vt[h * head : (h + 1) * head]
            va[h, head:, :] = jnp.ones((EXT, length), BF16)

    def naturals(pair):
        ps = slice(pair * LANES, (pair + 1) * LANES)
        o["q"][:, ps] = qt[ps].T
        o["v"][:, ps] = vt[ps].T

    chunk = nq
    work = [(h, qc) for h in range(heads) for qc in range(nq // chunk)]
    per_pair = 2 * (nq // chunk)

    def lanes_of(qc):
        return slice(qc * chunk, (qc + 1) * chunk)

    def score(i, a, rhs):
        h, qc = work[i]
        if half:
            at = pl.ds(pl.multiple_of((n - 1 - a) * LANES + c * nq, LANES), chunk)
        else:
            at = pl.ds((n - 1 - a) * LANES + qc * chunk, chunk)
        s_a = mm(kk[h, a * LANES : (a + 1) * LANES, :], rhs) + bias[h, :, at]
        s_buf[i % 2, a * LANES : (a + 1) * LANES, :chunk] = s_a
        return fold(s_a, jnp.maximum)

    def power(i, a, top):
        h, qc = work[i]
        e = jnp.exp2(s_buf[i % 2, a * LANES : (a + 1) * LANES, :chunk] - top)
        o["e"][h, a * LANES : (a + 1) * LANES, lanes_of(qc)] = e.astype(BF16)

    def attend(i):
        h, qc = work[i]
        hs, qs = slice(h * head, (h + 1) * head), lanes_of(qc)
        raw = mm(va[h], o["e"][h, :, qs])
        inv = 1.0 / raw[head : head + 1, :]
        o["r"][h : h + 1, qs] = inv
        o["att"][hs, qs] = (raw[:head, :] * inv).astype(BF16)

    pair_ready(0)
    wait("bias")
    copies(o["x"], o["seg"], o["n1"], o["kt"])
    top = None
    for i in range(len(work) + 1):
        if i == len(work) // 2:
            wait("rest")
            o["through"]()
            copies(*[(o["e"], h) for h in range(heads // 2 - 1)])
        tops = []
        if i < len(work):
            h, qc = work[i]
            hs, qs = slice(h * head, (h + 1) * head), lanes_of(qc)
            rhs = jnp.concatenate([q_hi[hs, qs], q_lo[hs, qs], q_aug[:, qs]], axis=0)
        for a in range(n):
            if i < len(work):
                tops.append(score(i, a, rhs))
            if i > 0:
                power(i - 1, a, top)
        if i < len(work):
            top = jnp.max(functools.reduce(jnp.maximum, tops), axis=0, keepdims=True)
            if i % per_pair == 0 and i // per_pair < heads // 2 - 1:
                pair_ready(i // per_pair + 1)
            if i % per_pair == 1:
                naturals(i // per_pair)
        if i > 0:
            attend(i - 1)
    if half:
        x_q = x_b[:, mine].astype(F32)
    else:
        x_q = x_b[...].astype(F32)
    o["mid"][...] = x_q + mm(wout_t[...], o["att"][...])
    for b in range(nq // span):
        norm_into(n1, o["mid"], slice(b * span, (b + 1) * span), nffn)
    ff = wg_t.shape[0]
    step = 256
    for b in range(ff // step):
        cs = slice(b * step, (b + 1) * step)
        gate = mm(wg_t[cs, :], n1[:, :nq])
        up = mm(wu_t[cs, :], n1[:, :nq])
        sq = gate * gate
        th = jnp.tanh(gate * (0.7978845608028654 + (0.7978845608028654 * 0.044715) * sq))
        half_th = 0.5 + 0.5 * th
        gelu = gate * half_th
        slope = half_th + (gelu - gelu * th) * (0.7978845608028654 + (3 * 0.7978845608028654 * 0.044715) * sq)
        o["hid"][cs, :] = (gelu * up).astype(BF16)
        o["a"][cs, :] = (up * slope).astype(BF16)
        o["ge"][cs, :] = gelu.astype(BF16)
    copies(*[(o["e"], h) for h in range(heads // 2 - 1, heads)])
    copies(*[o[k] for k in ("r", "att", "q", "v", "mid", "hid", "a", "ge")])
    res = tok.at[:, :nq]
    res[...] = o["mid"][...] + mm(wd_t[...], o["hid"][...])
    valid = (seg[0:1, mine] != 0.0).astype(F32)
    parts = []
    for r in chunks(width):
        part = None
        for b in range(nq // span):
            blk = res[r, b * span : (b + 1) * span] * valid[:, b * span : (b + 1) * span]
            part = blk if part is None else part + blk
        parts.append(part)
    o["pool"][...] = jnp.broadcast_to(col_sum(jnp.concatenate(parts, axis=0).T), o["pool"].shape)
    send_blocks(half, res, o["blocks"], span)


def send_blocks(half, res, outs, span):
    me, _, c = position()
    for k, out in enumerate(outs):
        block = (c + k) % 2 if half else me ^ k
        at = pl.multiple_of(block * span, span)
        out[:span, :] = res[:, pl.ds(at, span)].astype(BF16).T


FORWARD_OUTS = ("kt", "q", "v", "x", "seg", "e", "r", "att", "mid", "hid", "a", "ge", "pool", "n1")


def forward_outs(half, n, span, width, inner, heads, ff):
    length = n * span
    nq = length // 2 if half else length
    shapes = (
        ((inner, length), BF16), ((nq, inner), BF16), ((length, inner), BF16), ((width, nq), BF16), ((8, length), F32),
        ((heads, length, nq), BF16), ((8, nq), F32), ((inner, nq), BF16), ((width, nq), F32), ((ff, nq), BF16),
        ((ff, nq), BF16), ((ff, nq), BF16), ((8, width), F32), ((width, nq), BF16),
    )
    return shapes


def forward_kernel(kinds, n, per, heads, *refs):
    yield
    count = len(FORWARD_OUTS)
    tokens, seg_ids, bias, wqkv_t, wout_t, wg_t, wu_t, wd_t, nattn, nffn = refs[:10]
    near, far, again = refs[10:13]
    had = 0 if kinds[0][0] == 0 else 1
    before = refs[13 : 16 if had else 14]
    at = 16 if had else 14
    outs = [refs[at + i * count : at + (i + 1) * count] for i in range(len(kinds))]
    at += count * len(kinds)
    extra = 3 if had else 5
    block_outs = refs[at : at + extra]
    at += extra
    bufs = [refs[at + i * count : at + (i + 1) * count] for i in range(len(kinds))]
    at += count * len(kinds)
    blocks = refs[at : at + extra]
    at += extra
    own, tok, seg, n1, kk, va, x_b, s_buf, bias_b, wqkv_b, wout_b, wg_b, wu_b, wd_b, in_sems, out_sems = refs[at:]
    me, p, c = position()
    ins = Copies(in_sems)
    owns = []
    for i, (slot, half) in enumerate(kinds):
        row = per * p + (per - 1 if half else 2 * c + slot)
        owns.append((ins.start(tokens.at[row], own.at[i]), row))
    waits = {
        "qkv": [ins.start(wqkv_t, wqkv_b)],
        "bias": [ins.start(bias, bias_b)],
        "rest": [ins.start(a, b) for a, b in ((wout_t, wout_b), (wg_t, wg_b), (wu_t, wu_b), (wd_t, wd_b))],
    }

    def wait(what):
        for copy in waits.pop(what, ()):
            copy.wait()

    writes = Copies(out_sems)
    pending = []
    if had:
        through = [ins.start(a, b.at[pl.ds(0, a.shape[0])]) for a, b in zip(before, blocks)]
    else:
        todo = rows_to_send(per, (0, 1, 2))
        through = [ins.start(before[0].at[row], blocks[3 + which].at[i]) for which, i, row in todo]

    def pass_through():
        while through:
            through.pop().wait()
            if not through:
                if had:
                    pending.extend(writes.start(b.at[pl.ds(0, a.shape[0])], o.at[pl.ds(0, a.shape[0])]) for a, b, o in zip(before, blocks, block_outs))
                else:
                    pending.extend(writes.start(b, o) for b, o in zip(blocks[3:], block_outs[3:]))

    for copy, _ in owns:
        copy.wait()
    deferred = []

    def flush():
        while deferred:
            deferred.pop(0)()

    for i, (slot, half) in enumerate(kinds):
        row = owns[i][1]
        o = dict(zip(FORWARD_OUTS, bufs[i]))
        dst = dict(zip(FORWARD_OUTS, outs[i]))
        b = had + i
        o["blocks"] = (blocks[0].at[b], blocks[1].at[b], blocks[2].at[2 * b], blocks[2].at[2 * b + 1])
        o["through"] = pass_through
        names = {id(v): k for k, v in o.items()}

        def copies(*what, o=o, dst=dst, names=names):
            flush()
            for item in what:
                if isinstance(item, tuple):
                    ref, h = item
                    pending.append(writes.start(ref.at[h], dst[names[id(ref)]].at[h]))
                else:
                    pending.append(writes.start(item, dst[names[id(item)]]))

        c1, y_mine, c2_mine = near.at[i], far.at[2 * i], again.at[2 * i + (not half)]
        own_seg = seg_ids[pl.ds(row, 1), :].astype(F32)
        forward_slot(
            half, n, (own.at[i], c1, y_mine, c2_mine, own_seg), (tok, seg.at[i], n1.at[i], kk, va, x_b.at[i], s_buf),
            (bias_b, wqkv_b, wout_b, wg_b, wu_b, wd_b, nattn, nffn), wait, o, copies,
        )
        def ends(o=o, dst=dst, b=b):
            pending.append(writes.start(o["pool"], dst["pool"]))
            pending.append(writes.start(blocks[0].at[b], block_outs[0].at[b]))
            pending.append(writes.start(blocks[1].at[b], block_outs[1].at[b]))
            pending.append(writes.start(blocks[2].at[pl.ds(2 * b, 2)], block_outs[2].at[pl.ds(2 * b, 2)]))

        deferred.append(ends)
    flush()
    for copy in pending:
        copy.wait()


def middle_kernel(n, per, *refs):
    yield
    grad_y, eg, w_head, w_down, w_gate, w_up, w_out, nffn, pool_other = refs[:9]
    at = 9
    near, far, again = refs[at : at + 3]
    at += 3
    names = ("mid", "a", "ge", "hid", "att", "seg", "r", "pool")
    srcs = [dict(zip(names, refs[at + 8 * i : at + 8 * i + 8])) for i in range(3)]
    at += 24
    ga_o, gt_o = refs[at : at + 3], refs[at + 3 : at + 6]
    own_o, send_o, gnf_o, emb_o, pg_o = refs[at + 6 : at + 11]
    at += 11
    big = ("mid", "a", "ge")
    bufs = [dict(zip(big, refs[at + 3 * i : at + 3 * i + 3])) for i in range(3)]
    at += 9
    own, res, gyt, part, gb, n2, gg, gu, ga, att, hid, packed, gt, wh, wd, wg, wu, wo, sems, out_sems = refs[at:]
    span, width = own.shape[1:]
    length = n * span
    ff = w_gate.shape[1]
    inner = w_out.shape[0]
    head = inner // 6
    wide = w_head.shape[1]
    me, p, c = position()
    ins = Copies(sems)
    owns = []
    for i in range(3):
        row = per * p + (per - 1 if i == 2 else 2 * c + i)
        owns.append(ins.start(grad_y.at[row], own.at[i]))
    weights = {k: ins.start(a, b) for k, a, b in (("h", w_head, wh), ("d", w_down, wd))}
    for k, a, b in (("g", w_gate, wg), ("u", w_up, wu), ("o", w_out, wo)):
        weights[k] = ins.start(a, b)
    lanes = [pl.ds(i * length, length // 2 if i == 2 else length) for i in range(3)]
    loads = []
    for i in range(3):
        loads.append([ins.start(srcs[i][k], bufs[i][k]) for k in big])
    late_loads = []
    for i in range(3):
        late_loads.append(ins.start(srcs[i]["hid"], hid.at[:, lanes[i]]))
        late_loads.append(ins.start(srcs[i]["att"], att.at[:, lanes[i]]))

    def need(*names):
        for k in names:
            if k in weights:
                weights.pop(k).wait()

    for i in range(3):
        owns[i].wait()
    need("h")
    pools, cots, counts = [], [], []
    for i in range(3):
        half = i == 2
        for k, piece in enumerate((own.at[i], near.at[i], far.at[2 * i], again.at[2 * i + (not half)])):
            place = pl.multiple_of((me ^ k) * span, span)
            gyt[i, :, pl.ds(place, span)] = piece[...].T
        count = jnp.sum((srcs[i]["seg"][0:1, :] != 0.0).astype(F32), axis=1, keepdims=True)
        pool = srcs[i]["pool"][0:1, :]
        if half:
            pool = pool + pool_other[0:1, :]
        pools.append(pool / count)
        counts.append(count)
        row = per * p + (per - 1 if half else 2 * c + i)
        cots.append(eg[pl.ds(row, 1), :])
    proj = wide_dots(pools, wh[...], mm)
    g_projs = []
    for i in range(3):
        inv = lax.rsqrt(jnp.sum(proj[i] * proj[i], axis=1, keepdims=True) + EPS)
        emb = proj[i] * inv
        g_proj = inv * (cots[i] - emb * jnp.sum(emb * cots[i], axis=1, keepdims=True))
        emb_o[i] = jnp.broadcast_to(emb, emb_o.shape[1:])
        once = jnp.where(c == 0, 1.0, 0.0) if i == 2 else 1.0
        for q in range((width + wide) // 256):
            piece = pools[i][:, q * 256 : (q + 1) * 256] if q < width // 256 else g_proj[:, q * 256 - width : (q + 1) * 256 - width]
            pg_o[5 * i + q : 5 * i + q + 1, :] = piece * once
        g_projs.append(g_proj)
    g_pools = wide_dots(g_projs, wh[...], mm_nt)
    g_cols = [jnp.broadcast_to(g / k, (span, width)).T for g, k in zip(g_pools, counts)]
    need("d", "g", "u", "o")
    for copy in loads[0]:
        copy.wait()
    sizes = [length, length, length // 2]
    starts = [0, length, 2 * length]

    def outer(i, b, r):
        if i == 2:
            place = pl.ds(pl.multiple_of((c * (sizes[2] // span) + b) * span, span), span)
        else:
            place = pl.ds(b * span, span)
        valid = (srcs[i]["seg"][0:1, place] != 0.0).astype(F32)
        return gyt[i, r, place].astype(F32) + valid * g_cols[i][r, :]

    def branch(i, b):
        for r in chunks(width):
            gb[r, starts[i] + b * span : starts[i] + (b + 1) * span] = outer(i, b, r).astype(BF16)

    step = 256

    def gates(i, b):
        cs, ls = slice(b * step, (b + 1) * step), slice(starts[i], starts[i] + sizes[i])
        g_hid = mm(wd[cs, :], gb[:, ls])
        gg[cs, ls] = (g_hid * bufs[i]["a"][cs, :].astype(F32)).astype(BF16)
        gu[cs, ls] = (g_hid * bufs[i]["ge"][cs, :].astype(F32)).astype(BF16)

    def normed(i):
        ls = slice(starts[i], starts[i] + sizes[i])
        res[i % 2, :, : sizes[i]] = mm(wg[...], gg[:, ls]) + mm(wu[...], gu[:, ls])

    def norm(i, b):
        mid, ds = bufs[i]["mid"], res.at[i % 2]
        bs = slice(b * span, (b + 1) * span)
        ls = slice(starts[i] + b * span, starts[i] + (b + 1) * span)
        sq = cross = None
        for r in chunks(width):
            m = mid[r, bs]
            t = fold(m * m, jnp.add)
            u = fold(ds[r, bs] * nffn[r, :] * m, jnp.add)
            sq, cross = (t, u) if sq is None else (sq + t, cross + u)
        inv2 = lax.rsqrt(jnp.sum(sq, axis=0, keepdims=True) / width + EPS)
        mean = inv2 * jnp.sum(cross, axis=0, keepdims=True) / width
        for r in chunks(width):
            hat = mid[r, bs] * inv2
            n2[r, ls] = (hat * nffn[r, :]).astype(BF16)
            gn = ds[r, bs]
            if i == 0 and b == 0:
                part[r, :] = gn * hat
            else:
                part[r, :] += gn * hat
            ga[r, ls] = (outer(i, b, r) + inv2 * (gn * nffn[r, :] - hat * mean)).astype(BF16)

    def attended(i):
        ls = slice(starts[i], starts[i] + sizes[i])
        gatt = mm(wo[...], ga[:, ls]).astype(BF16).astype(F32)
        for h in range(6):
            hs = slice(h * head, (h + 1) * head)
            gt[hs, ls] = (gatt[hs, :] * srcs[i]["r"][h : h + 1, :]).astype(BF16)

    def store(at, value):
        rows = value.shape[0] // 2
        for side in range(2):
            packed[side, :, at : at + value.shape[1]] = value[side * rows : (side + 1) * rows].astype(BF16)

    outs = Copies(out_sems)
    pending = []

    def send(lo, hi):
        pending.append(outs.start(packed.at[c, :, pl.ds(lo, hi - lo)], own_o.at[:, pl.ds(lo, hi - lo)]))
        pending.append(outs.start(packed.at[1 - c, :, pl.ds(lo, hi - lo)], send_o.at[:, pl.ds(lo, hi - lo)]))

    blocks = [k // span for k in sizes]
    for b in range(blocks[0]):
        branch(0, b)
    for b in range(ff // step):
        gates(0, b)
    for i in (1, 2):
        for copy in loads[i]:
            copy.wait()
    normed(0)
    for b in range(blocks[1]):
        branch(1, b)
    for b in range(ff // step):
        gates(1, b)
        norm(0, b)
    normed(1)
    attended(0)
    for b in range(blocks[2]):
        branch(2, b)
    for b in range(ff // step):
        gates(2, b)
        norm(1, b)
    normed(2)
    attended(1)
    for copy in late_loads:
        copy.wait()
    top = 2 * ff
    for b in range(2):
        store(top + b * width, mm_nt(hid[b * width : (b + 1) * width, :], gb[...]))
        norm(2, b)
    attended(2)
    for i in range(3):
        ls = pl.ds(starts[i], sizes[i])
        pending.append(outs.start(ga.at[:, ls], ga_o[i]))
        pending.append(outs.start(gt.at[:, ls], gt_o[i]))
    send(top, top + 2 * width)
    for b in range(2):
        cs = slice(b * 512, (b + 1) * 512)
        store(b * 512, mm_nt(n2[...], gg[cs, :]))
    send(0, ff)
    for b in range(2):
        cs = slice(b * 512, (b + 1) * 512)
        store(ff + b * 512, mm_nt(n2[...], gu[cs, :]))
    store(top + 2 * width, mm_nt(ga[...], att[...]))
    gnf_o[...] = jnp.broadcast_to(col_sum(part[...].T), gnf_o.shape)
    pg_o[15:16, :] = jnp.zeros((1, 256), F32)
    send(ff, 2 * ff)
    send(top + 2 * width, top + 2 * width + inner)
    for copy in pending:
        copy.wait()


def attention_back(core, n, q_nat, v_nat, kt, e_wait, e_b, att, gt, gs, table, kv_side, line, gq_o, put_kv):
    heads = e_b.shape[0]
    inner = kt.shape[0]
    head = inner // heads
    length = kt.shape[1]
    half = core is not None
    nq = length // 2 if half else length
    lane = lax.broadcasted_iota(jnp.int32, (length, LANES), 1)
    gt_nat = gt[...].T
    zeros = jnp.zeros((head, nq), BF16)
    width = 4 * LANES
    table[:, :, :LANES] = jnp.zeros((2, LANES, LANES), F32)

    def scores(h, a, rhs, delta, far, seen):
        ps = slice(h // 2 * LANES, (h // 2 + 1) * LANES)
        ks = slice(a * LANES, (a + 1) * LANES)
        g_s = e_b[h, ks, :].astype(F32) * (mm(v_nat[ks, ps], rhs) - delta)
        gs[h % 2, ks, :nq] = g_s.astype(BF16)
        t = table.at[h % 2]
        for b in range(nq // LANES):
            blk = g_s[:, b * LANES : (b + 1) * LANES]
            d = (2 * core if half else 0) + b - a
            if abs(d) <= 1:
                at = (d + 2) * LANES
                if d in seen:
                    t[:, at : at + LANES] += blk
                else:
                    t[:, at : at + LANES] = blk
                    seen.add(d)
            else:
                far[d < 0].append(fold(blk, jnp.add))

    def lines(h, far):
        t = table.at[h % 2]
        line(h, slice(LANES, LANES + width), diagonal_sums(t))
        if far[0]:
            line(h, slice(6 * LANES, 7 * LANES), jnp.sum(sum(far[0]), axis=0, keepdims=True))
        if far[1]:
            line(h, slice(0, LANES), jnp.sum(sum(far[1]), axis=0, keepdims=True))

    def weigh(h, which):
        hs, ps = slice(h * head, (h + 1) * head), slice(h // 2 * LANES, (h // 2 + 1) * LANES)
        g = gs.at[h % 2]
        if which == 0:
            gq_o[hs, :] = mm(kt[hs, :], g[:, :nq]).astype(BF16)
            return
        value = mm(g[:, :nq], q_nat[:, ps]) if which == 1 else mm(e_b[h], gt_nat[:, ps])
        if h % 2 == 0:
            kv_side[which - 1] = value
        else:
            put_kv(h // 2, which - 1, jnp.where(lane < head, kv_side[which - 1], value).astype(BF16).T)

    old = None
    for h in range(heads + 1):
        far = [[], []]
        if h < heads:
            if h % 2 == 0:
                e_wait(h // 2)
            hs = slice(h * head, (h + 1) * head)
            g_h = gt[hs, :]
            delta = col_sum(g_h.astype(F32) * att[hs, :].astype(F32))
            rhs = jnp.concatenate([g_h, zeros] if h % 2 == 0 else [zeros, g_h], axis=0)
            seen = set()
        for a in range(n):
            if h < heads:
                scores(h, a, rhs, delta, far, seen)
            if h > 0:
                if a < 3:
                    weigh(h - 1, a)
                else:
                    lines(h - 1, old)
        old = far


def half_back_kernel(n, q_nat, v_nat, kt, e_in, att, gt, gq_o, keep_o, send_o, line_o, e_b, gs, table, kv_side, kv, sems):
    ins = Copies(sems)
    loads = [ins.start(e_in.at[pl.ds(0, 2)], e_b.at[pl.ds(0, 2)])]
    yield
    loads += [ins.start(e_in.at[pl.ds(h, 2)], e_b.at[pl.ds(h, 2)]) for h in range(2, e_in.shape[0], 2)]
    inner = kt.shape[0]

    def put(pair, which, value):
        kv[which * inner + pair * LANES : which * inner + (pair + 1) * LANES, :] = value.astype(BF16)

    def line(h, lanes, value):
        line_o[h : h + 1, lanes] = value

    line_o[...] = jnp.zeros_like(line_o)
    _, _, c = position()
    for core in range(2):

        @pl.when(c == core)
        def _(core=core):
            attention_back(
                core, n, q_nat, v_nat, kt, lambda p: loads[p].wait(), e_b, att, gt, gs, table, kv_side, line, gq_o, put
            )

    nq = kt.shape[1] // 2
    keep_o[...] = kv[:, pl.ds(pl.multiple_of(c * nq, nq), nq)]
    send_o[...] = kv[:, pl.ds(pl.multiple_of((1 - c) * nq, nq), nq)]


def backward_kernel(
    slot, n,
    q_nat, v_nat, kt, e_in, att, gt, line_in, xt, ga, w_query, w_key, w_value, nattn, emb, part_in, *refs,
):
    if slot:
        gq0, gq_half, keep, got, n1_0, n1_1, n1_2, own_o, send_o, gq2, *refs = refs
        *refs, m0, m1, m2, g0, packed = refs
    line_o, gq_o, b_own, b_c, b_y, part_o, gq, e_b, gs, table, kv_side, res, xb, gb, wb, part, sems = refs
    ins = Copies(sems)
    loads = [ins.start(e_in.at[pl.ds(0, 2)], e_b.at[pl.ds(0, 2)])]
    yield
    loads += [ins.start(e_in.at[pl.ds(h, 2)], e_b.at[pl.ds(h, 2)]) for h in range(2, e_in.shape[0], 2)]
    more = [ins.start(a, b) for a, b in ((xt, xb), (ga, gb))]
    more += [ins.start(w, wb.at[:, pl.ds(i * w.shape[1], w.shape[1])]) for i, w in enumerate((w_query, w_key, w_value))]
    if slot:
        more += [ins.start(a, b) for a, b in ((gq0, g0), (n1_0, m0), (n1_1, m1), (n1_2, m2))]
    inner = kt.shape[0]

    def put(pair, which, value):
        at = (1 + which) * inner + pair * LANES
        gq[at : at + LANES, :] = value.astype(BF16)

    def line(h, lanes, value):
        line_o[h : h + 1, lanes] = line_in[h : h + 1, lanes] + value

    line_o[...] = line_in[...]
    if slot:
        gq2[:inner, :] = gq_half[...]
        gq2[inner:, :] = (keep[...].astype(F32) + got[...].astype(F32)).astype(BF16)
    attention_back(
        None, n, q_nat, v_nat, kt, lambda p: loads[p].wait(), e_b, att, gt, gs, table, kv_side, line, gq.at[:inner, :], put
    )
    for copy in more:
        copy.wait()
    if slot:
        part[...] = part_in[...]
        _, _, c = position()
    span = b_own.shape[1] - EXT

    def late_sums(b):
        lo, hi = b * 256, (b + 1) * 256 if b < 3 else 3 * inner
        cs = slice(lo, hi)
        value = mm_nt(m0[...], g0[cs, :]) + mm_nt(m1[...], gq[cs, :]) + mm_nt(m2[...], gq2[cs, :])
        rows = own_o.shape[0]
        for side in range(2):
            packed[side, :, cs] = value[side * rows : (side + 1) * rows].astype(BF16)

    input_rows(
        slot, False, gq, xb, gb, wb, nattn, emb, res, part, (b_own.at[0], b_c.at[0], b_y.at[0], b_y.at[1]), span,
        late_sums if slot else None,
    )
    part_o[...] = part[...]
    outs = [ins.start(gq, gq_o)]
    if slot:
        outs += [ins.start(packed.at[c], own_o), ins.start(packed.at[1 - c], send_o)]
    for copy in outs:
        copy.wait()


def input_rows(slot, half, gq, xt, ga, w_qkv, nattn, emb, res, part, outs, span, between=None):
    width, nq = res.shape[0], gq.shape[1]
    res[:, :nq] = mm(w_qkv[...], gq[...])
    for b in range(nq // span):
        bs = slice(b * span, (b + 1) * span)
        sq = cross = None
        for r in chunks(width):
            x = xt[r, bs].astype(F32)
            t = fold(x * x, jnp.add)
            u = fold(res[r, bs] * nattn[r, :] * x, jnp.add)
            sq, cross = (t, u) if sq is None else (sq + t, cross + u)
        inv = lax.rsqrt(jnp.sum(sq, axis=0, keepdims=True) / width + EPS)
        mean = inv * jnp.sum(cross, axis=0, keepdims=True) / width
        for r in chunks(width):
            hat = xt[r, bs].astype(F32) * inv
            gn = res[r, bs]
            if slot == 0 and b == 0:
                part[r, :] = gn * hat
            else:
                part[r, :] += gn * hat
            res[r, bs] = ga[r, bs].astype(F32) + inv * (gn * nattn[r, :] - hat * mean)
        if between is not None:
            between(b)
    send_blocks(half, res, outs, span)
    row = emb[slot, 0:1, :]
    high = row.astype(BF16).astype(F32)
    rest = jnp.zeros((1, 2 * width - row.shape[1]), F32)
    at = lax.broadcasted_iota(jnp.int32, (EXT, width), 0)
    lines = jnp.zeros((EXT, width), F32)
    for i, v in enumerate((high, row - high)):
        lines = jnp.where(at == 2 * i, v[:, :width], lines)
        lines = jnp.where(at == 2 * i + 1, jnp.concatenate([v[:, width:], rest], axis=1), lines)
    for out in outs:
        out[span:, :] = lines.astype(BF16)


def inputs_kernel(
    gq, xt, ga, w_query, w_key, w_value, nattn, emb, part_in, line_in, gnf, indicator,
    b_own, b_c, b_y, small,
    res, part, w_qkv,
):
    small[...] = jnp.zeros_like(small)
    part[...] = part_in[...]
    for i, w in enumerate((w_query, w_key, w_value)):
        w_qkv[:, i * w.shape[1] : (i + 1) * w.shape[1]] = w[...]
    width = res.shape[0]
    span = b_own.shape[1] - EXT
    input_rows(2, True, gq, xt, ga, w_qkv, nattn, emb, res, part, (b_own.at[0], b_c.at[0], b_y.at[0], b_y.at[1]), span)
    gna = col_sum(part[...].T)
    for i in range(width // LANES):
        small[i : i + 1, :] = gnf[0:1, i * LANES : (i + 1) * LANES]
        small[4 + i : 5 + i, :] = gna[:, i * LANES : (i + 1) * LANES]
    lines = line_in[...]
    hi = lines.astype(BF16)
    lo = (lines - hi.astype(F32)).astype(BF16)
    small[8:16, :] = mm_nt(hi, indicator[...]) + mm_nt(lo, indicator[...])


def unpack_kernel(per, with_emb, *refs):
    groups = (len(refs) - 1 - (3 if with_emb else 1)) // 4
    out = refs[4 * groups]
    sems = refs[-1]
    ways = []
    for g in range(groups):
        own, c1, y, d = refs[4 * g : 4 * g + 4]
        ways += [(own.at[i], c1.at[i], y.at[2 * i], d.at[2 * i + 1]) for i in range(own.shape[0])]
    own0 = ways[0][0]
    me, p, _ = position()
    rows, span, width = out.shape
    for r in range(rows):
        pair, j = divmod(r, per)
        slot = 2 if j == per - 1 else j % 2
        core = p if slot == 2 else j // 2
        k = me ^ (pair * 2 + core)
        for which in range(4):
            ref = ways[slot][which]

            @pl.when(k == which)
            def _(ref=ref, r=r):
                pltpu.make_async_copy(ref.at[pl.ds(0, span)], out.at[r], sems.at[r]).start()
                if with_emb:
                    pltpu.make_async_copy(ref.at[pl.ds(span, EXT)], refs[4 * groups + 2].at[r], sems.at[rows + r]).start()

    if with_emb:
        emb, got = refs[4 * groups + 1 : 4 * groups + 3]
        for r in range(rows):
            pltpu.make_async_copy(own0.at[pl.ds(span, EXT)], got.at[r], sems.at[rows + r]).wait()
            value = got[r].astype(F32)
            emb[r : r + 1, :width] = value[0:1, :] + value[2:3, :]
            emb[r : r + 1, width:] = (value[1:2, :] + value[3:4, :])[:, : emb.shape[1] - width]
    for r in range(rows):
        pltpu.make_async_copy(own0.at[pl.ds(0, span)], out.at[r], sems.at[r]).wait()


def place(step):
    if step is None:
        return 0, 1
    axis, stride, radix = step
    return (lax.axis_index(axis) // stride) % radix, radix


def combine_kernel(plan, *refs):
    at = sum(len(arrays) for pieces, _ in plan for arrays, _, _ in pieces)
    outs = at + sum(place(step)[1] for _, step in plan)
    ins, at, scratch = 0, at, outs
    for pieces, step in plan:
        off = 0
        total = refs[scratch] if step else refs[at]
        for arrays, lo, hi in pieces:
            value = sum(refs[ins + i][..., lo:hi].astype(F32) for i in range(len(arrays)))
            ins += len(arrays)
            total[..., off : off + hi - lo] = value.astype(BF16)
            off += hi - lo
        if step:
            d, radix = place(step)
            for k in range(radix):
                refs[at + k][...] = total[d ^ k]
            at += radix
            scratch += 1
        else:
            at += 1


def join_kernel(plan, *refs):
    ins, at = 0, sum(place(step)[1] for step, _ in plan)
    for step, cuts in plan:
        d, radix = place(step)
        for lo, hi in cuts:
            for k in range(radix):
                refs[at][d ^ k] = refs[ins + k][:, lo:hi]
            at += 1
        ins += radix


def merge_kernel(step, cut, late_cut, own, got, late, late_got, a_o, b_o):
    d, _ = place(step)
    total = (late[...].astype(F32) + late_got[...].astype(F32)).astype(BF16)
    rows, wide = own.shape
    for src, at in ((own, d), (got, d ^ 1)):
        a_o[at, :, :cut] = src[:, :cut]
        b_o[at, :, : wide - cut] = src[:, cut:]
    for side in range(2):
        part = total[side * rows : (side + 1) * rows]
        a_o[side, :, cut:] = part[:, :late_cut]
        b_o[side, :, wide - cut :] = part[:, late_cut:]


FINISH_OUTS = 7


def finish_kernel(second, cut, block, *refs):
    if second:
        b_own, a, b, *rest = refs
        outs, rest = rest[FINISH_OUTS : 2 * FINISH_OUTS], rest[2 * FINISH_OUTS :]
        head_o, nf_o, na_o, table_o, gate, up, down, out, qkv, head, sems = rest
    else:
        a, b, *rest = refs
        outs, (gate, up, down, out, qkv, sems) = rest[:FINISH_OUTS], rest[FINISH_OUTS:]
    gate_o, up_o, down_o, out_o, *qkv_o = outs
    _, _, c = position()
    rows = a.shape[0]
    ff = gate.shape[1]
    width = gate_o.shape[0]
    inner = out.shape[0]
    rest = ff - (cut - ff)
    start = pl.multiple_of(((1 - c) if second else c) * rows, rows)
    at = pl.ds(start, rows)
    copies = Copies(sems)
    gate[...] = a[:, :ff].astype(F32)
    pending = [copies.start(gate, gate_o.at[at])]
    down[0] = b[:, rest : rest + width].astype(F32)
    pending.append(copies.start(down.at[0], down_o.at[at]))
    down[1] = b[:, rest + width : rest + 2 * width].astype(F32)
    pending.append(copies.start(down.at[1], down_o.at[pl.ds(pl.multiple_of(width + start, rows), rows)]))
    up[:, : cut - ff] = a[:, ff:cut].astype(F32)
    up[:, cut - ff :] = b[:, :rest].astype(F32)
    pending.append(copies.start(up, up_o.at[at]))
    late_a = a.shape[1] - cut
    late_b = b.shape[1] - LANES - (3 * inner - late_a)
    for i in range(3):
        lo, hi = i * inner, (i + 1) * inner
        mid = min(max(late_a, lo), hi)
        if mid > lo:
            qkv[i, :, : mid - lo] = a[:, cut + lo : cut + mid].astype(F32)
        if mid < hi:
            qkv[i, :, mid - lo :] = b[:, late_b + mid - late_a : late_b + hi - late_a].astype(F32)
        pending.append(copies.start(qkv.at[i], qkv_o[i].at[at]))
    out[...] = b[:, rest + 2 * width : rest + 2 * width + inner].astype(F32).T
    pending.append(copies.start(out, out_o.at[:, at]))
    if second:
        row = lax.broadcasted_iota(jnp.int32, (rows, 256), 0) % 16
        small = None
        for ref in (b_own, b):
            g = ref[:, late_b - 256 : late_b].astype(F32)
            turned = {t: pltpu.roll(g, rows - t, 0).astype(BF16) for t in range(1, 5)}
            for i in range(2):
                kept = jnp.where((row < 15) & (row % 5 == i), g, 0.0).T.astype(BF16)
                for j in range(3):
                    term = mm(kept, turned[2 + j - i])
                    place_ = (slice(i * 256, (i + 1) * 256), slice(j * 256, (j + 1) * 256))
                    if ref is b_own:
                        head[place_] = term
                    else:
                        head[place_] += term
            for r in range(0, rows, block):
                value = ref[r : r + 16, ref.shape[1] - LANES :].astype(F32)
                small = value if small is None else small + value
        pending.append(copies.start(head, head_o))
        for i in range(nf_o.shape[1] // LANES):
            nf_o[:, i * LANES : (i + 1) * LANES] = small[i : i + 1, :]
            na_o[:, i * LANES : (i + 1) * LANES] = small[4 + i : 5 + i, :]
        table_o[...] = small[8 : 8 + table_o.shape[0], : table_o.shape[1]]
    for copy in pending:
        copy.wait()


def sds(shape, dtype=BF16):
    return jax.ShapeDtypeStruct(shape, dtype)


def call(
    kernel, outs, args, scratch=(), specs=None, out_specs=None, flops=0, name=None, vmem=56, deps=(), aliases=None, overlap=False
):
    count, n_out = len(args), len(outs) if isinstance(outs, tuple) else 1
    specs = list(specs or [VMEM] * count)
    out_specs = list(out_specs or [VMEM] * n_out)
    out_list = list(outs) if isinstance(outs, tuple) else [outs]
    loads = [i for i in range(count) if overlap and specs[i] is VMEM]
    stores = [i for i in range(n_out) if overlap and out_specs[i] is VMEM]
    bufs = [pltpu.VMEM(args[i].shape, args[i].dtype) for i in loads] + [pltpu.VMEM(out_list[i].shape, out_list[i].dtype) for i in stores]
    if overlap:
        bufs.append(pltpu.SemaphoreType.DMA((len(loads) + len(stores),)))

    def body(*refs):
        ins, refs = list(refs[:count]), refs[count + len(deps) :]
        res, refs = list(refs[:n_out]), refs[n_out:]
        if overlap:
            bufs_, refs = refs[: len(bufs)], refs[len(bufs) :]
            copies = Copies(bufs_[-1])
            pending = []
            for i, buf in zip(loads, bufs_):
                pending.append(copies.start(ins[i], buf))
                ins[i] = buf
            out_refs = list(res)
            for i, buf in zip(stores, bufs_[len(loads) :]):
                res[i] = buf
            run = kernel(*ins, *res, *refs)
            if run is not None:
                next(run)
            for copy in pending:
                copy.wait()
            if run is not None:
                next(run, None)
        else:
            kernel(*ins, *res, *refs)
        if overlap:
            pending = [copies.start(res[i], out_refs[i]) for i in stores]
            for copy in pending:
                copy.wait()

    if overlap:
        specs = [ANY if s is VMEM else s for s in specs]
        out_specs = [ANY if s is VMEM else s for s in out_specs]
    return pl.pallas_call(
        body,
        out_shape=outs,
        in_specs=specs + [ANY] * len(deps),
        out_specs=tuple(out_specs) if isinstance(outs, tuple) else out_specs[0],
        scratch_shapes=bufs + list(scratch),
        compiler_params=pltpu.CompilerParams(vmem_limit_bytes=vmem * 2**20),
        cost_estimate=pl.CostEstimate(flops=flops, bytes_accessed=10_000_000, transcendentals=0),
        input_output_aliases=aliases or {},
        name=name,
    )(*args, *deps)


def swap(x, axis, k):
    n = lax.axis_size(axis)
    return lax.ppermute(x, axis, [(i, i ^ k) for i in range(n)])


def after(x, *deps):
    return lax.optimization_barrier((x, *deps))[0]


def together(*trees):
    leaves, shape = jax.tree.flatten(trees)
    return jax.tree.unflatten(shape, lax.optimization_barrier(leaves))


def row_digits():
    return [("rows", 1 << i, 2) for i in range(lax.axis_size("rows").bit_length() - 1)]


def shards(
    tokens, seg_ids, w_query, w_key, w_value, w_out, w_gate, w_up, w_down, w_head, norm_attn, norm_ffn,
    bucket_bias_table, grad_y, embedding_gradient,
):
    rows, span, width = tokens.shape
    buckets, heads = bucket_bias_table.shape
    n = lax.axis_size("seq")
    inner = w_query.shape[1]
    ff = w_gate.shape[1]
    wide = w_head.shape[1]
    length = n * span
    per = rows // 2
    assert n == 4 and per == 5
    slots = 3

    groups = ((0,), (1, 2))
    shapes = [(k, span + EXT, width) for slots in groups for k in (2 * len(slots) - (2 in slots), len(slots))]
    todo = sum(k for k, _, _ in shapes)
    y_a, c_a, y_b, c_b = call(
        functools.partial(pack_kernel, per, groups, EXT), tuple(sds(k) for k in shapes), (tokens, seg_ids),
        [pltpu.VMEM((todo, span + EXT, width), BF16), pltpu.SemaphoreType.DMA((2 * todo,))], [ANY, VMEM], (ANY,) * 4,
        vmem=60, name="pack", overlap=True,
    )

    def pass_on(got, *deps):
        near, far = got
        return near, far, swap(after(far, *deps) if deps else far, "seq", 1)

    line = 2 * length
    x_a = swap(c_a, "seq", 1), swap(y_a, "seq", 2)
    bias, ind, nattn, nffn, wqkv_t, wout_t, wg_t, wu_t, wd_t = call(
        functools.partial(prepare_kernel, n),
        (
            sds((heads, LANES, line), F32), sds((LANES, line)), sds((width, LANES), F32), sds((width, LANES), F32),
            sds((3 * inner, width)), sds((width, inner)), sds((ff, width)), sds((ff, width)),
            sds((width, ff)),
        ),
        (
            bucket_bias_table.T, norm_attn[None], norm_ffn[None], w_query, w_key, w_value, w_out, w_gate, w_up, w_down,
        ),
        [pltpu.VMEM((LANES, LANES), F32)], name="prepare", flops=4_000_000_000, overlap=True,
    )
    x_a, y_b, c_b, nattn = together(x_a, y_b, c_b, nattn)
    x_b = swap(c_b, "seq", 1), swap(y_b, "seq", 2)
    x_a = pass_on(x_a)

    def collect(own, c, y):
        return own, swap(c, "seq", 1), swap(y, "seq", 2)

    def collect_rest(part, *deps):
        return *part, swap(after(part[2], *deps), "seq", 1)

    def run_forward(kinds, pieces, before=(), deps=()):
        shapes = [s for _, half in kinds for s in forward_outs(half, n, span, width, inner, heads, ff)]
        had = len(before) and before[0].shape[0]
        shapes += [((k * (len(kinds) + had), span, width), BF16) for k in (1, 1, 2)]
        if not had:
            shapes += [((2 * slots - 1, span, width), BF16), ((slots, span, width), BF16)]
        outs = tuple(sds(*s) for s in shapes)
        args = [tokens, seg_ids, bias, wqkv_t, wout_t, wg_t, wu_t, wd_t, nattn, nffn]
        specs = [ANY, VMEM] + [ANY] * 6 + [VMEM] * 2
        args += [*pieces, *(before or (grad_y,))]
        specs += [VMEM] * 3 + [ANY] * (3 if had else 1)
        scratch = [pltpu.VMEM(*s) for s in shapes]
        scratch += [
            pltpu.VMEM((len(kinds), span, width), BF16), pltpu.VMEM((length, width), F32),
            pltpu.VMEM((len(kinds), LANES, length), F32), pltpu.VMEM((len(kinds), width, length), BF16),
            pltpu.VMEM((heads, length, 2 * LANES), BF16), pltpu.VMEM((heads, inner // heads + EXT, length), BF16),
            pltpu.VMEM((len(kinds), width, length), BF16),
            pltpu.VMEM((2, length, length), F32), pltpu.VMEM(bias.shape, F32), *[pltpu.VMEM(w.shape, BF16) for w in (wqkv_t, wout_t, wg_t, wu_t, wd_t)],
            pltpu.SemaphoreType.DMA((12 + len(kinds) + 3 * slots,)), pltpu.SemaphoreType.DMA((24 * len(kinds) + 6,)),
        ]
        res = call(
            functools.partial(forward_kernel, kinds, n, per, heads), outs, args, scratch, specs, tuple(ANY for _ in outs),
            4_000_000_000 * len(kinds), "forward", deps=deps, overlap=True,
        )
        count = len(FORWARD_OUTS)
        at = count * len(kinds)
        rows_ = [dict(zip(FORWARD_OUTS, res[i * count : (i + 1) * count])) for i in range(len(kinds))]
        return rows_, res[at : at + 3], res[at + 3 :]

    fwd, blocks, packed_g = run_forward([(0, False)], x_a, deps=(y_b, c_b))
    x_b = pass_on(x_b, fwd[0]["r"])
    gys = swap(packed_g[1], "seq", 1), swap(packed_g[0], "seq", 2)
    fwd_b, blocks, _ = run_forward([(1, False), (2, True)], x_b, blocks, deps=packed_g)
    blocks = collect(*blocks)
    fwd += fwd_b
    gys = pass_on(gys, fwd[1]["r"])
    pool_other = swap(fwd[2]["pool"], "seq", 1)

    def unpack(parts, with_emb, deps=()):
        args = [a for group in parts for a in group]
        outs = (sds((rows, span, width)),) + ((sds((rows, wide), F32),) if with_emb else ())
        scratch = [pltpu.VMEM((rows, EXT, width), BF16)] if with_emb else []
        return call(
            functools.partial(unpack_kernel, per, with_emb), outs, args, scratch + [pltpu.SemaphoreType.DMA((2 * rows,))],
            [ANY] * len(args), (ANY, VMEM)[: len(outs)], vmem=16, name="unpack", deps=deps,
        )


    packed_w = 2 * ff + 2 * width + inner
    nqs = [length, length, length // 2]
    args = [grad_y, embedding_gradient, w_head, w_down, w_gate, w_up, w_out, nffn, pool_other]
    specs = [ANY, VMEM] + [ANY] * 5 + [VMEM] * 2
    args += list(gys)
    specs += [VMEM] * 3
    for f in fwd:
        args += [f[k] for k in ("mid", "a", "ge", "hid", "att", "seg", "r", "pool")]
        specs += [ANY] * 5 + [VMEM] * 3
    outs = tuple(
        [sds((width, q)) for q in nqs] + [sds((inner, q)) for q in nqs]
        + [sds((width // 2, packed_w))] * 2 + [sds((8, width), F32), sds((3, 8, wide), F32), sds((16, 256), F32)]
    )
    scratch = []
    for q in nqs:
        scratch += [pltpu.VMEM((width, q), F32), pltpu.VMEM((ff, q), BF16), pltpu.VMEM((ff, q), BF16)]
    total = sum(nqs)
    scratch += [
        pltpu.VMEM((3, span, width), BF16), pltpu.VMEM((2, width, length), F32), pltpu.VMEM((3, width, length), BF16),
        pltpu.VMEM((width, LANES), F32), pltpu.VMEM((width, total), BF16), pltpu.VMEM((width, total), BF16),
        pltpu.VMEM((ff, total), BF16), pltpu.VMEM((ff, total), BF16), pltpu.VMEM((width, total), BF16),
        pltpu.VMEM((inner, total), BF16), pltpu.VMEM((ff, total), BF16), pltpu.VMEM((2, width // 2, packed_w), BF16), pltpu.VMEM((inner, total), BF16),
        *[pltpu.VMEM(w.shape, BF16) for w in (w_head, w_down, w_gate, w_up, w_out)],
        pltpu.SemaphoreType.DMA((23,)), pltpu.SemaphoreType.DMA((14,)),
    ]
    m = call(functools.partial(middle_kernel, n, per), outs, args, scratch, specs, [ANY] * 8 + [VMEM] * 3, flops=15_000_000_000, name="middle", overlap=True)
    m, blocks = together(m, blocks)
    ga, gt = m[:3], m[3:6]
    own, send, gnf, emb, pg = m[6:]

    core = ("seq", 1, 2)
    far = ("seq", 2, 2)
    digits = row_digits()
    block = width // 2 // far[2]
    for d in digits:
        block //= d[2]

    def send_shares(parts, s):
        return [swap(p, s[0], k * s[1]) for k, p in enumerate(parts) if k]

    def send_all(v, s):
        return [swap(v, s[0], k * s[1]) for k in range(1, s[2])]

    def combine(groups, deps=()):
        args, outs, scratch, plan = [], [], [], []
        for pieces, step in groups:
            rows_, wide_ = pieces[0][0][0].shape[0], sum(hi - lo for _, lo, hi in pieces)
            radix = step[2] if step else 1
            shape = (radix, rows_ // radix) if step else (rows_,)
            for arrays, _, _ in pieces:
                args += [a.reshape(shape + a.shape[-1:]) for a in arrays]
            outs += [sds((rows_ // radix, wide_))] * radix
            scratch += [pltpu.VMEM(shape + (wide_,), BF16)] if step else []
            plan.append((pieces, step))
        plan = [([(range(len(a)), lo, hi) for a, lo, hi in pieces], step) for pieces, step in plan]
        res = call(functools.partial(combine_kernel, plan), tuple(outs), args, scratch, vmem=24, name="combine", deps=deps)
        out = []
        for _, step in plan:
            radix = step[2] if step else 1
            out.append(list(res[:radix]))
            res = res[radix:]
        return out

    def joined(groups, deps=()):
        args, outs, plan = [], [], []
        for v, got, step, cuts in groups:
            cuts = cuts or [(0, v.shape[1])]
            args += [v] + got
            outs += [sds((step[2], v.shape[0], hi - lo)) for lo, hi in cuts]
            plan.append((step, cuts))
        res = call(functools.partial(join_kernel, plan), tuple(outs), args, vmem=24, name="join", deps=deps)
        return [r.reshape(-1, r.shape[-1]) for r in res]

    def all_of(*arrays):
        return [(list(arrays), 0, arrays[0].shape[1])]

    nh = length // 2
    half = call(
        functools.partial(half_back_kernel, n),
        (sds((inner, nh)), sds((2 * inner, nh)), sds((2 * inner, nh)), sds((8, line), F32)),
        (fwd[2]["q"], fwd[2]["v"], fwd[2]["kt"], fwd[2]["e"], fwd[2]["att"], gt[2]),
        [
            pltpu.VMEM((heads, length, nh), BF16), pltpu.VMEM((2, length, nh), BF16), pltpu.VMEM((2, LANES, 4 * LANES), F32),
            pltpu.VMEM((2, length, LANES), F32), pltpu.VMEM((2 * inner, length), BF16), pltpu.SemaphoreType.DMA((heads,)),
        ],
        [VMEM] * 3 + [ANY] + [VMEM] * 2, flops=2_000_000_000, name="half_back", deps=(send,), overlap=True,
    )
    got = swap(send, "seq", 1)
    block_parts = [collect_rest(blocks)]
    half, got, block_parts = together(half, got, block_parts)
    gq_half, keep, send_kv, lines_sum = half
    got_kv = swap(send_kv, "seq", 1)
    cut = packed_w // 2 // LANES * LANES
    sa, sb = [digits[0], far], [far, digits[0]]
    pa, pb = combine([([([own, got], 0, cut)], sa[0]), ([([own, got], cut, packed_w)], sb[0])])

    piece = tuple(sds((i, span + EXT, width)) for i in (1, 1, 2))

    def run_back(j, lines_sum, part, deps, extra=()):
        f = fwd[j]
        scratch = [
            pltpu.VMEM((3 * inner, length), BF16), pltpu.VMEM((heads, length, length), BF16),
            pltpu.VMEM((2, length, length), BF16), pltpu.VMEM((2, LANES, 4 * LANES), F32), pltpu.VMEM((2, length, LANES), F32), pltpu.VMEM((width, length), F32),
            pltpu.VMEM((width, length), BF16), pltpu.VMEM((width, length), BF16), pltpu.VMEM((width, 3 * inner), BF16),
            pltpu.VMEM((width, LANES), F32), pltpu.SemaphoreType.DMA((heads // 2 + 14,)),
        ]
        late_outs = ()
        if extra:
            late_outs = (sds((width // 2, 3 * inner)), sds((width // 2, 3 * inner)), sds((3 * inner, nh)))
            scratch += [pltpu.VMEM((width, q), BF16) for q in nqs]
            scratch += [pltpu.VMEM((3 * inner, length), BF16), pltpu.VMEM((2, width // 2, 3 * inner), BF16)]
        res = call(
            functools.partial(backward_kernel, j, n),
            (*late_outs, sds((8, line), F32), sds((3 * inner, length)), *piece, sds((width, LANES), F32)),
            (f["q"], f["v"], f["kt"], f["e"], f["att"], gt[j], lines_sum, f["x"], ga[j], w_query, w_key, w_value, nattn, emb, part, *extra),
            scratch, [VMEM] * 3 + [ANY] + [VMEM] * 3 + [ANY] * 5 + [VMEM] * 3 + ([ANY] + [VMEM] * 3 + [ANY] * 3 if extra else []),
            ([ANY] * 2 + [VMEM] if extra else []) + [VMEM, ANY] + [VMEM] * 4, flops=4_000_000_000, name="backward", deps=deps, overlap=True,
        )
        late, (line_o, gq, *blocks, part) = res[: len(late_outs)], res[len(late_outs) :]
        return line_o, gq, blocks, part, late

    back = run_back(0, lines_sum, nattn, (pa[1], pb[1]))
    ra, rb = send_shares(pa, sa[0]), send_shares(pb, sb[0])
    back, ra, rb, got_kv = together(back, ra, rb, got_kv)
    pa, pb = combine([(all_of(pa[0], *ra), sa[1]), (all_of(pb[0], *rb), sb[1])])
    back2 = run_back(
        1, back[0], back[3], (pa[1], pb[1]), (back[1], gq_half, keep, got_kv, *[f["n1"] for f in fwd])
    )
    ra, rb = send_shares(pa, sa[1]), send_shares(pb, sb[1])
    back2, ra, rb = together(back2, ra, rb)
    late_own, late_send, gq2 = back2[4]

    late_got = swap(late_send, "seq", 1)
    (parts,) = combine([(all_of(pa[0], *ra) + all_of(pb[0], *rb), digits[1])])
    z_got = send_shares(parts, digits[1])
    x_b = collect(*back2[2])
    late_cut = 2 * inner
    la, lb = combine([([([late_own, late_got], 0, late_cut)], sa[0]), ([([late_own, late_got], late_cut, 3 * inner)], sb[0])])
    lga, lgb = send_shares(la, sa[0]), send_shares(lb, sb[0])
    late_sends = (la[1], lb[1])
    for step in digits[2:]:
        (parts,) = combine([(all_of(parts[0], *z_got), step)], deps=late_sends)
        z_got = send_shares(parts, step)
        late_sends = ()
    lga, lgb = together(lga, lgb)
    la, lb = combine([(all_of(la[0], *lga), sa[1]), (all_of(lb[0], *lgb), sb[1])])
    lga, lgb = send_shares(la, sa[1]), send_shares(lb, sb[1])
    *x_c, small = call(
        inputs_kernel, (*piece, sds((width // 8, LANES), F32)),
        (gq2, fwd[2]["x"], ga[2], w_query, w_key, w_value, nattn, emb, back2[3], back2[0], gnf, ind),
        [pltpu.VMEM((width, nh), F32), pltpu.VMEM((width, LANES), F32), pltpu.VMEM((width, 3 * inner), BF16)],
        flops=3_000_000_000, name="inputs", vmem=16,
        deps=tuple(parts[1:]) + (la[1], lb[1]),
    )
    pg_b = pg.astype(BF16).reshape(block, -1)
    ((ab,),) = combine([(all_of(parts[0], *z_got) + all_of(pg_b), None)], deps=(la[1], lb[1]))
    ab_got = send_all(ab, digits[-1])
    lga, lgb, x_c, small, x_b = together(lga, lgb, x_c, small, x_b)
    x_a = collect(*back[2])
    x_c = collect(*x_c)
    ((late,),) = combine([(all_of(la[0], *lga) + all_of(lb[0], *lgb) + all_of(small), None)], deps=(ab,))
    strides = digits[1:]
    for step, back_step in zip(strides[:-1], strides[:0:-1]):
        late_got = swap(late, *step[:2])
        x_b = collect_rest(x_b) if len(x_b) == 3 else x_b
        ((late,),) = combine([(all_of(late, late_got), None)])
        (ab,) = joined([(ab, ab_got, back_step, None)], deps=(late,))
        ab_got = send_all(ab, digits[digits.index(back_step) - 1])
    late_got = swap(late, *strides[-1][:2])
    (block_out,) = unpack(block_parts, False, deps=(late,))
    late_got, ab_got, block_out, x_a, x_b, x_c = together(late_got, ab_got, block_out, x_a, x_b, x_c)
    wide_a, wide_b = cut + late_cut, ab.shape[1] - cut + late.shape[1] - late_cut
    a, b = call(
        functools.partial(merge_kernel, digits[1], cut, late_cut),
        (sds((2, ab.shape[0], wide_a)), sds((2, ab.shape[0], wide_b))), (ab, *ab_got, late, late_got), vmem=24, name="merge",
    )
    a, b = a.reshape(-1, wide_a), b.reshape(-1, wide_b)
    ga_, gb_ = send_all(a, sa[1]), send_all(b, sb[1])
    x_a = collect_rest(x_a)
    x_c = collect_rest(x_c)
    ga_, gb_, x_a, x_c = together(ga_, gb_, x_a, x_c)
    a, b = joined([(a, ga_, sa[1], None), (b, gb_, sb[1], None)])
    ga_, gb_ = send_all(a, sa[0]), send_all(b, sb[0])
    grad_x, embedding = unpack([x_a, x_b, x_c], True, deps=(a, b))
    ga_, gb_, grad_x = together(ga_, gb_, grad_x)
    a, b = joined([(a, ga_, sa[0], None), (b, gb_, sb[0], None)])
    a_got, b_got = swap(a, "seq", 1), swap(b, "seq", 1)
    outs = (
        sds((width, ff), F32), sds((width, ff), F32), sds((ff, width), F32), sds((inner, width), F32),
        *[sds((width, inner), F32)] * 3,
    )
    halves = [
        pltpu.VMEM((width // 2, ff), F32), pltpu.VMEM((width // 2, ff), F32), pltpu.VMEM((2, width // 2, width), F32),
        pltpu.VMEM((inner, width // 2), F32), pltpu.VMEM((3, width // 2, inner), F32),
    ]
    first = call(
        functools.partial(finish_kernel, False, cut, width // 8), outs, (a, b), halves + [pltpu.SemaphoreType.DMA((9,))],
        out_specs=(ANY,) * FINISH_OUTS, name="finish", vmem=24,
    )
    first, a_got, b_got = together(first, a_got, b_got)
    *grads, grad_head, grad_norm_ffn, grad_norm_attn, grad_table = call(
        functools.partial(finish_kernel, True, cut, width // 8),
        outs + (sds((width, wide), F32), sds((1, width), F32), sds((1, width), F32), sds((heads, buckets), F32)),
        (b, a_got, b_got, *first), halves + [pltpu.VMEM((width, wide), F32), pltpu.SemaphoreType.DMA((9,))],
        [VMEM] * 3 + [ANY] * FINISH_OUTS, (ANY,) * (FINISH_OUTS + 1) + (VMEM,) * 3, name="finish", vmem=24,
        aliases={3 + i: i for i in range(FINISH_OUTS)},
    )
    if block != 16:
        lo, hi = packed_w - cut, ab.shape[1] - cut
        pg_all = jnp.concatenate([b[:, lo:hi], b_got[:, lo:hi]]).reshape(-1, 16, 256)[:, :15].reshape(-1, width + wide)
        grad_head = lax.dot_general(
            pg_all[:, :width], pg_all[:, width:], (((0,), (0,)), ((), ())), preferred_element_type=F32
        )
    grad_gate, grad_up, grad_down, grad_out, grad_query, grad_key, grad_value = grads
    return (
        block_out, embedding, grad_x, grad_query, grad_key, grad_value, grad_out, grad_gate, grad_up, grad_down, grad_head,
        grad_norm_attn[0], grad_norm_ffn[0], grad_table.T,
    )


def solution(mesh):
    by_pos = P("rows", "seq", None)
    by_row = P("rows", None)
    return jax.shard_map(
        shards,
        mesh=mesh,
        in_specs=(by_pos, P("rows", "seq"), *[P()] * 11, by_pos, by_row),
        out_specs=(by_pos, by_row, by_pos, *[P()] * 11),
        check_vma=False,
    )
```

```python
import functools

import jax
import jax.numpy as jnp
from jax import lax
from jax.experimental import pallas as pl
from jax.experimental.pallas import tpu as pltpu
from jax.sharding import PartitionSpec as P

EPS = 1e-06
LIMITS = (12, 16, 23, 32, 46, 64, 91)
TOP_PRECISION = lax.Precision.HIGHEST
F32 = jnp.float32
BF16 = jnp.bfloat16
MASK_STEP = 2.0**30
LOG2E = 1.4426950408889634
VMEM = pl.BlockSpec(memory_space=pltpu.VMEM)
ANY = pl.BlockSpec(memory_space=pl.ANY)
LANES = 128
EXT = 16


def mm(a, b):
    return lax.dot_general(a, b, (((1,), (0,)), ((), ())), preferred_element_type=F32)


def mm_nt(a, b):
    return lax.dot_general(a, b, (((1,), (1,)), ((), ())), preferred_element_type=F32)


def bucket_index(offset):
    distance = jnp.abs(offset)
    far_bucket = 8 + sum(((distance >= threshold).astype(jnp.int32) for threshold in LIMITS))
    near_bucket = jnp.where(distance < 8, distance, far_bucket)
    return near_bucket + 16 * (offset > 0).astype(jnp.int32)


def wide_dots(rows, mat, dot):
    at = lax.broadcasted_iota(jnp.int32, (16, rows[0].shape[1]), 0)
    lhs = jnp.zeros(at.shape, F32)
    for i, v in enumerate(rows):
        for j in range(3):
            part = v.astype(BF16).astype(F32)
            lhs = jnp.where(at == 3 * i + j, part, lhs)
            v = v - part
    out = dot(lhs.astype(BF16), mat)
    return [jnp.sum(out[3 * i : 3 * i + 3], axis=0, keepdims=True) for i in range(len(rows))]


def fold(x, op):
    while x.shape[0] > 8:
        half = x.shape[0] // 2
        x = op(x[:half], x[half:])
    return x


def col_sum(x):
    return jnp.sum(fold(x, jnp.add), axis=0, keepdims=True)


def diagonal_sums(table):
    height, width = table.shape
    acc = table[0:8, :]
    for u in range(8, height, 8):
        acc += pltpu.roll(table[u : u + 8, :], width - u, 1)
    row = lax.broadcasted_iota(jnp.int32, acc.shape, 0)
    for bit in (1, 2, 4):
        acc = jnp.where((row & bit) != 0, pltpu.roll(acc, width - bit, 1), acc)
    return jnp.sum(acc, axis=0, keepdims=True)


def position():
    me = lax.axis_index("seq")
    return me, me // 2, me % 2


class Copies:
    def __init__(self, sems):
        self.sems = sems
        self.used = 0

    def start(self, src, dst):
        copy = pltpu.make_async_copy(src, dst, self.sems.at[self.used])
        self.used += 1
        copy.start()
        return copy


def rows_to_send(per, slots):
    _, p, c = position()
    todo = []
    for i, j in enumerate(slots):
        if j == 2:
            todo += [(0, 2 * i, per * (1 - p) + per - 1), (1, i, per * p + per - 1)]
        else:
            todo.append((0, 2 * i, per * (1 - p) + 2 * c + j))
            todo.append((0, 2 * i + 1, per * (1 - p) + 2 * (1 - c) + j))
            todo.append((1, i, per * p + 2 * (1 - c) + j))
    return todo


def pack_kernel(per, groups, ext, tok, seg, *refs):
    outs, (buf, sems) = refs[:-2], refs[-2:]
    span = tok.shape[1]
    copies = Copies(sems)
    todo = [(2 * g, *t) for g, slots in enumerate(groups) for t in rows_to_send(per, slots)]
    loads = [copies.start(tok.at[row], buf.at[k, pl.ds(0, span)]) for k, (_, _, _, row) in enumerate(todo)]
    yield
    for k, (_, _, _, row) in enumerate(todo):
        value = jnp.broadcast_to(seg[pl.ds(row, 1), :].astype(F32), (ext, span)).astype(BF16)
        buf[k, span:, :] = jnp.concatenate([value] * (tok.shape[2] // span), axis=1)
    stores = []
    for k, (at, which, i, _) in enumerate(todo):
        loads[k].wait()
        stores.append(copies.start(buf.at[k], outs[at + which].at[i]))
    for copy in stores:
        copy.wait()


def prepare_kernel(
    n, table, norm_a, norm_f, wq, wk, wv, wo, wg, wu, wd,
    bias_o, ind_o, na_o, nf_o, wqkv_t, wo_t, wg_t, wu_t, wd_t,
    square,
):
    yield
    heads, _, line = bias_o.shape
    inner = wq.shape[1]
    length = line // 2
    col = lax.broadcasted_iota(jnp.int32, (LANES, line), 1)
    offset = length - LANES - jnp.where(col < line - LANES, col, col - line)
    ind = (bucket_index(offset) == lax.broadcasted_iota(jnp.int32, (LANES, line), 0)).astype(F32).astype(BF16)
    ind_o[...] = ind
    square[...] = jnp.zeros_like(square)
    square[: table.shape[0], : table.shape[1]] = table[...]
    rest = square[:8, :]
    lines = None
    for _ in range(3):
        part = rest.astype(BF16)
        rest = rest - part.astype(F32)
        term = mm(part, ind)
        lines = term if lines is None else lines + term
    lines = lines * LOG2E
    for h in range(heads):
        bias_o[h] = pltpu.roll(jnp.broadcast_to(lines[h : h + 1, :], (LANES, line)), 0, 1, stride=1, stride_axis=0)
    for src, dst in ((norm_a, na_o), (norm_f, nf_o)):
        dst[...] = jnp.broadcast_to(src[...], (LANES, src.shape[1])).T
    for i, w in enumerate((wq, wk, wv)):
        wqkv_t[i * inner : (i + 1) * inner, :] = w[...].T
    wo_t[...] = wo[...].T
    size = 256
    one = lax.broadcasted_iota(jnp.int32, (size, size), 0) == lax.broadcasted_iota(jnp.int32, (size, size), 1)
    one = one.astype(F32).astype(BF16)
    for src, dst in ((wg, wg_t), (wu, wu_t), (wd, wd_t)):
        for at in range(0, dst.shape[0], size):
            dst[at : at + size, :] = mm_nt(one, src[:, at : at + size]).astype(BF16)


STEP = 32


def chunks(height):
    return [slice(r, r + STEP) for r in range(0, height, STEP)]


def norm_into(out, src, cols, gain):
    total = None
    for r in chunks(src.shape[0]):
        x = src[r, cols].astype(F32)
        x = fold(x * x, jnp.add)
        total = x if total is None else total + x
    inv = lax.rsqrt(jnp.sum(total, axis=0, keepdims=True) / src.shape[0] + EPS)
    for r in chunks(src.shape[0]):
        out[r, cols] = (src[r, cols].astype(F32) * inv * gain[r, :]).astype(BF16)


def forward_slot(half, n, rows, bufs, w, wait, outs, copies):
    own, c1, y, c2, own_seg = rows
    tok, seg, n1, kk, va, x_b, s_buf = bufs
    bias, wqkv_t, wout_t, wg_t, wu_t, wd_t, nattn, nffn = w
    o = outs
    width = wqkv_t.shape[1]
    inner = wout_t.shape[1]
    heads = bias.shape[0]
    head = inner // heads
    span = own.shape[0]
    length = n * span
    me, p, c = position()
    for k, (piece, ids) in enumerate(((own, own_seg), (c1, None), (y, None), (c2, None))):
        at = pl.multiple_of((me ^ k) * span, span)
        x_b[:, pl.ds(at, span)] = piece[:span, :].T
        ids = piece[span : span + EXT, :span].astype(F32)[0:1, :] if ids is None else ids
        seg[:, pl.ds(at, span)] = jnp.broadcast_to(ids, (LANES, span))
    for b in range(n):
        norm_into(n1, x_b, slice(b * span, (b + 1) * span), nattn)
    nq = length // 2 if half else length
    if half:
        mine = pl.ds(pl.multiple_of(c * nq, nq), nq)
        o["x"][...] = x_b[:, mine]
        o["n1"][...] = n1[:, mine]
    else:
        mine = slice(0, nq)
        o["x"][...] = x_b[...]
        o["n1"][...] = n1[...]
    o["seg"][...] = seg[0:8, :]
    ids = lax.broadcasted_iota(jnp.int32, (LANES, length), 0).astype(F32)
    one = (seg[...] == ids).astype(F32)
    k_aug = ((one - 1.0) * MASK_STEP).T.astype(BF16)
    ids = lax.broadcasted_iota(jnp.int32, (LANES, nq), 0).astype(F32)
    q_aug = (seg[:, mine] == ids).astype(BF16)
    wait("qkv")
    if half:
        qt = mm(wqkv_t[:inner, :], n1[:, mine]).astype(BF16)
        kvt = mm(wqkv_t[inner:, :], n1[...]).astype(BF16)
        kt, vt = kvt[:inner], kvt[inner:]
    else:
        qkvt = mm(wqkv_t[...], n1[...]).astype(BF16)
        qt, kt, vt = qkvt[:inner], qkvt[inner : 2 * inner], qkvt[2 * inner :]
    o["kt"][...] = kt
    q2 = qt.astype(F32) * LOG2E
    q_hi = q2.astype(BF16)
    q_lo = (q2 - q_hi.astype(F32)).astype(BF16)
    lane = lax.broadcasted_iota(jnp.int32, (length, LANES), 1)

    def pair_ready(pair):
        ps = slice(pair * LANES, (pair + 1) * LANES)
        both = kt[ps].T.astype(F32)
        turned = pltpu.roll(both, head, 1)
        kk[2 * pair, :, :LANES] = jnp.where(lane < head, both, turned).astype(BF16)
        kk[2 * pair + 1, :, :LANES] = jnp.where(lane < head, turned, both).astype(BF16)
        for h in (2 * pair, 2 * pair + 1):
            kk[h, :, LANES:] = k_aug
            va[h, :head, :] = vt[h * head : (h + 1) * head]
            va[h, head:, :] = jnp.ones((EXT, length), BF16)

    def naturals(pair):
        ps = slice(pair * LANES, (pair + 1) * LANES)
        o["q"][:, ps] = qt[ps].T
        o["v"][:, ps] = vt[ps].T

    chunk = nq
    work = [(h, qc) for h in range(heads) for qc in range(nq // chunk)]
    per_pair = 2 * (nq // chunk)

    def lanes_of(qc):
        return slice(qc * chunk, (qc + 1) * chunk)

    def score(i, a, rhs):
        h, qc = work[i]
        if half:
            at = pl.ds(pl.multiple_of((n - 1 - a) * LANES + c * nq, LANES), chunk)
        else:
            at = pl.ds((n - 1 - a) * LANES + qc * chunk, chunk)
        s_a = mm(kk[h, a * LANES : (a + 1) * LANES, :], rhs) + bias[h, :, at]
        s_buf[i % 2, a * LANES : (a + 1) * LANES, :chunk] = s_a
        return fold(s_a, jnp.maximum)

    def power(i, a, top):
        h, qc = work[i]
        e = jnp.exp2(s_buf[i % 2, a * LANES : (a + 1) * LANES, :chunk] - top)
        o["e"][h, a * LANES : (a + 1) * LANES, lanes_of(qc)] = e.astype(BF16)

    def attend(i):
        h, qc = work[i]
        hs, qs = slice(h * head, (h + 1) * head), lanes_of(qc)
        raw = mm(va[h], o["e"][h, :, qs])
        inv = 1.0 / raw[head : head + 1, :]
        o["r"][h : h + 1, qs] = inv
        o["att"][hs, qs] = (raw[:head, :] * inv).astype(BF16)

    pair_ready(0)
    wait("bias")
    copies(o["x"], o["seg"], o["n1"], o["kt"])
    top = None
    for i in range(len(work) + 1):
        if i == len(work) // 2:
            wait("rest")
            o["through"]()
            copies(*[(o["e"], h) for h in range(heads // 2 - 1)])
        tops = []
        if i < len(work):
            h, qc = work[i]
            hs, qs = slice(h * head, (h + 1) * head), lanes_of(qc)
            rhs = jnp.concatenate([q_hi[hs, qs], q_lo[hs, qs], q_aug[:, qs]], axis=0)
        for a in range(n):
            if i < len(work):
                tops.append(score(i, a, rhs))
            if i > 0:
                power(i - 1, a, top)
        if i < len(work):
            top = jnp.max(functools.reduce(jnp.maximum, tops), axis=0, keepdims=True)
            if i % per_pair == 0 and i // per_pair < heads // 2 - 1:
                pair_ready(i // per_pair + 1)
            if i % per_pair == 1:
                naturals(i // per_pair)
        if i > 0:
            attend(i - 1)
    if half:
        x_q = x_b[:, mine].astype(F32)
    else:
        x_q = x_b[...].astype(F32)
    o["mid"][...] = x_q + mm(wout_t[...], o["att"][...])
    for b in range(nq // span):
        norm_into(n1, o["mid"], slice(b * span, (b + 1) * span), nffn)
    ff = wg_t.shape[0]
    step = 256
    for b in range(ff // step):
        cs = slice(b * step, (b + 1) * step)
        gate = mm(wg_t[cs, :], n1[:, :nq])
        up = mm(wu_t[cs, :], n1[:, :nq])
        sq = gate * gate
        th = jnp.tanh(gate * (0.7978845608028654 + (0.7978845608028654 * 0.044715) * sq))
        half_th = 0.5 + 0.5 * th
        gelu = gate * half_th
        slope = half_th + (gelu - gelu * th) * (0.7978845608028654 + (3 * 0.7978845608028654 * 0.044715) * sq)
        o["hid"][cs, :] = (gelu * up).astype(BF16)
        o["a"][cs, :] = (up * slope).astype(BF16)
        o["ge"][cs, :] = gelu.astype(BF16)
    copies(*[(o["e"], h) for h in range(heads // 2 - 1, heads)])
    copies(*[o[k] for k in ("r", "att", "q", "v", "mid", "hid", "a", "ge")])
    res = tok.at[:, :nq]
    res[...] = o["mid"][...] + mm(wd_t[...], o["hid"][...])
    valid = (seg[0:1, mine] != 0.0).astype(F32)
    parts = []
    for r in chunks(width):
        part = None
        for b in range(nq // span):
            blk = res[r, b * span : (b + 1) * span] * valid[:, b * span : (b + 1) * span]
            part = blk if part is None else part + blk
        parts.append(part)
    o["pool"][...] = jnp.broadcast_to(col_sum(jnp.concatenate(parts, axis=0).T), o["pool"].shape)
    send_blocks(half, res, o["blocks"], span)


def send_blocks(half, res, outs, span):
    me, _, c = position()
    for k, out in enumerate(outs):
        block = (c + k) % 2 if half else me ^ k
        at = pl.multiple_of(block * span, span)
        out[:span, :] = res[:, pl.ds(at, span)].astype(BF16).T


FORWARD_OUTS = ("kt", "q", "v", "x", "seg", "e", "r", "att", "mid", "hid", "a", "ge", "pool", "n1")


def forward_outs(half, n, span, width, inner, heads, ff):
    length = n * span
    nq = length // 2 if half else length
    shapes = (
        ((inner, length), BF16), ((nq, inner), BF16), ((length, inner), BF16), ((width, nq), BF16), ((8, length), F32),
        ((heads, length, nq), BF16), ((8, nq), F32), ((inner, nq), BF16), ((width, nq), F32), ((ff, nq), BF16),
        ((ff, nq), BF16), ((ff, nq), BF16), ((8, width), F32), ((width, nq), BF16),
    )
    return shapes


def forward_kernel(kinds, n, per, heads, *refs):
    yield
    count = len(FORWARD_OUTS)
    tokens, seg_ids, bias, wqkv_t, wout_t, wg_t, wu_t, wd_t, nattn, nffn = refs[:10]
    near, far, again = refs[10:13]
    had = 0 if kinds[0][0] == 0 else 1
    before = refs[13 : 16 if had else 14]
    at = 16 if had else 14
    outs = [refs[at + i * count : at + (i + 1) * count] for i in range(len(kinds))]
    at += count * len(kinds)
    extra = 3 if had else 5
    block_outs = refs[at : at + extra]
    at += extra
    bufs = [refs[at + i * count : at + (i + 1) * count] for i in range(len(kinds))]
    at += count * len(kinds)
    blocks = refs[at : at + extra]
    at += extra
    own, tok, seg, n1, kk, va, x_b, s_buf, bias_b, wqkv_b, wout_b, wg_b, wu_b, wd_b, in_sems, out_sems = refs[at:]
    me, p, c = position()
    ins = Copies(in_sems)
    owns = []
    for i, (slot, half) in enumerate(kinds):
        row = per * p + (per - 1 if half else 2 * c + slot)
        owns.append((ins.start(tokens.at[row], own.at[i]), row))
    waits = {
        "qkv": [ins.start(wqkv_t, wqkv_b)],
        "bias": [ins.start(bias, bias_b)],
    }
    through = []

    def start_rest():
        pairs = ((wout_t, wout_b), (wg_t, wg_b), (wu_t, wu_b), (wd_t, wd_b))
        waits["rest"] = [ins.start(a, b) for a, b in pairs]
        if had:
            through.extend(ins.start(a, b.at[pl.ds(0, a.shape[0])]) for a, b in zip(before, blocks))
        else:
            todo = rows_to_send(per, (0, 1, 2))
            through.extend(ins.start(before[0].at[row], blocks[3 + which].at[i]) for which, i, row in todo)

    if had:
        start_rest()

    def wait(what):
        for copy in waits.pop(what, ()):
            copy.wait()
        if what == "qkv" and not had:
            start_rest()

    writes = Copies(out_sems)
    pending = []
    def pass_through():
        while through:
            through.pop().wait()
            if not through:
                if had:
                    pending.extend(writes.start(b.at[pl.ds(0, a.shape[0])], o.at[pl.ds(0, a.shape[0])]) for a, b, o in zip(before, blocks, block_outs))
                else:
                    pending.extend(writes.start(b, o) for b, o in zip(blocks[3:], block_outs[3:]))

    for copy, _ in owns:
        copy.wait()
    deferred = []

    def flush():
        while deferred:
            deferred.pop(0)()

    for i, (slot, half) in enumerate(kinds):
        row = owns[i][1]
        o = dict(zip(FORWARD_OUTS, bufs[i]))
        dst = dict(zip(FORWARD_OUTS, outs[i]))
        b = had + i
        o["blocks"] = (blocks[0].at[b], blocks[1].at[b], blocks[2].at[2 * b], blocks[2].at[2 * b + 1])
        o["through"] = pass_through
        names = {id(v): k for k, v in o.items()}

        def copies(*what, o=o, dst=dst, names=names):
            flush()
            for item in what:
                if isinstance(item, tuple):
                    ref, h = item
                    pending.append(writes.start(ref.at[h], dst[names[id(ref)]].at[h]))
                else:
                    pending.append(writes.start(item, dst[names[id(item)]]))

        c1, y_mine, c2_mine = near.at[i], far.at[2 * i], again.at[2 * i + (not half)]
        own_seg = seg_ids[pl.ds(row, 1), :].astype(F32)
        forward_slot(
            half, n, (own.at[i], c1, y_mine, c2_mine, own_seg), (tok, seg.at[i], n1.at[i], kk, va, x_b.at[i], s_buf),
            (bias_b, wqkv_b, wout_b, wg_b, wu_b, wd_b, nattn, nffn), wait, o, copies,
        )
        def ends(o=o, dst=dst, b=b):
            pending.append(writes.start(o["pool"], dst["pool"]))
            pending.append(writes.start(blocks[0].at[b], block_outs[0].at[b]))
            pending.append(writes.start(blocks[1].at[b], block_outs[1].at[b]))
            pending.append(writes.start(blocks[2].at[pl.ds(2 * b, 2)], block_outs[2].at[pl.ds(2 * b, 2)]))

        deferred.append(ends)
    flush()
    for copy in pending:
        copy.wait()


def middle_kernel(n, per, *refs):
    yield
    grad_y, eg, w_head, w_down, w_gate, w_up, w_out, nffn, pool_other = refs[:9]
    at = 9
    near, far, again = refs[at : at + 3]
    at += 3
    names = ("mid", "a", "ge", "hid", "att", "seg", "r", "pool")
    srcs = [dict(zip(names, refs[at + 8 * i : at + 8 * i + 8])) for i in range(3)]
    at += 24
    ga_o, gt_o = refs[at : at + 3], refs[at + 3 : at + 6]
    own_o, send_o, gnf_o, emb_o, pg_o = refs[at + 6 : at + 11]
    at += 11
    big = ("mid", "a", "ge")
    bufs = [dict(zip(big, refs[at + 3 * i : at + 3 * i + 3])) for i in range(3)]
    at += 9
    own, res, gyt, part, gb, n2, gg, gu, ga, att, hid, packed, gt, wh, wd, wg, wu, wo, sems, out_sems = refs[at:]
    span, width = own.shape[1:]
    length = n * span
    ff = w_gate.shape[1]
    inner = w_out.shape[0]
    head = inner // 6
    wide = w_head.shape[1]
    me, p, c = position()
    ins = Copies(sems)
    owns = []
    for i in range(3):
        row = per * p + (per - 1 if i == 2 else 2 * c + i)
        owns.append(ins.start(grad_y.at[row], own.at[i]))
    weights = {k: ins.start(a, b) for k, a, b in (("h", w_head, wh), ("d", w_down, wd))}
    for k, a, b in (("g", w_gate, wg), ("u", w_up, wu), ("o", w_out, wo)):
        weights[k] = ins.start(a, b)
    lanes = [pl.ds(i * length, length // 2 if i == 2 else length) for i in range(3)]
    loads = []
    for i in range(3):
        loads.append([ins.start(srcs[i][k], bufs[i][k]) for k in big])
    late_loads = []
    for i in range(3):
        late_loads.append(ins.start(srcs[i]["hid"], hid.at[:, lanes[i]]))
        late_loads.append(ins.start(srcs[i]["att"], att.at[:, lanes[i]]))

    def need(*names):
        for k in names:
            if k in weights:
                weights.pop(k).wait()

    for i in range(3):
        owns[i].wait()
    need("h")
    pools, cots, counts = [], [], []
    for i in range(3):
        half = i == 2
        for k, piece in enumerate((own.at[i], near.at[i], far.at[2 * i], again.at[2 * i + (not half)])):
            place = pl.multiple_of((me ^ k) * span, span)
            gyt[i, :, pl.ds(place, span)] = piece[...].T
        count = jnp.sum((srcs[i]["seg"][0:1, :] != 0.0).astype(F32), axis=1, keepdims=True)
        pool = srcs[i]["pool"][0:1, :]
        if half:
            pool = pool + pool_other[0:1, :]
        pools.append(pool / count)
        counts.append(count)
        row = per * p + (per - 1 if half else 2 * c + i)
        cots.append(eg[pl.ds(row, 1), :])
    proj = wide_dots(pools, wh[...], mm)
    g_projs = []
    for i in range(3):
        inv = lax.rsqrt(jnp.sum(proj[i] * proj[i], axis=1, keepdims=True) + EPS)
        emb = proj[i] * inv
        g_proj = inv * (cots[i] - emb * jnp.sum(emb * cots[i], axis=1, keepdims=True))
        emb_o[i] = jnp.broadcast_to(emb, emb_o.shape[1:])
        once = jnp.where(c == 0, 1.0, 0.0) if i == 2 else 1.0
        for q in range((width + wide) // 256):
            piece = pools[i][:, q * 256 : (q + 1) * 256] if q < width // 256 else g_proj[:, q * 256 - width : (q + 1) * 256 - width]
            pg_o[5 * i + q : 5 * i + q + 1, :] = piece * once
        g_projs.append(g_proj)
    g_pools = wide_dots(g_projs, wh[...], mm_nt)
    g_cols = [jnp.broadcast_to(g / k, (span, width)).T for g, k in zip(g_pools, counts)]
    need("d", "g", "u", "o")
    for copy in loads[0]:
        copy.wait()
    sizes = [length, length, length // 2]
    starts = [0, length, 2 * length]

    def outer(i, b, r):
        if i == 2:
            place = pl.ds(pl.multiple_of((c * (sizes[2] // span) + b) * span, span), span)
        else:
            place = pl.ds(b * span, span)
        valid = (srcs[i]["seg"][0:1, place] != 0.0).astype(F32)
        return gyt[i, r, place].astype(F32) + valid * g_cols[i][r, :]

    def branch(i, b):
        for r in chunks(width):
            gb[r, starts[i] + b * span : starts[i] + (b + 1) * span] = outer(i, b, r).astype(BF16)

    step = 256

    def gates(i, b):
        cs, ls = slice(b * step, (b + 1) * step), slice(starts[i], starts[i] + sizes[i])
        g_hid = mm(wd[cs, :], gb[:, ls])
        gg[cs, ls] = (g_hid * bufs[i]["a"][cs, :].astype(F32)).astype(BF16)
        gu[cs, ls] = (g_hid * bufs[i]["ge"][cs, :].astype(F32)).astype(BF16)

    def normed(i):
        ls = slice(starts[i], starts[i] + sizes[i])
        res[i % 2, :, : sizes[i]] = mm(wg[...], gg[:, ls]) + mm(wu[...], gu[:, ls])

    def norm(i, b):
        mid, ds = bufs[i]["mid"], res.at[i % 2]
        bs = slice(b * span, (b + 1) * span)
        ls = slice(starts[i] + b * span, starts[i] + (b + 1) * span)
        sq = cross = None
        for r in chunks(width):
            m = mid[r, bs]
            t = fold(m * m, jnp.add)
            u = fold(ds[r, bs] * nffn[r, :] * m, jnp.add)
            sq, cross = (t, u) if sq is None else (sq + t, cross + u)
        inv2 = lax.rsqrt(jnp.sum(sq, axis=0, keepdims=True) / width + EPS)
        mean = inv2 * jnp.sum(cross, axis=0, keepdims=True) / width
        for r in chunks(width):
            hat = mid[r, bs] * inv2
            n2[r, ls] = (hat * nffn[r, :]).astype(BF16)
            gn = ds[r, bs]
            if i == 0 and b == 0:
                part[r, :] = gn * hat
            else:
                part[r, :] += gn * hat
            ga[r, ls] = (outer(i, b, r) + inv2 * (gn * nffn[r, :] - hat * mean)).astype(BF16)

    def attended(i):
        ls = slice(starts[i], starts[i] + sizes[i])
        gatt = mm(wo[...], ga[:, ls]).astype(BF16).astype(F32)
        for h in range(6):
            hs = slice(h * head, (h + 1) * head)
            gt[hs, ls] = (gatt[hs, :] * srcs[i]["r"][h : h + 1, :]).astype(BF16)

    def store(at, value):
        rows = value.shape[0] // 2
        for side in range(2):
            packed[side, :, at : at + value.shape[1]] = value[side * rows : (side + 1) * rows].astype(BF16)

    outs = Copies(out_sems)
    pending = []

    def send(lo, hi):
        pending.append(outs.start(packed.at[c, :, pl.ds(lo, hi - lo)], own_o.at[:, pl.ds(lo, hi - lo)]))
        pending.append(outs.start(packed.at[1 - c, :, pl.ds(lo, hi - lo)], send_o.at[:, pl.ds(lo, hi - lo)]))

    blocks = [k // span for k in sizes]
    for b in range(blocks[0]):
        branch(0, b)
    for b in range(ff // step):
        gates(0, b)
    for i in (1, 2):
        for copy in loads[i]:
            copy.wait()
    normed(0)
    for b in range(blocks[1]):
        branch(1, b)
    for b in range(ff // step):
        gates(1, b)
        norm(0, b)
    normed(1)
    attended(0)
    for b in range(blocks[2]):
        branch(2, b)
    for b in range(ff // step):
        gates(2, b)
        norm(1, b)
    normed(2)
    attended(1)
    for copy in late_loads:
        copy.wait()
    top = 2 * ff
    for b in range(2):
        store(top + b * width, mm_nt(hid[b * width : (b + 1) * width, :], gb[...]))
        norm(2, b)
    attended(2)
    for i in range(3):
        ls = pl.ds(starts[i], sizes[i])
        pending.append(outs.start(ga.at[:, ls], ga_o[i]))
        pending.append(outs.start(gt.at[:, ls], gt_o[i]))
    send(top, top + 2 * width)
    for b in range(2):
        cs = slice(b * 512, (b + 1) * 512)
        store(b * 512, mm_nt(n2[...], gg[cs, :]))
    send(0, ff)
    for b in range(2):
        cs = slice(b * 512, (b + 1) * 512)
        store(ff + b * 512, mm_nt(n2[...], gu[cs, :]))
    store(top + 2 * width, mm_nt(ga[...], att[...]))
    gnf_o[...] = jnp.broadcast_to(col_sum(part[...].T), gnf_o.shape)
    pg_o[15:16, :] = jnp.zeros((1, 256), F32)
    send(ff, 2 * ff)
    send(top + 2 * width, top + 2 * width + inner)
    for copy in pending:
        copy.wait()


def attention_back(core, n, q_nat, v_nat, kt, e_wait, e_b, att, gt, gs, table, kv_side, line, gq_o, put_kv):
    heads = e_b.shape[0]
    inner = kt.shape[0]
    head = inner // heads
    length = kt.shape[1]
    half = core is not None
    nq = length // 2 if half else length
    lane = lax.broadcasted_iota(jnp.int32, (length, LANES), 1)
    gt_nat = gt[...].T
    zeros = jnp.zeros((head, nq), BF16)
    width = 4 * LANES
    table[:, :, :LANES] = jnp.zeros((2, LANES, LANES), F32)

    def scores(h, a, rhs, delta, far, seen):
        ps = slice(h // 2 * LANES, (h // 2 + 1) * LANES)
        ks = slice(a * LANES, (a + 1) * LANES)
        g_s = e_b[h, ks, :].astype(F32) * (mm(v_nat[ks, ps], rhs) - delta)
        gs[h % 2, ks, :nq] = g_s.astype(BF16)
        t = table.at[h % 2]
        for b in range(nq // LANES):
            blk = g_s[:, b * LANES : (b + 1) * LANES]
            d = (2 * core if half else 0) + b - a
            if abs(d) <= 1:
                at = (d + 2) * LANES
                if d in seen:
                    t[:, at : at + LANES] += blk
                else:
                    t[:, at : at + LANES] = blk
                    seen.add(d)
            else:
                far[d < 0].append(fold(blk, jnp.add))

    def lines(h, far):
        t = table.at[h % 2]
        line(h, slice(LANES, LANES + width), diagonal_sums(t))
        if far[0]:
            line(h, slice(6 * LANES, 7 * LANES), jnp.sum(sum(far[0]), axis=0, keepdims=True))
        if far[1]:
            line(h, slice(0, LANES), jnp.sum(sum(far[1]), axis=0, keepdims=True))

    def weigh(h, which):
        hs, ps = slice(h * head, (h + 1) * head), slice(h // 2 * LANES, (h // 2 + 1) * LANES)
        g = gs.at[h % 2]
        if which == 0:
            gq_o[hs, :] = mm(kt[hs, :], g[:, :nq]).astype(BF16)
            return
        value = mm(g[:, :nq], q_nat[:, ps]) if which == 1 else mm(e_b[h], gt_nat[:, ps])
        if h % 2 == 0:
            kv_side[which - 1] = value
        else:
            put_kv(h // 2, which - 1, jnp.where(lane < head, kv_side[which - 1], value).astype(BF16).T)

    old = None
    for h in range(heads + 1):
        far = [[], []]
        if h < heads:
            if h % 2 == 0:
                e_wait(h // 2)
            hs = slice(h * head, (h + 1) * head)
            g_h = gt[hs, :]
            delta = col_sum(g_h.astype(F32) * att[hs, :].astype(F32))
            rhs = jnp.concatenate([g_h, zeros] if h % 2 == 0 else [zeros, g_h], axis=0)
            seen = set()
        for a in range(n):
            if h < heads:
                scores(h, a, rhs, delta, far, seen)
            if h > 0:
                if a < 3:
                    weigh(h - 1, a)
                else:
                    lines(h - 1, old)
        old = far


def half_back_kernel(n, q_nat, v_nat, kt, e_in, att, gt, gq_o, keep_o, send_o, line_o, e_b, gs, table, kv_side, kv, sems):
    ins = Copies(sems)
    loads = [ins.start(e_in.at[pl.ds(0, 2)], e_b.at[pl.ds(0, 2)])]
    yield
    loads += [ins.start(e_in.at[pl.ds(h, 2)], e_b.at[pl.ds(h, 2)]) for h in range(2, e_in.shape[0], 2)]
    inner = kt.shape[0]

    def put(pair, which, value):
        kv[which * inner + pair * LANES : which * inner + (pair + 1) * LANES, :] = value.astype(BF16)

    def line(h, lanes, value):
        line_o[h : h + 1, lanes] = value

    line_o[...] = jnp.zeros_like(line_o)
    _, _, c = position()
    for core in range(2):

        @pl.when(c == core)
        def _(core=core):
            attention_back(
                core, n, q_nat, v_nat, kt, lambda p: loads[p].wait(), e_b, att, gt, gs, table, kv_side, line, gq_o, put
            )

    nq = kt.shape[1] // 2
    keep_o[...] = kv[:, pl.ds(pl.multiple_of(c * nq, nq), nq)]
    send_o[...] = kv[:, pl.ds(pl.multiple_of((1 - c) * nq, nq), nq)]


def backward_kernel(
    slot, n,
    q_nat, v_nat, kt, e_in, att, gt, line_in, xt, ga, w_query, w_key, w_value, nattn, emb, part_in, *refs,
):
    if slot:
        gq0, gq_half, keep, got, n1_0, n1_1, n1_2, own_o, send_o, gq2, *refs = refs
        *refs, m0, m1, m2, g0, packed = refs
    line_o, gq_o, b_own, b_c, b_y, part_o, gq, e_b, gs, table, kv_side, res, xb, gb, wb, part, sems = refs
    ins = Copies(sems)
    loads = [ins.start(e_in.at[pl.ds(0, 2)], e_b.at[pl.ds(0, 2)])]
    yield
    loads += [ins.start(e_in.at[pl.ds(h, 2)], e_b.at[pl.ds(h, 2)]) for h in range(2, e_in.shape[0], 2)]
    more = [ins.start(a, b) for a, b in ((xt, xb), (ga, gb))]
    more += [ins.start(w, wb.at[:, pl.ds(i * w.shape[1], w.shape[1])]) for i, w in enumerate((w_query, w_key, w_value))]
    if slot:
        more += [ins.start(a, b) for a, b in ((gq0, g0), (n1_0, m0), (n1_1, m1), (n1_2, m2))]
    inner = kt.shape[0]

    def put(pair, which, value):
        at = (1 + which) * inner + pair * LANES
        gq[at : at + LANES, :] = value.astype(BF16)

    def line(h, lanes, value):
        line_o[h : h + 1, lanes] = line_in[h : h + 1, lanes] + value

    line_o[...] = line_in[...]
    if slot:
        gq2[:inner, :] = gq_half[...]
        gq2[inner:, :] = (keep[...].astype(F32) + got[...].astype(F32)).astype(BF16)
    attention_back(
        None, n, q_nat, v_nat, kt, lambda p: loads[p].wait(), e_b, att, gt, gs, table, kv_side, line, gq.at[:inner, :], put
    )
    for copy in more:
        copy.wait()
    if slot:
        part[...] = part_in[...]
        _, _, c = position()
    span = b_own.shape[1] - EXT

    def late_sums(b):
        lo, hi = b * 256, (b + 1) * 256 if b < 3 else 3 * inner
        cs = slice(lo, hi)
        value = mm_nt(m0[...], g0[cs, :]) + mm_nt(m1[...], gq[cs, :]) + mm_nt(m2[...], gq2[cs, :])
        rows = own_o.shape[0]
        for side in range(2):
            packed[side, :, cs] = value[side * rows : (side + 1) * rows].astype(BF16)

    input_rows(
        slot, False, gq, xb, gb, wb, nattn, emb, res, part, (b_own.at[0], b_c.at[0], b_y.at[0], b_y.at[1]), span,
        late_sums if slot else None,
    )
    part_o[...] = part[...]
    outs = [ins.start(gq, gq_o)]
    if slot:
        outs += [ins.start(packed.at[c], own_o), ins.start(packed.at[1 - c], send_o)]
    for copy in outs:
        copy.wait()


def input_rows(slot, half, gq, xt, ga, w_qkv, nattn, emb, res, part, outs, span, between=None):
    width, nq = res.shape[0], gq.shape[1]
    res[:, :nq] = mm(w_qkv[...], gq[...])
    for b in range(nq // span):
        bs = slice(b * span, (b + 1) * span)
        sq = cross = None
        for r in chunks(width):
            x = xt[r, bs].astype(F32)
            t = fold(x * x, jnp.add)
            u = fold(res[r, bs] * nattn[r, :] * x, jnp.add)
            sq, cross = (t, u) if sq is None else (sq + t, cross + u)
        inv = lax.rsqrt(jnp.sum(sq, axis=0, keepdims=True) / width + EPS)
        mean = inv * jnp.sum(cross, axis=0, keepdims=True) / width
        for r in chunks(width):
            hat = xt[r, bs].astype(F32) * inv
            gn = res[r, bs]
            if slot == 0 and b == 0:
                part[r, :] = gn * hat
            else:
                part[r, :] += gn * hat
            res[r, bs] = ga[r, bs].astype(F32) + inv * (gn * nattn[r, :] - hat * mean)
        if between is not None:
            between(b)
    send_blocks(half, res, outs, span)
    row = emb[slot, 0:1, :]
    high = row.astype(BF16).astype(F32)
    rest = jnp.zeros((1, 2 * width - row.shape[1]), F32)
    at = lax.broadcasted_iota(jnp.int32, (EXT, width), 0)
    lines = jnp.zeros((EXT, width), F32)
    for i, v in enumerate((high, row - high)):
        lines = jnp.where(at == 2 * i, v[:, :width], lines)
        lines = jnp.where(at == 2 * i + 1, jnp.concatenate([v[:, width:], rest], axis=1), lines)
    for out in outs:
        out[span:, :] = lines.astype(BF16)


def inputs_kernel(
    gq, xt, ga, w_query, w_key, w_value, nattn, emb, part_in, line_in, gnf, indicator,
    b_own, b_c, b_y, small,
    res, part, w_qkv,
):
    small[...] = jnp.zeros_like(small)
    part[...] = part_in[...]
    for i, w in enumerate((w_query, w_key, w_value)):
        w_qkv[:, i * w.shape[1] : (i + 1) * w.shape[1]] = w[...]
    width = res.shape[0]
    span = b_own.shape[1] - EXT
    input_rows(2, True, gq, xt, ga, w_qkv, nattn, emb, res, part, (b_own.at[0], b_c.at[0], b_y.at[0], b_y.at[1]), span)
    gna = col_sum(part[...].T)
    for i in range(width // LANES):
        small[i : i + 1, :] = gnf[0:1, i * LANES : (i + 1) * LANES]
        small[4 + i : 5 + i, :] = gna[:, i * LANES : (i + 1) * LANES]
    lines = line_in[...]
    hi = lines.astype(BF16)
    lo = (lines - hi.astype(F32)).astype(BF16)
    small[8:16, :] = mm_nt(hi, indicator[...]) + mm_nt(lo, indicator[...])


def unpack_kernel(per, with_emb, *refs):
    groups = (len(refs) - 1 - (3 if with_emb else 1)) // 4
    out = refs[4 * groups]
    sems = refs[-1]
    ways = []
    for g in range(groups):
        own, c1, y, d = refs[4 * g : 4 * g + 4]
        ways += [(own.at[i], c1.at[i], y.at[2 * i], d.at[2 * i + 1]) for i in range(own.shape[0])]
    own0 = ways[0][0]
    me, p, _ = position()
    rows, span, width = out.shape
    for r in range(rows):
        pair, j = divmod(r, per)
        slot = 2 if j == per - 1 else j % 2
        core = p if slot == 2 else j // 2
        k = me ^ (pair * 2 + core)
        for which in range(4):
            ref = ways[slot][which]

            @pl.when(k == which)
            def _(ref=ref, r=r):
                pltpu.make_async_copy(ref.at[pl.ds(0, span)], out.at[r], sems.at[r]).start()
                if with_emb:
                    pltpu.make_async_copy(ref.at[pl.ds(span, EXT)], refs[4 * groups + 2].at[r], sems.at[rows + r]).start()

    if with_emb:
        emb, got = refs[4 * groups + 1 : 4 * groups + 3]
        for r in range(rows):
            pltpu.make_async_copy(own0.at[pl.ds(span, EXT)], got.at[r], sems.at[rows + r]).wait()
            value = got[r].astype(F32)
            emb[r : r + 1, :width] = value[0:1, :] + value[2:3, :]
            emb[r : r + 1, width:] = (value[1:2, :] + value[3:4, :])[:, : emb.shape[1] - width]
    for r in range(rows):
        pltpu.make_async_copy(own0.at[pl.ds(0, span)], out.at[r], sems.at[r]).wait()


def place(step):
    if step is None:
        return 0, 1
    axis, stride, radix = step
    return (lax.axis_index(axis) // stride) % radix, radix


def combine_kernel(plan, *refs):
    at = sum(len(arrays) for pieces, _ in plan for arrays, _, _ in pieces)
    outs = at + sum(place(step)[1] for _, step in plan)
    ins, at, scratch = 0, at, outs
    for pieces, step in plan:
        off = 0
        total = refs[scratch] if step else refs[at]
        for arrays, lo, hi in pieces:
            value = sum(refs[ins + i][..., lo:hi].astype(F32) for i in range(len(arrays)))
            ins += len(arrays)
            total[..., off : off + hi - lo] = value.astype(BF16)
            off += hi - lo
        if step:
            d, radix = place(step)
            for k in range(radix):
                refs[at + k][...] = total[d ^ k]
            at += radix
            scratch += 1
        else:
            at += 1


def join_kernel(plan, *refs):
    ins, at = 0, sum(place(step)[1] for step, _ in plan)
    for step, cuts in plan:
        d, radix = place(step)
        for lo, hi in cuts:
            for k in range(radix):
                refs[at][d ^ k] = refs[ins + k][:, lo:hi]
            at += 1
        ins += radix


def merge_kernel(step, cut, late_cut, own, got, late, late_got, a_o, b_o):
    d, _ = place(step)
    total = (late[...].astype(F32) + late_got[...].astype(F32)).astype(BF16)
    rows, wide = own.shape
    for src, at in ((own, d), (got, d ^ 1)):
        a_o[at, :, :cut] = src[:, :cut]
        b_o[at, :, : wide - cut] = src[:, cut:]
    for side in range(2):
        part = total[side * rows : (side + 1) * rows]
        a_o[side, :, cut:] = part[:, :late_cut]
        b_o[side, :, wide - cut :] = part[:, late_cut:]


FINISH_OUTS = 7


def finish_kernel(second, cut, block, *refs):
    if second:
        b_own, a, b, *rest = refs
        outs, rest = rest[FINISH_OUTS : 2 * FINISH_OUTS], rest[2 * FINISH_OUTS :]
        head_o, nf_o, na_o, table_o, gate, up, down, out, qkv, head, sems = rest
    else:
        a, b, *rest = refs
        outs, (gate, up, down, out, qkv, sems) = rest[:FINISH_OUTS], rest[FINISH_OUTS:]
    gate_o, up_o, down_o, out_o, *qkv_o = outs
    _, _, c = position()
    rows = a.shape[0]
    ff = gate.shape[1]
    width = gate_o.shape[0]
    inner = out.shape[0]
    rest = ff - (cut - ff)
    start = pl.multiple_of(((1 - c) if second else c) * rows, rows)
    at = pl.ds(start, rows)
    copies = Copies(sems)
    gate[...] = a[:, :ff].astype(F32)
    pending = [copies.start(gate, gate_o.at[at])]
    down[0] = b[:, rest : rest + width].astype(F32)
    pending.append(copies.start(down.at[0], down_o.at[at]))
    down[1] = b[:, rest + width : rest + 2 * width].astype(F32)
    pending.append(copies.start(down.at[1], down_o.at[pl.ds(pl.multiple_of(width + start, rows), rows)]))
    up[:, : cut - ff] = a[:, ff:cut].astype(F32)
    up[:, cut - ff :] = b[:, :rest].astype(F32)
    pending.append(copies.start(up, up_o.at[at]))
    late_a = a.shape[1] - cut
    late_b = b.shape[1] - LANES - (3 * inner - late_a)
    for i in range(3):
        lo, hi = i * inner, (i + 1) * inner
        mid = min(max(late_a, lo), hi)
        if mid > lo:
            qkv[i, :, : mid - lo] = a[:, cut + lo : cut + mid].astype(F32)
        if mid < hi:
            qkv[i, :, mid - lo :] = b[:, late_b + mid - late_a : late_b + hi - late_a].astype(F32)
        pending.append(copies.start(qkv.at[i], qkv_o[i].at[at]))
    out[...] = b[:, rest + 2 * width : rest + 2 * width + inner].astype(F32).T
    pending.append(copies.start(out, out_o.at[:, at]))
    if second:
        row = lax.broadcasted_iota(jnp.int32, (rows, 256), 0) % 16
        small = None
        for ref in (b_own, b):
            g = ref[:, late_b - 256 : late_b].astype(F32)
            turned = {t: pltpu.roll(g, rows - t, 0).astype(BF16) for t in range(1, 5)}
            for i in range(2):
                kept = jnp.where((row < 15) & (row % 5 == i), g, 0.0).T.astype(BF16)
                for j in range(3):
                    term = mm(kept, turned[2 + j - i])
                    place_ = (slice(i * 256, (i + 1) * 256), slice(j * 256, (j + 1) * 256))
                    if ref is b_own:
                        head[place_] = term
                    else:
                        head[place_] += term
            for r in range(0, rows, block):
                value = ref[r : r + 16, ref.shape[1] - LANES :].astype(F32)
                small = value if small is None else small + value
        pending.append(copies.start(head, head_o))
        for i in range(nf_o.shape[1] // LANES):
            nf_o[:, i * LANES : (i + 1) * LANES] = small[i : i + 1, :]
            na_o[:, i * LANES : (i + 1) * LANES] = small[4 + i : 5 + i, :]
        table_o[...] = small[8 : 8 + table_o.shape[0], : table_o.shape[1]]
    for copy in pending:
        copy.wait()


def sds(shape, dtype=BF16):
    return jax.ShapeDtypeStruct(shape, dtype)


def call(
    kernel, outs, args, scratch=(), specs=None, out_specs=None, flops=0, name=None, vmem=56, deps=(), aliases=None, overlap=False
):
    count, n_out = len(args), len(outs) if isinstance(outs, tuple) else 1
    specs = list(specs or [VMEM] * count)
    out_specs = list(out_specs or [VMEM] * n_out)
    out_list = list(outs) if isinstance(outs, tuple) else [outs]
    loads = [i for i in range(count) if overlap and specs[i] is VMEM]
    stores = [i for i in range(n_out) if overlap and out_specs[i] is VMEM]
    bufs = [pltpu.VMEM(args[i].shape, args[i].dtype) for i in loads] + [pltpu.VMEM(out_list[i].shape, out_list[i].dtype) for i in stores]
    if overlap:
        bufs.append(pltpu.SemaphoreType.DMA((len(loads) + len(stores),)))

    def body(*refs):
        ins, refs = list(refs[:count]), refs[count + len(deps) :]
        res, refs = list(refs[:n_out]), refs[n_out:]
        if overlap:
            bufs_, refs = refs[: len(bufs)], refs[len(bufs) :]
            copies = Copies(bufs_[-1])
            pending = []
            for i, buf in zip(loads, bufs_):
                pending.append(copies.start(ins[i], buf))
                ins[i] = buf
            out_refs = list(res)
            for i, buf in zip(stores, bufs_[len(loads) :]):
                res[i] = buf
            run = kernel(*ins, *res, *refs)
            if run is not None:
                next(run)
            for copy in pending:
                copy.wait()
            if run is not None:
                next(run, None)
        else:
            kernel(*ins, *res, *refs)
        if overlap:
            pending = [copies.start(res[i], out_refs[i]) for i in stores]
            for copy in pending:
                copy.wait()

    if overlap:
        specs = [ANY if s is VMEM else s for s in specs]
        out_specs = [ANY if s is VMEM else s for s in out_specs]
    return pl.pallas_call(
        body,
        out_shape=outs,
        in_specs=specs + [ANY] * len(deps),
        out_specs=tuple(out_specs) if isinstance(outs, tuple) else out_specs[0],
        scratch_shapes=bufs + list(scratch),
        compiler_params=pltpu.CompilerParams(vmem_limit_bytes=vmem * 2**20),
        cost_estimate=pl.CostEstimate(flops=flops, bytes_accessed=10_000_000, transcendentals=0),
        input_output_aliases=aliases or {},
        name=name,
    )(*args, *deps)


def swap(x, axis, k):
    n = lax.axis_size(axis)
    return lax.ppermute(x, axis, [(i, i ^ k) for i in range(n)])


def after(x, *deps):
    return lax.optimization_barrier((x, *deps))[0]


def together(*trees):
    leaves, shape = jax.tree.flatten(trees)
    return jax.tree.unflatten(shape, lax.optimization_barrier(leaves))


def row_digits():
    return [("rows", 1 << i, 2) for i in range(lax.axis_size("rows").bit_length() - 1)]


def shards(
    tokens, seg_ids, w_query, w_key, w_value, w_out, w_gate, w_up, w_down, w_head, norm_attn, norm_ffn,
    bucket_bias_table, grad_y, embedding_gradient,
):
    rows, span, width = tokens.shape
    buckets, heads = bucket_bias_table.shape
    n = lax.axis_size("seq")
    inner = w_query.shape[1]
    ff = w_gate.shape[1]
    wide = w_head.shape[1]
    length = n * span
    per = rows // 2
    assert n == 4 and per == 5
    slots = 3

    groups = ((0,), (1, 2))
    shapes = [(k, span + EXT, width) for slots in groups for k in (2 * len(slots) - (2 in slots), len(slots))]
    todo = sum(k for k, _, _ in shapes)
    y_a, c_a, y_b, c_b = call(
        functools.partial(pack_kernel, per, groups, EXT), tuple(sds(k) for k in shapes), (tokens, seg_ids),
        [pltpu.VMEM((todo, span + EXT, width), BF16), pltpu.SemaphoreType.DMA((2 * todo,))], [ANY, VMEM], (ANY,) * 4,
        vmem=60, name="pack", overlap=True,
    )

    def pass_on(got, *deps):
        near, far = got
        return near, far, swap(after(far, *deps) if deps else far, "seq", 1)

    line = 2 * length
    x_a = swap(c_a, "seq", 1), swap(y_a, "seq", 2)
    bias, ind, nattn, nffn, wqkv_t, wout_t, wg_t, wu_t, wd_t = call(
        functools.partial(prepare_kernel, n),
        (
            sds((heads, LANES, line), F32), sds((LANES, line)), sds((width, LANES), F32), sds((width, LANES), F32),
            sds((3 * inner, width)), sds((width, inner)), sds((ff, width)), sds((ff, width)),
            sds((width, ff)),
        ),
        (
            bucket_bias_table.T, norm_attn[None], norm_ffn[None], w_query, w_key, w_value, w_out, w_gate, w_up, w_down,
        ),
        [pltpu.VMEM((LANES, LANES), F32)], name="prepare", flops=4_000_000_000, overlap=True,
    )
    x_a, y_b, c_b, nattn = together(x_a, y_b, c_b, nattn)
    x_b = swap(c_b, "seq", 1), swap(y_b, "seq", 2)
    x_a = pass_on(x_a)

    def collect(own, c, y):
        return own, swap(c, "seq", 1), swap(y, "seq", 2)

    def collect_rest(part, *deps):
        return *part, swap(after(part[2], *deps), "seq", 1)

    def run_forward(kinds, pieces, before=(), deps=()):
        shapes = [s for _, half in kinds for s in forward_outs(half, n, span, width, inner, heads, ff)]
        had = len(before) and before[0].shape[0]
        shapes += [((k * (len(kinds) + had), span, width), BF16) for k in (1, 1, 2)]
        if not had:
            shapes += [((2 * slots - 1, span, width), BF16), ((slots, span, width), BF16)]
        outs = tuple(sds(*s) for s in shapes)
        args = [tokens, seg_ids, bias, wqkv_t, wout_t, wg_t, wu_t, wd_t, nattn, nffn]
        specs = [ANY, VMEM] + [ANY] * 6 + [VMEM] * 2
        args += [*pieces, *(before or (grad_y,))]
        specs += [VMEM] * 3 + [ANY] * (3 if had else 1)
        scratch = [pltpu.VMEM(*s) for s in shapes]
        scratch += [
            pltpu.VMEM((len(kinds), span, width), BF16), pltpu.VMEM((length, width), F32),
            pltpu.VMEM((len(kinds), LANES, length), F32), pltpu.VMEM((len(kinds), width, length), BF16),
            pltpu.VMEM((heads, length, 2 * LANES), BF16), pltpu.VMEM((heads, inner // heads + EXT, length), BF16),
            pltpu.VMEM((len(kinds), width, length), BF16),
            pltpu.VMEM((2, length, length), F32), pltpu.VMEM(bias.shape, F32), *[pltpu.VMEM(w.shape, BF16) for w in (wqkv_t, wout_t, wg_t, wu_t, wd_t)],
            pltpu.SemaphoreType.DMA((12 + len(kinds) + 3 * slots,)), pltpu.SemaphoreType.DMA((24 * len(kinds) + 6,)),
        ]
        res = call(
            functools.partial(forward_kernel, kinds, n, per, heads), outs, args, scratch, specs, tuple(ANY for _ in outs),
            4_000_000_000 * len(kinds), "forward", deps=deps, overlap=True,
        )
        count = len(FORWARD_OUTS)
        at = count * len(kinds)
        rows_ = [dict(zip(FORWARD_OUTS, res[i * count : (i + 1) * count])) for i in range(len(kinds))]
        return rows_, res[at : at + 3], res[at + 3 :]

    fwd, blocks, packed_g = run_forward([(0, False)], x_a, deps=(y_b, c_b))
    x_b = pass_on(x_b, fwd[0]["r"])
    gys = swap(packed_g[1], "seq", 1), swap(packed_g[0], "seq", 2)
    fwd_b, blocks, _ = run_forward([(1, False), (2, True)], x_b, blocks, deps=packed_g)
    blocks = collect(*blocks)
    fwd += fwd_b
    gys = pass_on(gys, fwd[1]["r"])
    pool_other = swap(fwd[2]["pool"], "seq", 1)

    def unpack(parts, with_emb, deps=()):
        args = [a for group in parts for a in group]
        outs = (sds((rows, span, width)),) + ((sds((rows, wide), F32),) if with_emb else ())
        scratch = [pltpu.VMEM((rows, EXT, width), BF16)] if with_emb else []
        return call(
            functools.partial(unpack_kernel, per, with_emb), outs, args, scratch + [pltpu.SemaphoreType.DMA((2 * rows,))],
            [ANY] * len(args), (ANY, VMEM)[: len(outs)], vmem=16, name="unpack", deps=deps,
        )


    packed_w = 2 * ff + 2 * width + inner
    nqs = [length, length, length // 2]
    args = [grad_y, embedding_gradient, w_head, w_down, w_gate, w_up, w_out, nffn, pool_other]
    specs = [ANY, VMEM] + [ANY] * 5 + [VMEM] * 2
    args += list(gys)
    specs += [VMEM] * 3
    for f in fwd:
        args += [f[k] for k in ("mid", "a", "ge", "hid", "att", "seg", "r", "pool")]
        specs += [ANY] * 5 + [VMEM] * 3
    outs = tuple(
        [sds((width, q)) for q in nqs] + [sds((inner, q)) for q in nqs]
        + [sds((width // 2, packed_w))] * 2 + [sds((8, width), F32), sds((3, 8, wide), F32), sds((16, 256), F32)]
    )
    scratch = []
    for q in nqs:
        scratch += [pltpu.VMEM((width, q), F32), pltpu.VMEM((ff, q), BF16), pltpu.VMEM((ff, q), BF16)]
    total = sum(nqs)
    scratch += [
        pltpu.VMEM((3, span, width), BF16), pltpu.VMEM((2, width, length), F32), pltpu.VMEM((3, width, length), BF16),
        pltpu.VMEM((width, LANES), F32), pltpu.VMEM((width, total), BF16), pltpu.VMEM((width, total), BF16),
        pltpu.VMEM((ff, total), BF16), pltpu.VMEM((ff, total), BF16), pltpu.VMEM((width, total), BF16),
        pltpu.VMEM((inner, total), BF16), pltpu.VMEM((ff, total), BF16), pltpu.VMEM((2, width // 2, packed_w), BF16), pltpu.VMEM((inner, total), BF16),
        *[pltpu.VMEM(w.shape, BF16) for w in (w_head, w_down, w_gate, w_up, w_out)],
        pltpu.SemaphoreType.DMA((23,)), pltpu.SemaphoreType.DMA((14,)),
    ]
    m = call(functools.partial(middle_kernel, n, per), outs, args, scratch, specs, [ANY] * 8 + [VMEM] * 3, flops=15_000_000_000, name="middle", overlap=True)
    m, blocks = together(m, blocks)
    ga, gt = m[:3], m[3:6]
    own, send, gnf, emb, pg = m[6:]

    core = ("seq", 1, 2)
    far = ("seq", 2, 2)
    digits = row_digits()
    block = width // 2 // far[2]
    for d in digits:
        block //= d[2]

    def send_shares(parts, s):
        return [swap(p, s[0], k * s[1]) for k, p in enumerate(parts) if k]

    def send_all(v, s):
        return [swap(v, s[0], k * s[1]) for k in range(1, s[2])]

    def combine(groups, deps=()):
        args, outs, scratch, plan = [], [], [], []
        for pieces, step in groups:
            rows_, wide_ = pieces[0][0][0].shape[0], sum(hi - lo for _, lo, hi in pieces)
            radix = step[2] if step else 1
            shape = (radix, rows_ // radix) if step else (rows_,)
            for arrays, _, _ in pieces:
                args += [a.reshape(shape + a.shape[-1:]) for a in arrays]
            outs += [sds((rows_ // radix, wide_))] * radix
            scratch += [pltpu.VMEM(shape + (wide_,), BF16)] if step else []
            plan.append((pieces, step))
        plan = [([(range(len(a)), lo, hi) for a, lo, hi in pieces], step) for pieces, step in plan]
        res = call(functools.partial(combine_kernel, plan), tuple(outs), args, scratch, vmem=24, name="combine", deps=deps)
        out = []
        for _, step in plan:
            radix = step[2] if step else 1
            out.append(list(res[:radix]))
            res = res[radix:]
        return out

    def joined(groups, deps=()):
        args, outs, plan = [], [], []
        for v, got, step, cuts in groups:
            cuts = cuts or [(0, v.shape[1])]
            args += [v] + got
            outs += [sds((step[2], v.shape[0], hi - lo)) for lo, hi in cuts]
            plan.append((step, cuts))
        res = call(functools.partial(join_kernel, plan), tuple(outs), args, vmem=24, name="join", deps=deps)
        return [r.reshape(-1, r.shape[-1]) for r in res]

    def all_of(*arrays):
        return [(list(arrays), 0, arrays[0].shape[1])]

    nh = length // 2
    half = call(
        functools.partial(half_back_kernel, n),
        (sds((inner, nh)), sds((2 * inner, nh)), sds((2 * inner, nh)), sds((8, line), F32)),
        (fwd[2]["q"], fwd[2]["v"], fwd[2]["kt"], fwd[2]["e"], fwd[2]["att"], gt[2]),
        [
            pltpu.VMEM((heads, length, nh), BF16), pltpu.VMEM((2, length, nh), BF16), pltpu.VMEM((2, LANES, 4 * LANES), F32),
            pltpu.VMEM((2, length, LANES), F32), pltpu.VMEM((2 * inner, length), BF16), pltpu.SemaphoreType.DMA((heads,)),
        ],
        [VMEM] * 3 + [ANY] + [VMEM] * 2, flops=2_000_000_000, name="half_back", deps=(send,), overlap=True,
    )
    got = swap(send, "seq", 1)
    block_parts = [collect_rest(blocks)]
    half, got, block_parts = together(half, got, block_parts)
    gq_half, keep, send_kv, lines_sum = half
    got_kv = swap(send_kv, "seq", 1)
    cut = packed_w // 2 // LANES * LANES
    sa, sb = [digits[0], far], [far, digits[0]]
    pa, pb = combine([([([own, got], 0, cut)], sa[0]), ([([own, got], cut, packed_w)], sb[0])])

    piece = tuple(sds((i, span + EXT, width)) for i in (1, 1, 2))

    def run_back(j, lines_sum, part, deps, extra=()):
        f = fwd[j]
        scratch = [
            pltpu.VMEM((3 * inner, length), BF16), pltpu.VMEM((heads, length, length), BF16),
            pltpu.VMEM((2, length, length), BF16), pltpu.VMEM((2, LANES, 4 * LANES), F32), pltpu.VMEM((2, length, LANES), F32), pltpu.VMEM((width, length), F32),
            pltpu.VMEM((width, length), BF16), pltpu.VMEM((width, length), BF16), pltpu.VMEM((width, 3 * inner), BF16),
            pltpu.VMEM((width, LANES), F32), pltpu.SemaphoreType.DMA((heads // 2 + 14,)),
        ]
        late_outs = ()
        if extra:
            late_outs = (sds((width // 2, 3 * inner)), sds((width // 2, 3 * inner)), sds((3 * inner, nh)))
            scratch += [pltpu.VMEM((width, q), BF16) for q in nqs]
            scratch += [pltpu.VMEM((3 * inner, length), BF16), pltpu.VMEM((2, width // 2, 3 * inner), BF16)]
        res = call(
            functools.partial(backward_kernel, j, n),
            (*late_outs, sds((8, line), F32), sds((3 * inner, length)), *piece, sds((width, LANES), F32)),
            (f["q"], f["v"], f["kt"], f["e"], f["att"], gt[j], lines_sum, f["x"], ga[j], w_query, w_key, w_value, nattn, emb, part, *extra),
            scratch, [VMEM] * 3 + [ANY] + [VMEM] * 3 + [ANY] * 5 + [VMEM] * 3 + ([ANY] + [VMEM] * 3 + [ANY] * 3 if extra else []),
            ([ANY] * 2 + [VMEM] if extra else []) + [VMEM, ANY] + [VMEM] * 4, flops=4_000_000_000, name="backward", deps=deps, overlap=True,
        )
        late, (line_o, gq, *blocks, part) = res[: len(late_outs)], res[len(late_outs) :]
        return line_o, gq, blocks, part, late

    back = run_back(0, lines_sum, nattn, (pa[1], pb[1]))
    ra, rb = send_shares(pa, sa[0]), send_shares(pb, sb[0])
    back, ra, rb, got_kv = together(back, ra, rb, got_kv)
    pa, pb = combine([(all_of(pa[0], *ra), sa[1]), (all_of(pb[0], *rb), sb[1])])
    back2 = run_back(
        1, back[0], back[3], (pa[1], pb[1]), (back[1], gq_half, keep, got_kv, *[f["n1"] for f in fwd])
    )
    ra, rb = send_shares(pa, sa[1]), send_shares(pb, sb[1])
    back2, ra, rb = together(back2, ra, rb)
    late_own, late_send, gq2 = back2[4]

    late_got, x_a_near = swap(late_send, "seq", 1), swap(back[2][1], "seq", 1)
    (parts,) = combine([(all_of(pa[0], *ra) + all_of(pb[0], *rb), digits[1])])
    z_got = send_shares(parts, digits[1])
    late_got, x_a_near = together(late_got, x_a_near)
    x_b = collect(*back2[2])
    late_cut = 2 * inner
    la, lb = combine([([([late_own, late_got], 0, late_cut)], sa[0]), ([([late_own, late_got], late_cut, 3 * inner)], sb[0])])
    lga, lgb = send_shares(la, sa[0]), send_shares(lb, sb[0])
    late_sends = (la[1], lb[1])
    for step in digits[2:]:
        (parts,) = combine([(all_of(parts[0], *z_got), step)], deps=late_sends)
        z_got = send_shares(parts, step)
        late_sends = ()
    lga, lgb = together(lga, lgb)
    la, lb = combine([(all_of(la[0], *lga), sa[1]), (all_of(lb[0], *lgb), sb[1])])
    lga, lgb = send_shares(la, sa[1]), send_shares(lb, sb[1])
    *x_c, small = call(
        inputs_kernel, (*piece, sds((width // 8, LANES), F32)),
        (gq2, fwd[2]["x"], ga[2], w_query, w_key, w_value, nattn, emb, back2[3], back2[0], gnf, ind),
        [pltpu.VMEM((width, nh), F32), pltpu.VMEM((width, LANES), F32), pltpu.VMEM((width, 3 * inner), BF16)],
        flops=3_000_000_000, name="inputs", vmem=16,
        deps=tuple(parts[1:]) + (la[1], lb[1]),
    )
    pg_b = pg.astype(BF16).reshape(block, -1)
    ((ab,),) = combine([(all_of(parts[0], *z_got) + all_of(pg_b), None)], deps=(la[1], lb[1]))
    ab_got = send_all(ab, digits[-1])
    lga, lgb, x_c, small, x_b = together(lga, lgb, x_c, small, x_b)
    x_a = back[2][0], x_a_near, swap(back[2][2], "seq", 2)
    x_c = collect(*x_c)
    ((late,),) = combine([(all_of(la[0], *lga) + all_of(lb[0], *lgb) + all_of(small), None)], deps=(ab,))
    strides = digits[1:]
    for step, back_step in zip(strides[:-1], strides[:0:-1]):
        late_got = swap(late, *step[:2])
        x_b = collect_rest(x_b) if len(x_b) == 3 else x_b
        ((late,),) = combine([(all_of(late, late_got), None)])
        (ab,) = joined([(ab, ab_got, back_step, None)], deps=(late,))
        ab_got = send_all(ab, digits[digits.index(back_step) - 1])
    late_got = swap(late, *strides[-1][:2])
    (block_out,) = unpack(block_parts, False, deps=(late,))
    late_got, ab_got, block_out, x_a, x_b, x_c = together(late_got, ab_got, block_out, x_a, x_b, x_c)
    wide_a, wide_b = cut + late_cut, ab.shape[1] - cut + late.shape[1] - late_cut
    a, b = call(
        functools.partial(merge_kernel, digits[1], cut, late_cut),
        (sds((2, ab.shape[0], wide_a)), sds((2, ab.shape[0], wide_b))), (ab, *ab_got, late, late_got), vmem=24, name="merge",
    )
    a, b = a.reshape(-1, wide_a), b.reshape(-1, wide_b)
    ga_, gb_ = send_all(a, sa[1]), send_all(b, sb[1])
    x_a = collect_rest(x_a)
    x_c = collect_rest(x_c)
    ga_, gb_, x_a, x_c = together(ga_, gb_, x_a, x_c)
    a, b = joined([(a, ga_, sa[1], None), (b, gb_, sb[1], None)])
    ga_, gb_ = send_all(a, sa[0]), send_all(b, sb[0])
    grad_x, embedding = unpack([x_a, x_b, x_c], True, deps=(a, b))
    ga_, gb_, grad_x = together(ga_, gb_, grad_x)
    a, b = joined([(a, ga_, sa[0], None), (b, gb_, sb[0], None)])
    a_got, b_got = swap(a, "seq", 1), swap(b, "seq", 1)
    outs = (
        sds((width, ff), F32), sds((width, ff), F32), sds((ff, width), F32), sds((inner, width), F32),
        *[sds((width, inner), F32)] * 3,
    )
    halves = [
        pltpu.VMEM((width // 2, ff), F32), pltpu.VMEM((width // 2, ff), F32), pltpu.VMEM((2, width // 2, width), F32),
        pltpu.VMEM((inner, width // 2), F32), pltpu.VMEM((3, width // 2, inner), F32),
    ]
    first = call(
        functools.partial(finish_kernel, False, cut, width // 8), outs, (a, b), halves + [pltpu.SemaphoreType.DMA((9,))],
        out_specs=(ANY,) * FINISH_OUTS, name="finish", vmem=24,
    )
    first, a_got, b_got = together(first, a_got, b_got)
    *grads, grad_head, grad_norm_ffn, grad_norm_attn, grad_table = call(
        functools.partial(finish_kernel, True, cut, width // 8),
        outs + (sds((width, wide), F32), sds((1, width), F32), sds((1, width), F32), sds((heads, buckets), F32)),
        (b, a_got, b_got, *first), halves + [pltpu.VMEM((width, wide), F32), pltpu.SemaphoreType.DMA((9,))],
        [VMEM] * 3 + [ANY] * FINISH_OUTS, (ANY,) * (FINISH_OUTS + 1) + (VMEM,) * 3, name="finish", vmem=24,
        aliases={3 + i: i for i in range(FINISH_OUTS)},
    )
    if block != 16:
        lo, hi = packed_w - cut, ab.shape[1] - cut
        pg_all = jnp.concatenate([b[:, lo:hi], b_got[:, lo:hi]]).reshape(-1, 16, 256)[:, :15].reshape(-1, width + wide)
        grad_head = lax.dot_general(
            pg_all[:, :width], pg_all[:, width:], (((0,), (0,)), ((), ())), preferred_element_type=F32
        )
    grad_gate, grad_up, grad_down, grad_out, grad_query, grad_key, grad_value = grads
    return (
        block_out, embedding, grad_x, grad_query, grad_key, grad_value, grad_out, grad_gate, grad_up, grad_down, grad_head,
        grad_norm_attn[0], grad_norm_ffn[0], grad_table.T,
    )


def solution(mesh):
    by_pos = P("rows", "seq", None)
    by_row = P("rows", None)
    return jax.shard_map(
        shards,
        mesh=mesh,
        in_specs=(by_pos, P("rows", "seq"), *[P()] * 11, by_pos, by_row),
        out_specs=(by_pos, by_row, by_pos, *[P()] * 11),
        check_vma=False,
    )
```
